32 devices in a mesh: dp: 4 (over z), fsdp: 8 (over y, x, core).
Axes of the slice: x: 2, y: 2, z: 4, core: 2. Of those that a mesh axis runs over, the one named last changes fastest.
Arguments:
- windows: float32 [27648, 3600], P(('dp', 'fsdp')), may hold values from -6 to 6
- targets: float32 [27648, 720], P(('dp', 'fsdp')), may hold values from -24 to 24
- horizon: int32 [27648], P(('dp', 'fsdp')), may hold values from 96 to 720, as said below
- step_count: int32 [1], replicated, may hold values from 2 to 20
- first_w: float32 [4950, 512], P(None, 'fsdp'), may hold values from -0.1875 to 0.1875
- first_w_avg: float32 [4950, 512], P(None, 'fsdp'), may hold values from -5.722046e-06 to 5.722046e-06
- first_w_sq: float32 [4950, 512], P(None, 'fsdp'), may hold values from 1.1100048e-14 to 4.4400193e-14
- hidden_w: float32 [3, 3, 512, 512], P(None, None, 'fsdp'), may hold values from -0.375 to 0.375
- hidden_w_avg: float32 [3, 3, 512, 512], P(None, None, 'fsdp'), may hold values from -5.722046e-06 to 5.722046e-06
- hidden_w_sq: float32 [3, 3, 512, 512], P(None, None, 'fsdp'), may hold values from 1.1100048e-14 to 4.4400193e-14
- back_w: float32 [2, 512, 3600], P(None, 'fsdp'), may hold values from -0.375 to 0.375
- back_w_avg: float32 [2, 512, 3600], P(None, 'fsdp'), may hold values from -5.722046e-06 to 5.722046e-06
- back_w_sq: float32 [2, 512, 3600], P(None, 'fsdp'), may hold values from 1.1100048e-14 to 4.4400193e-14
- fore_w: float32 [512, 810], P('fsdp'), may hold values from -0.09375 to 0.09375
- fore_w_avg: float32 [512, 810], P('fsdp'), may hold values from -5.722046e-06 to 5.722046e-06
- fore_w_sq: float32 [512, 810], P('fsdp'), may hold values from 1.1100048e-14 to 4.4400193e-14
- bias_vec: float32 [14154], replicated, may hold values from -1.5 to 1.5
- bias_avg: float32 [14154], replicated, may hold values from -2.2888184e-05 to 2.2888184e-05
- bias_sq: float32 [14154], replicated, may hold values from 1.7760077e-13 to 7.104031e-13
Outputs:
- loss: float32 [], replicated
- grad_norm: float32 [], replicated
- new_first_avg: float32 [4950, 512], P(None, 'fsdp')
- new_first_sq: float32 [4950, 512], P(None, 'fsdp')
- new_first_w: float32 [4950, 512], P(None, 'fsdp')
- new_hidden_avg: float32 [3, 3, 512, 512], P(None, None, 'fsdp')
- new_hidden_sq: float32 [3, 3, 512, 512], P(None, None, 'fsdp')
- new_hidden_w: float32 [3, 3, 512, 512], P(None, None, 'fsdp')
- new_back_avg: float32 [2, 512, 3600], P(None, 'fsdp')
- new_back_sq: float32 [2, 512, 3600], P(None, 'fsdp')
- new_back_w: float32 [2, 512, 3600], P(None, 'fsdp')
- new_fore_avg: float32 [512, 810], P('fsdp')
- new_fore_sq: float32 [512, 810], P('fsdp')
- new_fore_w: float32 [512, 810], P('fsdp')
- new_bias_avg: float32 [14154], replicated
- new_bias_sq: float32 [14154], replicated
- new_bias_vec: float32 [14154], replicated
- first_copy: bfloat16 [4950, 512], P(None, 'fsdp')
- hidden_copy: bfloat16 [3, 3, 512, 512], P(None, None, 'fsdp')
- back_copy: bfloat16 [2, 512, 3600], P(None, 'fsdp')
- fore_copy: bfloat16 [512, 810], P('fsdp')
The draws below stay inside these ranges and needn't reach their ends.
Inputs may be any that keep to these rules, and one draw needn't show every extreme that they name: Each horizon is 96, 336 or 720.
All inputs are finite; a program needn't handle non-finite values.
Results may differ from the reference program's by a relative error of at most 0.006.
Values may be sent and summed in bfloat16 or wider, within the bound.
A program may use at most 256 MiB of HBM per device.

```python
import math
import jax
import jax.numpy as jnp
import numpy as np
from jax import lax

L = 3600
H = 720
WIDTH = 512
ROWS = 27648
P_ALL = 4950
F_ALL = 810
NBIAS = 14154
NPARAM = 9008970


def draw_horizon(key, part):
    pick_key, coin_key = jax.random.split(key, 2)
    position = jnp.arange(ROWS, dtype=jnp.int32)
    tier_index = position * 3 // ROWS
    random_tier = jax.random.randint(pick_key, (ROWS,), 0, 3)
    coin_flip = jax.random.randint(coin_key, (ROWS,), 0, 4)
    tier_index = jnp.where(coin_flip == 0, random_tier, tier_index)
    tier_index = tier_index.at[0].set(2)
    tier_index = tier_index.at[ROWS - 1].set(0)
    lengths_table = jnp.array([H * 2 // 15, H * 7 // 15, H], jnp.int32)
    return lengths_table[tier_index]


def draw_targets(key, part):
    key = jax.random.fold_in(key, 11)
    scale_key, value_key = jax.random.split(key, 2)
    row_log = jax.random.uniform(scale_key, (ROWS, 1), jnp.float32, jnp.log(2.0), jnp.log(4.0))
    values = jnp.clip(jax.random.normal(value_key, (ROWS, H), jnp.float32), -6.0, 6.0)
    return (jnp.exp(row_log) * values).astype(jnp.float32)


def steps_of(rng, extent, cuts, low, high):
    gain, own = 1.0, jax.random.fold_in(rng, 6)
    for dim, shards_of in cuts:
        steps = jnp.exp(jax.random.uniform(jax.random.fold_in(own, dim), (shards_of,), jnp.float32, low / len(cuts), high / len(cuts)))
        gain = gain * jnp.repeat(steps, extent[dim] // shards_of).reshape([-1 if axis == dim else 1 for axis in range(len(extent))])
    return gain


def gaussian(own_key, extent, width, reach, shards=(), kind=jnp.bfloat16):
    drawn = width * jax.random.normal(own_key, extent, jnp.float32)
    if shards:
        drawn = drawn * steps_of(own_key, extent, shards, -0.22, 0.18)
    return jnp.clip(drawn, -reach, reach).astype(kind)


def setup_inputs(seed: int = 0) -> dict:
    splits = jax.random.split(jax.random.key(seed), 20)
    windows = gaussian(splits[0], (ROWS, L), 1.0, 6.0, ((0, 32),), jnp.float32)
    targets = draw_targets(jax.random.fold_in(splits[19], 71), 0)
    horizon = draw_horizon(jax.random.fold_in(splits[19], 71), 0)
    step_count = jax.random.randint(splits[3], (1,), 2, 21).astype(jnp.int32)
    first_w = gaussian(splits[4], (P_ALL, WIDTH), (L // 4) ** -0.5, 0.1875, ((1, 8),), jnp.float32)
    first_w_avg = gaussian(splits[5], (P_ALL, WIDTH), (0.11 * 0.01 / NPARAM ** 0.5), 5.7220458984375e-06, ((1, 8),), jnp.float32)
    first_w_sq = jnp.clip(jnp.exp(math.log(4.4400193157517753e-14) - 1.3862944 * jax.random.uniform(splits[6], (P_ALL, WIDTH), jnp.float32) ** steps_of(splits[6], (P_ALL, WIDTH), ((1, 8),), -0.2, 0.2)), 1.1100048289379438e-14, 4.4400193157517753e-14)
    hidden_w = gaussian(splits[7], (3, 3, WIDTH, WIDTH), (WIDTH // 2) ** -0.5, 0.375, ((2, 8),), jnp.float32)
    hidden_w_avg = gaussian(splits[8], (3, 3, WIDTH, WIDTH), (0.11 * 0.01 / NPARAM ** 0.5), 5.7220458984375e-06, ((2, 8),), jnp.float32)
    hidden_w_sq = jnp.clip(jnp.exp(math.log(4.4400193157517753e-14) - 1.3862944 * jax.random.uniform(splits[9], (3, 3, WIDTH, WIDTH), jnp.float32) ** steps_of(splits[9], (3, 3, WIDTH, WIDTH), ((2, 8),), -0.2, 0.2)), 1.1100048289379438e-14, 4.4400193157517753e-14)
    back_w = gaussian(splits[10], (2, WIDTH, L), (WIDTH // 2) ** -0.5, 0.375, ((1, 8),), jnp.float32)
    back_w_avg = gaussian(splits[11], (2, WIDTH, L), (0.11 * 0.01 / NPARAM ** 0.5), 5.7220458984375e-06, ((1, 8),), jnp.float32)
    back_w_sq = jnp.clip(jnp.exp(math.log(4.4400193157517753e-14) - 1.3862944 * jax.random.uniform(splits[12], (2, WIDTH, L), jnp.float32) ** steps_of(splits[12], (2, WIDTH, L), ((1, 8),), -0.2, 0.2)), 1.1100048289379438e-14, 4.4400193157517753e-14)
    fore_w = gaussian(splits[13], (WIDTH, F_ALL), (8 * WIDTH) ** -0.5, 0.09375, ((0, 8),), jnp.float32)
    fore_w_avg = gaussian(splits[14], (WIDTH, F_ALL), (0.11 * 0.01 / NPARAM ** 0.5), 5.7220458984375e-06, ((0, 8),), jnp.float32)
    fore_w_sq = jnp.clip(jnp.exp(math.log(4.4400193157517753e-14) - 1.3862944 * jax.random.uniform(splits[15], (WIDTH, F_ALL), jnp.float32) ** steps_of(splits[15], (WIDTH, F_ALL), ((0, 8),), -0.2, 0.2)), 1.1100048289379438e-14, 4.4400193157517753e-14)
    bias_vec = gaussian(splits[16], (NBIAS,), 0.1, 1.5, (), jnp.float32)
    bias_avg = gaussian(splits[17], (NBIAS,), (0.44 * 0.01 / NPARAM ** 0.5), 2.288818359375e-05, (), jnp.float32)
    bias_sq = jnp.clip(jnp.exp(jax.random.uniform(splits[18], (NBIAS,), jnp.float32, math.log(1.7760077263007101e-13), math.log(7.104030905202841e-13))), 1.7760077263007101e-13, 7.104030905202841e-13)
    return {"windows": windows, "targets": targets, "horizon": horizon, "step_count": step_count, "first_w": first_w, "first_w_avg": first_w_avg, "first_w_sq": first_w_sq, "hidden_w": hidden_w, "hidden_w_avg": hidden_w_avg, "hidden_w_sq": hidden_w_sq, "back_w": back_w, "back_w_avg": back_w_avg, "back_w_sq": back_w_sq, "fore_w": fore_w, "fore_w_avg": fore_w_avg, "fore_w_sq": fore_w_sq, "bias_vec": bias_vec, "bias_avg": bias_avg, "bias_sq": bias_sq}


@jax.custom_vjp
def low(v):
    return lax.optimization_barrier(v.astype(jnp.bfloat16)).astype(jnp.float32)

@jax.custom_vjp
def low_back(v):
    return v

def low_keep(v):
    return (low(v), None)

def low_pass(kept, grad):
    return (grad,)

def back_keep(v):
    return (v, None)

def back_low(kept, grad):
    return (low(grad),)
low.defvjp(low_keep, low_pass)
low_back.defvjp(back_keep, back_low)
KERNELS = (8, 4, 1)
RATIOS = (24, 12, 1)
CLIP_MAX = 0.01
RATE = 0.02
BETA_ONE = 0.9
BETA_TWO = 0.999
EPSILON = 1e-08
DECAY = 0.01
DOT_EXACTNESS = lax.Precision.HIGHEST

def blend_coefficients(fine, coarse):
    column = np.arange(fine)
    numer = np.maximum((2 * column + 1) * coarse - fine, 0)
    lower_idx = numer // (2 * fine)
    frac = (numer - lower_idx * 2 * fine) / (2.0 * fine)
    upper_idx = np.minimum(lower_idx + 1, coarse - 1)
    matrix = np.zeros((coarse, fine), np.float32)
    matrix[lower_idx, column] += 1.0 - frac
    matrix[upper_idx, column] += frac
    return matrix

def mean_pool(values, kernel):
    if kernel == 1:
        return values
    return lax.optimization_barrier(jnp.mean(values.reshape(values.shape[0], values.shape[1] // kernel, kernel), axis=2))

def linear(inputs, weight, bias):
    return low_back(jnp.dot(low(inputs), low(weight), precision=DOT_EXACTNESS) + bias)

def block_loss(params, normed, observed_future, future_usable_flags, usable_tally):
    first_w, hidden_w, back_w, fore_w, bias_vec = params
    hidden_size = hidden_w.shape[-1]
    length = normed.shape[1]
    steps_ahead_total = observed_future.shape[1]
    residual = normed
    predicted_future = jnp.zeros(observed_future.shape, jnp.float32)
    row_start = 0
    col_start = 0
    for stack_id in range(3):
        pooled_len = length // KERNELS[stack_id]
        anchor_entries = steps_ahead_total // RATIOS[stack_id]
        hidden = jax.nn.silu(linear(mean_pool(residual, KERNELS[stack_id]), first_w[row_start:row_start + pooled_len], bias_vec[stack_id * hidden_size:(stack_id + 1) * hidden_size]))
        for layer_id in range(3):
            offset = (3 + 3 * stack_id + layer_id) * hidden_size
            hidden = jax.nn.silu(linear(hidden, hidden_w[stack_id, layer_id], bias_vec[offset:offset + hidden_size]))
        fore_start = 12 * hidden_size + 2 * length + col_start
        anchor_result = linear(hidden, fore_w[:, col_start:col_start + anchor_entries], bias_vec[fore_start:fore_start + anchor_entries])
        predicted_future = predicted_future + jnp.dot(anchor_result, jnp.asarray(blend_coefficients(steps_ahead_total, anchor_entries)), precision=DOT_EXACTNESS)
        if stack_id < 2:
            back_start = 12 * hidden_size + stack_id * length
            residual = residual - linear(hidden, back_w[stack_id], bias_vec[back_start:back_start + length])
        row_start += pooled_len
        col_start += anchor_entries
    return jnp.sum(future_usable_flags * (predicted_future - observed_future) ** 2) / usable_tally

def normalize(windows, targets):
    center = lax.optimization_barrier(jnp.mean(windows, axis=1, keepdims=True))
    spread = jnp.sqrt(lax.optimization_barrier(jnp.mean((windows - center) ** 2, axis=1, keepdims=True)) + 1e-05)
    return ((windows - center) / spread, (targets - center) / spread)

def adamw(weight, avg, square, grad, step_float):
    new_avg = BETA_ONE * avg + (1.0 - BETA_ONE) * grad
    new_sq = BETA_TWO * square + (1.0 - BETA_TWO) * grad * grad
    avg_hat = new_avg / (1.0 - BETA_ONE ** step_float)
    sq_hat = new_sq / (1.0 - BETA_TWO ** step_float)
    new_weight = weight - RATE * (avg_hat / (jnp.sqrt(sq_hat) + EPSILON) + DECAY * weight)
    return (new_avg, new_sq, new_weight)

def reference(windows, targets, horizon, step_count, first_w, first_w_avg, first_w_sq, hidden_w, hidden_w_avg, hidden_w_sq, back_w, back_w_avg, back_w_sq, fore_w, fore_w_avg, fore_w_sq, bias_vec, bias_avg, bias_sq):
    normed, observed_future = normalize(windows, targets)
    future_usable_flags = (jnp.arange(observed_future.shape[1], dtype=jnp.int32)[None, :] < horizon[:, None]).astype(jnp.float32)
    usable_tally = jnp.sum(horizon.astype(jnp.float32))
    params = (first_w, hidden_w, back_w, fore_w, bias_vec)
    rows_all = windows.shape[0]
    block = math.gcd(rows_all, 512)
    blocks = rows_all // block

    def one_block(carry, pieces):
        loss_sum, grads = carry
        value, pullback = jax.vjp(lambda weights: block_loss(weights, pieces[0], pieces[1], pieces[2], usable_tally), params)
        grad_now, = pullback(jnp.ones((), value.dtype))
        return ((loss_sum + value, jax.tree.map(jnp.add, grads, grad_now)), None)

    def split_rows(array):
        return array.reshape((blocks, block) + array.shape[1:])
    zero_array = jax.tree.map(jnp.zeros_like, params)
    (loss, grads), _ = lax.scan(one_block, (jnp.zeros((), jnp.float32), zero_array), (split_rows(normed), split_rows(observed_future), split_rows(future_usable_flags)))
    total_sq = sum((jnp.sum(grad * grad) for grad in grads))
    grad_norm = jnp.sqrt(total_sq)
    clip_factor = jnp.minimum(1.0, CLIP_MAX / grad_norm)
    step_float = step_count[0].astype(jnp.float32)
    states = ((first_w, first_w_avg, first_w_sq), (hidden_w, hidden_w_avg, hidden_w_sq), (back_w, back_w_avg, back_w_sq), (fore_w, fore_w_avg, fore_w_sq), (bias_vec, bias_avg, bias_sq))
    results = []
    for state, grad in zip(states, grads):
        results.append(adamw(state[0], state[1], state[2], grad * clip_factor, step_float))
    return (loss, grad_norm, results[0][0], results[0][1], results[0][2], results[1][0], results[1][1], results[1][2], results[2][0], results[2][1], results[2][2], results[3][0], results[3][1], results[3][2], results[4][0], results[4][1], results[4][2], results[0][2].astype(jnp.bfloat16), results[1][2].astype(jnp.bfloat16), results[2][2].astype(jnp.bfloat16), results[3][2].astype(jnp.bfloat16))
```

```python
import functools
import jax
import jax.numpy as jnp
import numpy as np
from jax import lax
from jax.experimental import pallas as pl
from jax.experimental.pallas import tpu as pltpu
from jax.sharding import PartitionSpec as P

KERNELS = (8, 4, 1)
RATIOS = (24, 12, 1)
CLIP_MAX = 0.01
RATE = 0.02
BETA_ONE = 0.9
BETA_TWO = 0.999
EPSILON = 1e-08
DECAY = 0.01
DOT_EXACTNESS = lax.Precision.HIGHEST


def blend_coefficients(fine, coarse):
    column = np.arange(fine)
    numer = np.maximum((2 * column + 1) * coarse - fine, 0)
    lower_idx = numer // (2 * fine)
    frac = (numer - lower_idx * 2 * fine) / (2.0 * fine)
    upper_idx = np.minimum(lower_idx + 1, coarse - 1)
    matrix = np.zeros((coarse, fine), np.float32)
    matrix[lower_idx, column] += 1.0 - frac
    matrix[upper_idx, column] += frac
    return matrix


def normalize(windows, targets):
    center = jnp.mean(windows, axis=1, keepdims=True)
    spread = jnp.sqrt(jnp.mean((windows - center) ** 2, axis=1, keepdims=True) + 1e-05)
    return ((windows - center) / spread, (targets - center) / spread)


def mean_pool(values, kernel):
    if kernel == 1:
        return values
    return jnp.mean(values.reshape(values.shape[0], values.shape[1] // kernel, kernel), axis=2)


def pool_back(d_pooled, kernel):
    if kernel == 1:
        return d_pooled
    spread_out = jnp.broadcast_to((d_pooled / kernel)[:, :, None], d_pooled.shape + (kernel,))
    return spread_out.reshape(d_pooled.shape[0], d_pooled.shape[1] * kernel)


def silu_slope(pre_act):
    gate = jax.nn.sigmoid(pre_act)
    return gate * (1.0 + pre_act * (1.0 - gate))


def stack_params(stack_id, gathered, bias_vec, length, steps_ahead_total):
    first_full, hidden_full, back_full, fore_full = gathered
    hidden_size = hidden_full.shape[-1]
    row_start = sum((length // KERNELS[earlier] for earlier in range(stack_id)))
    col_start = sum((steps_ahead_total // RATIOS[earlier] for earlier in range(stack_id)))
    pooled_len = length // KERNELS[stack_id]
    anchor_entries = steps_ahead_total // RATIOS[stack_id]
    layers = [
        (
            first_full[row_start : row_start + pooled_len],
            bias_vec[stack_id * hidden_size : (stack_id + 1) * hidden_size],
        )
    ]
    for layer_id in range(3):
        offset = (3 + 3 * stack_id + layer_id) * hidden_size
        layers.append((hidden_full[stack_id, layer_id], bias_vec[offset : offset + hidden_size]))
    fore_start = 12 * hidden_size + 2 * length + col_start
    fore_pair = (
        fore_full[:, col_start : col_start + anchor_entries],
        bias_vec[fore_start : fore_start + anchor_entries],
    )
    back_pair = None
    if stack_id < 2:
        back_start = 12 * hidden_size + stack_id * length
        back_pair = (back_full[stack_id], bias_vec[back_start : back_start + length])
    linear_upsample_anchors = jnp.asarray(blend_coefficients(steps_ahead_total, anchor_entries))
    return (layers, fore_pair, back_pair, linear_upsample_anchors)


def stack_forward(residual, stack_id, layers, fore_pair, back_pair, linear_upsample_anchors):
    inputs_kept = [mean_pool(residual, KERNELS[stack_id]).astype(jnp.bfloat16)]
    pre_kept = []
    for weight, bias in layers:
        pre_act = jnp.dot(inputs_kept[-1], weight, preferred_element_type=jnp.float32) + bias
        pre_kept.append(pre_act)
        inputs_kept.append(jax.nn.silu(pre_act).astype(jnp.bfloat16))
    anchor_result = (
        jnp.dot(inputs_kept[-1], fore_pair[0], preferred_element_type=jnp.float32) + fore_pair[1]
    )
    running_subtotal = jnp.dot(anchor_result, linear_upsample_anchors, precision=DOT_EXACTNESS)
    backcast = None
    if back_pair is not None:
        backcast = (
            jnp.dot(inputs_kept[-1], back_pair[0], preferred_element_type=jnp.float32)
            + back_pair[1]
        )
    return ((inputs_kept, pre_kept), running_subtotal, backcast)


def head_grads(last_act, d_low, weight):
    grad_w = jnp.dot(last_act.T, d_low, preferred_element_type=jnp.float32)
    grad_b = jnp.sum(d_low.astype(jnp.float32), axis=0)
    return ((grad_w, grad_b), jnp.dot(d_low, weight.T, preferred_element_type=jnp.float32))


def stack_backward(kept, anchor_cotangent, d_backcast, layers, fore_pair, back_pair, need_input):
    inputs_kept, pre_kept = kept
    last_act = inputs_kept[-1]
    fore_grads, d_hidden = head_grads(last_act, anchor_cotangent.astype(jnp.bfloat16), fore_pair[0])
    back_grads = None
    if back_pair is not None:
        back_grads, d_extra = head_grads(last_act, d_backcast.astype(jnp.bfloat16), back_pair[0])
        d_hidden = d_hidden + d_extra
    layer_grads = [None, None, None, None]
    for layer_id in (3, 2, 1, 0):
        d_pre = (d_hidden * silu_slope(pre_kept[layer_id])).astype(jnp.bfloat16)
        layer_grads[layer_id] = (
            jnp.dot(inputs_kept[layer_id].T, d_pre, preferred_element_type=jnp.float32),
            jnp.sum(d_pre.astype(jnp.float32), axis=0),
        )
        if layer_id > 0 or need_input:
            d_hidden = jnp.dot(d_pre, layers[layer_id][0].T, preferred_element_type=jnp.float32)
    return (layer_grads, fore_grads, back_grads, d_hidden)


def adamw(weight, avg, square, grad, step_float):
    new_avg = BETA_ONE * avg + (1.0 - BETA_ONE) * grad
    new_sq = BETA_TWO * square + (1.0 - BETA_TWO) * grad * grad
    avg_hat = new_avg / (1.0 - BETA_ONE**step_float)
    sq_hat = new_sq / (1.0 - BETA_TWO**step_float)
    new_weight = weight - RATE * (avg_hat / (jnp.sqrt(sq_hat) + EPSILON) + DECAY * weight)
    return (new_avg, new_sq, new_weight)


def body(
    windows,
    targets,
    horizon,
    step_count,
    first_w,
    first_w_avg,
    first_w_sq,
    hidden_w,
    hidden_w_avg,
    hidden_w_sq,
    back_w,
    back_w_avg,
    back_w_sq,
    fore_w,
    fore_w_avg,
    fore_w_sq,
    bias_vec,
    bias_avg,
    bias_sq,
):
    length = windows.shape[1]
    steps_ahead_total = targets.shape[1]
    normed, observed_future = normalize(windows, targets)
    future_usable_flags = (
        jnp.arange(steps_ahead_total, dtype=jnp.int32)[None, :] < horizon[:, None]
    ).astype(jnp.float32)
    usable_tally = lax.psum(jnp.sum(horizon.astype(jnp.float32)), ("dp", "fsdp"))
    shards = (
        first_w.astype(jnp.bfloat16),
        hidden_w.astype(jnp.bfloat16),
        back_w.astype(jnp.bfloat16),
        fore_w.astype(jnp.bfloat16),
    )
    gathered = (
        lax.all_gather(shards[0], "fsdp", axis=1, tiled=True),
        lax.all_gather(shards[1], "fsdp", axis=2, tiled=True),
        lax.all_gather(shards[2], "fsdp", axis=1, tiled=True),
        lax.all_gather(shards[3], "fsdp", axis=0, tiled=True),
    )
    residual = normed
    kept_stacks = []
    predicted_future = jnp.zeros(observed_future.shape, jnp.float32)
    for stack_id in range(3):
        layers, fore_pair, back_pair, linear_upsample_anchors = stack_params(
            stack_id, gathered, bias_vec, length, steps_ahead_total
        )
        kept, running_subtotal, backcast = stack_forward(
            residual, stack_id, layers, fore_pair, back_pair, linear_upsample_anchors
        )
        kept_stacks.append(kept)
        predicted_future = predicted_future + running_subtotal
        if backcast is not None:
            residual = residual - backcast
    residual_difference = predicted_future - observed_future
    loss_part = (
        jnp.sum(future_usable_flags * residual_difference * residual_difference) / usable_tally
    )
    future_slope_cotangent = 2.0 * future_usable_flags * residual_difference / usable_tally
    again = (
        lax.all_gather(shards[0], "fsdp", axis=1, tiled=True),
        lax.all_gather(shards[1], "fsdp", axis=2, tiled=True),
        lax.all_gather(shards[2], "fsdp", axis=1, tiled=True),
        lax.all_gather(shards[3], "fsdp", axis=0, tiled=True),
    )
    results = [None, None, None]
    d_residual = None
    for stack_id in (2, 1, 0):
        layers, fore_pair, back_pair, linear_upsample_anchors = stack_params(
            stack_id, again, bias_vec, length, steps_ahead_total
        )
        anchor_cotangent = jnp.dot(
            future_slope_cotangent, linear_upsample_anchors.T, precision=DOT_EXACTNESS
        )
        d_backcast = None if d_residual is None else -d_residual
        results[stack_id] = stack_backward(
            kept_stacks[stack_id],
            anchor_cotangent,
            d_backcast,
            layers,
            fore_pair,
            back_pair,
            stack_id > 0,
        )
        if stack_id > 0:
            spread_back = pool_back(results[stack_id][3], KERNELS[stack_id])
            d_residual = spread_back if d_residual is None else d_residual + spread_back
    grad_first = jnp.concatenate([results[stack_id][0][0][0] for stack_id in range(3)], axis=0)
    grad_hidden = jnp.stack(
        [
            jnp.stack([results[stack_id][0][layer_id][0] for layer_id in (1, 2, 3)])
            for stack_id in range(3)
        ]
    )
    grad_back = jnp.stack([results[stack_id][2][0] for stack_id in range(2)])
    grad_fore = jnp.concatenate([results[stack_id][1][0] for stack_id in range(3)], axis=1)
    bias_pieces = [results[stack_id][0][0][1] for stack_id in range(3)]
    bias_pieces += [
        results[stack_id][0][layer_id][1] for stack_id in range(3) for layer_id in (1, 2, 3)
    ]
    bias_pieces += [results[stack_id][2][1] for stack_id in range(2)]
    bias_pieces += [results[stack_id][1][1] for stack_id in range(3)]
    grad_bias = jnp.concatenate(bias_pieces)
    owned = (
        lax.psum_scatter(grad_first, "fsdp", scatter_dimension=1, tiled=True),
        lax.psum_scatter(grad_hidden, "fsdp", scatter_dimension=2, tiled=True),
        lax.psum_scatter(grad_back, "fsdp", scatter_dimension=1, tiled=True),
        lax.psum_scatter(grad_fore, "fsdp", scatter_dimension=0, tiled=True),
    )
    owned = lax.psum((owned[0], owned[1], owned[2], owned[3]), "dp")
    grad_bias, loss = lax.psum((grad_bias, loss_part), ("dp", "fsdp"))
    local_sq = sum((jnp.sum(grad * grad) for grad in owned))
    total_sq = lax.psum(local_sq, "fsdp") + jnp.sum(grad_bias * grad_bias)
    grad_norm = jnp.sqrt(total_sq)
    clip_factor = jnp.minimum(1.0, CLIP_MAX / grad_norm)
    step_float = step_count[0].astype(jnp.float32)
    states = (
        (first_w, first_w_avg, first_w_sq),
        (hidden_w, hidden_w_avg, hidden_w_sq),
        (back_w, back_w_avg, back_w_sq),
        (fore_w, fore_w_avg, fore_w_sq),
        (bias_vec, bias_avg, bias_sq),
    )
    grads_all = (owned[0], owned[1], owned[2], owned[3], grad_bias)
    updated = []
    for state, grad in zip(states, grads_all):
        updated.append(adamw(state[0], state[1], state[2], grad * clip_factor, step_float))
    return (
        loss,
        grad_norm,
        updated[0][0],
        updated[0][1],
        updated[0][2],
        updated[1][0],
        updated[1][1],
        updated[1][2],
        updated[2][0],
        updated[2][1],
        updated[2][2],
        updated[3][0],
        updated[3][1],
        updated[3][2],
        updated[4][0],
        updated[4][1],
        updated[4][2],
        updated[0][2].astype(jnp.bfloat16),
        updated[1][2].astype(jnp.bfloat16),
        updated[2][2].astype(jnp.bfloat16),
        updated[3][2].astype(jnp.bfloat16),
    )


MESH = pl.DeviceIdType.MESH
CHUNK = 1024


def tiled(width):
    return -(-width // 128) * 128


def packing(length, steps_ahead_total, hidden_size):
    pieces = {}
    cursor = 0
    for stack_id in range(3):
        widths = [("first", length // KERNELS[stack_id])]
        widths += [(layer_id, hidden_size) for layer_id in range(3)]
        if stack_id < 2:
            widths.append(("back", length))
        widths.append(("fore", steps_ahead_total // RATIOS[stack_id]))
        for name, width in widths:
            pieces[stack_id, name] = (cursor, width)
            cursor += tiled(width)
    total = -(-cursor // CHUNK) * CHUNK
    return pieces, total


def pack(parts, pieces, total):
    out = []
    cursor = 0
    for key, (start, width) in pieces.items():
        part = parts[key]
        out.append(jnp.pad(part, ((0, 0), (0, tiled(width) - width))))
        cursor = start + tiled(width)
    rows, dtype = out[0].shape[0], out[0].dtype
    if total > cursor:
        out.append(jnp.zeros((rows, total - cursor), dtype))
    return jnp.concatenate(out, axis=1)


def places():
    row = lax.axis_index("dp")
    me = lax.axis_index("fsdp")
    core = me % 2
    across_x = (me // 2) % 2
    across_y = me // 4
    other = me + 1 - 2 * core
    over_x = me + 2 - 4 * across_x
    over_y = me + 4 - 8 * across_y
    return row, me, core, other, over_x, over_y


def remote(src, dst, send_sem, recv_sem, device):
    return pltpu.make_async_remote_copy(
        src_ref=src, dst_ref=dst, send_sem=send_sem, recv_sem=recv_sem, device_id=device, device_id_type=MESH
    )


def gather_kernel(cuts, shard_ref, full_ref, own_sem, send_sem, recv_sem):
    row, me, core, other, over_x, over_y = places()
    diag = over_x + over_y - me
    barrier = pltpu.get_barrier_semaphore()
    for peer in (other, over_x, over_y):
        pl.semaphore_signal(barrier, inc=1, device_id=(row, peer), device_id_type=MESH)
    pl.semaphore_wait(barrier, 3)
    own = pltpu.make_async_copy(shard_ref, full_ref.at[me], own_sem)
    own.start()
    sends = []

    def send(kind, part, src, block, device):
        start, width = cuts[part]
        copy = remote(
            src.at[:, start : start + width],
            full_ref.at[block, :, start : start + width],
            send_sem.at[kind, part],
            recv_sem.at[kind, part],
            (row, device),
        )
        copy.start()
        sends.append(copy)
        return copy

    count = len(cuts)
    via_x = [None] * count
    via_y = [None] * count
    local = []
    for part in range(count):
        via_x[part] = send(0, part, shard_ref, me, over_x)
        via_y[part] = send(1, part, shard_ref, me, over_y)
        local.append(send(2, part, shard_ref, me, other))
    for part in range(count):
        via_x[part].wait_recv()
        local.append(send(3, part, full_ref.at[over_x], over_x, other))
        if part % 2 == 0:
            onward = send(6, part, full_ref.at[over_x], over_x, over_y)
        via_y[part].wait_recv()
        local.append(send(4, part, full_ref.at[over_y], over_y, other))
        if part % 2 == 1:
            onward = send(6, part, full_ref.at[over_y], over_y, over_x)
        onward.wait_recv()
        local.append(send(5, part, full_ref.at[diag], diag, other))
    for copy in local:
        copy.wait_recv()
    for copy in sends:
        copy.wait_send()
    own.wait()


def gather(shard, cuts):
    rows, total = shard.shape
    count = len(cuts)
    return pl.pallas_call(
        functools.partial(gather_kernel, cuts),
        out_shape=jax.ShapeDtypeStruct((8, rows, total), shard.dtype),
        in_specs=[pl.BlockSpec(memory_space=pltpu.HBM)],
        out_specs=pl.BlockSpec(memory_space=pltpu.HBM),
        scratch_shapes=[
            pltpu.SemaphoreType.DMA,
            pltpu.SemaphoreType.DMA((7, count)),
            pltpu.SemaphoreType.DMA((7, count)),
        ],
        compiler_params=pltpu.CompilerParams(collective_id=0, has_side_effects=True),
        name="gather_weights",
    )(shard)


def reduce_kernel(
    count, grad_ref, small_ref, out_ref, small_out_ref, square_ref,
    mine, from_core, s1, r1, keep, s2, r2, plane, zs, zr, zp_s, zp_r, final,
    small_s, small_r, square_s, square_r,
    load_sem, core_ss, core_rs, ss1, rs1, ss2, rs2, zss, zrs, pss, prs, fss, frs, small_ss, small_rs, sq_ss, sq_rs, out_sem,
):
    row, me, core, other, over_x, over_y = places()
    lane = core
    chip = me // 2
    chip_x = over_x // 2
    chip_y = over_y // 2
    chip_d = chip_x + chip_y - chip
    half = CHUNK // 2
    rows = grad_ref.shape[2]
    z_out = jnp.where(row < 2, row - 1, row + 1)
    z_out = jnp.clip(z_out, 0, 3)
    z_in = jnp.where(row < 2, row + 1, row - 1)
    middle = (row == 1) | (row == 2)

    barrier = pltpu.get_barrier_semaphore()
    for peer in range(1, 8):
        pl.semaphore_signal(barrier, inc=1, device_id=(row, (me + peer) % 8), device_id_type=MESH)
    for peer in range(1, 4):
        pl.semaphore_signal(barrier, inc=1, device_id=((row + peer) % 4, me), device_id_type=MESH)
    pl.semaphore_wait(barrier, 10)

    def columns(t):
        return pl.ds(pl.multiple_of(t * CHUNK, CHUNK), CHUNK)

    def load(t):
        return pltpu.make_async_copy(grad_ref.at[:, lane, :, columns(t)], mine.at[t % 2], load_sem.at[t % 2])

    def core_copy(t):
        return remote(
            grad_ref.at[:, 1 - lane, :, columns(t)], from_core.at[t], core_ss.at[t], core_rs.at[t], (row, other)
        )

    def first_x(t):
        return remote(s1.at[t, 0], r1.at[t, 0], ss1.at[t, 0], rs1.at[t, 0], (row, over_x))

    def first_y(t):
        return remote(s1.at[t, 1], r1.at[t, 1], ss1.at[t, 1], rs1.at[t, 1], (row, over_y))

    def second_y(t):
        return remote(s2.at[t, 0], r2.at[t, 0], ss2.at[t, 0], rs2.at[t, 0], (row, over_y))

    def second_x(t):
        return remote(s2.at[t, 1], r2.at[t, 1], ss2.at[t, 1], rs2.at[t, 1], (row, over_x))

    def z_all(t):
        return remote(zs.at[t], zr.at[t], zss.at[t], zrs.at[t], (z_in, me))

    def z_part(t):
        return remote(zp_s.at[t], zp_r.at[t], pss.at[t], prs.at[t], (z_in, me))

    def z_final(t, piece, way, device):
        return remote(final.at[t, piece], final.at[t, piece], fss.at[t, way], frs.at[t, piece], (device, me))

    near = jnp.where(row < 2, 0, 1)

    def stage_one(t):
        load(t).wait()

        @pl.when(t + 1 < count)
        def _():
            load(t + 1).start()

        core_copy(t).wait_recv()
        slot = t % 4
        for way, chips in ((0, (chip_x, chip_d)), (1, (chip_y, chip_d))):
            cols = slice(way * half, way * half + half)
            for k, c in enumerate(chips):
                s1[t, way, k] = (mine[t % 2, c, :, cols] + from_core[t, c, :, cols]).astype(jnp.bfloat16)
            (first_x, first_y)[way](t).start()
        for way, chips in ((0, (chip, chip_y)), (1, (chip, chip_x))):
            cols = slice(way * half, way * half + half)
            for k, c in enumerate(chips):
                keep[slot, way, k] = mine[t % 2, c, :, cols] + from_core[t, c, :, cols]

    def stage_two(t):
        slot = t % 4
        for way, copy, onward in ((0, first_x, second_y), (1, first_y, second_x)):
            copy(t).wait_recv()
            s2[t, way] = (keep[slot, way, 1] + r1[t, way, 1].astype(jnp.float32)).astype(jnp.bfloat16)
            onward(t).start()
            keep[slot, way, 0] = keep[slot, way, 0] + r1[t, way, 0].astype(jnp.float32)

    def stage_three(t):
        slot = t % 4
        for way, copy in ((0, second_y), (1, second_x)):
            copy(t).wait_recv()
            total = keep[slot, way, 0] + r2[t, way].astype(jnp.float32)
            plane[slot, way] = total
            zs[t, way] = total.astype(jnp.bfloat16)

        @pl.when(jnp.logical_not(middle))
        def _():
            z_all(t).start()

    def stage_four(t):
        @pl.when(middle)
        def _():
            slot = t % 4
            z_all(t).wait_recv()
            plane[slot, 0] = plane[slot, 0] + zr[t, 0].astype(jnp.float32)
            plane[slot, 1] = plane[slot, 1] + zr[t, 1].astype(jnp.float32)
            zp_s[t] = plane[slot, 1 - near].astype(jnp.bfloat16)
            z_part(t).start()

    def stage_five(t):
        @pl.when(middle)
        def _():
            slot = t % 4
            z_part(t).wait_recv()
            final[t, near] = (plane[slot, near] + zp_r[t].astype(jnp.float32)).astype(jnp.bfloat16)
            z_final(t, near, 0, z_in).start()
            z_final(t, near, 1, z_out).start()

    def stage_six(t):
        @pl.when(middle)
        def _():
            z_final(t, 1 - near, 2, z_out).wait_recv()
            z_final(t, 1 - near, 2, z_out).start()

        @pl.when(jnp.logical_not(middle))
        def _():
            z_final(t, 0, 0, z_in).wait_recv()
            z_final(t, 1, 1, z_in).wait_recv()

        pltpu.make_async_copy(final.at[t], out_ref.at[t], out_sem).start()
        got = final[t].astype(jnp.float32)
        got = got * got
        got = got[0] + got[1]
        acc = square_s[...]
        for k in range(0, rows, 8):
            for j in range(0, half, 128):
                acc = acc + got[k : k + 8, j : j + 128]
        square_s[...] = acc

    row_pair = row + 1 - 2 * (row % 2)
    row_far = row + 2 - 4 * (row // 2)
    hops = ((row, other), (row, over_x), (row, over_y), (row_pair, me), (row_far, me))

    def small_step(k):
        return remote(small_s.at[k], small_r.at[k], small_ss.at[k], small_rs.at[k], hops[k])

    def small_stage(k):
        if k == 0:
            small_s[0] = small_ref[...]
        else:
            small_step(k - 1).wait_recv()
            total = small_s[k - 1] + small_r[k - 1]
            if k < len(hops):
                small_s[k] = total
            else:
                small_out_ref[...] = total
        if k < len(hops):
            small_step(k).start()

    square_s[...] = jnp.zeros_like(square_s)
    load(0).start()

    def start_core(t, carry):
        core_copy(t).start()
        return carry

    lax.fori_loop(0, count, start_core, 0)

    def turn(t, carry):
        for lag, stage in ((0, stage_one), (1, stage_two), (2, stage_three), (3, stage_four), (4, stage_five), (5, stage_six)):
            @pl.when((t >= lag) & (t < count + lag))
            def _():
                stage(t - lag)

        for k in range(len(hops) + 1):
            @pl.when(t == 2 + 2 * k)
            def _():
                small_stage(k)
        return carry

    lax.fori_loop(0, count + 5, turn, 0)

    def square_copy(peer):
        device = (me + peer) % 8
        return remote(square_s, square_r.at[me], sq_ss.at[peer], sq_rs.at[peer], (row, device))

    def square_wait(peer):
        device = (me - peer + 8) % 8
        return remote(square_s, square_r.at[device], sq_ss.at[peer], sq_rs.at[peer], (row, device))

    for peer in range(1, 8):
        square_copy(peer).start()
    square_r[me] = square_s[...]
    for peer in range(1, 8):
        square_wait(peer).wait_recv()
    acc = square_r[0]
    for block in range(1, 8):
        acc = acc + square_r[block]
    square_ref[...] = acc

    def finish(t, carry):
        core_copy(t).wait_send()
        first_x(t).wait_send()
        first_y(t).wait_send()
        second_x(t).wait_send()
        second_y(t).wait_send()

        @pl.when(middle)
        def _():
            z_part(t).wait_send()
            z_final(t, near, 0, z_in).wait_send()
            z_final(t, near, 1, z_out).wait_send()
            z_final(t, 1 - near, 2, z_out).wait_send()

        @pl.when(jnp.logical_not(middle))
        def _():
            z_all(t).wait_send()

        pltpu.make_async_copy(final.at[t], out_ref.at[t], out_sem).wait()
        return carry

    lax.fori_loop(0, count, finish, 0)
    for k in range(len(hops)):
        small_step(k).wait_send()
    for peer in range(1, 8):
        square_copy(peer).wait_send()


def reduce_grads(grads, small):
    _, _, rows, total = grads.shape
    count = total // CHUNK
    half = CHUNK // 2
    low, wide = jnp.bfloat16, jnp.float32
    dma = pltpu.SemaphoreType.DMA
    return pl.pallas_call(
        functools.partial(reduce_kernel, count),
        out_shape=(
            jax.ShapeDtypeStruct((count, 2, rows, half), low),
            jax.ShapeDtypeStruct(small.shape, wide),
            jax.ShapeDtypeStruct((8, 128), wide),
        ),
        in_specs=[pl.BlockSpec(memory_space=pltpu.HBM), pl.BlockSpec(memory_space=pltpu.VMEM)],
        out_specs=(
            pl.BlockSpec(memory_space=pltpu.HBM),
            pl.BlockSpec(memory_space=pltpu.VMEM),
            pl.BlockSpec(memory_space=pltpu.VMEM),
        ),
        scratch_shapes=[
            pltpu.VMEM((2, 4, rows, CHUNK), wide),
            pltpu.VMEM((count, 4, rows, CHUNK), wide),
            pltpu.VMEM((count, 2, 2, rows, half), low),
            pltpu.VMEM((count, 2, 2, rows, half), low),
            pltpu.VMEM((4, 2, 2, rows, half), wide),
            pltpu.VMEM((count, 2, rows, half), low),
            pltpu.VMEM((count, 2, rows, half), low),
            pltpu.VMEM((4, 2, rows, half), wide),
            pltpu.VMEM((count, 2, rows, half), low),
            pltpu.VMEM((count, 2, rows, half), low),
            pltpu.VMEM((count, rows, half), low),
            pltpu.VMEM((count, rows, half), low),
            pltpu.VMEM((count, 2, rows, half), low),
            pltpu.VMEM((5,) + small.shape, wide),
            pltpu.VMEM((5,) + small.shape, wide),
            pltpu.VMEM((8, 128), wide),
            pltpu.VMEM((8, 8, 128), wide),
            dma((2,)),
            dma((count,)),
            dma((count,)),
            dma((count, 2)),
            dma((count, 2)),
            dma((count, 2)),
            dma((count, 2)),
            dma((count,)),
            dma((count,)),
            dma((count,)),
            dma((count,)),
            dma((count, 3)),
            dma((count, 2)),
            dma((5,)),
            dma((5,)),
            dma((8,)),
            dma((8,)),
            dma,
        ],
        compiler_params=pltpu.CompilerParams(
            collective_id=1, has_side_effects=True, vmem_limit_bytes=60 * 1024 * 1024
        ),
        name="reduce_grads",
    )(grads, small)


def fast_body(
    devices,
    windows,
    targets,
    horizon,
    step_count,
    first_w,
    first_w_avg,
    first_w_sq,
    hidden_w,
    hidden_w_avg,
    hidden_w_sq,
    back_w,
    back_w_avg,
    back_w_sq,
    fore_w,
    fore_w_avg,
    fore_w_sq,
    bias_vec,
    bias_avg,
    bias_sq,
):
    length = windows.shape[1]
    steps_ahead_total = targets.shape[1]
    hidden_size = hidden_w.shape[-1]
    pieces, total = packing(length, steps_ahead_total, hidden_size)

    def split(first, hidden, back, fore, stack_id):
        row_start = sum(length // KERNELS[earlier] for earlier in range(stack_id))
        col_start = sum(steps_ahead_total // RATIOS[earlier] for earlier in range(stack_id))
        parts = {(stack_id, "first"): first[row_start : row_start + length // KERNELS[stack_id]].T}
        for layer_id in range(3):
            parts[stack_id, layer_id] = hidden[stack_id, layer_id]
        if stack_id < 2:
            parts[stack_id, "back"] = back[stack_id]
        parts[stack_id, "fore"] = fore[:, col_start : col_start + steps_ahead_total // RATIOS[stack_id]]
        return parts

    low = jnp.bfloat16
    parts = {}
    for stack_id in range(3):
        parts.update(split(first_w.astype(low), hidden_w.astype(low), back_w.astype(low), fore_w.astype(low), stack_id))
    shard = pack(parts, pieces, total)
    cuts = []
    for stack_id in range(3):
        for names in (("first", 0, 1, 2), ("back", "fore")):
            names = [name for name in names if (stack_id, name) in pieces]
            start = pieces[stack_id, names[0]][0]
            stop = pieces[stack_id, names[-1]][0] + tiled(pieces[stack_id, names[-1]][1])
            cuts.append((start, stop - start))
    full = gather(shard, tuple(cuts)).reshape(hidden_size, total)

    def piece(key):
        start, width = pieces[key]
        return full[:, start : start + width]

    normed, observed_future = normalize(windows, targets)
    flags = (jnp.arange(steps_ahead_total, dtype=jnp.int32)[None, :] < horizon[:, None]).astype(jnp.float32)
    tally = jnp.sum(horizon.astype(jnp.float32))
    residual = normed
    kept_stacks = []
    stack_args = []
    predicted_future = jnp.zeros(observed_future.shape, jnp.float32)
    for stack_id in range(3):
        layers = [(piece((stack_id, "first")).T, bias_vec[stack_id * hidden_size : (stack_id + 1) * hidden_size])]
        for layer_id in range(3):
            offset = (3 + 3 * stack_id + layer_id) * hidden_size
            layers.append((piece((stack_id, layer_id)), bias_vec[offset : offset + hidden_size]))
        col_start = sum(steps_ahead_total // RATIOS[earlier] for earlier in range(stack_id))
        fore_start = 12 * hidden_size + 2 * length + col_start
        anchor_entries = steps_ahead_total // RATIOS[stack_id]
        fore_pair = (piece((stack_id, "fore")), bias_vec[fore_start : fore_start + anchor_entries])
        back_pair = None
        if stack_id < 2:
            back_start = 12 * hidden_size + stack_id * length
            back_pair = (piece((stack_id, "back")), bias_vec[back_start : back_start + length])
        upsample = jnp.asarray(blend_coefficients(steps_ahead_total, anchor_entries))
        stack_args.append((layers, fore_pair, back_pair, upsample))
        kept, running_subtotal, backcast = stack_forward(residual, stack_id, *stack_args[-1])
        kept_stacks.append(kept)
        predicted_future = predicted_future + running_subtotal
        if backcast is not None:
            residual = residual - backcast
    difference = predicted_future - observed_future
    loss_part = jnp.sum(flags * difference * difference)
    scale = 2.0 ** -int(np.ceil(np.log2(devices * windows.shape[0] * steps_ahead_total)))
    cotangent = (2.0 * scale) * flags * difference
    results = [None, None, None]
    d_residual = None
    for stack_id in (2, 1, 0):
        layers, fore_pair, back_pair, upsample = stack_args[stack_id]
        anchor_cotangent = jnp.dot(cotangent, upsample.T, precision=DOT_EXACTNESS)
        d_backcast = None if d_residual is None else -d_residual
        results[stack_id] = stack_backward(
            kept_stacks[stack_id], anchor_cotangent, d_backcast, layers, fore_pair, back_pair, stack_id > 0
        )
        if stack_id > 0:
            spread_back = pool_back(results[stack_id][3], KERNELS[stack_id])
            d_residual = spread_back if d_residual is None else d_residual + spread_back
    parts = {}
    for stack_id in range(3):
        parts[stack_id, "first"] = results[stack_id][0][0][0].T
        for layer_id in range(3):
            parts[stack_id, layer_id] = results[stack_id][0][layer_id + 1][0]
        if stack_id < 2:
            parts[stack_id, "back"] = results[stack_id][2][0]
        parts[stack_id, "fore"] = results[stack_id][1][0]
    grads = pack(parts, pieces, total)
    bias_pieces = [results[stack_id][0][0][1] for stack_id in range(3)]
    bias_pieces += [results[stack_id][0][layer_id][1] for stack_id in range(3) for layer_id in (1, 2, 3)]
    bias_pieces += [results[stack_id][2][1] for stack_id in range(2)]
    bias_pieces += [results[stack_id][1][1] for stack_id in range(3)]
    bias_count = bias_vec.shape[0]
    small_rows = -(-(bias_count + 2) // 1024) * 8
    small = jnp.concatenate(bias_pieces + [jnp.stack([loss_part, tally])])
    small = jnp.pad(small, (0, small_rows * 128 - small.shape[0])).reshape(small_rows, 128)
    grads = grads.reshape(4, 2, hidden_size // 8, total)
    owned, small, square = reduce_grads(grads, small)
    owned = owned.transpose(2, 0, 1, 3).reshape(hidden_size // 8, total)
    small = small.reshape(-1)
    grad_bias, loss_sum, tally = small[:bias_count], small[bias_count], small[bias_count + 1]
    factor = 1.0 / (scale * tally)
    loss = loss_sum / tally
    grad_norm = jnp.sqrt(jnp.sum(square) + jnp.sum(grad_bias * grad_bias)) * factor
    clip_factor = jnp.minimum(1.0, CLIP_MAX / grad_norm) * factor
    step_float = step_count[0].astype(jnp.float32)

    def grad_piece(key):
        start, width = pieces[key]
        return owned[:, start : start + width].astype(jnp.float32)

    grads_all = (
        jnp.concatenate([grad_piece((stack_id, "first")) for stack_id in range(3)], axis=1).T,
        jnp.stack([jnp.stack([grad_piece((stack_id, layer_id)) for layer_id in range(3)]) for stack_id in range(3)]),
        jnp.stack([grad_piece((stack_id, "back")) for stack_id in range(2)]),
        jnp.concatenate([grad_piece((stack_id, "fore")) for stack_id in range(3)], axis=1),
        grad_bias,
    )
    states = (
        (first_w, first_w_avg, first_w_sq),
        (hidden_w, hidden_w_avg, hidden_w_sq),
        (back_w, back_w_avg, back_w_sq),
        (fore_w, fore_w_avg, fore_w_sq),
        (bias_vec, bias_avg, bias_sq),
    )
    updated = []
    for state, grad in zip(states, grads_all):
        updated.append(adamw(state[0], state[1], state[2], grad * clip_factor, step_float))
    flat = [loss, grad_norm]
    for triple in updated:
        flat.extend(triple)
    flat += [triple[2].astype(low) for triple in updated[:4]]
    return tuple(flat)


def solution(mesh):
    fast = mesh.shape["fsdp"] == 8 and mesh.shape["dp"] == 4
    step = functools.partial(fast_body, mesh.shape["dp"] * mesh.shape["fsdp"]) if fast else body
    placed = (
        P(("dp", "fsdp"), None),
        P(("dp", "fsdp"), None),
        P(("dp", "fsdp")),
        P(),
        P(None, "fsdp"),
        P(None, "fsdp"),
        P(None, "fsdp"),
        P(None, None, "fsdp", None),
        P(None, None, "fsdp", None),
        P(None, None, "fsdp", None),
        P(None, "fsdp", None),
        P(None, "fsdp", None),
        P(None, "fsdp", None),
        P("fsdp", None),
        P("fsdp", None),
        P("fsdp", None),
        P(),
        P(),
        P(),
    )
    return jax.shard_map(
        step,
        mesh=mesh,
        in_specs=placed,
        out_specs=(
            P(),
            P(),
            P(None, "fsdp"),
            P(None, "fsdp"),
            P(None, "fsdp"),
            P(None, None, "fsdp", None),
            P(None, None, "fsdp", None),
            P(None, None, "fsdp", None),
            P(None, "fsdp", None),
            P(None, "fsdp", None),
            P(None, "fsdp", None),
            P("fsdp", None),
            P("fsdp", None),
            P("fsdp", None),
            P(),
            P(),
            P(),
            P(None, "fsdp"),
            P(None, None, "fsdp", None),
            P(None, "fsdp", None),
            P("fsdp", None),
        ),
        check_vma=False,
    )
```

```python
import functools
import jax
import jax.numpy as jnp
import numpy as np
from jax import lax
from jax.experimental import pallas as pl
from jax.experimental.pallas import tpu as pltpu
from jax.sharding import PartitionSpec as P

KERNELS = (8, 4, 1)
RATIOS = (24, 12, 1)
CLIP_MAX = 0.01
RATE = 0.02
BETA_ONE = 0.9
BETA_TWO = 0.999
EPSILON = 1e-08
DECAY = 0.01
DOT_EXACTNESS = lax.Precision.HIGHEST


def blend_coefficients(fine, coarse):
    column = np.arange(fine)
    numer = np.maximum((2 * column + 1) * coarse - fine, 0)
    lower_idx = numer // (2 * fine)
    frac = (numer - lower_idx * 2 * fine) / (2.0 * fine)
    upper_idx = np.minimum(lower_idx + 1, coarse - 1)
    matrix = np.zeros((coarse, fine), np.float32)
    matrix[lower_idx, column] += 1.0 - frac
    matrix[upper_idx, column] += frac
    return matrix


def normalize(windows, targets):
    center = jnp.mean(windows, axis=1, keepdims=True)
    spread = jnp.sqrt(jnp.mean((windows - center) ** 2, axis=1, keepdims=True) + 1e-05)
    return ((windows - center) / spread, (targets - center) / spread)


def mean_pool(values, kernel):
    if kernel == 1:
        return values
    return jnp.mean(values.reshape(values.shape[0], values.shape[1] // kernel, kernel), axis=2)


def pool_back(d_pooled, kernel):
    if kernel == 1:
        return d_pooled
    spread_out = jnp.broadcast_to((d_pooled / kernel)[:, :, None], d_pooled.shape + (kernel,))
    return spread_out.reshape(d_pooled.shape[0], d_pooled.shape[1] * kernel)


def silu_slope(pre_act):
    gate = jax.nn.sigmoid(pre_act)
    return gate * (1.0 + pre_act * (1.0 - gate))


def stack_params(stack_id, gathered, bias_vec, length, steps_ahead_total):
    first_full, hidden_full, back_full, fore_full = gathered
    hidden_size = hidden_full.shape[-1]
    row_start = sum((length // KERNELS[earlier] for earlier in range(stack_id)))
    col_start = sum((steps_ahead_total // RATIOS[earlier] for earlier in range(stack_id)))
    pooled_len = length // KERNELS[stack_id]
    anchor_entries = steps_ahead_total // RATIOS[stack_id]
    layers = [
        (
            first_full[row_start : row_start + pooled_len],
            bias_vec[stack_id * hidden_size : (stack_id + 1) * hidden_size],
        )
    ]
    for layer_id in range(3):
        offset = (3 + 3 * stack_id + layer_id) * hidden_size
        layers.append((hidden_full[stack_id, layer_id], bias_vec[offset : offset + hidden_size]))
    fore_start = 12 * hidden_size + 2 * length + col_start
    fore_pair = (
        fore_full[:, col_start : col_start + anchor_entries],
        bias_vec[fore_start : fore_start + anchor_entries],
    )
    back_pair = None
    if stack_id < 2:
        back_start = 12 * hidden_size + stack_id * length
        back_pair = (back_full[stack_id], bias_vec[back_start : back_start + length])
    linear_upsample_anchors = jnp.asarray(blend_coefficients(steps_ahead_total, anchor_entries))
    return (layers, fore_pair, back_pair, linear_upsample_anchors)


def stack_forward(residual, stack_id, layers, fore_pair, back_pair, linear_upsample_anchors):
    inputs_kept = [mean_pool(residual, KERNELS[stack_id]).astype(jnp.bfloat16)]
    pre_kept = []
    for weight, bias in layers:
        pre_act = jnp.dot(inputs_kept[-1], weight, preferred_element_type=jnp.float32) + bias
        pre_kept.append(pre_act)
        inputs_kept.append(jax.nn.silu(pre_act).astype(jnp.bfloat16))
    anchor_result = (
        jnp.dot(inputs_kept[-1], fore_pair[0], preferred_element_type=jnp.float32) + fore_pair[1]
    )
    running_subtotal = jnp.dot(anchor_result, linear_upsample_anchors, precision=DOT_EXACTNESS)
    backcast = None
    if back_pair is not None:
        backcast = (
            jnp.dot(inputs_kept[-1], back_pair[0], preferred_element_type=jnp.float32)
            + back_pair[1]
        )
    return ((inputs_kept, pre_kept), running_subtotal, backcast)


def head_grads(last_act, d_low, weight):
    grad_w = jnp.dot(last_act.T, d_low, preferred_element_type=jnp.float32)
    grad_b = jnp.sum(d_low.astype(jnp.float32), axis=0)
    return ((grad_w, grad_b), jnp.dot(d_low, weight.T, preferred_element_type=jnp.float32))


def stack_backward(kept, anchor_cotangent, d_backcast, layers, fore_pair, back_pair, need_input):
    inputs_kept, pre_kept = kept
    last_act = inputs_kept[-1]
    fore_grads, d_hidden = head_grads(last_act, anchor_cotangent.astype(jnp.bfloat16), fore_pair[0])
    back_grads = None
    if back_pair is not None:
        back_grads, d_extra = head_grads(last_act, d_backcast.astype(jnp.bfloat16), back_pair[0])
        d_hidden = d_hidden + d_extra
    layer_grads = [None, None, None, None]
    for layer_id in (3, 2, 1, 0):
        d_pre = (d_hidden * silu_slope(pre_kept[layer_id])).astype(jnp.bfloat16)
        layer_grads[layer_id] = (
            jnp.dot(inputs_kept[layer_id].T, d_pre, preferred_element_type=jnp.float32),
            jnp.sum(d_pre.astype(jnp.float32), axis=0),
        )
        if layer_id > 0 or need_input:
            d_hidden = jnp.dot(d_pre, layers[layer_id][0].T, preferred_element_type=jnp.float32)
    return (layer_grads, fore_grads, back_grads, d_hidden)


def adamw(weight, avg, square, grad, step_float):
    new_avg = BETA_ONE * avg + (1.0 - BETA_ONE) * grad
    new_sq = BETA_TWO * square + (1.0 - BETA_TWO) * grad * grad
    avg_hat = new_avg / (1.0 - BETA_ONE**step_float)
    sq_hat = new_sq / (1.0 - BETA_TWO**step_float)
    new_weight = weight - RATE * (avg_hat / (jnp.sqrt(sq_hat) + EPSILON) + DECAY * weight)
    return (new_avg, new_sq, new_weight)


def body(
    windows,
    targets,
    horizon,
    step_count,
    first_w,
    first_w_avg,
    first_w_sq,
    hidden_w,
    hidden_w_avg,
    hidden_w_sq,
    back_w,
    back_w_avg,
    back_w_sq,
    fore_w,
    fore_w_avg,
    fore_w_sq,
    bias_vec,
    bias_avg,
    bias_sq,
):
    length = windows.shape[1]
    steps_ahead_total = targets.shape[1]
    normed, observed_future = normalize(windows, targets)
    future_usable_flags = (
        jnp.arange(steps_ahead_total, dtype=jnp.int32)[None, :] < horizon[:, None]
    ).astype(jnp.float32)
    usable_tally = lax.psum(jnp.sum(horizon.astype(jnp.float32)), ("dp", "fsdp"))
    shards = (
        first_w.astype(jnp.bfloat16),
        hidden_w.astype(jnp.bfloat16),
        back_w.astype(jnp.bfloat16),
        fore_w.astype(jnp.bfloat16),
    )
    gathered = (
        lax.all_gather(shards[0], "fsdp", axis=1, tiled=True),
        lax.all_gather(shards[1], "fsdp", axis=2, tiled=True),
        lax.all_gather(shards[2], "fsdp", axis=1, tiled=True),
        lax.all_gather(shards[3], "fsdp", axis=0, tiled=True),
    )
    residual = normed
    kept_stacks = []
    predicted_future = jnp.zeros(observed_future.shape, jnp.float32)
    for stack_id in range(3):
        layers, fore_pair, back_pair, linear_upsample_anchors = stack_params(
            stack_id, gathered, bias_vec, length, steps_ahead_total
        )
        kept, running_subtotal, backcast = stack_forward(
            residual, stack_id, layers, fore_pair, back_pair, linear_upsample_anchors
        )
        kept_stacks.append(kept)
        predicted_future = predicted_future + running_subtotal
        if backcast is not None:
            residual = residual - backcast
    residual_difference = predicted_future - observed_future
    loss_part = (
        jnp.sum(future_usable_flags * residual_difference * residual_difference) / usable_tally
    )
    future_slope_cotangent = 2.0 * future_usable_flags * residual_difference / usable_tally
    again = (
        lax.all_gather(shards[0], "fsdp", axis=1, tiled=True),
        lax.all_gather(shards[1], "fsdp", axis=2, tiled=True),
        lax.all_gather(shards[2], "fsdp", axis=1, tiled=True),
        lax.all_gather(shards[3], "fsdp", axis=0, tiled=True),
    )
    results = [None, None, None]
    d_residual = None
    for stack_id in (2, 1, 0):
        layers, fore_pair, back_pair, linear_upsample_anchors = stack_params(
            stack_id, again, bias_vec, length, steps_ahead_total
        )
        anchor_cotangent = jnp.dot(
            future_slope_cotangent, linear_upsample_anchors.T, precision=DOT_EXACTNESS
        )
        d_backcast = None if d_residual is None else -d_residual
        results[stack_id] = stack_backward(
            kept_stacks[stack_id],
            anchor_cotangent,
            d_backcast,
            layers,
            fore_pair,
            back_pair,
            stack_id > 0,
        )
        if stack_id > 0:
            spread_back = pool_back(results[stack_id][3], KERNELS[stack_id])
            d_residual = spread_back if d_residual is None else d_residual + spread_back
    grad_first = jnp.concatenate([results[stack_id][0][0][0] for stack_id in range(3)], axis=0)
    grad_hidden = jnp.stack(
        [
            jnp.stack([results[stack_id][0][layer_id][0] for layer_id in (1, 2, 3)])
            for stack_id in range(3)
        ]
    )
    grad_back = jnp.stack([results[stack_id][2][0] for stack_id in range(2)])
    grad_fore = jnp.concatenate([results[stack_id][1][0] for stack_id in range(3)], axis=1)
    bias_pieces = [results[stack_id][0][0][1] for stack_id in range(3)]
    bias_pieces += [
        results[stack_id][0][layer_id][1] for stack_id in range(3) for layer_id in (1, 2, 3)
    ]
    bias_pieces += [results[stack_id][2][1] for stack_id in range(2)]
    bias_pieces += [results[stack_id][1][1] for stack_id in range(3)]
    grad_bias = jnp.concatenate(bias_pieces)
    owned = (
        lax.psum_scatter(grad_first, "fsdp", scatter_dimension=1, tiled=True),
        lax.psum_scatter(grad_hidden, "fsdp", scatter_dimension=2, tiled=True),
        lax.psum_scatter(grad_back, "fsdp", scatter_dimension=1, tiled=True),
        lax.psum_scatter(grad_fore, "fsdp", scatter_dimension=0, tiled=True),
    )
    owned = lax.psum((owned[0], owned[1], owned[2], owned[3]), "dp")
    grad_bias, loss = lax.psum((grad_bias, loss_part), ("dp", "fsdp"))
    local_sq = sum((jnp.sum(grad * grad) for grad in owned))
    total_sq = lax.psum(local_sq, "fsdp") + jnp.sum(grad_bias * grad_bias)
    grad_norm = jnp.sqrt(total_sq)
    clip_factor = jnp.minimum(1.0, CLIP_MAX / grad_norm)
    step_float = step_count[0].astype(jnp.float32)
    states = (
        (first_w, first_w_avg, first_w_sq),
        (hidden_w, hidden_w_avg, hidden_w_sq),
        (back_w, back_w_avg, back_w_sq),
        (fore_w, fore_w_avg, fore_w_sq),
        (bias_vec, bias_avg, bias_sq),
    )
    grads_all = (owned[0], owned[1], owned[2], owned[3], grad_bias)
    updated = []
    for state, grad in zip(states, grads_all):
        updated.append(adamw(state[0], state[1], state[2], grad * clip_factor, step_float))
    return (
        loss,
        grad_norm,
        updated[0][0],
        updated[0][1],
        updated[0][2],
        updated[1][0],
        updated[1][1],
        updated[1][2],
        updated[2][0],
        updated[2][1],
        updated[2][2],
        updated[3][0],
        updated[3][1],
        updated[3][2],
        updated[4][0],
        updated[4][1],
        updated[4][2],
        updated[0][2].astype(jnp.bfloat16),
        updated[1][2].astype(jnp.bfloat16),
        updated[2][2].astype(jnp.bfloat16),
        updated[3][2].astype(jnp.bfloat16),
    )


MESH = pl.DeviceIdType.MESH
CHUNK = 1024


def tiled(width):
    return -(-width // 128) * 128


def packing(length, steps_ahead_total, hidden_size):
    pieces = {}
    cursor = 0
    for stack_id in range(3):
        widths = [("first", length // KERNELS[stack_id])]
        widths += [(layer_id, hidden_size) for layer_id in range(3)]
        if stack_id < 2:
            widths.append(("back", length))
        widths.append(("fore", steps_ahead_total // RATIOS[stack_id]))
        for name, width in widths:
            pieces[stack_id, name] = (cursor, width)
            cursor += tiled(width)
    total = -(-cursor // CHUNK) * CHUNK
    return pieces, total


def pack(parts, pieces, total):
    out = []
    cursor = 0
    for key, (start, width) in pieces.items():
        part = parts[key]
        out.append(jnp.pad(part, ((0, 0), (0, tiled(width) - width))))
        cursor = start + tiled(width)
    rows, dtype = out[0].shape[0], out[0].dtype
    if total > cursor:
        out.append(jnp.zeros((rows, total - cursor), dtype))
    return jnp.concatenate(out, axis=1)


def places():
    row = lax.axis_index("dp")
    me = lax.axis_index("fsdp")
    core = me % 2
    across_x = (me // 2) % 2
    across_y = me // 4
    other = me + 1 - 2 * core
    over_x = me + 2 - 4 * across_x
    over_y = me + 4 - 8 * across_y
    return row, me, core, other, over_x, over_y


def remote(src, dst, send_sem, recv_sem, device):
    return pltpu.make_async_remote_copy(
        src_ref=src, dst_ref=dst, send_sem=send_sem, recv_sem=recv_sem, device_id=device, device_id_type=MESH
    )


HALF_LOW = 2


def row_plan(length, steps_ahead_total, hidden_size):
    rows = {}
    cursor = 0
    for stack_id in range(3):
        for name in ("first", 0, 1, 2):
            rows[stack_id, name] = (cursor, hidden_size)
            cursor += 1
    for stack_id in range(2):
        rows[stack_id, "back"] = (cursor, length)
        cursor += -(-length // hidden_size)
    for stack_id in range(3):
        width = steps_ahead_total // RATIOS[stack_id]
        rows[stack_id, "fore"] = (cursor, width)
        cursor += -(-width // hidden_size)
    return rows, cursor


def bias_order(length, steps_ahead_total, hidden_size):
    keys = [(stack_id, "first") for stack_id in range(3)]
    keys += [(stack_id, layer_id) for stack_id in range(3) for layer_id in range(3)]
    keys += [(stack_id, "back") for stack_id in range(2)]
    keys += [(stack_id, "fore") for stack_id in range(3)]
    return keys


def parts_low(value):
    high = value.astype(jnp.bfloat16)
    return high, (value - high.astype(jnp.float32)).astype(jnp.bfloat16)


NN = (((1,), (0,)), ((), ()))
NT = (((1,), (1,)), ((), ()))
TN = (((0,), (0,)), ((), ()))


def mul(left, right, dims=NN):
    return lax.dot_general(left, right, dims, preferred_element_type=jnp.float32)


def forward_kernel(
    plan,
    shard_ref, windows_ref, targets_ref, horizon_ref, bias_ref, up_high_ref, up_low_ref,
    w_out, a_out, slope_out, p0_out, p1_out, x2_out, g_out, small_ref,
    w, x, stage, a, slope, p0, p1, x2, fc, tt, g, dk, center_s, scale_s, pool8, pool4,
    own_sem, send_sem, recv_sem, win_sem, tt_sem, out_sem, w_sem,
):
    pieces, bias_rows, cut_width, count, scale = plan
    row, me, core, other, over_x, over_y = places()
    diag = over_x + over_y - me
    total_rows = windows_ref.shape[0]
    length = windows_ref.shape[1]
    hidden_size = a.shape[-1]
    steps_ahead = targets_ref.shape[0]
    block = total_rows // 2
    wide, low = jnp.float32, jnp.bfloat16
    wide_length = x.shape[1]
    tiles = [(k, min(hidden_size, wide_length - k)) for k in range(0, wide_length, hidden_size)]
    whole = wide_length // 128 * 128 - 128

    barrier = pltpu.get_barrier_semaphore()
    for peer in (other, over_x, over_y):
        pl.semaphore_signal(barrier, inc=1, device_id=(row, peer), device_id_type=MESH)
    pl.semaphore_wait(barrier, 3)

    def copy_of(kind, cut, src, holder, device):
        cols = slice(cut * cut_width, (cut + 1) * cut_width)
        return remote(
            src.at[:, cols], w.at[holder, :, cols], send_sem.at[kind, cut], recv_sem.at[kind, cut], (row, device)
        )

    def to_x(cut):
        return copy_of(0, cut, shard_ref, me, over_x)

    def to_y(cut):
        return copy_of(1, cut, shard_ref, me, over_y)

    def onward(cut):
        if cut % 2 == 0:
            return copy_of(2, cut, w.at[over_x], over_x, over_y)
        return copy_of(2, cut, w.at[over_y], over_y, over_x)

    def to_core(kind, cut):
        if kind == 0:
            return copy_of(3, cut, shard_ref, me, other)
        holder = (None, over_x, over_y, diag)[kind]
        return copy_of(3 + kind, cut, w.at[holder], holder, other)

    own = pltpu.make_async_copy(shard_ref, w.at[me], own_sem)
    own.start()

    def own_sends(cut):
        to_x(cut).start()
        to_y(cut).start()
        to_core(0, cut).start()

    def w_copy(cut):
        cols = slice(cut * cut_width, (cut + 1) * cut_width)
        return pltpu.make_async_copy(w.at[:, :, cols], w_out.at[:, :, cols], w_sem.at[cut])

    look = 4

    def pump(cut):
        if cut < count:
            to_x(cut).wait_recv()
            if cut % 2 == 0:
                onward(cut).start()
            to_core(1, cut).start()
            to_y(cut).wait_recv()
            if cut % 2 == 1:
                onward(cut).start()
            to_core(2, cut).start()
            if cut + look < count:
                own_sends(cut + look)
        if 0 <= cut - 1 < count:
            onward(cut - 1).wait_recv()
            to_core(3, cut - 1).start()
        if 0 <= cut - 2 < count:
            if cut == 2:
                own.wait()
            for kind in range(4):
                to_core(kind, cut - 2).wait_recv()
            w_copy(cut - 2).start()

    tasks = []

    def task(need, cost):
        def keep(body):
            tasks.append((need, cost, body))
            return body
        return keep

    def cut_of(key):
        start, width = pieces[key]
        return (start + tiled(width) - 1) // cut_width

    def weights(key, start=0, width=None):
        at, full_width = pieces[key]
        width = tiled(full_width) if width is None else width
        return w[:, :, at + start : at + start + width].reshape(hidden_size, width)

    def bias(key, start=0, width=None):
        at, full_width = bias_rows[key]
        width = hidden_size if width is None else width
        return bias_ref[at + start // hidden_size : at + start // hidden_size + 1, 0:width]

    def over_rows(body):
        def step(k, carry):
            body(pl.ds(pl.multiple_of(k * block, block), block))
            return carry
        lax.fori_loop(0, 2, step, 0)

    def outgoing(src, dst, slot):
        return pltpu.make_async_copy(src, dst, out_sem.at[slot])

    slots = stage.shape[0]
    strip = stage.shape[1]
    strips = total_rows // strip

    def window_copy(k):
        rows = pl.ds(pl.multiple_of(k * strip, strip), strip)
        return pltpu.make_async_copy(windows_ref.at[rows], stage.at[k % slots], win_sem.at[k % slots])

    for k in range(slots):
        window_copy(k).start()
    targets_copy = pltpu.make_async_copy(targets_ref, tt.at[0:steps_ahead], tt_sem)
    targets_copy.start()
    for cut in range(look):
        own_sends(cut)

    @task(-1, 1.0)
    def _():
        ids = lax.broadcasted_iota(jnp.int32, pool8.shape, 0)
        col = lax.broadcasted_iota(jnp.int32, pool8.shape, 1) * KERNELS[0]
        pool8[...] = jnp.where((ids >= col) & (ids < col + KERNELS[0]), 1.0 / KERNELS[0], 0.0).astype(low)
        ids = lax.broadcasted_iota(jnp.int32, pool4.shape, 0)
        col = lax.broadcasted_iota(jnp.int32, pool4.shape, 1) * KERNELS[1]
        pool4[...] = jnp.where((ids >= col) & (ids < col + KERNELS[1]), 1.0 / KERNELS[1], 0.0).astype(low)
        x[:, whole:] = jnp.zeros((total_rows, wide_length - whole), wide)

    groups = 3
    for group in range(groups):
        @task(-1, 3.0)
        def _(group=group):
            def step(k, carry):
                window_copy(k).wait()
                rows = pl.ds(pl.multiple_of(k * strip, strip), strip)
                value = stage[k % slots]
                center = jnp.sum(value, axis=1, keepdims=True) * (1.0 / length)
                value = value - center
                spread = jnp.sqrt(jnp.sum(value * value, axis=1, keepdims=True) * (1.0 / length) + 1e-05)
                factor = 1.0 / spread
                center_s[rows, :] = center
                scale_s[rows, :] = factor
                value = value * factor
                x[rows, 0:length] = value

                @pl.when(k + slots < strips)
                def _():
                    window_copy(k + slots).start()
                return carry
            lax.fori_loop(group * strips // groups, (group + 1) * strips // groups, step, 0)

    @task(-1, 3.0)
    def _():
        def body(rows):
            for k in range(0, wide_length, 1024):
                width = min(1024, wide_length - k)
                high, rest = parts_low(x[rows, k : k + width])
                pooled = mul(high, pool8[0:width]) + mul(rest, pool8[0:width])
                p0[rows, k // 8 : k // 8 + 128] = pooled.astype(low)
        over_rows(body)
        outgoing(p0, p0_out, 0).start()

    def activate(z, stack_id, j, rows):
        gate = jax.nn.sigmoid(z)
        act = z * gate
        a[j, rows, :] = act.astype(low)
        slope[j, rows, :] = (gate + act * (1.0 - gate)).astype(low)

    def send_layer(stack_id, j):
        outgoing(a.at[j], a_out.at[stack_id, j], 8 + 2 * j).start()
        outgoing(slope.at[j], slope_out.at[stack_id, j], 9 + 2 * j).start()

    def settle_layer(stack_id, j):
        outgoing(a.at[j], a_out.at[stack_id, j], 8 + 2 * j).wait()
        outgoing(slope.at[j], slope_out.at[stack_id, j], 9 + 2 * j).wait()

    for stack_id in range(3):
        inputs = (p0, p1, x2)[stack_id]

        @task(cut_of((stack_id, "first")), (1.3, 2.2, 6.0)[stack_id])
        def _(stack_id=stack_id, inputs=inputs):
            if stack_id > 0:
                settle_layer(stack_id - 1, 0)

            def body(rows):
                z = mul(inputs[rows, :], weights((stack_id, "first")), NT) + bias((stack_id, "first"))
                activate(z, stack_id, 0, rows)
            over_rows(body)
            send_layer(stack_id, 0)

        for layer_id in range(3):
            @task(cut_of((stack_id, layer_id)), 1.3)
            def _(stack_id=stack_id, layer_id=layer_id):
                if stack_id > 0:
                    settle_layer(stack_id - 1, layer_id + 1)

                def body(rows):
                    z = mul(a[layer_id, rows, :], weights((stack_id, layer_id))) + bias((stack_id, layer_id))
                    activate(z, stack_id, layer_id + 1, rows)
                over_rows(body)
                send_layer(stack_id, layer_id + 1)

        if stack_id < 2:
            for start, width in tiles:
                need = (pieces[stack_id, "back"][0] + start + width - 1) // cut_width

                @task(need, 1.4 if stack_id else 1.7)
                def _(stack_id=stack_id, start=start, width=width):
                    def body(rows):
                        cols = slice(start, start + width)
                        head = mul(a[3, rows, :], weights((stack_id, "back"), start, width))
                        rest = x[rows, cols] - (head + bias((stack_id, "back"), start, width))
                        if stack_id == 0:
                            x[rows, cols] = rest
                            high, tail = parts_low(rest)
                            pooled = mul(high, pool4[0:width]) + mul(tail, pool4[0:width])
                            p1[rows, start // 4 : start // 4 + 128] = pooled.astype(low)
                        else:
                            x2[rows, cols] = rest.astype(low)
                    over_rows(body)
                    if start + width == wide_length:
                        if stack_id == 0:
                            outgoing(p1, p1_out, 1).start()
                        else:
                            outgoing(x2, x2_out, 2).start()

            @task(cut_of((stack_id, "fore")), 1.5)
            def _(stack_id=stack_id):
                def body(rows):
                    knots = mul(a[3, rows, :], weights((stack_id, "fore"))) + bias((stack_id, "fore"), 0, 128)
                    high, rest = parts_low(knots)
                    ups = slice(128 * stack_id, 128 * stack_id + 128)
                    part = (
                        mul(high, up_high_ref[ups, :]) + mul(rest, up_high_ref[ups, :]) + mul(high, up_low_ref[ups, :])
                    )
                    fc[rows, :] = part if stack_id == 0 else fc[rows, :] + part
                over_rows(body)

    wide_steps = fc.shape[1]
    for start in range(0, wide_steps, 256):
        @task(cut_of((2, "fore")), 2.5)
        def _(start=start):
            if start == 0:
                targets_copy.wait()
                small_ref[...] = jnp.zeros_like(small_ref)
                small_ref[2:3, 0:128] = jnp.broadcast_to(jnp.sum(horizon_ref[...].astype(wide)), (1, 128))
            cols = slice(start, start + 256)
            head = mul(a[3], weights((2, "fore"), start, 256)) + bias_ref[
                bias_rows[2, "fore"][0] + start // hidden_size : bias_rows[2, "fore"][0] + start // hidden_size + 1,
                start % hidden_size : start % hidden_size + 256,
            ]
            goal = jnp.concatenate([tt[start : start + 128, :].T, tt[start + 128 : start + 256, :].T], axis=1)
            goal = (goal - center_s[...]) * scale_s[...]
            step = lax.broadcasted_iota(jnp.int32, (total_rows, 256), 1) + start
            diff = jnp.where(step < horizon_ref[...], fc[:, cols] + head - goal, 0.0)
            losses = jnp.sum(diff * diff, axis=0, keepdims=True)
            r = start // hidden_size
            small_ref[r : r + 1, start % hidden_size : start % hidden_size + 256] = losses
            diff = diff * (2.0 * scale)
            high, rest = parts_low(diff)
            g[:, cols] = high
            back = (
                mul(high, up_high_ref[:, cols], NT) + mul(rest, up_high_ref[:, cols], NT) + mul(high, up_low_ref[:, cols], NT)
            )
            dk[...] = back if start == 0 else dk[...] + back
            if start + 256 == wide_steps:
                g[:, wide_steps : wide_steps + 256] = dk[...].astype(low)
                outgoing(g, g_out, 3).start()

    queue = list(tasks)
    for cut in range(-1, count + 2):
        if cut >= 0:
            pump(cut)
        ready = cut - 2
        spent = 0.0
        while queue and queue[0][0] <= ready and (spent < 4.5 or cut == count + 1):
            _, cost, body = queue.pop(0)
            body()
            spent += cost
    for cut in range(count):
        to_x(cut).wait_send()
        to_y(cut).wait_send()
        onward(cut).wait_send()
        for kind in range(4):
            to_core(kind, cut).wait_send()
        w_copy(cut).wait()
    outgoing(p0, p0_out, 0).wait()
    outgoing(p1, p1_out, 1).wait()
    outgoing(x2, x2_out, 2).wait()
    outgoing(g, g_out, 3).wait()
    for j in range(4):
        settle_layer(2, j)


def forward(shard, windows, targets, horizon, bias_packed, up_high, up_low, pieces, bias_rows, scale):
    low, wide = jnp.bfloat16, jnp.float32
    rows, length = windows.shape
    hidden_size = bias_packed.shape[1]
    total = shard.shape[1]
    count = total // CHUNK
    wide_length = tiled(length)
    wide_steps = up_high.shape[1]
    p0_width, p1_width = tiled(length // KERNELS[0]), tiled(wide_length // KERNELS[1])
    strip = rows // 18
    hbm = pl.BlockSpec(memory_space=pltpu.HBM)
    vmem = pl.BlockSpec(memory_space=pltpu.VMEM)
    dma = pltpu.SemaphoreType.DMA
    shape = jax.ShapeDtypeStruct
    return pl.pallas_call(
        functools.partial(forward_kernel, (pieces, bias_rows, CHUNK, count, scale)),
        out_shape=(
            shape((8, hidden_size // 8, total), low),
            shape((3, 4, rows, hidden_size), low),
            shape((3, 4, rows, hidden_size), low),
            shape((rows, p0_width), low),
            shape((rows, p1_width), low),
            shape((rows, wide_length), low),
            shape((rows, wide_steps + 256), low),
            shape((8, hidden_size), wide),
        ),
        in_specs=[hbm, hbm, hbm, vmem, vmem, vmem, vmem],
        out_specs=(hbm,) * 7 + (vmem,),
        scratch_shapes=[
            pltpu.VMEM((8, hidden_size // 8, total), low),
            pltpu.VMEM((rows, wide_length), wide),
            pltpu.VMEM((4, strip, length), wide),
            pltpu.VMEM((4, rows, hidden_size), low),
            pltpu.VMEM((4, rows, hidden_size), low),
            pltpu.VMEM((rows, p0_width), low),
            pltpu.VMEM((rows, p1_width), low),
            pltpu.VMEM((rows, wide_length), low),
            pltpu.VMEM((rows, wide_steps), wide),
            pltpu.VMEM((wide_steps, rows), wide),
            pltpu.VMEM((rows, wide_steps + 256), low),
            pltpu.VMEM((rows, 256), wide),
            pltpu.VMEM((rows, 1), wide),
            pltpu.VMEM((rows, 1), wide),
            pltpu.VMEM((1024, 128), low),
            pltpu.VMEM((512, 128), low),
            dma,
            dma((7, count)),
            dma((7, count)),
            dma((4,)),
            dma,
            dma((16,)),
            dma((count,)),
        ],
        compiler_params=pltpu.CompilerParams(
            collective_id=0, has_side_effects=True, vmem_limit_bytes=63 * 1024 * 1024
        ),
        name="forward",
    )(shard, windows, targets.T, horizon.reshape(rows, 1), bias_packed, up_high, up_low)


def chunk_plan(length, steps_ahead_total, hidden_size):
    where = {}
    tile = hidden_size
    full, rest = tiled(length) // tile, tiled(length) % tile
    steps = tiled(steps_ahead_total)
    where[2, "fore"] = [(0, 0, tile), (1, 0, steps - tile)]
    for i in range(3):
        where[2, 2 - i] = [(2 + i, 0, tile)]
    t = 5
    where[2, "first"] = [(t + 2 * k, 0, tile) for k in range(full)] + [(t + 2 * full, 0, rest)]
    where[1, "back"] = [(t + 2 * k + 1, 0, tile) for k in range(full)] + [(t + 2 * full, rest, rest)]
    t += 2 * full
    where[1, "fore"] = [(t, 2 * rest, 128)]
    for i in range(3):
        where[1, 2 - i] = [(t + 1 + i, 0, tile)]
    t += 4
    where[1, "first"] = [(t, 0, tile), (t + 1, 0, tile)]
    t += 2
    where[0, "back"] = [(t + k, 0, tile) for k in range(full)] + [(t + full, 0, rest)]
    t += full
    where[0, "fore"] = [(t, rest, 128)]
    for i in range(3):
        where[0, 2 - i] = [(t + 1 + i, 0, tile)]
    where[0, "first"] = [(t + 4, 0, tile)]
    return where, t + 5


LAGS = (1, 3, 5, 7, 9, 11, 13)


def backward_kernel(
    plan,
    w_ref, a_ref, slope_ref, p0_ref, p1_ref, x2_ref, g_ref, forward_small_ref,
    out_ref, dx_ref, small_out_ref, square_ref,
    wh, wf2, wf, w1, wtile, wtail, a4, ah, sl, ytile, x2tail, g, dz, gb, dxb, dxt, da, spread,
    gbuf, from_core, s1, r1, keep, s2, r2, plane, zs, zr, zp_s, zp_r, final,
    small_s, small_r, square_s, square_r,
    wh_sem, wf_sem, wtile_sem, wtail_sem, a4_sem, ah_sem, sl_sem, y_sem, misc_sem, dx_sem,
    core_ss, core_rs, credit, ss1, rs1, ss2, rs2, zss, zrs, pss, prs, fss, frs, small_ss, small_rs, sq_ss, sq_rs, out_sem,
):
    pieces, bias_rows, count, full = plan
    row, me, core, other, over_x, over_y = places()
    lane = core
    chip, chip_x, chip_y = me // 2, over_x // 2, over_y // 2
    chip_d = chip_x + chip_y - chip
    wide, low = jnp.float32, jnp.bfloat16
    total_rows = a_ref.shape[2]
    tile = a_ref.shape[3]
    rest = x2tail.shape[1]
    block = total_rows // 2
    upper = row // 2
    z_in = row + 1 - 2 * upper
    is_edge = (row == 0) | (row == 3)
    z_out = (row + 3 + 2 * upper) % 4
    t_tail1 = 5 + 2 * full
    t_first1 = t_tail1 + 4
    t_back0 = t_first1 + 2
    t_tail0 = t_back0 + full

    barrier = pltpu.get_barrier_semaphore()
    for peer in range(1, 8):
        pl.semaphore_signal(barrier, inc=1, device_id=(row, (me + peer) % 8), device_id_type=MESH)
    for peer in range(1, 4):
        pl.semaphore_signal(barrier, inc=1, device_id=((row + peer) % 4, me), device_id_type=MESH)

    def local(src, dst, sem):
        return pltpu.make_async_copy(src, dst, sem)

    def w_cols(start, width):
        return w_ref.at[:, :, pl.ds(start, width)]

    def load_g():
        return local(g_ref, g, misc_sem.at[0])

    def load_x2tail():
        return local(x2_ref.at[:, full * tile : full * tile + rest], x2tail, misc_sem.at[1])

    def load_w1():
        return local(w_cols(pieces[1, "first"][0], w1.shape[2]), w1, misc_sem.at[2])

    def load_wf2():
        return local(w_cols(pieces[2, "fore"][0], wf2.shape[2]), wf2, misc_sem.at[3])

    def load_wf(stack_id):
        return local(w_cols(pieces[stack_id, "fore"][0], 128), wf.at[stack_id], wf_sem.at[stack_id])

    tails = ((2, "first"), (1, "back"), (0, "back"))

    def load_wtail(k):
        return local(w_cols(pieces[tails[k]][0] + full * tile, rest), wtail.at[k], wtail_sem.at[k])

    def load_a4(stack_id):
        return local(a_ref.at[stack_id, 3], a4.at[stack_id % 2], a4_sem.at[stack_id])

    def load_wh(i):
        return local(w_cols(pieces[2 - i // 3, 2 - i % 3][0], tile), wh.at[i], wh_sem.at[i])

    def wait_wh(i):
        local(w_cols(0, tile), wh.at[i], wh_sem.at[i]).wait()

    def load_ah(i):
        return local(a_ref.at[2 - i // 3, 2 - i % 3], ah.at[i % 3], ah_sem.at[i % 3])

    def load_sl(q):
        return local(slope_ref.at[2 - q // 4, 3 - q % 4], sl.at[q % 3], sl_sem.at[q % 3])

    def start_y(n):
        @pl.when(n < full)
        def _():
            cols = pl.ds(pl.multiple_of(n * tile, tile), tile)
            local(x2_ref.at[:, cols], ytile.at[n % 2], y_sem.at[n % 2]).start()

        @pl.when((n >= full) & (n < full + 2))
        def _():
            cols = pl.ds(pl.multiple_of((n - full) * tile, tile), tile)
            local(p1_ref.at[:, cols], ytile.at[n % 2], y_sem.at[n % 2]).start()

        @pl.when(n == full + 2)
        def _():
            local(p0_ref, ytile.at[n % 2], y_sem.at[n % 2]).start()

    def wait_y(n):
        local(p0_ref, ytile.at[n % 2], y_sem.at[n % 2]).wait()

    def start_wtile(m):
        def go(key, k):
            cols = pl.multiple_of(pieces[key][0] + k * tile, 128)
            local(w_cols(cols, tile), wtile.at[m % 3], wtile_sem.at[m % 3]).start()

        @pl.when((m < 2 * full) & (m % 2 == 0))
        def _():
            go((2, "first"), m // 2)

        @pl.when((m < 2 * full) & (m % 2 == 1))
        def _():
            go((1, "back"), m // 2)

        @pl.when((m >= 2 * full) & (m < 3 * full))
        def _():
            go((0, "back"), m - 2 * full)

    def wait_wtile(m):
        local(w_cols(0, tile), wtile.at[m % 3], wtile_sem.at[m % 3]).wait()

    def dx_cols(k):
        return dx_ref.at[:, pl.ds(pl.multiple_of(k * tile, tile), tile)]

    def dx_store(k):
        return local(dxb.at[k % 2], dx_cols(k), dx_sem.at[k % 2])

    def dx_load(k):
        return local(dx_cols(k), dxb.at[k % 2], dx_sem.at[k % 2])

    load_g().start()
    load_a4(2).start()
    load_wf2().start()
    for q in range(3):
        load_sl(q).start()
        load_ah(q).start()
        load_wh(q).start()
    for n in range(2):
        start_y(jnp.int32(n))
    for m in range(3):
        start_wtile(jnp.int32(m))
    load_a4(1).start()
    load_x2tail().start()
    for k in range(3):
        load_wtail(k).start()
    load_wf(1).start()
    load_wf(0).start()
    load_w1().start()
    for i in range(3, 9):
        load_wh(i).start()

    def core_copy(t):
        return remote(gbuf.at[t % 3, :, 1 - lane], from_core.at[t % 4], core_ss.at[t % 3], core_rs.at[t % 4], (row, other))

    def first_to(t, peer):
        return remote(s1.at[t % 4], r1.at[t], ss1.at[t % 4], rs1.at[t], (row, peer))

    def second_to(t, peer):
        return remote(s2.at[t % 4], r2.at[t], ss2.at[t % 4], rs2.at[t], (row, peer))

    def z_all(t):
        return remote(zs.at[t % 4], zr.at[t], zss.at[t % 4], zrs.at[t], (z_in, me))

    def z_part(t):
        return remote(zp_s.at[t % 4], zp_r.at[t], pss.at[t % 4], prs.at[t], (z_in, me))

    def z_final(t, way):
        return remote(final.at[t], final.at[t], fss.at[t, way], frs.at[t], ((z_in, z_out)[way], me))

    def owned(t):
        return row == 1 + (t // 2) % 2

    def by_parity(t, even, odd):
        pl.when(t % 2 == 0)(even)
        pl.when(t % 2 == 1)(odd)

    def emit(t):
        @pl.when(t >= 4)
        def _():
            pl.semaphore_wait(credit, 1)
        core_copy(t).start()

    def stage_one(t):
        core_copy(t).wait_recv()

        @pl.when(t >= 4)
        def _():
            first_to(t - 4, over_x).wait_send()

        def go(peer, sent, kept):
            for k, c in enumerate(sent):
                s1[t % 4, k] = (gbuf[t % 3, c, lane] + from_core[t % 4, c]).astype(low)
            first_to(t, peer).start()
            for k, c in enumerate(kept):
                keep[t % 6, k] = gbuf[t % 3, c, lane] + from_core[t % 4, c]

        by_parity(
            t,
            lambda: go(over_x, (chip_x, chip_d), (chip, chip_y)),
            lambda: go(over_y, (chip_y, chip_d), (chip, chip_x)),
        )

        @pl.when(t + 4 < count)
        def _():
            pl.semaphore_signal(credit, inc=1, device_id=(row, other), device_id_type=MESH)

    def stage_two(t):
        first_to(t, over_x).wait_recv()

        @pl.when(t >= 4)
        def _():
            second_to(t - 4, over_x).wait_send()
        s2[t % 4] = (keep[t % 6, 1] + r1[t, 1].astype(wide)).astype(low)
        by_parity(t, lambda: second_to(t, over_y).start(), lambda: second_to(t, over_x).start())
        keep[t % 6, 0] = keep[t % 6, 0] + r1[t, 0].astype(wide)

    def stage_three(t):
        second_to(t, over_x).wait_recv()
        total = keep[t % 6, 0] + r2[t].astype(wide)
        plane[t % 6] = total

        @pl.when(is_edge)
        def _():
            @pl.when(t >= 4)
            def _():
                z_all(t - 4).wait_send()
            zs[t % 4] = total.astype(low)
            z_all(t).start()

    def stage_four(t):
        @pl.when(jnp.logical_not(is_edge))
        def _():
            z_all(t).wait_recv()
            total = plane[t % 6] + zr[t].astype(wide)
            plane[t % 6] = total

            @pl.when(jnp.logical_not(owned(t)))
            def _():
                @pl.when(t >= 4)
                def _():
                    z_part(t - 4).wait_send()
                zp_s[t % 4] = total.astype(low)
                z_part(t).start()

    def stage_five(t):
        @pl.when(owned(t))
        def _():
            z_part(t).wait_recv()
            final[t] = (plane[t % 6] + zp_r[t].astype(wide)).astype(low)
            z_final(t, 0).start()
            z_final(t, 1).start()

    def stage_six(t):
        @pl.when(jnp.logical_not(is_edge) & jnp.logical_not(owned(t)))
        def _():
            z_final(t, 1).wait_recv()
            z_final(t, 1).start()

    def stage_seven(t):
        @pl.when(is_edge)
        def _():
            z_final(t, 0).wait_recv()
        local(final.at[t], out_ref.at[t], out_sem.at[t]).start()
        got = final[t].astype(wide)
        got = got * got
        acc = square_s[...]
        for k in range(0, got.shape[0], 8):
            for j in range(0, tile, 128):
                acc = acc + got[k : k + 8, j : j + 128]
        square_s[...] = acc

    stages = (stage_one, stage_two, stage_three, stage_four, stage_five, stage_six, stage_seven)

    def over_rows(body):
        def step(k, carry):
            body(pl.ds(pl.multiple_of(k * block, block), block), k)
            return carry
        lax.fori_loop(0, 2, step, 0)

    def add_row(r, value, k):
        width = value.shape[1]

        @pl.when(k == 0)
        def _():
            small_s[0, pl.ds(r, 1), 0:width] = value

        @pl.when(k > 0)
        def _():
            small_s[0, pl.ds(r, 1), 0:width] = small_s[0, pl.ds(r, 1), 0:width] + value

    def column_sums(value):
        return jnp.sum(value.astype(wide), axis=0, keepdims=True)

    def put(t, start, value):
        width = value.shape[1]
        gbuf[t % 3, :, :, :, start : start + width] = value.reshape(4, 2, tile // 8, width)

    def slot_free(t):
        @pl.when(t >= 3)
        def _():
            core_copy(t - 3).wait_send()

    def flat(value):
        return value.reshape(tile, value.shape[-1])

    def settle(q, r):
        load_sl(q).wait()

        def body(rows, k):
            low_dz = (da[rows, :] * sl[q % 3, rows, :].astype(wide)).astype(low)
            dz[rows, :] = low_dz
            add_row(r, column_sums(low_dz), k)
        over_rows(body)

        @pl.when(q + 3 < 12)
        def _():
            load_sl(q + 3).start()

    def fore_two_a(t):
        load_g().wait()
        load_a4(2).wait()
        put(t, 0, mul(a4[0], g[:, 0:tile], TN))
        emit(t)
        r = bias_rows[2, "fore"][0]
        small_s[0, r : r + 1, :] = column_sums(g[:, 0:tile])

    def fore_two_b(t):
        width = wf2.shape[2]
        put(t, 0, mul(a4[0], g[:, tile:width], TN))
        gbuf[t % 3, :, :, :, width - tile :] = jnp.zeros((4, 2, tile // 8, 2 * tile - width), wide)
        emit(t)
        load_a4(0).start()
        r = bias_rows[2, "fore"][0]
        small_s[0, r + 1 : r + 2, 0 : width - tile] = column_sums(g[:, tile:width])
        load_wf2().wait()

        def body(rows, k):
            da[rows, :] = mul(g[rows, 0:width], flat(wf2[...]), NT)
        over_rows(body)
        settle(jnp.int32(0), bias_rows[2, 2][0])

    def hidden(t, i):
        load_ah(i).wait()
        slot_free(t)
        put(t, 0, mul(ah[i % 3], dz[...], TN))
        emit(t)

        @pl.when(i + 3 < 9)
        def _():
            load_ah(i + 3).start()
        wait_wh(i)
        q = i + 1 + i // 3
        load_sl(q).wait()
        r = 4 * (2 - i // 3) + 2 - i % 3

        def body(rows, k):
            d = mul(dz[rows, :], flat(wh[i]), NT)
            low_dz = (d * sl[q % 3, rows, :].astype(wide)).astype(low)
            dz[rows, :] = low_dz
            add_row(r, column_sums(low_dz), k)
        over_rows(body)

        @pl.when(q + 3 < 12)
        def _():
            load_sl(q + 3).start()

    def first_two(t, k):
        wait_y(k)
        slot_free(t)
        put(t, 0, mul(dz[...], ytile[k % 2], TN))
        emit(t)
        start_y(k + 2)
        m = 2 * k
        wait_wtile(m)

        @pl.when(k >= 2)
        def _():
            dx_store(k - 2).wait()
        r = bias_rows[1, "back"][0] + k

        def body(rows, b):
            dx = mul(dz[rows, :], flat(wtile[m % 3]))
            dxb[k % 2, rows, :] = dx
            low_gb = (-dx).astype(low)
            gb[rows, :] = low_gb
            add_row(r, column_sums(low_gb), b)
        over_rows(body)
        dx_store(k).start()
        start_wtile(m + 3)

    def back_head(stack_id, m, first):
        def body(rows, b):
            part = mul(gb[rows, :], flat(wtile[m % 3]), NT)

            @pl.when(first)
            def _():
                da[rows, :] = part

            @pl.when(jnp.logical_not(first))
            def _():
                da[rows, :] = da[rows, :] + part
        over_rows(body)
        start_wtile(m + 3)

    def back_one(t, k):
        @pl.when(k == 0)
        def _():
            load_a4(1).wait()
        slot_free(t)
        put(t, 0, mul(a4[1], gb[...], TN))
        emit(t)
        m = 2 * k + 1
        wait_wtile(m)
        back_head(1, m, k == 0)

    def tail_one(t):
        load_x2tail().wait()
        for k in range(3):
            load_wtail(k).wait()
        load_wf(1).wait()
        slot_free(t)

        def body(rows, k):
            dx = mul(dz[rows, :], flat(wtail[0]))
            dxt[rows, :] = dx
            low_gb = (-dx).astype(low)
            gb[rows, 0:rest] = low_gb
            gb[rows, rest : rest + 128] = g[rows, 896:1024]
            add_row(bias_rows[1, "back"][0] + full, column_sums(low_gb), k)
            add_row(bias_rows[1, "fore"][0], column_sums(g[rows, 896:1024]), k)
            da[rows, :] = (
                da[rows, :] + mul(low_gb, flat(wtail[1]), NT) + mul(g[rows, 896:1024], flat(wf[1]), NT)
            )
        over_rows(body)
        put(t, 0, mul(dz[...], x2tail[...], TN))
        put(t, rest, mul(a4[1], gb[:, 0 : rest + 128], TN))
        gbuf[t % 3, :, :, :, 2 * rest + 128 :] = jnp.zeros((4, 2, tile // 8, tile - 2 * rest - 128), wide)
        emit(t)
        for k in (full - 2, full - 1):
            dx_store(jnp.int32(k)).wait()
        for k in range(2):
            dx_load(jnp.int32(k)).start()
        settle(jnp.int32(4), bias_rows[1, 2][0])

    def first_one(t, k):
        wait_y(k)
        slot_free(t)
        put(t, 0, mul(dz[...], ytile[k % 2], TN))
        emit(t)
        start_y(k + 2)

    def pooled_back(rows, cols, width):
        high, tail = parts_low(mul(dz[rows, :], flat(w1[:, :, cols])))
        return mul(high, spread[:, 0:width]) + mul(tail, spread[:, 0:width])

    def back_zero(t, k):
        @pl.when(k == 0)
        def _():
            load_w1().wait()
            load_a4(0).wait()
        dx_load(k).wait()
        r = bias_rows[0, "back"][0] + k

        def body(rows, b):
            cols = pl.ds(pl.multiple_of(k * 128, 128), 128)
            low_gb = (-(dxb[k % 2, rows, :] + pooled_back(rows, cols, tile))).astype(low)
            gb[rows, :] = low_gb
            add_row(r, column_sums(low_gb), b)
        over_rows(body)

        @pl.when(k + 2 < full)
        def _():
            dx_load(k + 2).start()
        slot_free(t)
        put(t, 0, mul(a4[0], gb[...], TN))
        emit(t)
        m = 2 * full + k
        wait_wtile(m)
        back_head(0, m, k == 0)

    def tail_zero(t):
        load_wf(0).wait()

        def body(rows, k):
            low_gb = (-(dxt[rows, :] + pooled_back(rows, slice(full * 128, full * 128 + 128), rest))).astype(low)
            gb[rows, 0:rest] = low_gb
            gb[rows, rest : rest + 128] = g[rows, 768:896]
            add_row(bias_rows[0, "back"][0] + full, column_sums(low_gb), k)
            add_row(bias_rows[0, "fore"][0], column_sums(g[rows, 768:896]), k)
            da[rows, :] = (
                da[rows, :] + mul(low_gb, flat(wtail[2]), NT) + mul(g[rows, 768:896], flat(wf[0]), NT)
            )
        over_rows(body)
        slot_free(t)
        put(t, 0, mul(a4[0], gb[:, 0 : rest + 128], TN))
        gbuf[t % 3, :, :, :, rest + 128 :] = jnp.zeros((4, 2, tile // 8, tile - rest - 128), wide)
        emit(t)
        settle(jnp.int32(8), bias_rows[0, 2][0])

    row_pair = row + 1 - 2 * (row % 2)
    row_far = row + 2 - 4 * (row // 2)
    hops = ((row, other), (row, over_x), (row, over_y), (row_pair, me), (row_far, me))

    def small_step(k):
        return remote(small_s.at[k], small_r.at[k], small_ss.at[k], small_rs.at[k], hops[k])

    def small_stage(k):
        if k > 0:
            small_step(k - 1).wait_recv()
            total = small_s[k - 1] + small_r[k - 1]
            if k < len(hops):
                small_s[k] = total
            else:
                small_out_ref[...] = total
        if k < len(hops):
            small_step(k).start()

    square_s[...] = jnp.zeros_like(square_s)
    small_s[0] = jnp.zeros(small_s.shape[1:], wide)
    extra = small_s.shape[1] - 8
    small_s[0, extra:, :] = forward_small_ref[...]
    ids = lax.broadcasted_iota(jnp.int32, spread.shape, 0) * KERNELS[1]
    col = lax.broadcasted_iota(jnp.int32, spread.shape, 1)
    spread[...] = jnp.where((col >= ids) & (col < ids + KERNELS[1]), 1.0 / KERNELS[1], 0.0).astype(low)

    pl.semaphore_wait(barrier, 10)

    def turn(t, carry):
        pl.when(t == 0)(lambda: fore_two_a(t))
        pl.when(t == 1)(lambda: fore_two_b(t))

        @pl.when(((t >= 2) & (t < 5)) | ((t > t_tail1) & (t < t_first1)) | ((t > t_tail0) & (t < t_tail0 + 4)))
        def _():
            past_one = (t + count - t_tail1) // count
            past_zero = (t + count - t_tail0) // count
            hidden(t, t - 2 - past_one * (t_tail1 - 4) - past_zero * (t_tail0 - t_tail1 - 3))

        in_pair = (t >= 5) & (t < t_tail1)
        pl.when(in_pair & (t % 2 == 1))(lambda: first_two(t, (t - 5) // 2))
        pl.when(in_pair & (t % 2 == 0))(lambda: back_one(t, (t - 6) // 2))
        pl.when(t == t_tail1)(lambda: tail_one(t))
        pl.when(((t >= t_first1) & (t < t_back0)))(lambda: first_one(t, t - t_first1 + full))
        pl.when(((t >= t_back0) & (t < t_tail0)))(lambda: back_zero(t, t - t_back0))
        pl.when(t == t_tail0)(lambda: tail_zero(t))
        pl.when(t == t_tail0 + 4)(lambda: first_one(t, t - t_tail0 - 4 + full + 2))

        for k in range(len(hops) + 1):
            pl.when(t == count + 2 * k)(functools.partial(small_stage, k))
        for lag, stage in zip(LAGS, stages):
            pl.when((t >= lag) & (t < count + lag))(functools.partial(stage, t - lag))
        return carry

    lax.fori_loop(0, count + LAGS[-1], turn, 0)

    def square_copy(peer):
        return remote(square_s, square_r.at[me], sq_ss.at[peer], sq_rs.at[peer], (row, (me + peer) % 8))

    def square_wait(peer):
        return remote(square_s, square_r.at[(me - peer + 8) % 8], sq_ss.at[peer], sq_rs.at[peer], (row, (me + peer) % 8))

    for peer in range(1, 8):
        square_copy(peer).start()
    square_r[me] = square_s[...]
    for peer in range(1, 8):
        square_wait(peer).wait_recv()
    acc = square_r[0]
    for k in range(1, 8):
        acc = acc + square_r[k]
    square_ref[...] = acc

    def finish(t, carry):
        @pl.when(t >= count - 3)
        def _():
            core_copy(t).wait_send()

        @pl.when(t >= count - 4)
        def _():
            first_to(t, over_x).wait_send()
            second_to(t, over_x).wait_send()

            @pl.when(is_edge)
            def _():
                z_all(t).wait_send()

        @pl.when(jnp.logical_not(is_edge))
        def _():
            @pl.when(owned(t))
            def _():
                z_final(t, 0).wait_send()
            z_final(t, 1).wait_send()

            @pl.when((t >= count - 4) & jnp.logical_not(owned(t)))
            def _():
                z_part(t).wait_send()
        local(final.at[t], out_ref.at[t], out_sem.at[t]).wait()
        return carry

    lax.fori_loop(0, count, finish, 0)
    for k in range(len(hops)):
        small_step(k).wait_send()
    for peer in range(1, 8):
        square_copy(peer).wait_send()


def backward(w, a, slope, p0, p1, x2, g, small, pieces, bias_rows, row_count, count):
    low, wide = jnp.bfloat16, jnp.float32
    rows, tile = a.shape[2], a.shape[3]
    part = tile // 8
    full, rest = x2.shape[1] // tile, x2.shape[1] % tile
    wide_steps = g.shape[1] - 256
    small_rows = row_count + 8
    hbm = pl.BlockSpec(memory_space=pltpu.HBM)
    vmem = pl.BlockSpec(memory_space=pltpu.VMEM)
    dma = pltpu.SemaphoreType.DMA
    shape = jax.ShapeDtypeStruct
    return pl.pallas_call(
        functools.partial(backward_kernel, (pieces, bias_rows, count, full)),
        out_shape=(
            shape((count, part, tile), low),
            shape((rows, full * tile), wide),
            shape((small_rows, tile), wide),
            shape((8, 128), wide),
        ),
        in_specs=[hbm] * 7 + [vmem],
        out_specs=(hbm, hbm, vmem, vmem),
        scratch_shapes=[
            pltpu.VMEM((9, 8, part, tile), low),
            pltpu.VMEM((8, part, wide_steps), low),
            pltpu.VMEM((2, 8, part, 128), low),
            pltpu.VMEM((8, part, p1.shape[1]), low),
            pltpu.VMEM((3, 8, part, tile), low),
            pltpu.VMEM((3, 8, part, rest), low),
            pltpu.VMEM((2, rows, tile), low),
            pltpu.VMEM((3, rows, tile), low),
            pltpu.VMEM((3, rows, tile), low),
            pltpu.VMEM((2, rows, tile), low),
            pltpu.VMEM((rows, rest), low),
            pltpu.VMEM(g.shape, low),
            pltpu.VMEM((rows, tile), low),
            pltpu.VMEM((rows, tile), low),
            pltpu.VMEM((2, rows, tile), wide),
            pltpu.VMEM((rows, rest), wide),
            pltpu.VMEM((rows, tile), wide),
            pltpu.VMEM((128, tile), low),
            pltpu.VMEM((3, 4, 2, part, tile), wide),
            pltpu.VMEM((4, 4, part, tile), wide),
            pltpu.VMEM((4, 2, part, tile), low),
            pltpu.VMEM((count, 2, part, tile), low),
            pltpu.VMEM((6, 2, part, tile), wide),
            pltpu.VMEM((4, part, tile), low),
            pltpu.VMEM((count, part, tile), low),
            pltpu.VMEM((6, part, tile), wide),
            pltpu.VMEM((4, part, tile), low),
            pltpu.VMEM((count, part, tile), low),
            pltpu.VMEM((4, part, tile), low),
            pltpu.VMEM((count, part, tile), low),
            pltpu.VMEM((count, part, tile), low),
            pltpu.VMEM((5, small_rows, tile), wide),
            pltpu.VMEM((5, small_rows, tile), wide),
            pltpu.VMEM((8, 128), wide),
            pltpu.VMEM((8, 8, 128), wide),
            dma((9,)),
            dma((2,)),
            dma((3,)),
            dma((3,)),
            dma((3,)),
            dma((3,)),
            dma((3,)),
            dma((2,)),
            dma((4,)),
            dma((2,)),
            dma((3,)),
            dma((4,)),
            pltpu.SemaphoreType.REGULAR,
            dma((4,)),
            dma((count,)),
            dma((4,)),
            dma((count,)),
            dma((4,)),
            dma((count,)),
            dma((4,)),
            dma((count,)),
            dma((count, 2)),
            dma((count,)),
            dma((5,)),
            dma((5,)),
            dma((8,)),
            dma((8,)),
            dma((count,)),
        ],
        compiler_params=pltpu.CompilerParams(
            collective_id=1, has_side_effects=True, vmem_limit_bytes=63 * 1024 * 1024
        ),
        name="backward",
    )(w, a, slope, p0, p1, x2, g, small)


def prelude(devices, windows, targets, first_w, hidden_w, back_w, fore_w, bias_vec):
    length = windows.shape[1]
    steps_ahead_total = targets.shape[1]
    hidden_size = hidden_w.shape[-1]
    low = jnp.bfloat16
    pieces, total = packing(length, steps_ahead_total, hidden_size)
    rows, row_count = row_plan(length, steps_ahead_total, hidden_size)
    row_count = -(-row_count // 8) * 8
    parts = {}
    first_low, hidden_low, back_low, fore_low = first_w.T.astype(low), hidden_w.astype(low), back_w.astype(low), fore_w.astype(low)
    row_start = 0
    col_start = 0
    for stack_id in range(3):
        width = length // KERNELS[stack_id]
        parts[stack_id, "first"] = first_low[:, row_start : row_start + width]
        row_start += width
        for layer_id in range(3):
            parts[stack_id, layer_id] = hidden_low[stack_id, layer_id]
        if stack_id < 2:
            parts[stack_id, "back"] = back_low[stack_id]
        width = steps_ahead_total // RATIOS[stack_id]
        parts[stack_id, "fore"] = fore_low[:, col_start : col_start + width]
        col_start += width
    shard = pack(parts, pieces, total)
    spans = {}
    cursor = 0
    for key in bias_order(length, steps_ahead_total, hidden_size):
        spans[key] = cursor
        cursor += rows[key][1]
    lines = []
    for key, (_, width) in rows.items():
        line = bias_vec[spans[key] : spans[key] + width]
        lines.append(jnp.pad(line, (0, -width % hidden_size)))
    lines = jnp.concatenate(lines)
    lines = jnp.pad(lines, (0, row_count * hidden_size - lines.shape[0])).reshape(row_count, hidden_size)
    ups = np.zeros((256, tiled(steps_ahead_total)), np.float32)
    for stack_id in range(2):
        knots = steps_ahead_total // RATIOS[stack_id]
        ups[128 * stack_id : 128 * stack_id + knots, :steps_ahead_total] = blend_coefficients(steps_ahead_total, knots)
    ups_high = ups.astype(jnp.bfloat16)
    ups_low = (ups - ups_high.astype(np.float32)).astype(jnp.bfloat16)
    scale = 2.0 ** -int(np.ceil(np.log2(devices * windows.shape[0] * steps_ahead_total)))
    return pieces, total, rows, spans, shard, lines, jnp.asarray(ups_high), jnp.asarray(ups_low), scale


def fast_body(
    devices,
    windows,
    targets,
    horizon,
    step_count,
    first_w,
    first_w_avg,
    first_w_sq,
    hidden_w,
    hidden_w_avg,
    hidden_w_sq,
    back_w,
    back_w_avg,
    back_w_sq,
    fore_w,
    fore_w_avg,
    fore_w_sq,
    bias_vec,
    bias_avg,
    bias_sq,
):
    low = jnp.bfloat16
    length, steps_ahead_total, hidden_size = windows.shape[1], targets.shape[1], hidden_w.shape[-1]
    pieces, total, rows, spans, shard, lines, up_high, up_low, scale = prelude(
        devices, windows, targets, first_w, hidden_w, back_w, fore_w, bias_vec
    )
    w, a, slope, p0, p1, x2, g, small = forward(
        shard, windows, targets, horizon, lines, up_high, up_low, pieces, rows, scale
    )
    where, count = chunk_plan(length, steps_ahead_total, hidden_size)
    row_count = lines.shape[0]
    owned, _, small, square = backward(w, a, slope, p0, p1, x2, g, small, pieces, rows, row_count, count)
    loss_sum = jnp.sum(small[row_count : row_count + 2])
    tally = small[row_count + 2, 0]
    bias_pieces = []
    for key in bias_order(length, steps_ahead_total, hidden_size):
        at, width = rows[key]
        bias_pieces.append(small[at : at - (-width // hidden_size)].reshape(-1)[:width])
    grad_bias = jnp.concatenate(bias_pieces)
    factor = 1.0 / (scale * tally)
    loss = loss_sum / tally
    grad_norm = jnp.sqrt(jnp.sum(square) + jnp.sum(grad_bias * grad_bias)) * factor
    clip_factor = jnp.minimum(1.0, CLIP_MAX / grad_norm) * factor
    step_float = step_count[0].astype(jnp.float32)

    def grad_piece(key):
        width = pieces[key][1]
        parts = [owned[t, :, start : start + size] for t, start, size in where[key]]
        return jnp.concatenate(parts, axis=1)[:, :width].astype(jnp.float32)

    grads_all = (
        jnp.concatenate([grad_piece((stack_id, "first")) for stack_id in range(3)], axis=1).T,
        jnp.stack([jnp.stack([grad_piece((stack_id, layer_id)) for layer_id in range(3)]) for stack_id in range(3)]),
        jnp.stack([grad_piece((stack_id, "back")) for stack_id in range(2)]),
        jnp.concatenate([grad_piece((stack_id, "fore")) for stack_id in range(3)], axis=1),
        grad_bias,
    )
    states = (
        (first_w, first_w_avg, first_w_sq),
        (hidden_w, hidden_w_avg, hidden_w_sq),
        (back_w, back_w_avg, back_w_sq),
        (fore_w, fore_w_avg, fore_w_sq),
        (bias_vec, bias_avg, bias_sq),
    )
    updated = []
    for state, grad in zip(states, grads_all):
        updated.append(adamw(state[0], state[1], state[2], grad * clip_factor, step_float))
    flat = [loss, grad_norm]
    for triple in updated:
        flat.extend(triple)
    flat += [triple[2].astype(low) for triple in updated[:4]]
    return tuple(flat)


def solution(mesh):
    fast = mesh.shape["fsdp"] == 8 and mesh.shape["dp"] == 4
    step = functools.partial(fast_body, mesh.shape["dp"] * mesh.shape["fsdp"]) if fast else body
    placed = (
        P(("dp", "fsdp"), None),
        P(("dp", "fsdp"), None),
        P(("dp", "fsdp")),
        P(),
        P(None, "fsdp"),
        P(None, "fsdp"),
        P(None, "fsdp"),
        P(None, None, "fsdp", None),
        P(None, None, "fsdp", None),
        P(None, None, "fsdp", None),
        P(None, "fsdp", None),
        P(None, "fsdp", None),
        P(None, "fsdp", None),
        P("fsdp", None),
        P("fsdp", None),
        P("fsdp", None),
        P(),
        P(),
        P(),
    )
    return jax.shard_map(
        step,
        mesh=mesh,
        in_specs=placed,
        out_specs=(
            P(),
            P(),
            P(None, "fsdp"),
            P(None, "fsdp"),
            P(None, "fsdp"),
            P(None, None, "fsdp", None),
            P(None, None, "fsdp", None),
            P(None, None, "fsdp", None),
            P(None, "fsdp", None),
            P(None, "fsdp", None),
            P(None, "fsdp", None),
            P("fsdp", None),
            P("fsdp", None),
            P("fsdp", None),
            P(),
            P(),
            P(),
            P(None, "fsdp"),
            P(None, None, "fsdp", None),
            P(None, "fsdp", None),
            P("fsdp", None),
        ),
        check_vma=False,
    )
```

```python
import functools
import jax
import jax.numpy as jnp
import numpy as np
from jax import lax
from jax.experimental import pallas as pl
from jax.experimental.pallas import tpu as pltpu
from jax.sharding import PartitionSpec as P

KERNELS = (8, 4, 1)
RATIOS = (24, 12, 1)
CLIP_MAX = 0.01
RATE = 0.02
BETA_ONE = 0.9
BETA_TWO = 0.999
EPSILON = 1e-08
DECAY = 0.01
DOT_EXACTNESS = lax.Precision.HIGHEST


def blend_coefficients(fine, coarse):
    column = np.arange(fine)
    numer = np.maximum((2 * column + 1) * coarse - fine, 0)
    lower_idx = numer // (2 * fine)
    frac = (numer - lower_idx * 2 * fine) / (2.0 * fine)
    upper_idx = np.minimum(lower_idx + 1, coarse - 1)
    matrix = np.zeros((coarse, fine), np.float32)
    matrix[lower_idx, column] += 1.0 - frac
    matrix[upper_idx, column] += frac
    return matrix


def normalize(windows, targets):
    center = jnp.mean(windows, axis=1, keepdims=True)
    spread = jnp.sqrt(jnp.mean((windows - center) ** 2, axis=1, keepdims=True) + 1e-05)
    return ((windows - center) / spread, (targets - center) / spread)


def mean_pool(values, kernel):
    if kernel == 1:
        return values
    return jnp.mean(values.reshape(values.shape[0], values.shape[1] // kernel, kernel), axis=2)


def pool_back(d_pooled, kernel):
    if kernel == 1:
        return d_pooled
    spread_out = jnp.broadcast_to((d_pooled / kernel)[:, :, None], d_pooled.shape + (kernel,))
    return spread_out.reshape(d_pooled.shape[0], d_pooled.shape[1] * kernel)


def silu_slope(pre_act):
    gate = jax.nn.sigmoid(pre_act)
    return gate * (1.0 + pre_act * (1.0 - gate))


def stack_params(stack_id, gathered, bias_vec, length, steps_ahead_total):
    first_full, hidden_full, back_full, fore_full = gathered
    hidden_size = hidden_full.shape[-1]
    row_start = sum((length // KERNELS[earlier] for earlier in range(stack_id)))
    col_start = sum((steps_ahead_total // RATIOS[earlier] for earlier in range(stack_id)))
    pooled_len = length // KERNELS[stack_id]
    anchor_entries = steps_ahead_total // RATIOS[stack_id]
    layers = [
        (
            first_full[row_start : row_start + pooled_len],
            bias_vec[stack_id * hidden_size : (stack_id + 1) * hidden_size],
        )
    ]
    for layer_id in range(3):
        offset = (3 + 3 * stack_id + layer_id) * hidden_size
        layers.append((hidden_full[stack_id, layer_id], bias_vec[offset : offset + hidden_size]))
    fore_start = 12 * hidden_size + 2 * length + col_start
    fore_pair = (
        fore_full[:, col_start : col_start + anchor_entries],
        bias_vec[fore_start : fore_start + anchor_entries],
    )
    back_pair = None
    if stack_id < 2:
        back_start = 12 * hidden_size + stack_id * length
        back_pair = (back_full[stack_id], bias_vec[back_start : back_start + length])
    linear_upsample_anchors = jnp.asarray(blend_coefficients(steps_ahead_total, anchor_entries))
    return (layers, fore_pair, back_pair, linear_upsample_anchors)


def stack_forward(residual, stack_id, layers, fore_pair, back_pair, linear_upsample_anchors):
    inputs_kept = [mean_pool(residual, KERNELS[stack_id]).astype(jnp.bfloat16)]
    pre_kept = []
    for weight, bias in layers:
        pre_act = jnp.dot(inputs_kept[-1], weight, preferred_element_type=jnp.float32) + bias
        pre_kept.append(pre_act)
        inputs_kept.append(jax.nn.silu(pre_act).astype(jnp.bfloat16))
    anchor_result = (
        jnp.dot(inputs_kept[-1], fore_pair[0], preferred_element_type=jnp.float32) + fore_pair[1]
    )
    running_subtotal = jnp.dot(anchor_result, linear_upsample_anchors, precision=DOT_EXACTNESS)
    backcast = None
    if back_pair is not None:
        backcast = (
            jnp.dot(inputs_kept[-1], back_pair[0], preferred_element_type=jnp.float32)
            + back_pair[1]
        )
    return ((inputs_kept, pre_kept), running_subtotal, backcast)


def head_grads(last_act, d_low, weight):
    grad_w = jnp.dot(last_act.T, d_low, preferred_element_type=jnp.float32)
    grad_b = jnp.sum(d_low.astype(jnp.float32), axis=0)
    return ((grad_w, grad_b), jnp.dot(d_low, weight.T, preferred_element_type=jnp.float32))


def stack_backward(kept, anchor_cotangent, d_backcast, layers, fore_pair, back_pair, need_input):
    inputs_kept, pre_kept = kept
    last_act = inputs_kept[-1]
    fore_grads, d_hidden = head_grads(last_act, anchor_cotangent.astype(jnp.bfloat16), fore_pair[0])
    back_grads = None
    if back_pair is not None:
        back_grads, d_extra = head_grads(last_act, d_backcast.astype(jnp.bfloat16), back_pair[0])
        d_hidden = d_hidden + d_extra
    layer_grads = [None, None, None, None]
    for layer_id in (3, 2, 1, 0):
        d_pre = (d_hidden * silu_slope(pre_kept[layer_id])).astype(jnp.bfloat16)
        layer_grads[layer_id] = (
            jnp.dot(inputs_kept[layer_id].T, d_pre, preferred_element_type=jnp.float32),
            jnp.sum(d_pre.astype(jnp.float32), axis=0),
        )
        if layer_id > 0 or need_input:
            d_hidden = jnp.dot(d_pre, layers[layer_id][0].T, preferred_element_type=jnp.float32)
    return (layer_grads, fore_grads, back_grads, d_hidden)


def adamw(weight, avg, square, grad, step_float):
    new_avg = BETA_ONE * avg + (1.0 - BETA_ONE) * grad
    new_sq = BETA_TWO * square + (1.0 - BETA_TWO) * grad * grad
    avg_hat = new_avg / (1.0 - BETA_ONE**step_float)
    sq_hat = new_sq / (1.0 - BETA_TWO**step_float)
    new_weight = weight - RATE * (avg_hat / (jnp.sqrt(sq_hat) + EPSILON) + DECAY * weight)
    return (new_avg, new_sq, new_weight)


def body(
    windows,
    targets,
    horizon,
    step_count,
    first_w,
    first_w_avg,
    first_w_sq,
    hidden_w,
    hidden_w_avg,
    hidden_w_sq,
    back_w,
    back_w_avg,
    back_w_sq,
    fore_w,
    fore_w_avg,
    fore_w_sq,
    bias_vec,
    bias_avg,
    bias_sq,
):
    length = windows.shape[1]
    steps_ahead_total = targets.shape[1]
    normed, observed_future = normalize(windows, targets)
    future_usable_flags = (
        jnp.arange(steps_ahead_total, dtype=jnp.int32)[None, :] < horizon[:, None]
    ).astype(jnp.float32)
    usable_tally = lax.psum(jnp.sum(horizon.astype(jnp.float32)), ("dp", "fsdp"))
    shards = (
        first_w.astype(jnp.bfloat16),
        hidden_w.astype(jnp.bfloat16),
        back_w.astype(jnp.bfloat16),
        fore_w.astype(jnp.bfloat16),
    )
    gathered = (
        lax.all_gather(shards[0], "fsdp", axis=1, tiled=True),
        lax.all_gather(shards[1], "fsdp", axis=2, tiled=True),
        lax.all_gather(shards[2], "fsdp", axis=1, tiled=True),
        lax.all_gather(shards[3], "fsdp", axis=0, tiled=True),
    )
    residual = normed
    kept_stacks = []
    predicted_future = jnp.zeros(observed_future.shape, jnp.float32)
    for stack_id in range(3):
        layers, fore_pair, back_pair, linear_upsample_anchors = stack_params(
            stack_id, gathered, bias_vec, length, steps_ahead_total
        )
        kept, running_subtotal, backcast = stack_forward(
            residual, stack_id, layers, fore_pair, back_pair, linear_upsample_anchors
        )
        kept_stacks.append(kept)
        predicted_future = predicted_future + running_subtotal
        if backcast is not None:
            residual = residual - backcast
    residual_difference = predicted_future - observed_future
    loss_part = (
        jnp.sum(future_usable_flags * residual_difference * residual_difference) / usable_tally
    )
    future_slope_cotangent = 2.0 * future_usable_flags * residual_difference / usable_tally
    again = (
        lax.all_gather(shards[0], "fsdp", axis=1, tiled=True),
        lax.all_gather(shards[1], "fsdp", axis=2, tiled=True),
        lax.all_gather(shards[2], "fsdp", axis=1, tiled=True),
        lax.all_gather(shards[3], "fsdp", axis=0, tiled=True),
    )
    results = [None, None, None]
    d_residual = None
    for stack_id in (2, 1, 0):
        layers, fore_pair, back_pair, linear_upsample_anchors = stack_params(
            stack_id, again, bias_vec, length, steps_ahead_total
        )
        anchor_cotangent = jnp.dot(
            future_slope_cotangent, linear_upsample_anchors.T, precision=DOT_EXACTNESS
        )
        d_backcast = None if d_residual is None else -d_residual
        results[stack_id] = stack_backward(
            kept_stacks[stack_id],
            anchor_cotangent,
            d_backcast,
            layers,
            fore_pair,
            back_pair,
            stack_id > 0,
        )
        if stack_id > 0:
            spread_back = pool_back(results[stack_id][3], KERNELS[stack_id])
            d_residual = spread_back if d_residual is None else d_residual + spread_back
    grad_first = jnp.concatenate([results[stack_id][0][0][0] for stack_id in range(3)], axis=0)
    grad_hidden = jnp.stack(
        [
            jnp.stack([results[stack_id][0][layer_id][0] for layer_id in (1, 2, 3)])
            for stack_id in range(3)
        ]
    )
    grad_back = jnp.stack([results[stack_id][2][0] for stack_id in range(2)])
    grad_fore = jnp.concatenate([results[stack_id][1][0] for stack_id in range(3)], axis=1)
    bias_pieces = [results[stack_id][0][0][1] for stack_id in range(3)]
    bias_pieces += [
        results[stack_id][0][layer_id][1] for stack_id in range(3) for layer_id in (1, 2, 3)
    ]
    bias_pieces += [results[stack_id][2][1] for stack_id in range(2)]
    bias_pieces += [results[stack_id][1][1] for stack_id in range(3)]
    grad_bias = jnp.concatenate(bias_pieces)
    owned = (
        lax.psum_scatter(grad_first, "fsdp", scatter_dimension=1, tiled=True),
        lax.psum_scatter(grad_hidden, "fsdp", scatter_dimension=2, tiled=True),
        lax.psum_scatter(grad_back, "fsdp", scatter_dimension=1, tiled=True),
        lax.psum_scatter(grad_fore, "fsdp", scatter_dimension=0, tiled=True),
    )
    owned = lax.psum((owned[0], owned[1], owned[2], owned[3]), "dp")
    grad_bias, loss = lax.psum((grad_bias, loss_part), ("dp", "fsdp"))
    local_sq = sum((jnp.sum(grad * grad) for grad in owned))
    total_sq = lax.psum(local_sq, "fsdp") + jnp.sum(grad_bias * grad_bias)
    grad_norm = jnp.sqrt(total_sq)
    clip_factor = jnp.minimum(1.0, CLIP_MAX / grad_norm)
    step_float = step_count[0].astype(jnp.float32)
    states = (
        (first_w, first_w_avg, first_w_sq),
        (hidden_w, hidden_w_avg, hidden_w_sq),
        (back_w, back_w_avg, back_w_sq),
        (fore_w, fore_w_avg, fore_w_sq),
        (bias_vec, bias_avg, bias_sq),
    )
    grads_all = (owned[0], owned[1], owned[2], owned[3], grad_bias)
    updated = []
    for state, grad in zip(states, grads_all):
        updated.append(adamw(state[0], state[1], state[2], grad * clip_factor, step_float))
    return (
        loss,
        grad_norm,
        updated[0][0],
        updated[0][1],
        updated[0][2],
        updated[1][0],
        updated[1][1],
        updated[1][2],
        updated[2][0],
        updated[2][1],
        updated[2][2],
        updated[3][0],
        updated[3][1],
        updated[3][2],
        updated[4][0],
        updated[4][1],
        updated[4][2],
        updated[0][2].astype(jnp.bfloat16),
        updated[1][2].astype(jnp.bfloat16),
        updated[2][2].astype(jnp.bfloat16),
        updated[3][2].astype(jnp.bfloat16),
    )


MESH = pl.DeviceIdType.MESH
CHUNK = 1024


def tiled(width):
    return -(-width // 128) * 128


def packing(length, steps_ahead_total, hidden_size):
    pieces = {}
    cursor = 0
    for stack_id in range(3):
        widths = [("first", length // KERNELS[stack_id])]
        widths += [(layer_id, hidden_size) for layer_id in range(3)]
        if stack_id < 2:
            widths.append(("back", length))
        widths.append(("fore", steps_ahead_total // RATIOS[stack_id]))
        for name, width in widths:
            pieces[stack_id, name] = (cursor, width)
            cursor += tiled(width)
    total = -(-cursor // CHUNK) * CHUNK
    return pieces, total


def pack(parts, pieces, total):
    out = []
    cursor = 0
    for key, (start, width) in pieces.items():
        part = parts[key]
        out.append(jnp.pad(part, ((0, 0), (0, tiled(width) - width))))
        cursor = start + tiled(width)
    rows, dtype = out[0].shape[0], out[0].dtype
    if total > cursor:
        out.append(jnp.zeros((rows, total - cursor), dtype))
    return jnp.concatenate(out, axis=1)


def places():
    row = lax.axis_index("dp")
    me = lax.axis_index("fsdp")
    core = me % 2
    across_x = (me // 2) % 2
    across_y = me // 4
    other = me + 1 - 2 * core
    over_x = me + 2 - 4 * across_x
    over_y = me + 4 - 8 * across_y
    return row, me, core, other, over_x, over_y


def remote(src, dst, send_sem, recv_sem, device):
    return pltpu.make_async_remote_copy(
        src_ref=src, dst_ref=dst, send_sem=send_sem, recv_sem=recv_sem, device_id=device, device_id_type=MESH
    )


HALF_LOW = 2


def row_plan(length, steps_ahead_total, hidden_size):
    rows = {}
    cursor = 0
    for stack_id in range(3):
        for name in ("first", 0, 1, 2):
            rows[stack_id, name] = (cursor, hidden_size)
            cursor += 1
    for stack_id in range(2):
        rows[stack_id, "back"] = (cursor, length)
        cursor += -(-length // hidden_size)
    for stack_id in range(3):
        width = steps_ahead_total // RATIOS[stack_id]
        rows[stack_id, "fore"] = (cursor, width)
        cursor += -(-width // hidden_size)
    return rows, cursor


def bias_order(length, steps_ahead_total, hidden_size):
    keys = [(stack_id, "first") for stack_id in range(3)]
    keys += [(stack_id, layer_id) for stack_id in range(3) for layer_id in range(3)]
    keys += [(stack_id, "back") for stack_id in range(2)]
    keys += [(stack_id, "fore") for stack_id in range(3)]
    return keys


def parts_low(value):
    high = value.astype(jnp.bfloat16)
    return high, (value - high.astype(jnp.float32)).astype(jnp.bfloat16)


NN = (((1,), (0,)), ((), ()))
NT = (((1,), (1,)), ((), ()))
TN = (((0,), (0,)), ((), ()))


def mul(left, right, dims=NN):
    return lax.dot_general(left, right, dims, preferred_element_type=jnp.float32)


def forward_kernel(
    plan,
    first_ref, hidden_ref, back_ref, fore_ref, windows_ref, targets_ref, horizon_ref, flat_ref, up_high_ref, up_low_ref,
    w_out, a_out, slope_out, p0_out, p1_out, x2_out, g_out, small_ref,
    w, x, stage, a, slope, p0, p1, x2, fc, tt, g, dk, center_s, scale_s, pool8, pool4,
    bias_ref, first_s, hidden_s, back_s, fore_s,
    raw_sem, send_sem, recv_sem, win_sem, tt_sem, out_sem, w_sem,
):
    pieces, bias_rows, spans, cut_width, count, scale = plan
    row, me, core, other, over_x, over_y = places()
    diag = over_x + over_y - me
    total_rows = windows_ref.shape[0]
    length = windows_ref.shape[1]
    hidden_size = a.shape[-1]
    steps_ahead = targets_ref.shape[0]
    block = total_rows // 2
    wide, low = jnp.float32, jnp.bfloat16
    wide_length = x.shape[1]
    tiles = [(k, min(hidden_size, wide_length - k)) for k in range(0, wide_length, hidden_size)]
    whole = wide_length // 128 * 128 - 128

    barrier = pltpu.get_barrier_semaphore()
    for peer in (other, over_x, over_y):
        pl.semaphore_signal(barrier, inc=1, device_id=(row, peer), device_id_type=MESH)

    def copy_of(kind, cut, src, holder, device):
        cols = slice(cut * cut_width, (cut + 1) * cut_width)
        return remote(
            src.at[:, cols], w.at[holder, :, cols], send_sem.at[kind, cut], recv_sem.at[kind, cut], (row, device)
        )

    def to_x(cut):
        return copy_of(0, cut, w.at[me], me, over_x)

    def to_y(cut):
        return copy_of(1, cut, w.at[me], me, over_y)

    def onward(cut):
        if cut % 2 == 0:
            return copy_of(2, cut, w.at[over_x], over_x, over_y)
        return copy_of(2, cut, w.at[over_y], over_y, over_x)

    def to_core(kind, cut):
        if kind == 0:
            return copy_of(3, cut, w.at[me], me, other)
        holder = (None, over_x, over_y, diag)[kind]
        return copy_of(3 + kind, cut, w.at[holder], holder, other)

    def own_sends(cut):
        to_x(cut).start()
        to_y(cut).start()
        to_core(0, cut).start()

    def w_copy(cut):
        cols = slice(cut * cut_width, (cut + 1) * cut_width)
        return pltpu.make_async_copy(w.at[:, :, cols], w_out.at[:, :, cols], w_sem.at[cut])

    look = 4

    def pump(cut):
        if cut < count:
            to_x(cut).wait_recv()
            if cut % 2 == 0:
                onward(cut).start()
            to_core(1, cut).start()
            to_y(cut).wait_recv()
            if cut % 2 == 1:
                onward(cut).start()
            to_core(2, cut).start()
            if cut + look < count:
                own_sends(cut + look)
        if 0 <= cut - 1 < count:
            onward(cut - 1).wait_recv()
            to_core(3, cut - 1).start()
        if 0 <= cut - 2 < count:
            for kind in range(4):
                to_core(kind, cut - 2).wait_recv()
            w_copy(cut - 2).start()

    tasks = []

    def task(need, cost):
        def keep(body):
            tasks.append((need, cost, body))
            return body
        return keep

    def cut_of(key):
        start, width = pieces[key]
        return (start + tiled(width) - 1) // cut_width

    def weights(key, start=0, width=None):
        at, full_width = pieces[key]
        width = tiled(full_width) if width is None else width
        return w[:, :, at + start : at + start + width].reshape(hidden_size, width)

    def bias(key, start=0, width=None):
        at, full_width = bias_rows[key]
        width = hidden_size if width is None else width
        return bias_ref[at + start // hidden_size : at + start // hidden_size + 1, 0:width]

    def over_rows(body):
        def step(k, carry):
            body(pl.ds(pl.multiple_of(k * block, block), block))
            return carry
        lax.fori_loop(0, 2, step, 0)

    def outgoing(src, dst, slot):
        return pltpu.make_async_copy(src, dst, out_sem.at[slot])

    slots = stage.shape[0]
    strip = stage.shape[1]
    strips = total_rows // strip

    def window_copy(k):
        rows = pl.ds(pl.multiple_of(k * strip, strip), strip)
        return pltpu.make_async_copy(windows_ref.at[rows], stage.at[k % slots], win_sem.at[k % slots])

    raw = [
        pltpu.make_async_copy(src, dst, raw_sem.at[k])
        for k, (src, dst) in enumerate(
            ((first_ref, first_s), (hidden_ref, hidden_s), (back_ref, back_s), (fore_ref, fore_s))
        )
    ]
    for copy in raw:
        copy.start()
    for k in range(slots):
        window_copy(k).start()
    targets_copy = pltpu.make_async_copy(targets_ref, tt.at[0:steps_ahead], tt_sem)
    targets_copy.start()

    def pack_piece(key, value):
        start, width = pieces[key]
        if width % 128:
            edge = start + width // 128 * 128
            w[me, :, edge : edge + 128] = jnp.zeros((value.shape[0], 128), low)
        w[me, :, start : start + width] = value.astype(low)

    def pack_stack(stack_id):
        width = pieces[stack_id, "first"][1]
        begin = sum(pieces[earlier, "first"][1] for earlier in range(stack_id))
        pack_piece((stack_id, "first"), first_s[:, begin : begin + width])
        for layer_id in range(3):
            pack_piece((stack_id, layer_id), hidden_s[3 * stack_id + layer_id])
        if stack_id < 2:
            pack_piece((stack_id, "back"), back_s[stack_id])
        width = pieces[stack_id, "fore"][1]
        begin = sum(pieces[earlier, "fore"][1] for earlier in range(stack_id))
        pack_piece((stack_id, "fore"), fore_s[:, begin : begin + width])

    raw[0].wait()
    raw[1].wait()
    raw[2].wait()
    raw[3].wait()
    pack_stack(0)
    pl.semaphore_wait(barrier, 3)
    for cut in range(look):
        own_sends(cut)
    pack_stack(1)
    pack_stack(2)
    packed = max(start + tiled(width) for start, width in pieces.values())
    if packed < w.shape[2]:
        w[me, :, packed:] = jnp.zeros((w.shape[1], w.shape[2] - packed), low)
    bias_ref[...] = jnp.zeros_like(bias_ref)
    for key, (at, width) in bias_rows.items():
        for k in range(0, width, hidden_size):
            flat = spans[key] + k
            todo = min(hidden_size, width - k)
            r, o = flat // hidden_size, flat % hidden_size
            here = min(todo, hidden_size - o)
            bias_ref[at + k // hidden_size : at + k // hidden_size + 1, 0:here] = flat_ref[r : r + 1, o : o + here]
            if here < todo:
                bias_ref[at + k // hidden_size : at + k // hidden_size + 1, here:todo] = flat_ref[r + 1 : r + 2, 0 : todo - here]

    @task(-1, 1.0)
    def _():
        ids = lax.broadcasted_iota(jnp.int32, pool8.shape, 0)
        col = lax.broadcasted_iota(jnp.int32, pool8.shape, 1) * KERNELS[0]
        pool8[...] = jnp.where((ids >= col) & (ids < col + KERNELS[0]), 1.0 / KERNELS[0], 0.0).astype(low)
        ids = lax.broadcasted_iota(jnp.int32, pool4.shape, 0)
        col = lax.broadcasted_iota(jnp.int32, pool4.shape, 1) * KERNELS[1]
        pool4[...] = jnp.where((ids >= col) & (ids < col + KERNELS[1]), 1.0 / KERNELS[1], 0.0).astype(low)
        x[:, whole:] = jnp.zeros((total_rows, wide_length - whole), wide)

    groups = 3
    for group in range(groups):
        @task(-1, 3.0)
        def _(group=group):
            def step(k, carry):
                window_copy(k).wait()
                rows = pl.ds(pl.multiple_of(k * strip, strip), strip)
                value = stage[k % slots]
                center = jnp.sum(value, axis=1, keepdims=True) * (1.0 / length)
                value = value - center
                spread = jnp.sqrt(jnp.sum(value * value, axis=1, keepdims=True) * (1.0 / length) + 1e-05)
                factor = 1.0 / spread
                center_s[rows, :] = center
                scale_s[rows, :] = factor
                value = value * factor
                x[rows, 0:length] = value

                @pl.when(k + slots < strips)
                def _():
                    window_copy(k + slots).start()
                return carry
            lax.fori_loop(group * strips // groups, (group + 1) * strips // groups, step, 0)

    @task(-1, 3.0)
    def _():
        def body(rows):
            for k in range(0, wide_length, 1024):
                width = min(1024, wide_length - k)
                high, rest = parts_low(x[rows, k : k + width])
                pooled = mul(high, pool8[0:width]) + mul(rest, pool8[0:width])
                p0[rows, k // 8 : k // 8 + 128] = pooled.astype(low)
        over_rows(body)
        outgoing(p0, p0_out, 0).start()

    def activate(z, stack_id, j, rows):
        gate = jax.nn.sigmoid(z)
        act = z * gate
        a[j, rows, :] = act.astype(low)
        slope[j % 2, rows, :] = (gate + act * (1.0 - gate)).astype(low)

    def a_copy(stack_id, j):
        return outgoing(a.at[j], a_out.at[stack_id, j], 8 + j)

    def slope_copy(stack_id, j):
        return outgoing(slope.at[j % 2], slope_out.at[stack_id, j], 12 + j % 2)

    def send_layer(stack_id, j):
        a_copy(stack_id, j).start()
        slope_copy(stack_id, j).start()

    def settle_layer(stack_id, j):
        if stack_id > 0:
            a_copy(stack_id - 1, j).wait()
        n = 4 * stack_id + j - 2
        if n >= 0:
            slope_copy(n // 4, n % 4).wait()

    for stack_id in range(3):
        inputs = (p0, p1, x2)[stack_id]

        @task(cut_of((stack_id, "first")), (1.3, 2.2, 6.0)[stack_id])
        def _(stack_id=stack_id, inputs=inputs):
            settle_layer(stack_id, 0)

            def body(rows):
                z = mul(inputs[rows, :], weights((stack_id, "first")), NT) + bias((stack_id, "first"))
                activate(z, stack_id, 0, rows)
            over_rows(body)
            send_layer(stack_id, 0)

        for layer_id in range(3):
            @task(cut_of((stack_id, layer_id)), 1.3)
            def _(stack_id=stack_id, layer_id=layer_id):
                settle_layer(stack_id, layer_id + 1)

                def body(rows):
                    z = mul(a[layer_id, rows, :], weights((stack_id, layer_id))) + bias((stack_id, layer_id))
                    activate(z, stack_id, layer_id + 1, rows)
                over_rows(body)
                send_layer(stack_id, layer_id + 1)

        if stack_id < 2:
            for start, width in tiles:
                need = (pieces[stack_id, "back"][0] + start + width - 1) // cut_width

                @task(need, 1.4 if stack_id else 1.7)
                def _(stack_id=stack_id, start=start, width=width):
                    def body(rows):
                        cols = slice(start, start + width)
                        head = mul(a[3, rows, :], weights((stack_id, "back"), start, width))
                        rest = x[rows, cols] - (head + bias((stack_id, "back"), start, width))
                        if stack_id == 0:
                            x[rows, cols] = rest
                            high, tail = parts_low(rest)
                            pooled = mul(high, pool4[0:width]) + mul(tail, pool4[0:width])
                            p1[rows, start // 4 : start // 4 + 128] = pooled.astype(low)
                        else:
                            x2[rows, cols] = rest.astype(low)
                    over_rows(body)
                    if start + width == wide_length:
                        if stack_id == 0:
                            outgoing(p1, p1_out, 1).start()
                        else:
                            outgoing(x2, x2_out, 2).start()

            @task(cut_of((stack_id, "fore")), 1.5)
            def _(stack_id=stack_id):
                def body(rows):
                    knots = mul(a[3, rows, :], weights((stack_id, "fore"))) + bias((stack_id, "fore"), 0, 128)
                    high, rest = parts_low(knots)
                    ups = slice(128 * stack_id, 128 * stack_id + 128)
                    part = (
                        mul(high, up_high_ref[ups, :]) + mul(rest, up_high_ref[ups, :]) + mul(high, up_low_ref[ups, :])
                    )
                    fc[rows, :] = part if stack_id == 0 else fc[rows, :] + part
                over_rows(body)

    wide_steps = fc.shape[1]
    for start in range(0, wide_steps, 256):
        @task(cut_of((2, "fore")), 2.5)
        def _(start=start):
            if start == 0:
                targets_copy.wait()
                small_ref[...] = jnp.zeros_like(small_ref)
                small_ref[2:3, 0:128] = jnp.broadcast_to(jnp.sum(horizon_ref[...].astype(wide)), (1, 128))
            cols = slice(start, start + 256)
            head = mul(a[3], weights((2, "fore"), start, 256)) + bias_ref[
                bias_rows[2, "fore"][0] + start // hidden_size : bias_rows[2, "fore"][0] + start // hidden_size + 1,
                start % hidden_size : start % hidden_size + 256,
            ]
            goal = jnp.concatenate([tt[start : start + 128, :].T, tt[start + 128 : start + 256, :].T], axis=1)
            goal = (goal - center_s[...]) * scale_s[...]
            step = lax.broadcasted_iota(jnp.int32, (total_rows, 256), 1) + start
            diff = jnp.where(step < horizon_ref[...], fc[:, cols] + head - goal, 0.0)
            losses = jnp.sum(diff * diff, axis=0, keepdims=True)
            r = start // hidden_size
            small_ref[r : r + 1, start % hidden_size : start % hidden_size + 256] = losses
            diff = diff * (2.0 * scale)
            high, rest = parts_low(diff)
            g[:, cols] = high
            back = (
                mul(high, up_high_ref[:, cols], NT) + mul(rest, up_high_ref[:, cols], NT) + mul(high, up_low_ref[:, cols], NT)
            )
            dk[...] = back if start == 0 else dk[...] + back
            if start + 256 == wide_steps:
                g[:, wide_steps : wide_steps + 256] = dk[...].astype(low)
                outgoing(g, g_out, 3).start()

    queue = list(tasks)
    for cut in range(-1, count + 2):
        if cut >= 0:
            pump(cut)
        ready = cut - 2
        spent = 0.0
        while queue and queue[0][0] <= ready and (spent < 4.5 or cut == count + 1):
            _, cost, body = queue.pop(0)
            body()
            spent += cost
    for cut in range(count):
        to_x(cut).wait_send()
        to_y(cut).wait_send()
        onward(cut).wait_send()
        for kind in range(4):
            to_core(kind, cut).wait_send()
        w_copy(cut).wait()
    outgoing(p0, p0_out, 0).wait()
    outgoing(p1, p1_out, 1).wait()
    outgoing(x2, x2_out, 2).wait()
    outgoing(g, g_out, 3).wait()
    for j in range(4):
        a_copy(2, j).wait()
    for j in (2, 3):
        slope_copy(2, j).wait()


def forward(first, hidden, back, fore, windows, targets, horizon, flat, up_high, up_low, pieces, bias_rows, spans, scale, total):
    low, wide = jnp.bfloat16, jnp.float32
    rows, length = windows.shape
    part, hidden_size = hidden.shape[1:]
    count = total // CHUNK
    wide_length = tiled(length)
    wide_steps = up_high.shape[1]
    p0_width, p1_width = tiled(length // KERNELS[0]), tiled(wide_length // KERNELS[1])
    row_count = -(-max(at - (-width // hidden_size) for at, width in bias_rows.values()) // 8) * 8
    strip = rows // 36
    hbm = pl.BlockSpec(memory_space=pltpu.HBM)
    vmem = pl.BlockSpec(memory_space=pltpu.VMEM)
    dma = pltpu.SemaphoreType.DMA
    shape = jax.ShapeDtypeStruct
    return pl.pallas_call(
        functools.partial(forward_kernel, (pieces, bias_rows, spans, CHUNK, count, scale)),
        out_shape=(
            shape((8, part, total), low),
            shape((3, 4, rows, hidden_size), low),
            shape((3, 4, rows, hidden_size), low),
            shape((rows, p0_width), low),
            shape((rows, p1_width), low),
            shape((rows, wide_length), low),
            shape((rows, wide_steps + 256), low),
            shape((8, hidden_size), wide),
        ),
        in_specs=[hbm] * 6 + [vmem] * 4,
        out_specs=(hbm,) * 7 + (vmem,),
        scratch_shapes=[
            pltpu.VMEM((8, part, total), low),
            pltpu.VMEM((rows, wide_length), wide),
            pltpu.VMEM((3, strip, length), wide),
            pltpu.VMEM((4, rows, hidden_size), low),
            pltpu.VMEM((2, rows, hidden_size), low),
            pltpu.VMEM((rows, p0_width), low),
            pltpu.VMEM((rows, p1_width), low),
            pltpu.VMEM((rows, wide_length), low),
            pltpu.VMEM((rows, wide_steps), wide),
            pltpu.VMEM((wide_steps, rows), wide),
            pltpu.VMEM((rows, wide_steps + 256), low),
            pltpu.VMEM((rows, 256), wide),
            pltpu.VMEM((rows, 1), wide),
            pltpu.VMEM((rows, 1), wide),
            pltpu.VMEM((1024, 128), low),
            pltpu.VMEM((512, 128), low),
            pltpu.VMEM((row_count, hidden_size), wide),
            pltpu.VMEM(first.shape, wide),
            pltpu.VMEM(hidden.shape, wide),
            pltpu.VMEM(back.shape, wide),
            pltpu.VMEM(fore.shape, wide),
            dma((4,)),
            dma((7, count)),
            dma((7, count)),
            dma((3,)),
            dma,
            dma((16,)),
            dma((count,)),
        ],
        compiler_params=pltpu.CompilerParams(
            collective_id=0, has_side_effects=True, vmem_limit_bytes=63 * 1024 * 1024
        ),
        name="forward",
    )(first, hidden, back, fore, windows, targets.T, horizon.reshape(rows, 1), flat, up_high, up_low)


def chunk_plan(length, steps_ahead_total, hidden_size):
    where = {}
    tile = hidden_size
    full, rest = tiled(length) // tile, tiled(length) % tile
    steps = tiled(steps_ahead_total)
    where[2, "fore"] = [(0, 0, tile), (1, 0, steps - tile)]
    for i in range(3):
        where[2, 2 - i] = [(2 + i, 0, tile)]
    t = 5
    where[2, "first"] = [(t + 2 * k, 0, tile) for k in range(full)] + [(t + 2 * full, 0, rest)]
    where[1, "back"] = [(t + 2 * k + 1, 0, tile) for k in range(full)] + [(t + 2 * full, rest, rest)]
    t += 2 * full
    where[1, "fore"] = [(t, 2 * rest, 128)]
    for i in range(3):
        where[1, 2 - i] = [(t + 1 + i, 0, tile)]
    t += 4
    where[1, "first"] = [(t, 0, tile), (t + 1, 0, tile)]
    t += 2
    where[0, "back"] = [(t + k, 0, tile) for k in range(full)] + [(t + full, 0, rest)]
    t += full
    where[0, "fore"] = [(t, rest, 128)]
    for i in range(3):
        where[0, 2 - i] = [(t + 1 + i, 0, tile)]
    where[0, "first"] = [(t + 4, 0, tile)]
    return where, t + 5


LAGS = (1, 3, 5, 7, 9, 11, 13)


def backward_kernel(
    plan,
    w_ref, a_ref, slope_ref, p0_ref, p1_ref, x2_ref, g_ref, forward_small_ref,
    out_ref, dx_ref, flat_ref, result_ref,
    wh, wf2, wf, w1, wtile, wtail, a4, ah, sl, ytile, x2tail, g, dz, gb, dxb, dxt, da, spread,
    gbuf, from_core, s1, r1, keep, s2, r2, plane, zs, zr, zp_s, zp_r, final,
    small_s, small_r, small_sum, square_s, square_r,
    wh_sem, wf_sem, wtile_sem, wtail_sem, a4_sem, ah_sem, sl_sem, y_sem, misc_sem, dx_sem,
    core_ss, core_rs, credit, ss1, rs1, ss2, rs2, zss, zrs, pss, prs, fss, frs, small_ss, small_rs, sq_ss, sq_rs, out_sem,
):
    pieces, bias_rows, spans, scale, count, full = plan
    row, me, core, other, over_x, over_y = places()
    lane = core
    chip, chip_x, chip_y = me // 2, over_x // 2, over_y // 2
    chip_d = chip_x + chip_y - chip
    wide, low = jnp.float32, jnp.bfloat16
    total_rows = a_ref.shape[2]
    tile = a_ref.shape[3]
    rest = x2tail.shape[1]
    upper = row // 2
    z_in = row + 1 - 2 * upper
    is_edge = (row == 0) | (row == 3)
    z_out = (row + 3 + 2 * upper) % 4
    t_tail1 = 5 + 2 * full
    t_first1 = t_tail1 + 4
    t_back0 = t_first1 + 2
    t_tail0 = t_back0 + full

    barrier = pltpu.get_barrier_semaphore()
    for peer in range(1, 8):
        pl.semaphore_signal(barrier, inc=1, device_id=(row, (me + peer) % 8), device_id_type=MESH)
    for peer in range(1, 4):
        pl.semaphore_signal(barrier, inc=1, device_id=((row + peer) % 4, me), device_id_type=MESH)

    def local(src, dst, sem):
        return pltpu.make_async_copy(src, dst, sem)

    def w_cols(start, width):
        return w_ref.at[:, :, pl.ds(start, width)]

    def load_g():
        return local(g_ref, g, misc_sem.at[0])

    def load_x2tail():
        return local(x2_ref.at[:, full * tile : full * tile + rest], x2tail, misc_sem.at[1])

    def load_w1():
        return local(w_cols(pieces[1, "first"][0], w1.shape[2]), w1, misc_sem.at[2])

    def load_wf2():
        return local(w_cols(pieces[2, "fore"][0], wf2.shape[2]), wf2, misc_sem.at[3])

    def load_wf(stack_id):
        return local(w_cols(pieces[stack_id, "fore"][0], 128), wf.at[stack_id], wf_sem.at[stack_id])

    tails = ((2, "first"), (1, "back"), (0, "back"))

    def load_wtail(k):
        return local(w_cols(pieces[tails[k]][0] + full * tile, rest), wtail.at[k], wtail_sem.at[k])

    def load_a4(stack_id):
        return local(a_ref.at[stack_id, 3], a4.at[stack_id % 2], a4_sem.at[stack_id])

    def load_wh(i):
        return local(w_cols(pieces[2 - i // 3, 2 - i % 3][0], tile), wh.at[i], wh_sem.at[i])

    def wait_wh(i):
        local(w_cols(0, tile), wh.at[i], wh_sem.at[i]).wait()

    def load_ah(i):
        return local(a_ref.at[2 - i // 3, 2 - i % 3], ah.at[i % 3], ah_sem.at[i % 3])

    def load_sl(q):
        return local(slope_ref.at[2 - q // 4, 3 - q % 4], sl.at[q % 3], sl_sem.at[q % 3])

    def start_y(n):
        @pl.when(n < full)
        def _():
            cols = pl.ds(pl.multiple_of(n * tile, tile), tile)
            local(x2_ref.at[:, cols], ytile.at[n % 2], y_sem.at[n % 2]).start()

        @pl.when((n >= full) & (n < full + 2))
        def _():
            cols = pl.ds(pl.multiple_of((n - full) * tile, tile), tile)
            local(p1_ref.at[:, cols], ytile.at[n % 2], y_sem.at[n % 2]).start()

        @pl.when(n == full + 2)
        def _():
            local(p0_ref, ytile.at[n % 2], y_sem.at[n % 2]).start()

    def wait_y(n):
        local(p0_ref, ytile.at[n % 2], y_sem.at[n % 2]).wait()

    def start_wtile(m):
        def go(key, k):
            cols = pl.multiple_of(pieces[key][0] + k * tile, 128)
            local(w_cols(cols, tile), wtile.at[m % 3], wtile_sem.at[m % 3]).start()

        @pl.when((m < 2 * full) & (m % 2 == 0))
        def _():
            go((2, "first"), m // 2)

        @pl.when((m < 2 * full) & (m % 2 == 1))
        def _():
            go((1, "back"), m // 2)

        @pl.when((m >= 2 * full) & (m < 3 * full))
        def _():
            go((0, "back"), m - 2 * full)

    def wait_wtile(m):
        local(w_cols(0, tile), wtile.at[m % 3], wtile_sem.at[m % 3]).wait()

    def dx_cols(k):
        return dx_ref.at[:, pl.ds(pl.multiple_of(k * tile, tile), tile)]

    def dx_store(k):
        return local(dxb.at[k % 2], dx_cols(k), dx_sem.at[k % 2])

    def dx_load(k):
        return local(dx_cols(k), dxb.at[k % 2], dx_sem.at[k % 2])

    load_g().start()
    load_a4(2).start()
    load_wf2().start()
    for q in range(3):
        load_sl(q).start()
        load_ah(q).start()
        load_wh(q).start()
    for n in range(2):
        start_y(jnp.int32(n))
    for m in range(3):
        start_wtile(jnp.int32(m))
    load_a4(1).start()
    load_x2tail().start()
    for k in range(3):
        load_wtail(k).start()
    load_wf(1).start()
    load_wf(0).start()
    load_w1().start()
    for i in range(3, 9):
        load_wh(i).start()

    def core_copy(t):
        return remote(gbuf.at[t % 3, :, 1 - lane], from_core.at[t % 4], core_ss.at[t % 3], core_rs.at[t % 4], (row, other))

    def first_to(t, peer):
        return remote(s1.at[t % 4], r1.at[t], ss1.at[t % 4], rs1.at[t], (row, peer))

    def second_to(t, peer):
        return remote(s2.at[t % 4], r2.at[t], ss2.at[t % 4], rs2.at[t], (row, peer))

    def z_all(t):
        return remote(zs.at[t % 4], zr.at[t], zss.at[t % 4], zrs.at[t], (z_in, me))

    def z_part(t):
        return remote(zp_s.at[t % 4], zp_r.at[t], pss.at[t % 4], prs.at[t], (z_in, me))

    def z_final(t, way):
        return remote(final.at[t], final.at[t], fss.at[t, way], frs.at[t], ((z_in, z_out)[way], me))

    def owned(t):
        return row == 1 + (t // 2) % 2

    def by_parity(t, even, odd):
        pl.when(t % 2 == 0)(even)
        pl.when(t % 2 == 1)(odd)

    def emit(t):
        @pl.when(t >= 4)
        def _():
            pl.semaphore_wait(credit, 1)
        core_copy(t).start()

    def stage_one(t):
        core_copy(t).wait_recv()

        @pl.when(t >= 4)
        def _():
            first_to(t - 4, over_x).wait_send()

        def go(peer, sent, kept):
            for k, c in enumerate(sent):
                s1[t % 4, k] = (gbuf[t % 3, c, lane] + from_core[t % 4, c]).astype(low)
            first_to(t, peer).start()
            for k, c in enumerate(kept):
                keep[t % 6, k] = gbuf[t % 3, c, lane] + from_core[t % 4, c]

        by_parity(
            t,
            lambda: go(over_x, (chip_x, chip_d), (chip, chip_y)),
            lambda: go(over_y, (chip_y, chip_d), (chip, chip_x)),
        )

        @pl.when(t + 4 < count)
        def _():
            pl.semaphore_signal(credit, inc=1, device_id=(row, other), device_id_type=MESH)

    def stage_two(t):
        first_to(t, over_x).wait_recv()

        @pl.when(t >= 4)
        def _():
            second_to(t - 4, over_x).wait_send()
        s2[t % 4] = (keep[t % 6, 1] + r1[t, 1].astype(wide)).astype(low)
        by_parity(t, lambda: second_to(t, over_y).start(), lambda: second_to(t, over_x).start())
        keep[t % 6, 0] = keep[t % 6, 0] + r1[t, 0].astype(wide)

    def stage_three(t):
        second_to(t, over_x).wait_recv()
        total = keep[t % 6, 0] + r2[t].astype(wide)
        plane[t % 6] = total

        @pl.when(is_edge)
        def _():
            @pl.when(t >= 4)
            def _():
                z_all(t - 4).wait_send()
            zs[t % 4] = total.astype(low)
            z_all(t).start()

    def stage_four(t):
        @pl.when(jnp.logical_not(is_edge))
        def _():
            z_all(t).wait_recv()
            total = plane[t % 6] + zr[t].astype(wide)
            plane[t % 6] = total

            @pl.when(jnp.logical_not(owned(t)))
            def _():
                @pl.when(t >= 4)
                def _():
                    z_part(t - 4).wait_send()
                zp_s[t % 4] = total.astype(low)
                z_part(t).start()

    def stage_five(t):
        @pl.when(owned(t))
        def _():
            z_part(t).wait_recv()
            final[t] = (plane[t % 6] + zp_r[t].astype(wide)).astype(low)
            z_final(t, 0).start()
            z_final(t, 1).start()

    def stage_six(t):
        @pl.when(jnp.logical_not(is_edge) & jnp.logical_not(owned(t)))
        def _():
            z_final(t, 1).wait_recv()
            z_final(t, 1).start()

    def stage_seven(t):
        @pl.when(is_edge)
        def _():
            z_final(t, 0).wait_recv()
        local(final.at[t], out_ref.at[t], out_sem.at[t]).start()
        got = final[t].astype(wide)
        got = got * got
        acc = square_s[...]
        for k in range(0, got.shape[0], 8):
            for j in range(0, tile, 128):
                acc = acc + got[k : k + 8, j : j + 128]
        square_s[...] = acc

    stages = (stage_one, stage_two, stage_three, stage_four, stage_five, stage_six, stage_seven)

    def over_rows(body):
        body(slice(None), 0)

    def add_row(r, value, k):
        small_s[0, pl.ds(r, 1), 0 : value.shape[1]] = value

    def column_sums(value):
        return jnp.sum(value.astype(wide), axis=0, keepdims=True)

    def put(t, start, value):
        width = value.shape[1]
        gbuf[t % 3, :, :, :, start : start + width] = value.reshape(4, 2, tile // 8, width)

    def slot_free(t):
        @pl.when(t >= 3)
        def _():
            core_copy(t - 3).wait_send()

    def flat(value):
        return value.reshape(tile, value.shape[-1])

    def settle(q, r):
        load_sl(q).wait()

        def body(rows, k):
            low_dz = (da[rows, :] * sl[q % 3, rows, :].astype(wide)).astype(low)
            dz[rows, :] = low_dz
            add_row(r, column_sums(low_dz), k)
        over_rows(body)

        @pl.when(q + 3 < 12)
        def _():
            load_sl(q + 3).start()

    def fore_two_a(t):
        load_g().wait()
        load_a4(2).wait()
        put(t, 0, mul(a4[0], g[:, 0:tile], TN))
        emit(t)
        r = bias_rows[2, "fore"][0]
        small_s[0, r : r + 1, :] = column_sums(g[:, 0:tile])

    def fore_two_b(t):
        width = wf2.shape[2]
        put(t, 0, mul(a4[0], g[:, tile:width], TN))
        gbuf[t % 3, :, :, :, width - tile :] = jnp.zeros((4, 2, tile // 8, 2 * tile - width), wide)
        emit(t)
        load_a4(0).start()
        r = bias_rows[2, "fore"][0]
        small_s[0, r + 1 : r + 2, 0 : width - tile] = column_sums(g[:, tile:width])
        load_wf2().wait()

        def body(rows, k):
            da[rows, :] = mul(g[rows, 0:width], flat(wf2[...]), NT)
        over_rows(body)
        settle(jnp.int32(0), bias_rows[2, 2][0])

    def hidden(t, i):
        load_ah(i).wait()
        slot_free(t)
        put(t, 0, mul(ah[i % 3], dz[...], TN))
        emit(t)

        @pl.when(i + 3 < 9)
        def _():
            load_ah(i + 3).start()
        wait_wh(i)
        q = i + 1 + i // 3
        load_sl(q).wait()
        r = 4 * (2 - i // 3) + 2 - i % 3

        def body(rows, k):
            d = mul(dz[rows, :], flat(wh[i]), NT)
            low_dz = (d * sl[q % 3, rows, :].astype(wide)).astype(low)
            dz[rows, :] = low_dz
            add_row(r, column_sums(low_dz), k)
        over_rows(body)

        @pl.when(q + 3 < 12)
        def _():
            load_sl(q + 3).start()

    def first_two(t, k):
        wait_y(k)
        slot_free(t)
        put(t, 0, mul(dz[...], ytile[k % 2], TN))
        emit(t)
        start_y(k + 2)
        m = 2 * k
        wait_wtile(m)

        @pl.when(k >= 2)
        def _():
            dx_store(k - 2).wait()
        r = bias_rows[1, "back"][0] + k

        def body(rows, b):
            dx = mul(dz[rows, :], flat(wtile[m % 3]))
            dxb[k % 2, rows, :] = dx
            low_gb = (-dx).astype(low)
            gb[rows, :] = low_gb
            add_row(r, column_sums(low_gb), b)
        over_rows(body)
        dx_store(k).start()
        start_wtile(m + 3)

    def back_head(stack_id, m, first):
        def body(rows, b):
            part = mul(gb[rows, :], flat(wtile[m % 3]), NT)

            @pl.when(first)
            def _():
                da[rows, :] = part

            @pl.when(jnp.logical_not(first))
            def _():
                da[rows, :] = da[rows, :] + part
        over_rows(body)
        start_wtile(m + 3)

    def back_one(t, k):
        @pl.when(k == 0)
        def _():
            load_a4(1).wait()
        slot_free(t)
        put(t, 0, mul(a4[1], gb[...], TN))
        emit(t)
        m = 2 * k + 1
        wait_wtile(m)
        back_head(1, m, k == 0)

    def tail_one(t):
        load_x2tail().wait()
        for k in range(3):
            load_wtail(k).wait()
        load_wf(1).wait()
        slot_free(t)

        def body(rows, k):
            dx = mul(dz[rows, :], flat(wtail[0]))
            dxt[rows, :] = dx
            low_gb = (-dx).astype(low)
            gb[rows, 0:rest] = low_gb
            gb[rows, rest : rest + 128] = g[rows, 896:1024]
            add_row(bias_rows[1, "back"][0] + full, column_sums(low_gb), k)
            add_row(bias_rows[1, "fore"][0], column_sums(g[rows, 896:1024]), k)
            da[rows, :] = (
                da[rows, :] + mul(low_gb, flat(wtail[1]), NT) + mul(g[rows, 896:1024], flat(wf[1]), NT)
            )
        over_rows(body)
        put(t, 0, mul(dz[...], x2tail[...], TN))
        put(t, rest, mul(a4[1], gb[:, 0 : rest + 128], TN))
        gbuf[t % 3, :, :, :, 2 * rest + 128 :] = jnp.zeros((4, 2, tile // 8, tile - 2 * rest - 128), wide)
        emit(t)
        for k in (full - 2, full - 1):
            dx_store(jnp.int32(k)).wait()
        for k in range(2):
            dx_load(jnp.int32(k)).start()
        settle(jnp.int32(4), bias_rows[1, 2][0])

    def first_one(t, k):
        wait_y(k)
        slot_free(t)
        put(t, 0, mul(dz[...], ytile[k % 2], TN))
        emit(t)
        start_y(k + 2)

    def pooled_back(rows, cols, width):
        high, tail = parts_low(mul(dz[rows, :], flat(w1[:, :, cols])))
        return mul(high, spread[:, 0:width]) + mul(tail, spread[:, 0:width])

    def back_zero(t, k):
        @pl.when(k == 0)
        def _():
            load_w1().wait()
            load_a4(0).wait()
        dx_load(k).wait()
        r = bias_rows[0, "back"][0] + k

        def body(rows, b):
            cols = pl.ds(pl.multiple_of(k * 128, 128), 128)
            low_gb = (-(dxb[k % 2, rows, :] + pooled_back(rows, cols, tile))).astype(low)
            gb[rows, :] = low_gb
            add_row(r, column_sums(low_gb), b)
        over_rows(body)

        @pl.when(k + 2 < full)
        def _():
            dx_load(k + 2).start()
        slot_free(t)
        put(t, 0, mul(a4[0], gb[...], TN))
        emit(t)
        m = 2 * full + k
        wait_wtile(m)
        back_head(0, m, k == 0)

    def tail_zero(t):
        load_wf(0).wait()

        def body(rows, k):
            low_gb = (-(dxt[rows, :] + pooled_back(rows, slice(full * 128, full * 128 + 128), rest))).astype(low)
            gb[rows, 0:rest] = low_gb
            gb[rows, rest : rest + 128] = g[rows, 768:896]
            add_row(bias_rows[0, "back"][0] + full, column_sums(low_gb), k)
            add_row(bias_rows[0, "fore"][0], column_sums(g[rows, 768:896]), k)
            da[rows, :] = (
                da[rows, :] + mul(low_gb, flat(wtail[2]), NT) + mul(g[rows, 768:896], flat(wf[0]), NT)
            )
        over_rows(body)
        slot_free(t)
        put(t, 0, mul(a4[0], gb[:, 0 : rest + 128], TN))
        gbuf[t % 3, :, :, :, rest + 128 :] = jnp.zeros((4, 2, tile // 8, tile - rest - 128), wide)
        emit(t)
        settle(jnp.int32(8), bias_rows[0, 2][0])

    row_pair = row + 1 - 2 * (row % 2)
    row_far = row + 2 - 4 * (row // 2)
    hops = ((row, other), (row, over_x), (row, over_y), (row_pair, me), (row_far, me))

    def small_step(k):
        return remote(small_s.at[k], small_r.at[k], small_ss.at[k], small_rs.at[k], hops[k])

    def small_stage(k):
        if k > 0:
            small_step(k - 1).wait_recv()
            total = small_s[k - 1] + small_r[k - 1]
            if k < len(hops):
                small_s[k] = total
            else:
                small_sum[...] = total
        if k < len(hops):
            small_step(k).start()

    square_s[...] = jnp.zeros_like(square_s)
    small_s[0] = jnp.zeros(small_s.shape[1:], wide)
    extra = small_s.shape[1] - 8
    small_s[0, extra:, :] = forward_small_ref[...]
    ids = lax.broadcasted_iota(jnp.int32, spread.shape, 0) * KERNELS[1]
    col = lax.broadcasted_iota(jnp.int32, spread.shape, 1)
    spread[...] = jnp.where((col >= ids) & (col < ids + KERNELS[1]), 1.0 / KERNELS[1], 0.0).astype(low)

    pl.semaphore_wait(barrier, 10)

    def turn(t, carry):
        pl.when(t == 0)(lambda: fore_two_a(t))
        pl.when(t == 1)(lambda: fore_two_b(t))

        @pl.when(((t >= 2) & (t < 5)) | ((t > t_tail1) & (t < t_first1)) | ((t > t_tail0) & (t < t_tail0 + 4)))
        def _():
            past_one = (t + count - t_tail1) // count
            past_zero = (t + count - t_tail0) // count
            hidden(t, t - 2 - past_one * (t_tail1 - 4) - past_zero * (t_tail0 - t_tail1 - 3))

        in_pair = (t >= 5) & (t < t_tail1)
        pl.when(in_pair & (t % 2 == 1))(lambda: first_two(t, (t - 5) // 2))
        pl.when(in_pair & (t % 2 == 0))(lambda: back_one(t, (t - 6) // 2))
        pl.when(t == t_tail1)(lambda: tail_one(t))
        pl.when(((t >= t_first1) & (t < t_back0)))(lambda: first_one(t, t - t_first1 + full))
        pl.when(((t >= t_back0) & (t < t_tail0)))(lambda: back_zero(t, t - t_back0))
        pl.when(t == t_tail0)(lambda: tail_zero(t))
        pl.when(t == t_tail0 + 4)(lambda: first_one(t, t - t_tail0 - 4 + full + 2))

        for k in range(len(hops) + 1):
            pl.when(t == count + 2 * k)(functools.partial(small_stage, k))
        for lag, stage in zip(LAGS, stages):
            pl.when((t >= lag) & (t < count + lag))(functools.partial(stage, t - lag))
        return carry

    lax.fori_loop(0, count + LAGS[-1], turn, 0)

    def square_copy(peer):
        return remote(square_s, square_r.at[me], sq_ss.at[peer], sq_rs.at[peer], (row, (me + peer) % 8))

    def square_wait(peer):
        return remote(square_s, square_r.at[(me - peer + 8) % 8], sq_ss.at[peer], sq_rs.at[peer], (row, (me + peer) % 8))

    for peer in range(1, 8):
        square_copy(peer).start()
    square_r[me] = square_s[...]
    for peer in range(1, 8):
        square_wait(peer).wait_recv()
    acc = square_r[0]
    for k in range(1, 8):
        acc = acc + square_r[k]
    tile_rows = small_s.shape[1] - 8
    biases = small_sum[0:tile_rows, :]
    total = jnp.sum(acc, keepdims=True) + jnp.sum(biases * biases, keepdims=True)
    tally = small_sum[tile_rows + 2 : tile_rows + 3, 0:1]
    factor = (1.0 / scale) / tally
    norm = jnp.sqrt(total) * factor
    result_ref[0:1, :] = jnp.broadcast_to(norm, (1, 128))
    loss = jnp.sum(small_sum[tile_rows : tile_rows + 2, :], keepdims=True) / tally
    result_ref[1:2, :] = jnp.broadcast_to(loss, (1, 128))
    result_ref[2:3, :] = jnp.broadcast_to(jnp.minimum(1.0, CLIP_MAX / norm) * factor, (1, 128))
    flat_ref[...] = jnp.zeros_like(flat_ref)
    for key, (at, width) in bias_rows.items():
        for k in range(0, width, tile):
            begin = spans[key] + k
            todo = min(tile, width - k)
            r, o = begin // tile, begin % tile
            here = min(todo, tile - o)
            line = slice(at + k // tile, at + k // tile + 1)
            flat_ref[r : r + 1, o : o + here] = small_sum[line, 0:here]
            if here < todo:
                flat_ref[r + 1 : r + 2, 0 : todo - here] = small_sum[line, here:todo]

    def finish(t, carry):
        @pl.when(t >= count - 3)
        def _():
            core_copy(t).wait_send()

        @pl.when(t >= count - 4)
        def _():
            first_to(t, over_x).wait_send()
            second_to(t, over_x).wait_send()

            @pl.when(is_edge)
            def _():
                z_all(t).wait_send()

        @pl.when(jnp.logical_not(is_edge))
        def _():
            @pl.when(owned(t))
            def _():
                z_final(t, 0).wait_send()
            z_final(t, 1).wait_send()

            @pl.when((t >= count - 4) & jnp.logical_not(owned(t)))
            def _():
                z_part(t).wait_send()
        local(final.at[t], out_ref.at[t], out_sem.at[t]).wait()
        return carry

    lax.fori_loop(0, count, finish, 0)
    for k in range(len(hops)):
        small_step(k).wait_send()
    for peer in range(1, 8):
        square_copy(peer).wait_send()


def backward(w, a, slope, p0, p1, x2, g, small, pieces, bias_rows, spans, scale, row_count, flat_rows, count):
    low, wide = jnp.bfloat16, jnp.float32
    rows, tile = a.shape[2], a.shape[3]
    part = tile // 8
    full, rest = x2.shape[1] // tile, x2.shape[1] % tile
    wide_steps = g.shape[1] - 256
    small_rows = row_count + 8
    hbm = pl.BlockSpec(memory_space=pltpu.HBM)
    vmem = pl.BlockSpec(memory_space=pltpu.VMEM)
    dma = pltpu.SemaphoreType.DMA
    shape = jax.ShapeDtypeStruct
    return pl.pallas_call(
        functools.partial(backward_kernel, (pieces, bias_rows, spans, scale, count, full)),
        out_shape=(
            shape((count, part, tile), low),
            shape((rows, full * tile), wide),
            shape((flat_rows, tile), wide),
            shape((8, 128), wide),
        ),
        in_specs=[hbm] * 7 + [vmem],
        out_specs=(hbm, hbm, vmem, vmem),
        scratch_shapes=[
            pltpu.VMEM((9, 8, part, tile), low),
            pltpu.VMEM((8, part, wide_steps), low),
            pltpu.VMEM((2, 8, part, 128), low),
            pltpu.VMEM((8, part, p1.shape[1]), low),
            pltpu.VMEM((3, 8, part, tile), low),
            pltpu.VMEM((3, 8, part, rest), low),
            pltpu.VMEM((2, rows, tile), low),
            pltpu.VMEM((3, rows, tile), low),
            pltpu.VMEM((3, rows, tile), low),
            pltpu.VMEM((2, rows, tile), low),
            pltpu.VMEM((rows, rest), low),
            pltpu.VMEM(g.shape, low),
            pltpu.VMEM((rows, tile), low),
            pltpu.VMEM((rows, tile), low),
            pltpu.VMEM((2, rows, tile), wide),
            pltpu.VMEM((rows, rest), wide),
            pltpu.VMEM((rows, tile), wide),
            pltpu.VMEM((128, tile), low),
            pltpu.VMEM((3, 4, 2, part, tile), wide),
            pltpu.VMEM((4, 4, part, tile), wide),
            pltpu.VMEM((4, 2, part, tile), low),
            pltpu.VMEM((count, 2, part, tile), low),
            pltpu.VMEM((6, 2, part, tile), wide),
            pltpu.VMEM((4, part, tile), low),
            pltpu.VMEM((count, part, tile), low),
            pltpu.VMEM((6, part, tile), wide),
            pltpu.VMEM((4, part, tile), low),
            pltpu.VMEM((count, part, tile), low),
            pltpu.VMEM((4, part, tile), low),
            pltpu.VMEM((count, part, tile), low),
            pltpu.VMEM((count, part, tile), low),
            pltpu.VMEM((5, small_rows, tile), wide),
            pltpu.VMEM((5, small_rows, tile), wide),
            pltpu.VMEM((small_rows, tile), wide),
            pltpu.VMEM((8, 128), wide),
            pltpu.VMEM((8, 8, 128), wide),
            dma((9,)),
            dma((2,)),
            dma((3,)),
            dma((3,)),
            dma((3,)),
            dma((3,)),
            dma((3,)),
            dma((2,)),
            dma((4,)),
            dma((2,)),
            dma((3,)),
            dma((4,)),
            pltpu.SemaphoreType.REGULAR,
            dma((4,)),
            dma((count,)),
            dma((4,)),
            dma((count,)),
            dma((4,)),
            dma((count,)),
            dma((4,)),
            dma((count,)),
            dma((count, 2)),
            dma((count,)),
            dma((5,)),
            dma((5,)),
            dma((8,)),
            dma((8,)),
            dma((count,)),
        ],
        compiler_params=pltpu.CompilerParams(
            collective_id=1, has_side_effects=True, vmem_limit_bytes=63 * 1024 * 1024
        ),
        name="backward",
    )(w, a, slope, p0, p1, x2, g, small)


def adamw_kernel(
    plan, step_ref, result_ref, grad_ref, *refs,
):
    where, pieces, count = plan
    groups = [refs[3 * k : 3 * k + 3] for k in range(4)]
    outs = [refs[12 + 4 * k : 16 + 4 * k] for k in range(4)]
    held = [refs[28 + 3 * k : 31 + 3 * k] for k in range(4)]
    copies = refs[40:44]
    grads, first_g, fore_g, grad_sem, in_sem, out_sem = refs[44:]
    wide, low = jnp.float32, jnp.bfloat16
    clip = result_ref[2:3, 0:1]
    steps = jnp.full((1, 1), 1.0, wide) * step_ref[0].astype(wide)
    mean_fix = 1.0 / (1.0 - jnp.exp(steps * float(np.log(BETA_ONE))))
    square_fix = 1.0 / (1.0 - jnp.exp(steps * float(np.log(BETA_TWO))))
    tile = grads.shape[2]

    units = [(1, k) for k in range(0, 9, 3)] + [(2, 0), (2, 1), (3, None), (0, None)]

    def view(ref, group, lead):
        if lead is None:
            return ref
        return ref.at[lead : lead + 3] if group == 1 else ref.at[lead]

    loads = []
    for n, (group, lead) in enumerate(units):
        loads.append(
            [
                pltpu.make_async_copy(view(groups[group][k], group, lead), view(held[group][k], group, lead), in_sem.at[n, k])
                for k in range(3)
            ]
        )
    whole = pltpu.make_async_copy(grad_ref, grads, grad_sem)
    whole.start()
    for unit in loads:
        for copy in unit:
            copy.start()
    whole.wait()

    for key_group, target in (("first", first_g), ("fore", fore_g)):
        begin = 0
        for stack_id in range(3):
            done = 0
            width = pieces[stack_id, key_group][1]
            for t, start, size in where[stack_id, key_group]:
                size = min(size, width - done)
                if size > 0:
                    target[:, begin + done : begin + done + size] = grads[t, :, start : start + size].astype(wide)
                done += size
            begin += width

    def update(group, index, grad):
        weight, avg, square = (held[group][k][index] for k in range(3))
        grad = grad * clip
        new_avg = BETA_ONE * avg + (1.0 - BETA_ONE) * grad
        new_sq = BETA_TWO * square + (1.0 - BETA_TWO) * grad * grad
        step = (new_avg * mean_fix) / (jnp.sqrt(new_sq * square_fix) + EPSILON) + DECAY * weight
        new_weight = weight - RATE * step
        held[group][0][index] = new_weight
        held[group][1][index] = new_avg
        held[group][2][index] = new_sq
        copies[group][index] = new_weight.astype(low)

    def rows_of(body, rows=64, step=16):
        def go(k, carry):
            body(pl.ds(pl.multiple_of(k * step, step), step))
            return carry
        lax.fori_loop(0, rows // step, go, 0)

    part = grads.shape[1]
    stores = []
    for n, (group, lead) in enumerate(units):
        for copy in loads[n]:
            copy.wait()
        if group == 1:
            for k in range(lead, lead + 3):
                t = where[k // 3, k % 3][0][0]
                rows_of(lambda rows: update(1, (k, rows), grads[t, rows, :].astype(wide)), part)
        elif group == 2:
            spots = where[lead, "back"]
            length = held[2][0].shape[2]

            def tiles(rows):
                done = 0
                for t, start, size in spots:
                    size = min(size, length - done)
                    update(2, (lead, rows, slice(done, done + size)), grads[t, rows, start : start + size].astype(wide))
                    done += size
            rows_of(tiles, part)
        else:
            target = first_g if group == 0 else fore_g
            rows_of(lambda rows: update(group, (rows,), target[rows, :]), part)
        for k in range(3):
            stores.append(
                pltpu.make_async_copy(view(held[group][k], group, lead), view(outs[group][k], group, lead), out_sem.at[n, k])
            )
        stores.append(
            pltpu.make_async_copy(view(copies[group], group, lead), view(outs[group][3], group, lead), out_sem.at[n, 3])
        )
        for copy in stores[-4:]:
            copy.start()
    for copy in stores:
        copy.wait()


def adamw_all(step_count, result, grads, states, where, pieces):
    low, wide = jnp.bfloat16, jnp.float32
    hbm = pl.BlockSpec(memory_space=pltpu.HBM)
    shape = jax.ShapeDtypeStruct
    shapes = [state[0].shape for state in states]
    dma = pltpu.SemaphoreType.DMA
    return pl.pallas_call(
        functools.partial(adamw_kernel, (where, pieces, grads.shape[0])),
        out_shape=tuple(shape(s, kind) for s in shapes for kind in (wide, wide, wide, low)),
        in_specs=[pl.BlockSpec(memory_space=pltpu.SMEM), pl.BlockSpec(memory_space=pltpu.VMEM)] + [hbm] * 13,
        out_specs=(hbm,) * 16,
        scratch_shapes=[pltpu.VMEM(s, wide) for s in shapes for _ in range(3)]
        + [pltpu.VMEM(s, low) for s in shapes]
        + [
            pltpu.VMEM(grads.shape, low),
            pltpu.VMEM(shapes[0], wide),
            pltpu.VMEM(shapes[3], wide),
            dma,
            dma((7, 3)),
            dma((7, 4)),
        ],
        compiler_params=pltpu.CompilerParams(vmem_limit_bytes=60 * 1024 * 1024),
        name="adamw",
    )(step_count, result, grads, *[array for state in states for array in state])


def fast_body(
    devices,
    windows,
    targets,
    horizon,
    step_count,
    first_w,
    first_w_avg,
    first_w_sq,
    hidden_w,
    hidden_w_avg,
    hidden_w_sq,
    back_w,
    back_w_avg,
    back_w_sq,
    fore_w,
    fore_w_avg,
    fore_w_sq,
    bias_vec,
    bias_avg,
    bias_sq,
):
    length, steps_ahead_total, hidden_size = windows.shape[1], targets.shape[1], hidden_w.shape[-1]
    part = hidden_w.shape[2]
    pieces, total = packing(length, steps_ahead_total, hidden_size)
    rows, row_count = row_plan(length, steps_ahead_total, hidden_size)
    row_count = -(-row_count // 8) * 8
    where, count = chunk_plan(length, steps_ahead_total, hidden_size)
    spans = {}
    cursor = 0
    for key in bias_order(length, steps_ahead_total, hidden_size):
        spans[key] = cursor
        cursor += rows[key][1]
    bias_count = bias_vec.shape[0]
    flat_rows = -(-bias_count // (8 * hidden_size)) * 8
    flat = jnp.pad(bias_vec, (0, flat_rows * hidden_size - bias_count)).reshape(flat_rows, hidden_size)
    ups = np.zeros((256, tiled(steps_ahead_total)), np.float32)
    for stack_id in range(2):
        knots = steps_ahead_total // RATIOS[stack_id]
        ups[128 * stack_id : 128 * stack_id + knots, :steps_ahead_total] = blend_coefficients(steps_ahead_total, knots)
    up_high = ups.astype(jnp.bfloat16)
    up_low = (ups - up_high.astype(np.float32)).astype(jnp.bfloat16)
    scale = 2.0 ** -int(np.ceil(np.log2(devices * windows.shape[0] * steps_ahead_total)))

    def lead(array):
        return array.reshape((-1,) + array.shape[2:]) if array.ndim == 4 else array

    states = (
        (first_w.T, first_w_avg.T, first_w_sq.T),
        (lead(hidden_w), lead(hidden_w_avg), lead(hidden_w_sq)),
        (back_w, back_w_avg, back_w_sq),
        (fore_w, fore_w_avg, fore_w_sq),
    )
    w, a, slope, p0, p1, x2, g, small = forward(
        states[0][0], states[1][0], back_w, fore_w, windows, targets, horizon, flat,
        jnp.asarray(up_high), jnp.asarray(up_low), pieces, rows, spans, scale, total,
    )
    owned, _, flat_grad, result = backward(
        w, a, slope, p0, p1, x2, g, small, pieces, rows, spans, scale, row_count, flat_rows, count
    )
    new = adamw_all(step_count, result, owned, states, where, pieces)
    first_new, hidden_new, back_new, fore_new = (new[4 * k : 4 * k + 4] for k in range(4))
    grad_bias = flat_grad.reshape(-1)[:bias_count] * result[2, 0]
    bias_new = adamw(bias_vec, bias_avg, bias_sq, grad_bias, step_count[0].astype(jnp.float32))
    shape = hidden_w.shape
    first_new = [array.T for array in first_new]
    hidden_new = [array.reshape(shape) for array in hidden_new]
    flat_out = [result[1, 0], result[0, 0]]
    for weight, avg, square, _ in (first_new, hidden_new, back_new, fore_new):
        flat_out += [avg, square, weight]
    flat_out += list(bias_new)
    flat_out += [group[3] for group in (first_new, hidden_new, back_new, fore_new)]
    return tuple(flat_out)


def solution(mesh):
    fast = mesh.shape["fsdp"] == 8 and mesh.shape["dp"] == 4
    step = functools.partial(fast_body, mesh.shape["dp"] * mesh.shape["fsdp"]) if fast else body
    placed = (
        P(("dp", "fsdp"), None),
        P(("dp", "fsdp"), None),
        P(("dp", "fsdp")),
        P(),
        P(None, "fsdp"),
        P(None, "fsdp"),
        P(None, "fsdp"),
        P(None, None, "fsdp", None),
        P(None, None, "fsdp", None),
        P(None, None, "fsdp", None),
        P(None, "fsdp", None),
        P(None, "fsdp", None),
        P(None, "fsdp", None),
        P("fsdp", None),
        P("fsdp", None),
        P("fsdp", None),
        P(),
        P(),
        P(),
    )
    return jax.shard_map(
        step,
        mesh=mesh,
        in_specs=placed,
        out_specs=(
            P(),
            P(),
            P(None, "fsdp"),
            P(None, "fsdp"),
            P(None, "fsdp"),
            P(None, None, "fsdp", None),
            P(None, None, "fsdp", None),
            P(None, None, "fsdp", None),
            P(None, "fsdp", None),
            P(None, "fsdp", None),
            P(None, "fsdp", None),
            P("fsdp", None),
            P("fsdp", None),
            P("fsdp", None),
            P(),
            P(),
            P(),
            P(None, "fsdp"),
            P(None, None, "fsdp", None),
            P(None, "fsdp", None),
            P("fsdp", None),
        ),
        check_vma=False,
    )
```

```python
import functools
import jax
import jax.numpy as jnp
import numpy as np
from jax import lax
from jax.experimental import pallas as pl
from jax.experimental.pallas import tpu as pltpu
from jax.sharding import PartitionSpec as P

KERNELS = (8, 4, 1)
RATIOS = (24, 12, 1)
CLIP_MAX = 0.01
RATE = 0.02
BETA_ONE = 0.9
BETA_TWO = 0.999
EPSILON = 1e-08
DECAY = 0.01
DOT_EXACTNESS = lax.Precision.HIGHEST


def blend_coefficients(fine, coarse):
    column = np.arange(fine)
    numer = np.maximum((2 * column + 1) * coarse - fine, 0)
    lower_idx = numer // (2 * fine)
    frac = (numer - lower_idx * 2 * fine) / (2.0 * fine)
    upper_idx = np.minimum(lower_idx + 1, coarse - 1)
    matrix = np.zeros((coarse, fine), np.float32)
    matrix[lower_idx, column] += 1.0 - frac
    matrix[upper_idx, column] += frac
    return matrix


def normalize(windows, targets):
    center = jnp.mean(windows, axis=1, keepdims=True)
    spread = jnp.sqrt(jnp.mean((windows - center) ** 2, axis=1, keepdims=True) + 1e-05)
    return ((windows - center) / spread, (targets - center) / spread)


def mean_pool(values, kernel):
    if kernel == 1:
        return values
    return jnp.mean(values.reshape(values.shape[0], values.shape[1] // kernel, kernel), axis=2)


def pool_back(d_pooled, kernel):
    if kernel == 1:
        return d_pooled
    spread_out = jnp.broadcast_to((d_pooled / kernel)[:, :, None], d_pooled.shape + (kernel,))
    return spread_out.reshape(d_pooled.shape[0], d_pooled.shape[1] * kernel)


def silu_slope(pre_act):
    gate = jax.nn.sigmoid(pre_act)
    return gate * (1.0 + pre_act * (1.0 - gate))


def stack_params(stack_id, gathered, bias_vec, length, steps_ahead_total):
    first_full, hidden_full, back_full, fore_full = gathered
    hidden_size = hidden_full.shape[-1]
    row_start = sum((length // KERNELS[earlier] for earlier in range(stack_id)))
    col_start = sum((steps_ahead_total // RATIOS[earlier] for earlier in range(stack_id)))
    pooled_len = length // KERNELS[stack_id]
    anchor_entries = steps_ahead_total // RATIOS[stack_id]
    layers = [
        (
            first_full[row_start : row_start + pooled_len],
            bias_vec[stack_id * hidden_size : (stack_id + 1) * hidden_size],
        )
    ]
    for layer_id in range(3):
        offset = (3 + 3 * stack_id + layer_id) * hidden_size
        layers.append((hidden_full[stack_id, layer_id], bias_vec[offset : offset + hidden_size]))
    fore_start = 12 * hidden_size + 2 * length + col_start
    fore_pair = (
        fore_full[:, col_start : col_start + anchor_entries],
        bias_vec[fore_start : fore_start + anchor_entries],
    )
    back_pair = None
    if stack_id < 2:
        back_start = 12 * hidden_size + stack_id * length
        back_pair = (back_full[stack_id], bias_vec[back_start : back_start + length])
    linear_upsample_anchors = jnp.asarray(blend_coefficients(steps_ahead_total, anchor_entries))
    return (layers, fore_pair, back_pair, linear_upsample_anchors)


def stack_forward(residual, stack_id, layers, fore_pair, back_pair, linear_upsample_anchors):
    inputs_kept = [mean_pool(residual, KERNELS[stack_id]).astype(jnp.bfloat16)]
    pre_kept = []
    for weight, bias in layers:
        pre_act = jnp.dot(inputs_kept[-1], weight, preferred_element_type=jnp.float32) + bias
        pre_kept.append(pre_act)
        inputs_kept.append(jax.nn.silu(pre_act).astype(jnp.bfloat16))
    anchor_result = (
        jnp.dot(inputs_kept[-1], fore_pair[0], preferred_element_type=jnp.float32) + fore_pair[1]
    )
    running_subtotal = jnp.dot(anchor_result, linear_upsample_anchors, precision=DOT_EXACTNESS)
    backcast = None
    if back_pair is not None:
        backcast = (
            jnp.dot(inputs_kept[-1], back_pair[0], preferred_element_type=jnp.float32)
            + back_pair[1]
        )
    return ((inputs_kept, pre_kept), running_subtotal, backcast)


def head_grads(last_act, d_low, weight):
    grad_w = jnp.dot(last_act.T, d_low, preferred_element_type=jnp.float32)
    grad_b = jnp.sum(d_low.astype(jnp.float32), axis=0)
    return ((grad_w, grad_b), jnp.dot(d_low, weight.T, preferred_element_type=jnp.float32))


def stack_backward(kept, anchor_cotangent, d_backcast, layers, fore_pair, back_pair, need_input):
    inputs_kept, pre_kept = kept
    last_act = inputs_kept[-1]
    fore_grads, d_hidden = head_grads(last_act, anchor_cotangent.astype(jnp.bfloat16), fore_pair[0])
    back_grads = None
    if back_pair is not None:
        back_grads, d_extra = head_grads(last_act, d_backcast.astype(jnp.bfloat16), back_pair[0])
        d_hidden = d_hidden + d_extra
    layer_grads = [None, None, None, None]
    for layer_id in (3, 2, 1, 0):
        d_pre = (d_hidden * silu_slope(pre_kept[layer_id])).astype(jnp.bfloat16)
        layer_grads[layer_id] = (
            jnp.dot(inputs_kept[layer_id].T, d_pre, preferred_element_type=jnp.float32),
            jnp.sum(d_pre.astype(jnp.float32), axis=0),
        )
        if layer_id > 0 or need_input:
            d_hidden = jnp.dot(d_pre, layers[layer_id][0].T, preferred_element_type=jnp.float32)
    return (layer_grads, fore_grads, back_grads, d_hidden)


def adamw(weight, avg, square, grad, step_float):
    new_avg = BETA_ONE * avg + (1.0 - BETA_ONE) * grad
    new_sq = BETA_TWO * square + (1.0 - BETA_TWO) * grad * grad
    avg_hat = new_avg / (1.0 - BETA_ONE**step_float)
    sq_hat = new_sq / (1.0 - BETA_TWO**step_float)
    new_weight = weight - RATE * (avg_hat / (jnp.sqrt(sq_hat) + EPSILON) + DECAY * weight)
    return (new_avg, new_sq, new_weight)


def body(
    windows,
    targets,
    horizon,
    step_count,
    first_w,
    first_w_avg,
    first_w_sq,
    hidden_w,
    hidden_w_avg,
    hidden_w_sq,
    back_w,
    back_w_avg,
    back_w_sq,
    fore_w,
    fore_w_avg,
    fore_w_sq,
    bias_vec,
    bias_avg,
    bias_sq,
):
    length = windows.shape[1]
    steps_ahead_total = targets.shape[1]
    normed, observed_future = normalize(windows, targets)
    future_usable_flags = (
        jnp.arange(steps_ahead_total, dtype=jnp.int32)[None, :] < horizon[:, None]
    ).astype(jnp.float32)
    usable_tally = lax.psum(jnp.sum(horizon.astype(jnp.float32)), ("dp", "fsdp"))
    shards = (
        first_w.astype(jnp.bfloat16),
        hidden_w.astype(jnp.bfloat16),
        back_w.astype(jnp.bfloat16),
        fore_w.astype(jnp.bfloat16),
    )
    gathered = (
        lax.all_gather(shards[0], "fsdp", axis=1, tiled=True),
        lax.all_gather(shards[1], "fsdp", axis=2, tiled=True),
        lax.all_gather(shards[2], "fsdp", axis=1, tiled=True),
        lax.all_gather(shards[3], "fsdp", axis=0, tiled=True),
    )
    residual = normed
    kept_stacks = []
    predicted_future = jnp.zeros(observed_future.shape, jnp.float32)
    for stack_id in range(3):
        layers, fore_pair, back_pair, linear_upsample_anchors = stack_params(
            stack_id, gathered, bias_vec, length, steps_ahead_total
        )
        kept, running_subtotal, backcast = stack_forward(
            residual, stack_id, layers, fore_pair, back_pair, linear_upsample_anchors
        )
        kept_stacks.append(kept)
        predicted_future = predicted_future + running_subtotal
        if backcast is not None:
            residual = residual - backcast
    residual_difference = predicted_future - observed_future
    loss_part = (
        jnp.sum(future_usable_flags * residual_difference * residual_difference) / usable_tally
    )
    future_slope_cotangent = 2.0 * future_usable_flags * residual_difference / usable_tally
    again = (
        lax.all_gather(shards[0], "fsdp", axis=1, tiled=True),
        lax.all_gather(shards[1], "fsdp", axis=2, tiled=True),
        lax.all_gather(shards[2], "fsdp", axis=1, tiled=True),
        lax.all_gather(shards[3], "fsdp", axis=0, tiled=True),
    )
    results = [None, None, None]
    d_residual = None
    for stack_id in (2, 1, 0):
        layers, fore_pair, back_pair, linear_upsample_anchors = stack_params(
            stack_id, again, bias_vec, length, steps_ahead_total
        )
        anchor_cotangent = jnp.dot(
            future_slope_cotangent, linear_upsample_anchors.T, precision=DOT_EXACTNESS
        )
        d_backcast = None if d_residual is None else -d_residual
        results[stack_id] = stack_backward(
            kept_stacks[stack_id],
            anchor_cotangent,
            d_backcast,
            layers,
            fore_pair,
            back_pair,
            stack_id > 0,
        )
        if stack_id > 0:
            spread_back = pool_back(results[stack_id][3], KERNELS[stack_id])
            d_residual = spread_back if d_residual is None else d_residual + spread_back
    grad_first = jnp.concatenate([results[stack_id][0][0][0] for stack_id in range(3)], axis=0)
    grad_hidden = jnp.stack(
        [
            jnp.stack([results[stack_id][0][layer_id][0] for layer_id in (1, 2, 3)])
            for stack_id in range(3)
        ]
    )
    grad_back = jnp.stack([results[stack_id][2][0] for stack_id in range(2)])
    grad_fore = jnp.concatenate([results[stack_id][1][0] for stack_id in range(3)], axis=1)
    bias_pieces = [results[stack_id][0][0][1] for stack_id in range(3)]
    bias_pieces += [
        results[stack_id][0][layer_id][1] for stack_id in range(3) for layer_id in (1, 2, 3)
    ]
    bias_pieces += [results[stack_id][2][1] for stack_id in range(2)]
    bias_pieces += [results[stack_id][1][1] for stack_id in range(3)]
    grad_bias = jnp.concatenate(bias_pieces)
    owned = (
        lax.psum_scatter(grad_first, "fsdp", scatter_dimension=1, tiled=True),
        lax.psum_scatter(grad_hidden, "fsdp", scatter_dimension=2, tiled=True),
        lax.psum_scatter(grad_back, "fsdp", scatter_dimension=1, tiled=True),
        lax.psum_scatter(grad_fore, "fsdp", scatter_dimension=0, tiled=True),
    )
    owned = lax.psum((owned[0], owned[1], owned[2], owned[3]), "dp")
    grad_bias, loss = lax.psum((grad_bias, loss_part), ("dp", "fsdp"))
    local_sq = sum((jnp.sum(grad * grad) for grad in owned))
    total_sq = lax.psum(local_sq, "fsdp") + jnp.sum(grad_bias * grad_bias)
    grad_norm = jnp.sqrt(total_sq)
    clip_factor = jnp.minimum(1.0, CLIP_MAX / grad_norm)
    step_float = step_count[0].astype(jnp.float32)
    states = (
        (first_w, first_w_avg, first_w_sq),
        (hidden_w, hidden_w_avg, hidden_w_sq),
        (back_w, back_w_avg, back_w_sq),
        (fore_w, fore_w_avg, fore_w_sq),
        (bias_vec, bias_avg, bias_sq),
    )
    grads_all = (owned[0], owned[1], owned[2], owned[3], grad_bias)
    updated = []
    for state, grad in zip(states, grads_all):
        updated.append(adamw(state[0], state[1], state[2], grad * clip_factor, step_float))
    return (
        loss,
        grad_norm,
        updated[0][0],
        updated[0][1],
        updated[0][2],
        updated[1][0],
        updated[1][1],
        updated[1][2],
        updated[2][0],
        updated[2][1],
        updated[2][2],
        updated[3][0],
        updated[3][1],
        updated[3][2],
        updated[4][0],
        updated[4][1],
        updated[4][2],
        updated[0][2].astype(jnp.bfloat16),
        updated[1][2].astype(jnp.bfloat16),
        updated[2][2].astype(jnp.bfloat16),
        updated[3][2].astype(jnp.bfloat16),
    )


MESH = pl.DeviceIdType.MESH
CHUNK = 1024


def tiled(width):
    return -(-width // 128) * 128


def packing(length, steps_ahead_total, hidden_size):
    pieces = {}
    cursor = 0
    for stack_id in range(3):
        widths = [("first", length // KERNELS[stack_id])]
        widths += [(layer_id, hidden_size) for layer_id in range(3)]
        if stack_id < 2:
            widths.append(("back", length))
        widths.append(("fore", steps_ahead_total // RATIOS[stack_id]))
        for name, width in widths:
            pieces[stack_id, name] = (cursor, width)
            cursor += tiled(width)
    total = -(-cursor // CHUNK) * CHUNK
    return pieces, total


def pack(parts, pieces, total):
    out = []
    cursor = 0
    for key, (start, width) in pieces.items():
        part = parts[key]
        out.append(jnp.pad(part, ((0, 0), (0, tiled(width) - width))))
        cursor = start + tiled(width)
    rows, dtype = out[0].shape[0], out[0].dtype
    if total > cursor:
        out.append(jnp.zeros((rows, total - cursor), dtype))
    return jnp.concatenate(out, axis=1)


def places():
    row = lax.axis_index("dp")
    me = lax.axis_index("fsdp")
    core = me % 2
    across_x = (me // 2) % 2
    across_y = me // 4
    other = me + 1 - 2 * core
    over_x = me + 2 - 4 * across_x
    over_y = me + 4 - 8 * across_y
    return row, me, core, other, over_x, over_y


def remote(src, dst, send_sem, recv_sem, device):
    return pltpu.make_async_remote_copy(
        src_ref=src, dst_ref=dst, send_sem=send_sem, recv_sem=recv_sem, device_id=device, device_id_type=MESH
    )


HALF_LOW = 2


def row_plan(length, steps_ahead_total, hidden_size):
    rows = {}
    cursor = 0
    for stack_id in range(3):
        for name in ("first", 0, 1, 2):
            rows[stack_id, name] = (cursor, hidden_size)
            cursor += 1
    for stack_id in range(2):
        rows[stack_id, "back"] = (cursor, length)
        cursor += -(-length // hidden_size)
    for stack_id in range(3):
        width = steps_ahead_total // RATIOS[stack_id]
        rows[stack_id, "fore"] = (cursor, width)
        cursor += -(-width // hidden_size)
    return rows, cursor


def bias_order(length, steps_ahead_total, hidden_size):
    keys = [(stack_id, "first") for stack_id in range(3)]
    keys += [(stack_id, layer_id) for stack_id in range(3) for layer_id in range(3)]
    keys += [(stack_id, "back") for stack_id in range(2)]
    keys += [(stack_id, "fore") for stack_id in range(3)]
    return keys


def parts_low(value):
    high = value.astype(jnp.bfloat16)
    return high, (value - high.astype(jnp.float32)).astype(jnp.bfloat16)


NN = (((1,), (0,)), ((), ()))
NT = (((1,), (1,)), ((), ()))
TN = (((0,), (0,)), ((), ()))


def mul(left, right, dims=NN):
    return lax.dot_general(left, right, dims, preferred_element_type=jnp.float32)


def cut_classes(count):
    pattern = "eoeo" + "eob" * count
    return (pattern[: count - 2] + "bb")[:count]


def forward_kernel(
    plan,
    first_ref, hidden_ref, back_ref, fore_ref, windows_ref, targets_ref, horizon_ref, flat_ref, up_high_ref, up_low_ref,
    w_out, a_out, slope_out, p0_out, p1_out, x2_out, g_out, small_ref,
    w, x, stage, a, slope, p0, p1, x2, fc, tt, g, dk, center_s, scale_s, pool8, pool4,
    bias_ref, first_s, hidden_s, back_s, fore_s,
    raw_sem, send_sem, recv_sem, win_sem, tt_sem, out_sem, w_sem,
):
    pieces, bias_rows, spans, cut_width, count, scale = plan
    row, me, core, other, over_x, over_y = places()
    diag = over_x + over_y - me
    total_rows = windows_ref.shape[0]
    length = windows_ref.shape[1]
    hidden_size = a.shape[-1]
    steps_ahead = targets_ref.shape[0]
    block = total_rows // 2
    wide, low = jnp.float32, jnp.bfloat16
    wide_length = x.shape[1]
    tiles = [(k, min(hidden_size, wide_length - k)) for k in range(0, wide_length, hidden_size)]
    whole = wide_length // 128 * 128 - 128

    barrier = pltpu.get_barrier_semaphore()
    for peer in (other, over_x, over_y):
        pl.semaphore_signal(barrier, inc=1, device_id=(row, peer), device_id_type=MESH)
    pl.semaphore_signal(barrier, inc=1, device_id=(row + 1 - 2 * (row % 2), me), device_id_type=MESH)

    classes = cut_classes(count)
    turn_of = [classes[:cut].count(classes[cut]) % 2 for cut in range(count)]
    even_plane = row % 2 == 0
    z_pair = row + 1 - 2 * (row % 2)

    def copy_of(kind, cut, src, holder, device):
        cols = slice(cut * cut_width, (cut + 1) * cut_width)
        return remote(src.at[:, cols], w.at[holder, :, cols], send_sem.at[kind, cut], recv_sem.at[kind, cut], device)

    def to_x(cut):
        return copy_of(0, cut, w.at[me], me, (row, over_x))

    def to_y(cut):
        return copy_of(1, cut, w.at[me], me, (row, over_y))

    def onward(cut):
        if turn_of[cut] == 0:
            return copy_of(2, cut, w.at[over_x], over_x, (row, over_y))
        return copy_of(2, cut, w.at[over_y], over_y, (row, over_x))

    def to_core(kind, cut):
        holder = (me, over_x, over_y, diag)[kind]
        return copy_of(3 + kind, cut, w.at[holder], holder, (row, other))

    def to_z(kind, cut):
        holder = (None, over_x, over_y, diag)[kind]
        return copy_of(6 + kind, cut, w.at[holder], holder, (z_pair, me))

    def gathers(cut, body):
        if classes[cut] == "b":
            body()
        else:
            pl.when(even_plane if classes[cut] == "e" else jnp.logical_not(even_plane))(body)

    def receives(cut, body):
        if classes[cut] != "b":
            pl.when(jnp.logical_not(even_plane) if classes[cut] == "e" else even_plane)(body)

    def own_sends(cut):
        def body():
            to_x(cut).start()
            to_y(cut).start()
        gathers(cut, body)
        to_core(0, cut).start()

    def w_copy(cut):
        cols = slice(cut * cut_width, (cut + 1) * cut_width)
        return pltpu.make_async_copy(w.at[:, :, cols], w_out.at[:, :, cols], w_sem.at[cut])

    look, lag_diag, lag_z = 4, 2, 6
    arrived = set()

    def pump(cut):
        if cut < count:
            def body():
                to_x(cut).wait_recv()
                if turn_of[cut] == 0:
                    onward(cut).start()
                if classes[cut] != "b":
                    to_z(1, cut).start()
                to_core(1, cut).start()
                to_y(cut).wait_recv()
                if turn_of[cut] == 1:
                    onward(cut).start()
                if classes[cut] != "b":
                    to_z(2, cut).start()
                to_core(2, cut).start()
            gathers(cut, body)
            if cut + look < count:
                own_sends(cut + look)
        past = cut - lag_diag
        if 0 <= past < count:
            def body():
                onward(past).wait_recv()
                if classes[past] != "b":
                    to_z(3, past).start()
                to_core(3, past).start()
            gathers(past, body)
        gone = cut - lag_z
        if 0 <= gone < count:
            def body():
                for kind in (1, 2, 3):
                    to_z(kind, gone).wait_recv()
                    to_core(kind, gone).start()
            receives(gone, body)
        for done in range(count):
            if done not in arrived and cut - done >= (lag_diag + 1 if classes[done] == "b" else lag_z + 1):
                for kind in range(4):
                    to_core(kind, done).wait_recv()
                w_copy(done).start()
                arrived.add(done)

    tasks = []

    def task(need, cost):
        def keep(body):
            tasks.append((need, cost, body))
            return body
        return keep

    def cut_of(key):
        start, width = pieces[key]
        return (start + tiled(width) - 1) // cut_width

    def weights(key, start=0, width=None):
        at, full_width = pieces[key]
        width = tiled(full_width) if width is None else width
        return w[:, :, at + start : at + start + width].reshape(hidden_size, width)

    def bias(key, start=0, width=None):
        at, full_width = bias_rows[key]
        width = hidden_size if width is None else width
        return bias_ref[at + start // hidden_size : at + start // hidden_size + 1, 0:width]

    def over_rows(body):
        def step(k, carry):
            body(pl.ds(pl.multiple_of(k * block, block), block))
            return carry
        lax.fori_loop(0, 2, step, 0)

    def outgoing(src, dst, slot):
        return pltpu.make_async_copy(src, dst, out_sem.at[slot])

    slots = stage.shape[0]
    strip = stage.shape[1]
    strips = total_rows // strip

    def window_copy(k):
        rows = pl.ds(pl.multiple_of(k * strip, strip), strip)
        return pltpu.make_async_copy(windows_ref.at[rows], stage.at[k % slots], win_sem.at[k % slots])

    raw = [
        pltpu.make_async_copy(src, dst, raw_sem.at[k])
        for k, (src, dst) in enumerate(
            ((first_ref, first_s), (hidden_ref, hidden_s), (back_ref, back_s), (fore_ref, fore_s))
        )
    ]
    for copy in raw:
        copy.start()
    for k in range(slots):
        window_copy(k).start()
    targets_copy = pltpu.make_async_copy(targets_ref, tt.at[0:steps_ahead], tt_sem)
    targets_copy.start()

    def pack_piece(key, value):
        start, width = pieces[key]
        if width % 128:
            edge = start + width // 128 * 128
            w[me, :, edge : edge + 128] = jnp.zeros((value.shape[0], 128), low)
        w[me, :, start : start + width] = value.astype(low)

    def pack_stack(stack_id):
        width = pieces[stack_id, "first"][1]
        begin = sum(pieces[earlier, "first"][1] for earlier in range(stack_id))
        pack_piece((stack_id, "first"), first_s[:, begin : begin + width])
        for layer_id in range(3):
            pack_piece((stack_id, layer_id), hidden_s[3 * stack_id + layer_id])
        if stack_id < 2:
            pack_piece((stack_id, "back"), back_s[stack_id])
        width = pieces[stack_id, "fore"][1]
        begin = sum(pieces[earlier, "fore"][1] for earlier in range(stack_id))
        pack_piece((stack_id, "fore"), fore_s[:, begin : begin + width])

    raw[0].wait()
    raw[1].wait()
    raw[2].wait()
    raw[3].wait()
    pack_stack(0)
    pl.semaphore_wait(barrier, 4)
    for cut in range(look):
        own_sends(cut)
    pack_stack(1)
    pack_stack(2)
    packed = max(start + tiled(width) for start, width in pieces.values())
    if packed < w.shape[2]:
        w[me, :, packed:] = jnp.zeros((w.shape[1], w.shape[2] - packed), low)
    bias_ref[...] = jnp.zeros_like(bias_ref)
    for key, (at, width) in bias_rows.items():
        for k in range(0, width, hidden_size):
            flat = spans[key] + k
            todo = min(hidden_size, width - k)
            r, o = flat // hidden_size, flat % hidden_size
            here = min(todo, hidden_size - o)
            bias_ref[at + k // hidden_size : at + k // hidden_size + 1, 0:here] = flat_ref[r : r + 1, o : o + here]
            if here < todo:
                bias_ref[at + k // hidden_size : at + k // hidden_size + 1, here:todo] = flat_ref[r + 1 : r + 2, 0 : todo - here]

    @task(-1, 1.0)
    def _():
        ids = lax.broadcasted_iota(jnp.int32, pool8.shape, 0)
        col = lax.broadcasted_iota(jnp.int32, pool8.shape, 1) * KERNELS[0]
        pool8[...] = jnp.where((ids >= col) & (ids < col + KERNELS[0]), 1.0 / KERNELS[0], 0.0).astype(low)
        ids = lax.broadcasted_iota(jnp.int32, pool4.shape, 0)
        col = lax.broadcasted_iota(jnp.int32, pool4.shape, 1) * KERNELS[1]
        pool4[...] = jnp.where((ids >= col) & (ids < col + KERNELS[1]), 1.0 / KERNELS[1], 0.0).astype(low)
        x[:, whole:] = jnp.zeros((total_rows, wide_length - whole), wide)

    groups = 3
    for group in range(groups):
        @task(-1, 3.0)
        def _(group=group):
            def step(k, carry):
                window_copy(k).wait()
                rows = pl.ds(pl.multiple_of(k * strip, strip), strip)
                value = stage[k % slots]
                center = jnp.sum(value, axis=1, keepdims=True) * (1.0 / length)
                value = value - center
                spread = jnp.sqrt(jnp.sum(value * value, axis=1, keepdims=True) * (1.0 / length) + 1e-05)
                factor = 1.0 / spread
                center_s[rows, :] = center
                scale_s[rows, :] = factor
                value = value * factor
                x[rows, 0:length] = value

                @pl.when(k + slots < strips)
                def _():
                    window_copy(k + slots).start()
                return carry
            lax.fori_loop(group * strips // groups, (group + 1) * strips // groups, step, 0)

    @task(-1, 3.0)
    def _():
        def body(rows):
            for k in range(0, wide_length, 1024):
                width = min(1024, wide_length - k)
                high, rest = parts_low(x[rows, k : k + width])
                pooled = mul(high, pool8[0:width]) + mul(rest, pool8[0:width])
                p0[rows, k // 8 : k // 8 + 128] = pooled.astype(low)
        over_rows(body)
        outgoing(p0, p0_out, 0).start()

    def activate(z, stack_id, j, rows):
        gate = jax.nn.sigmoid(z)
        act = z * gate
        a[j, rows, :] = act.astype(low)
        slope[j % 2, rows, :] = (gate + act * (1.0 - gate)).astype(low)

    def a_copy(stack_id, j):
        return outgoing(a.at[j], a_out.at[stack_id, j], 8 + j)

    def slope_copy(stack_id, j):
        return outgoing(slope.at[j % 2], slope_out.at[stack_id, j], 12 + j % 2)

    def send_layer(stack_id, j):
        a_copy(stack_id, j).start()
        slope_copy(stack_id, j).start()

    def settle_layer(stack_id, j):
        if stack_id > 0:
            a_copy(stack_id - 1, j).wait()
        n = 4 * stack_id + j - 2
        if n >= 0:
            slope_copy(n // 4, n % 4).wait()

    for stack_id in range(3):
        inputs = (p0, p1, x2)[stack_id]

        @task(cut_of((stack_id, "first")), (1.3, 2.2, 6.0)[stack_id])
        def _(stack_id=stack_id, inputs=inputs):
            settle_layer(stack_id, 0)

            def body(rows):
                z = mul(inputs[rows, :], weights((stack_id, "first")), NT) + bias((stack_id, "first"))
                activate(z, stack_id, 0, rows)
            over_rows(body)
            send_layer(stack_id, 0)

        for layer_id in range(3):
            @task(cut_of((stack_id, layer_id)), 1.3)
            def _(stack_id=stack_id, layer_id=layer_id):
                settle_layer(stack_id, layer_id + 1)

                def body(rows):
                    z = mul(a[layer_id, rows, :], weights((stack_id, layer_id))) + bias((stack_id, layer_id))
                    activate(z, stack_id, layer_id + 1, rows)
                over_rows(body)
                send_layer(stack_id, layer_id + 1)

        if stack_id < 2:
            for start, width in tiles:
                need = (pieces[stack_id, "back"][0] + start + width - 1) // cut_width

                @task(need, 1.4 if stack_id else 1.7)
                def _(stack_id=stack_id, start=start, width=width):
                    def body(rows):
                        cols = slice(start, start + width)
                        head = mul(a[3, rows, :], weights((stack_id, "back"), start, width))
                        rest = x[rows, cols] - (head + bias((stack_id, "back"), start, width))
                        if stack_id == 0:
                            x[rows, cols] = rest
                            high, tail = parts_low(rest)
                            pooled = mul(high, pool4[0:width]) + mul(tail, pool4[0:width])
                            p1[rows, start // 4 : start // 4 + 128] = pooled.astype(low)
                        else:
                            x2[rows, cols] = rest.astype(low)
                    over_rows(body)
                    if start + width == wide_length:
                        if stack_id == 0:
                            outgoing(p1, p1_out, 1).start()
                        else:
                            outgoing(x2, x2_out, 2).start()

            @task(cut_of((stack_id, "fore")), 1.5)
            def _(stack_id=stack_id):
                def body(rows):
                    knots = mul(a[3, rows, :], weights((stack_id, "fore"))) + bias((stack_id, "fore"), 0, 128)
                    high, rest = parts_low(knots)
                    ups = slice(128 * stack_id, 128 * stack_id + 128)
                    part = (
                        mul(high, up_high_ref[ups, :]) + mul(rest, up_high_ref[ups, :]) + mul(high, up_low_ref[ups, :])
                    )
                    fc[rows, :] = part if stack_id == 0 else fc[rows, :] + part
                over_rows(body)

    wide_steps = fc.shape[1]
    for start in range(0, wide_steps, 256):
        @task(cut_of((2, "fore")), 2.5)
        def _(start=start):
            if start == 0:
                targets_copy.wait()
                small_ref[...] = jnp.zeros_like(small_ref)
                small_ref[2:3, 0:128] = jnp.broadcast_to(jnp.sum(horizon_ref[...].astype(wide)), (1, 128))
            cols = slice(start, start + 256)
            head = mul(a[3], weights((2, "fore"), start, 256)) + bias_ref[
                bias_rows[2, "fore"][0] + start // hidden_size : bias_rows[2, "fore"][0] + start // hidden_size + 1,
                start % hidden_size : start % hidden_size + 256,
            ]
            goal = jnp.concatenate([tt[start : start + 128, :].T, tt[start + 128 : start + 256, :].T], axis=1)
            goal = (goal - center_s[...]) * scale_s[...]
            step = lax.broadcasted_iota(jnp.int32, (total_rows, 256), 1) + start
            diff = jnp.where(step < horizon_ref[...], fc[:, cols] + head - goal, 0.0)
            losses = jnp.sum(diff * diff, axis=0, keepdims=True)
            r = start // hidden_size
            small_ref[r : r + 1, start % hidden_size : start % hidden_size + 256] = losses
            diff = diff * (2.0 * scale)
            high, rest = parts_low(diff)
            g[:, cols] = high
            back = (
                mul(high, up_high_ref[:, cols], NT) + mul(rest, up_high_ref[:, cols], NT) + mul(high, up_low_ref[:, cols], NT)
            )
            dk[...] = back if start == 0 else dk[...] + back
            if start + 256 == wide_steps:
                g[:, wide_steps : wide_steps + 256] = dk[...].astype(low)
                outgoing(g, g_out, 3).start()

    queue = list(tasks)
    last = count + lag_z
    for cut in range(-1, last + 1):
        if cut >= 0:
            pump(cut)
        ready = min((done for done in range(count) if done not in arrived), default=count) - 1
        spent = 0.0
        while queue and queue[0][0] <= ready and (spent < 4.0 or cut == last):
            _, cost, body = queue.pop(0)
            body()
            spent += cost
    for cut in range(count):
        def body():
            to_x(cut).wait_send()
            to_y(cut).wait_send()
            onward(cut).wait_send()
            if classes[cut] != "b":
                for kind in (1, 2, 3):
                    to_z(kind, cut).wait_send()
        gathers(cut, body)
        for kind in range(4):
            to_core(kind, cut).wait_send()
        w_copy(cut).wait()
    outgoing(p0, p0_out, 0).wait()
    outgoing(p1, p1_out, 1).wait()
    outgoing(x2, x2_out, 2).wait()
    outgoing(g, g_out, 3).wait()
    for j in range(4):
        a_copy(2, j).wait()
    for j in (2, 3):
        slope_copy(2, j).wait()


def forward(first, hidden, back, fore, windows, targets, horizon, flat, up_high, up_low, pieces, bias_rows, spans, scale, total):
    low, wide = jnp.bfloat16, jnp.float32
    rows, length = windows.shape
    part, hidden_size = hidden.shape[1:]
    count = total // CHUNK
    wide_length = tiled(length)
    wide_steps = up_high.shape[1]
    p0_width, p1_width = tiled(length // KERNELS[0]), tiled(wide_length // KERNELS[1])
    row_count = -(-max(at - (-width // hidden_size) for at, width in bias_rows.values()) // 8) * 8
    strip = rows // 36
    hbm = pl.BlockSpec(memory_space=pltpu.HBM)
    vmem = pl.BlockSpec(memory_space=pltpu.VMEM)
    dma = pltpu.SemaphoreType.DMA
    shape = jax.ShapeDtypeStruct
    return pl.pallas_call(
        functools.partial(forward_kernel, (pieces, bias_rows, spans, CHUNK, count, scale)),
        out_shape=(
            shape((8, part, total), low),
            shape((3, 4, rows, hidden_size), low),
            shape((3, 4, rows, hidden_size), low),
            shape((rows, p0_width), low),
            shape((rows, p1_width), low),
            shape((rows, wide_length), low),
            shape((rows, wide_steps + 256), low),
            shape((8, hidden_size), wide),
        ),
        in_specs=[hbm] * 6 + [vmem] * 4,
        out_specs=(hbm,) * 7 + (vmem,),
        scratch_shapes=[
            pltpu.VMEM((8, part, total), low),
            pltpu.VMEM((rows, wide_length), wide),
            pltpu.VMEM((3, strip, length), wide),
            pltpu.VMEM((4, rows, hidden_size), low),
            pltpu.VMEM((2, rows, hidden_size), low),
            pltpu.VMEM((rows, p0_width), low),
            pltpu.VMEM((rows, p1_width), low),
            pltpu.VMEM((rows, wide_length), low),
            pltpu.VMEM((rows, wide_steps), wide),
            pltpu.VMEM((wide_steps, rows), wide),
            pltpu.VMEM((rows, wide_steps + 256), low),
            pltpu.VMEM((rows, 256), wide),
            pltpu.VMEM((rows, 1), wide),
            pltpu.VMEM((rows, 1), wide),
            pltpu.VMEM((1024, 128), low),
            pltpu.VMEM((512, 128), low),
            pltpu.VMEM((row_count, hidden_size), wide),
            pltpu.VMEM(first.shape, wide),
            pltpu.VMEM(hidden.shape, wide),
            pltpu.VMEM(back.shape, wide),
            pltpu.VMEM(fore.shape, wide),
            dma((4,)),
            dma((10, count)),
            dma((10, count)),
            dma((3,)),
            dma,
            dma((16,)),
            dma((count,)),
        ],
        compiler_params=pltpu.CompilerParams(
            collective_id=0, has_side_effects=True, vmem_limit_bytes=63 * 1024 * 1024
        ),
        name="forward",
    )(first, hidden, back, fore, windows, targets.T, horizon.reshape(rows, 1), flat, up_high, up_low)


def chunk_plan(length, steps_ahead_total, hidden_size):
    where = {}
    tile = hidden_size
    full, rest = tiled(length) // tile, tiled(length) % tile
    steps = tiled(steps_ahead_total)
    where[2, "fore"] = [(0, 0, tile), (1, 0, steps - tile)]
    for i in range(3):
        where[2, 2 - i] = [(2 + i, 0, tile)]
    t = 5
    where[2, "first"] = [(t + 2 * k, 0, tile) for k in range(full)] + [(t + 2 * full, 0, rest)]
    where[1, "back"] = [(t + 2 * k + 1, 0, tile) for k in range(full)] + [(t + 2 * full, rest, rest)]
    t += 2 * full
    where[1, "fore"] = [(t, 2 * rest, 128)]
    for i in range(3):
        where[1, 2 - i] = [(t + 1 + i, 0, tile)]
    t += 4
    where[1, "first"] = [(t, 0, tile), (t + 1, 0, tile)]
    t += 2
    where[0, "back"] = [(t + k, 0, tile) for k in range(full)] + [(t + full, 0, rest)]
    t += full
    where[0, "fore"] = [(t, rest, 128)]
    for i in range(3):
        where[0, 2 - i] = [(t + 1 + i, 0, tile)]
    where[0, "first"] = [(t + 4, 0, tile)]
    return where, t + 5


LAGS = (1, 3, 5, 7, 9, 11, 13)


def backward_kernel(
    plan,
    w_ref, a_ref, slope_ref, p0_ref, p1_ref, x2_ref, g_ref, forward_small_ref,
    out_ref, dx_ref, flat_ref, result_ref,
    wh, wf2, wf, w1, wtile, wtail, a4, ah, sl, ytile, x2tail, g, dz, gb, dxb, dxt, da, spread,
    gbuf, from_core, s1, r1, keep, s2, r2, plane, zs, zr, zp_s, zp_r, final,
    small_s, small_r, small_sum, square_s, square_r,
    wh_sem, wf_sem, wtile_sem, wtail_sem, a4_sem, ah_sem, sl_sem, y_sem, misc_sem, dx_sem,
    core_ss, core_rs, credit, ss1, rs1, ss2, rs2, zss, zrs, pss, prs, fss, frs, small_ss, small_rs, sq_ss, sq_rs, out_sem,
):
    pieces, bias_rows, spans, scale, count, full = plan
    row, me, core, other, over_x, over_y = places()
    lane = core
    chip, chip_x, chip_y = me // 2, over_x // 2, over_y // 2
    chip_d = chip_x + chip_y - chip
    wide, low = jnp.float32, jnp.bfloat16
    total_rows = a_ref.shape[2]
    tile = a_ref.shape[3]
    rest = x2tail.shape[1]
    upper = row // 2
    z_in = row + 1 - 2 * upper
    is_edge = (row == 0) | (row == 3)
    z_out = (row + 3 + 2 * upper) % 4
    t_tail1 = 5 + 2 * full
    t_first1 = t_tail1 + 4
    t_back0 = t_first1 + 2
    t_tail0 = t_back0 + full

    barrier = pltpu.get_barrier_semaphore()
    for peer in range(1, 8):
        pl.semaphore_signal(barrier, inc=1, device_id=(row, (me + peer) % 8), device_id_type=MESH)
    for peer in range(1, 4):
        pl.semaphore_signal(barrier, inc=1, device_id=((row + peer) % 4, me), device_id_type=MESH)

    def local(src, dst, sem):
        return pltpu.make_async_copy(src, dst, sem)

    def w_cols(start, width):
        return w_ref.at[:, :, pl.ds(start, width)]

    def load_g():
        return local(g_ref, g, misc_sem.at[0])

    def load_x2tail():
        return local(x2_ref.at[:, full * tile : full * tile + rest], x2tail, misc_sem.at[1])

    def load_w1():
        return local(w_cols(pieces[1, "first"][0], w1.shape[2]), w1, misc_sem.at[2])

    def load_wf2():
        return local(w_cols(pieces[2, "fore"][0], wf2.shape[2]), wf2, misc_sem.at[3])

    def load_wf(stack_id):
        return local(w_cols(pieces[stack_id, "fore"][0], 128), wf.at[stack_id], wf_sem.at[stack_id])

    tails = ((2, "first"), (1, "back"), (0, "back"))

    def load_wtail(k):
        return local(w_cols(pieces[tails[k]][0] + full * tile, rest), wtail.at[k], wtail_sem.at[k])

    def load_a4(stack_id):
        return local(a_ref.at[stack_id, 3], a4.at[stack_id % 2], a4_sem.at[stack_id])

    def load_wh(i):
        return local(w_cols(pieces[2 - i // 3, 2 - i % 3][0], tile), wh.at[i], wh_sem.at[i])

    def wait_wh(i):
        local(w_cols(0, tile), wh.at[i], wh_sem.at[i]).wait()

    def load_ah(i):
        return local(a_ref.at[2 - i // 3, 2 - i % 3], ah.at[i % 3], ah_sem.at[i % 3])

    def load_sl(q):
        return local(slope_ref.at[2 - q // 4, 3 - q % 4], sl.at[q % 3], sl_sem.at[q % 3])

    def start_y(n):
        @pl.when(n < full)
        def _():
            cols = pl.ds(pl.multiple_of(n * tile, tile), tile)
            local(x2_ref.at[:, cols], ytile.at[n % 2], y_sem.at[n % 2]).start()

        @pl.when((n >= full) & (n < full + 2))
        def _():
            cols = pl.ds(pl.multiple_of((n - full) * tile, tile), tile)
            local(p1_ref.at[:, cols], ytile.at[n % 2], y_sem.at[n % 2]).start()

        @pl.when(n == full + 2)
        def _():
            local(p0_ref, ytile.at[n % 2], y_sem.at[n % 2]).start()

    def wait_y(n):
        local(p0_ref, ytile.at[n % 2], y_sem.at[n % 2]).wait()

    def start_wtile(m):
        def go(key, k):
            cols = pl.multiple_of(pieces[key][0] + k * tile, 128)
            local(w_cols(cols, tile), wtile.at[m % 3], wtile_sem.at[m % 3]).start()

        @pl.when((m < 2 * full) & (m % 2 == 0))
        def _():
            go((2, "first"), m // 2)

        @pl.when((m < 2 * full) & (m % 2 == 1))
        def _():
            go((1, "back"), m // 2)

        @pl.when((m >= 2 * full) & (m < 3 * full))
        def _():
            go((0, "back"), m - 2 * full)

    def wait_wtile(m):
        local(w_cols(0, tile), wtile.at[m % 3], wtile_sem.at[m % 3]).wait()

    def dx_cols(k):
        return dx_ref.at[:, pl.ds(pl.multiple_of(k * tile, tile), tile)]

    def dx_store(k):
        return local(dxb.at[k % 2], dx_cols(k), dx_sem.at[k % 2])

    def dx_load(k):
        return local(dx_cols(k), dxb.at[k % 2], dx_sem.at[k % 2])

    load_g().start()
    load_a4(2).start()
    load_wf2().start()
    for q in range(3):
        load_sl(q).start()
        load_ah(q).start()
        load_wh(q).start()
    for n in range(2):
        start_y(jnp.int32(n))
    for m in range(3):
        start_wtile(jnp.int32(m))
    load_a4(1).start()
    load_x2tail().start()
    for k in range(3):
        load_wtail(k).start()
    load_wf(1).start()
    load_wf(0).start()
    load_w1().start()
    for i in range(3, 9):
        load_wh(i).start()

    def core_copy(t):
        return remote(gbuf.at[t % 3, :, 1 - lane], from_core.at[t % 4], core_ss.at[t % 3], core_rs.at[t % 4], (row, other))

    def first_to(t, peer):
        return remote(s1.at[t % 4], r1.at[t], ss1.at[t % 4], rs1.at[t], (row, peer))

    def second_to(t, peer):
        return remote(s2.at[t % 4], r2.at[t], ss2.at[t % 4], rs2.at[t], (row, peer))

    def z_all(t):
        return remote(zs.at[t % 4], zr.at[t], zss.at[t % 4], zrs.at[t], (z_in, me))

    def z_part(t):
        return remote(zp_s.at[t % 4], zp_r.at[t], pss.at[t % 4], prs.at[t], (z_in, me))

    def z_final(t, way):
        return remote(final.at[t], final.at[t], fss.at[t, way], frs.at[t], ((z_in, z_out)[way], me))

    def owned(t):
        return row == 1 + (t // 2) % 2

    def by_parity(t, even, odd):
        pl.when(t % 2 == 0)(even)
        pl.when(t % 2 == 1)(odd)

    def emit(t):
        @pl.when(t >= 4)
        def _():
            pl.semaphore_wait(credit, 1)
        core_copy(t).start()

    def stage_one(t):
        core_copy(t).wait_recv()

        @pl.when(t >= 4)
        def _():
            first_to(t - 4, over_x).wait_send()

        def go(peer, sent, kept):
            for k, c in enumerate(sent):
                s1[t % 4, k] = (gbuf[t % 3, c, lane] + from_core[t % 4, c]).astype(low)
            first_to(t, peer).start()
            for k, c in enumerate(kept):
                keep[t % 6, k] = gbuf[t % 3, c, lane] + from_core[t % 4, c]

        by_parity(
            t,
            lambda: go(over_x, (chip_x, chip_d), (chip, chip_y)),
            lambda: go(over_y, (chip_y, chip_d), (chip, chip_x)),
        )

        @pl.when(t + 4 < count)
        def _():
            pl.semaphore_signal(credit, inc=1, device_id=(row, other), device_id_type=MESH)

    def stage_two(t):
        first_to(t, over_x).wait_recv()

        @pl.when(t >= 4)
        def _():
            second_to(t - 4, over_x).wait_send()
        s2[t % 4] = (keep[t % 6, 1] + r1[t, 1].astype(wide)).astype(low)
        by_parity(t, lambda: second_to(t, over_y).start(), lambda: second_to(t, over_x).start())
        keep[t % 6, 0] = keep[t % 6, 0] + r1[t, 0].astype(wide)

    def stage_three(t):
        second_to(t, over_x).wait_recv()
        total = keep[t % 6, 0] + r2[t].astype(wide)
        plane[t % 6] = total

        @pl.when(is_edge)
        def _():
            @pl.when(t >= 4)
            def _():
                z_all(t - 4).wait_send()
            zs[t % 4] = total.astype(low)
            z_all(t).start()

    def stage_four(t):
        @pl.when(jnp.logical_not(is_edge))
        def _():
            z_all(t).wait_recv()
            total = plane[t % 6] + zr[t].astype(wide)
            plane[t % 6] = total

            @pl.when(jnp.logical_not(owned(t)))
            def _():
                @pl.when(t >= 4)
                def _():
                    z_part(t - 4).wait_send()
                zp_s[t % 4] = total.astype(low)
                z_part(t).start()

    def stage_five(t):
        @pl.when(owned(t))
        def _():
            z_part(t).wait_recv()
            final[t] = (plane[t % 6] + zp_r[t].astype(wide)).astype(low)
            z_final(t, 0).start()
            z_final(t, 1).start()

    def stage_six(t):
        @pl.when(jnp.logical_not(is_edge) & jnp.logical_not(owned(t)))
        def _():
            z_final(t, 1).wait_recv()
            z_final(t, 1).start()

    def stage_seven(t):
        @pl.when(is_edge)
        def _():
            z_final(t, 0).wait_recv()
        local(final.at[t], out_ref.at[t], out_sem.at[t]).start()
        got = final[t].astype(wide)
        got = got * got
        acc = square_s[...]
        for k in range(0, got.shape[0], 8):
            for j in range(0, tile, 128):
                acc = acc + got[k : k + 8, j : j + 128]
        square_s[...] = acc

    stages = (stage_one, stage_two, stage_three, stage_four, stage_five, stage_six, stage_seven)

    def over_rows(body):
        body(slice(None), 0)

    def add_row(r, value, k):
        small_s[0, pl.ds(r, 1), 0 : value.shape[1]] = value

    def column_sums(value):
        return jnp.sum(value.astype(wide), axis=0, keepdims=True)

    def put(t, start, value):
        width = value.shape[1]
        gbuf[t % 3, :, :, :, start : start + width] = value.reshape(4, 2, tile // 8, width)

    def slot_free(t):
        @pl.when(t >= 3)
        def _():
            core_copy(t - 3).wait_send()

    def flat(value):
        return value.reshape(tile, value.shape[-1])

    def settle(q, r):
        load_sl(q).wait()

        def body(rows, k):
            low_dz = (da[rows, :] * sl[q % 3, rows, :].astype(wide)).astype(low)
            dz[rows, :] = low_dz
            add_row(r, column_sums(low_dz), k)
        over_rows(body)

        @pl.when(q + 3 < 12)
        def _():
            load_sl(q + 3).start()

    def fore_two_a(t):
        load_g().wait()
        load_a4(2).wait()
        put(t, 0, mul(a4[0], g[:, 0:tile], TN))
        emit(t)
        r = bias_rows[2, "fore"][0]
        small_s[0, r : r + 1, :] = column_sums(g[:, 0:tile])

    def fore_two_b(t):
        width = wf2.shape[2]
        put(t, 0, mul(a4[0], g[:, tile:width], TN))
        gbuf[t % 3, :, :, :, width - tile :] = jnp.zeros((4, 2, tile // 8, 2 * tile - width), wide)
        emit(t)
        load_a4(0).start()
        r = bias_rows[2, "fore"][0]
        small_s[0, r + 1 : r + 2, 0 : width - tile] = column_sums(g[:, tile:width])
        load_wf2().wait()

        def body(rows, k):
            da[rows, :] = mul(g[rows, 0:width], flat(wf2[...]), NT)
        over_rows(body)
        settle(jnp.int32(0), bias_rows[2, 2][0])

    def hidden(t, i):
        load_ah(i).wait()
        slot_free(t)
        put(t, 0, mul(ah[i % 3], dz[...], TN))
        emit(t)

        @pl.when(i + 3 < 9)
        def _():
            load_ah(i + 3).start()
        wait_wh(i)
        q = i + 1 + i // 3
        load_sl(q).wait()
        r = 4 * (2 - i // 3) + 2 - i % 3

        def body(rows, k):
            d = mul(dz[rows, :], flat(wh[i]), NT)
            low_dz = (d * sl[q % 3, rows, :].astype(wide)).astype(low)
            dz[rows, :] = low_dz
            add_row(r, column_sums(low_dz), k)
        over_rows(body)

        @pl.when(q + 3 < 12)
        def _():
            load_sl(q + 3).start()

    def first_two(t, k):
        wait_y(k)
        slot_free(t)
        put(t, 0, mul(dz[...], ytile[k % 2], TN))
        emit(t)
        start_y(k + 2)
        m = 2 * k
        wait_wtile(m)

        @pl.when(k >= 2)
        def _():
            dx_store(k - 2).wait()
        r = bias_rows[1, "back"][0] + k

        def body(rows, b):
            dx = mul(dz[rows, :], flat(wtile[m % 3]))
            dxb[k % 2, rows, :] = dx
            low_gb = (-dx).astype(low)
            gb[rows, :] = low_gb
            add_row(r, column_sums(low_gb), b)
        over_rows(body)
        dx_store(k).start()
        start_wtile(m + 3)

    def back_head(stack_id, m, first):
        def body(rows, b):
            part = mul(gb[rows, :], flat(wtile[m % 3]), NT)

            @pl.when(first)
            def _():
                da[rows, :] = part

            @pl.when(jnp.logical_not(first))
            def _():
                da[rows, :] = da[rows, :] + part
        over_rows(body)
        start_wtile(m + 3)

    def back_one(t, k):
        @pl.when(k == 0)
        def _():
            load_a4(1).wait()
        slot_free(t)
        put(t, 0, mul(a4[1], gb[...], TN))
        emit(t)
        m = 2 * k + 1
        wait_wtile(m)
        back_head(1, m, k == 0)

    def tail_one(t):
        load_x2tail().wait()
        for k in range(3):
            load_wtail(k).wait()
        load_wf(1).wait()
        slot_free(t)

        def body(rows, k):
            dx = mul(dz[rows, :], flat(wtail[0]))
            dxt[rows, :] = dx
            low_gb = (-dx).astype(low)
            gb[rows, 0:rest] = low_gb
            gb[rows, rest : rest + 128] = g[rows, 896:1024]
            add_row(bias_rows[1, "back"][0] + full, column_sums(low_gb), k)
            add_row(bias_rows[1, "fore"][0], column_sums(g[rows, 896:1024]), k)
            da[rows, :] = (
                da[rows, :] + mul(low_gb, flat(wtail[1]), NT) + mul(g[rows, 896:1024], flat(wf[1]), NT)
            )
        over_rows(body)
        put(t, 0, mul(dz[...], x2tail[...], TN))
        put(t, rest, mul(a4[1], gb[:, 0 : rest + 128], TN))
        gbuf[t % 3, :, :, :, 2 * rest + 128 :] = jnp.zeros((4, 2, tile // 8, tile - 2 * rest - 128), wide)
        emit(t)
        for k in (full - 2, full - 1):
            dx_store(jnp.int32(k)).wait()
        for k in range(2):
            dx_load(jnp.int32(k)).start()
        settle(jnp.int32(4), bias_rows[1, 2][0])

    def first_one(t, k):
        wait_y(k)
        slot_free(t)
        put(t, 0, mul(dz[...], ytile[k % 2], TN))
        emit(t)
        start_y(k + 2)

    def pooled_back(rows, cols, width):
        high, tail = parts_low(mul(dz[rows, :], flat(w1[:, :, cols])))
        return mul(high, spread[:, 0:width]) + mul(tail, spread[:, 0:width])

    def back_zero(t, k):
        @pl.when(k == 0)
        def _():
            load_w1().wait()
            load_a4(0).wait()
        dx_load(k).wait()
        r = bias_rows[0, "back"][0] + k

        def body(rows, b):
            cols = pl.ds(pl.multiple_of(k * 128, 128), 128)
            low_gb = (-(dxb[k % 2, rows, :] + pooled_back(rows, cols, tile))).astype(low)
            gb[rows, :] = low_gb
            add_row(r, column_sums(low_gb), b)
        over_rows(body)

        @pl.when(k + 2 < full)
        def _():
            dx_load(k + 2).start()
        slot_free(t)
        put(t, 0, mul(a4[0], gb[...], TN))
        emit(t)
        m = 2 * full + k
        wait_wtile(m)
        back_head(0, m, k == 0)

    def tail_zero(t):
        load_wf(0).wait()

        def body(rows, k):
            low_gb = (-(dxt[rows, :] + pooled_back(rows, slice(full * 128, full * 128 + 128), rest))).astype(low)
            gb[rows, 0:rest] = low_gb
            gb[rows, rest : rest + 128] = g[rows, 768:896]
            add_row(bias_rows[0, "back"][0] + full, column_sums(low_gb), k)
            add_row(bias_rows[0, "fore"][0], column_sums(g[rows, 768:896]), k)
            da[rows, :] = (
                da[rows, :] + mul(low_gb, flat(wtail[2]), NT) + mul(g[rows, 768:896], flat(wf[0]), NT)
            )
        over_rows(body)
        slot_free(t)
        put(t, 0, mul(a4[0], gb[:, 0 : rest + 128], TN))
        gbuf[t % 3, :, :, :, rest + 128 :] = jnp.zeros((4, 2, tile // 8, tile - rest - 128), wide)
        emit(t)
        settle(jnp.int32(8), bias_rows[0, 2][0])

    row_pair = row + 1 - 2 * (row % 2)
    row_far = row + 2 - 4 * (row // 2)
    hops = ((row, other), (row, over_x), (row, over_y), (row_pair, me), (row_far, me))

    def small_step(k):
        return remote(small_s.at[k], small_r.at[k], small_ss.at[k], small_rs.at[k], hops[k])

    def small_stage(k):
        if k > 0:
            small_step(k - 1).wait_recv()
            total = small_s[k - 1] + small_r[k - 1]
            if k < len(hops):
                small_s[k] = total
            else:
                small_sum[...] = total
        if k < len(hops):
            small_step(k).start()

    square_s[...] = jnp.zeros_like(square_s)
    small_s[0] = jnp.zeros(small_s.shape[1:], wide)
    extra = small_s.shape[1] - 8
    small_s[0, extra:, :] = forward_small_ref[...]
    ids = lax.broadcasted_iota(jnp.int32, spread.shape, 0) * KERNELS[1]
    col = lax.broadcasted_iota(jnp.int32, spread.shape, 1)
    spread[...] = jnp.where((col >= ids) & (col < ids + KERNELS[1]), 1.0 / KERNELS[1], 0.0).astype(low)

    pl.semaphore_wait(barrier, 10)

    def turn(t, carry):
        pl.when(t == 0)(lambda: fore_two_a(t))
        pl.when(t == 1)(lambda: fore_two_b(t))

        @pl.when(((t >= 2) & (t < 5)) | ((t > t_tail1) & (t < t_first1)) | ((t > t_tail0) & (t < t_tail0 + 4)))
        def _():
            past_one = (t + count - t_tail1) // count
            past_zero = (t + count - t_tail0) // count
            hidden(t, t - 2 - past_one * (t_tail1 - 4) - past_zero * (t_tail0 - t_tail1 - 3))

        in_pair = (t >= 5) & (t < t_tail1)
        pl.when(in_pair & (t % 2 == 1))(lambda: first_two(t, (t - 5) // 2))
        pl.when(in_pair & (t % 2 == 0))(lambda: back_one(t, (t - 6) // 2))
        pl.when(t == t_tail1)(lambda: tail_one(t))
        pl.when(((t >= t_first1) & (t < t_back0)))(lambda: first_one(t, t - t_first1 + full))
        pl.when(((t >= t_back0) & (t < t_tail0)))(lambda: back_zero(t, t - t_back0))
        pl.when(t == t_tail0)(lambda: tail_zero(t))
        pl.when(t == t_tail0 + 4)(lambda: first_one(t, t - t_tail0 - 4 + full + 2))

        for k in range(len(hops) + 1):
            pl.when(t == count + 2 * k)(functools.partial(small_stage, k))
        for lag, stage in zip(LAGS, stages):
            pl.when((t >= lag) & (t < count + lag))(functools.partial(stage, t - lag))
        return carry

    lax.fori_loop(0, count + LAGS[-1], turn, 0)

    def square_copy(peer):
        return remote(square_s, square_r.at[me], sq_ss.at[peer], sq_rs.at[peer], (row, (me + peer) % 8))

    def square_wait(peer):
        return remote(square_s, square_r.at[(me - peer + 8) % 8], sq_ss.at[peer], sq_rs.at[peer], (row, (me + peer) % 8))

    for peer in range(1, 8):
        square_copy(peer).start()
    square_r[me] = square_s[...]
    for peer in range(1, 8):
        square_wait(peer).wait_recv()
    acc = square_r[0]
    for k in range(1, 8):
        acc = acc + square_r[k]
    tile_rows = small_s.shape[1] - 8
    biases = small_sum[0:tile_rows, :]
    total = jnp.sum(acc, keepdims=True) + jnp.sum(biases * biases, keepdims=True)
    tally = small_sum[tile_rows + 2 : tile_rows + 3, 0:1]
    factor = (1.0 / scale) / tally
    norm = jnp.sqrt(total) * factor
    result_ref[0:1, :] = jnp.broadcast_to(norm, (1, 128))
    loss = jnp.sum(small_sum[tile_rows : tile_rows + 2, :], keepdims=True) / tally
    result_ref[1:2, :] = jnp.broadcast_to(loss, (1, 128))
    result_ref[2:3, :] = jnp.broadcast_to(jnp.minimum(1.0, CLIP_MAX / norm) * factor, (1, 128))
    flat_ref[...] = jnp.zeros_like(flat_ref)
    for key, (at, width) in bias_rows.items():
        for k in range(0, width, tile):
            begin = spans[key] + k
            todo = min(tile, width - k)
            r, o = begin // tile, begin % tile
            here = min(todo, tile - o)
            line = slice(at + k // tile, at + k // tile + 1)
            flat_ref[r : r + 1, o : o + here] = small_sum[line, 0:here]
            if here < todo:
                flat_ref[r + 1 : r + 2, 0 : todo - here] = small_sum[line, here:todo]

    def finish(t, carry):
        @pl.when(t >= count - 3)
        def _():
            core_copy(t).wait_send()

        @pl.when(t >= count - 4)
        def _():
            first_to(t, over_x).wait_send()
            second_to(t, over_x).wait_send()

            @pl.when(is_edge)
            def _():
                z_all(t).wait_send()

        @pl.when(jnp.logical_not(is_edge))
        def _():
            @pl.when(owned(t))
            def _():
                z_final(t, 0).wait_send()
            z_final(t, 1).wait_send()

            @pl.when((t >= count - 4) & jnp.logical_not(owned(t)))
            def _():
                z_part(t).wait_send()
        local(final.at[t], out_ref.at[t], out_sem.at[t]).wait()
        return carry

    lax.fori_loop(0, count, finish, 0)
    for k in range(len(hops)):
        small_step(k).wait_send()
    for peer in range(1, 8):
        square_copy(peer).wait_send()


def backward(w, a, slope, p0, p1, x2, g, small, pieces, bias_rows, spans, scale, row_count, flat_rows, count):
    low, wide = jnp.bfloat16, jnp.float32
    rows, tile = a.shape[2], a.shape[3]
    part = tile // 8
    full, rest = x2.shape[1] // tile, x2.shape[1] % tile
    wide_steps = g.shape[1] - 256
    small_rows = row_count + 8
    hbm = pl.BlockSpec(memory_space=pltpu.HBM)
    vmem = pl.BlockSpec(memory_space=pltpu.VMEM)
    dma = pltpu.SemaphoreType.DMA
    shape = jax.ShapeDtypeStruct
    return pl.pallas_call(
        functools.partial(backward_kernel, (pieces, bias_rows, spans, scale, count, full)),
        out_shape=(
            shape((count, part, tile), low),
            shape((rows, full * tile), wide),
            shape((flat_rows, tile), wide),
            shape((8, 128), wide),
        ),
        in_specs=[hbm] * 7 + [vmem],
        out_specs=(hbm, hbm, vmem, vmem),
        scratch_shapes=[
            pltpu.VMEM((9, 8, part, tile), low),
            pltpu.VMEM((8, part, wide_steps), low),
            pltpu.VMEM((2, 8, part, 128), low),
            pltpu.VMEM((8, part, p1.shape[1]), low),
            pltpu.VMEM((3, 8, part, tile), low),
            pltpu.VMEM((3, 8, part, rest), low),
            pltpu.VMEM((2, rows, tile), low),
            pltpu.VMEM((3, rows, tile), low),
            pltpu.VMEM((3, rows, tile), low),
            pltpu.VMEM((2, rows, tile), low),
            pltpu.VMEM((rows, rest), low),
            pltpu.VMEM(g.shape, low),
            pltpu.VMEM((rows, tile), low),
            pltpu.VMEM((rows, tile), low),
            pltpu.VMEM((2, rows, tile), wide),
            pltpu.VMEM((rows, rest), wide),
            pltpu.VMEM((rows, tile), wide),
            pltpu.VMEM((128, tile), low),
            pltpu.VMEM((3, 4, 2, part, tile), wide),
            pltpu.VMEM((4, 4, part, tile), wide),
            pltpu.VMEM((4, 2, part, tile), low),
            pltpu.VMEM((count, 2, part, tile), low),
            pltpu.VMEM((6, 2, part, tile), wide),
            pltpu.VMEM((4, part, tile), low),
            pltpu.VMEM((count, part, tile), low),
            pltpu.VMEM((6, part, tile), wide),
            pltpu.VMEM((4, part, tile), low),
            pltpu.VMEM((count, part, tile), low),
            pltpu.VMEM((4, part, tile), low),
            pltpu.VMEM((count, part, tile), low),
            pltpu.VMEM((count, part, tile), low),
            pltpu.VMEM((5, small_rows, tile), wide),
            pltpu.VMEM((5, small_rows, tile), wide),
            pltpu.VMEM((small_rows, tile), wide),
            pltpu.VMEM((8, 128), wide),
            pltpu.VMEM((8, 8, 128), wide),
            dma((9,)),
            dma((2,)),
            dma((3,)),
            dma((3,)),
            dma((3,)),
            dma((3,)),
            dma((3,)),
            dma((2,)),
            dma((4,)),
            dma((2,)),
            dma((3,)),
            dma((4,)),
            pltpu.SemaphoreType.REGULAR,
            dma((4,)),
            dma((count,)),
            dma((4,)),
            dma((count,)),
            dma((4,)),
            dma((count,)),
            dma((4,)),
            dma((count,)),
            dma((count, 2)),
            dma((count,)),
            dma((5,)),
            dma((5,)),
            dma((8,)),
            dma((8,)),
            dma((count,)),
        ],
        compiler_params=pltpu.CompilerParams(
            collective_id=1, has_side_effects=True, vmem_limit_bytes=63 * 1024 * 1024
        ),
        name="backward",
    )(w, a, slope, p0, p1, x2, g, small)


def adamw_kernel(
    plan, step_ref, result_ref, grad_ref, *refs,
):
    where, pieces, count = plan
    groups = [refs[3 * k : 3 * k + 3] for k in range(4)]
    outs = [refs[12 + 4 * k : 16 + 4 * k] for k in range(4)]
    held = [refs[28 + 3 * k : 31 + 3 * k] for k in range(4)]
    copies = refs[40:44]
    grads, first_g, fore_g, grad_sem, in_sem, out_sem = refs[44:]
    wide, low = jnp.float32, jnp.bfloat16
    clip = result_ref[2:3, 0:1]
    steps = jnp.full((1, 1), 1.0, wide) * step_ref[0].astype(wide)
    mean_fix = 1.0 / (1.0 - jnp.exp(steps * float(np.log(BETA_ONE))))
    square_fix = 1.0 / (1.0 - jnp.exp(steps * float(np.log(BETA_TWO))))
    tile = grads.shape[2]

    units = [(1, k) for k in range(0, 9, 3)] + [(2, 0), (2, 1), (3, None), (0, None)]

    def view(ref, group, lead):
        if lead is None:
            return ref
        return ref.at[lead : lead + 3] if group == 1 else ref.at[lead]

    loads = []
    for n, (group, lead) in enumerate(units):
        loads.append(
            [
                pltpu.make_async_copy(view(groups[group][k], group, lead), view(held[group][k], group, lead), in_sem.at[n, k])
                for k in range(3)
            ]
        )
    whole = pltpu.make_async_copy(grad_ref, grads, grad_sem)
    whole.start()
    for unit in loads:
        for copy in unit:
            copy.start()
    whole.wait()

    for key_group, target in (("first", first_g), ("fore", fore_g)):
        begin = 0
        for stack_id in range(3):
            done = 0
            width = pieces[stack_id, key_group][1]
            for t, start, size in where[stack_id, key_group]:
                size = min(size, width - done)
                if size > 0:
                    target[:, begin + done : begin + done + size] = grads[t, :, start : start + size].astype(wide)
                done += size
            begin += width

    def update(group, index, grad):
        weight, avg, square = (held[group][k][index] for k in range(3))
        grad = grad * clip
        new_avg = BETA_ONE * avg + (1.0 - BETA_ONE) * grad
        new_sq = BETA_TWO * square + (1.0 - BETA_TWO) * grad * grad
        step = (new_avg * mean_fix) / (jnp.sqrt(new_sq * square_fix) + EPSILON) + DECAY * weight
        new_weight = weight - RATE * step
        held[group][0][index] = new_weight
        held[group][1][index] = new_avg
        held[group][2][index] = new_sq
        copies[group][index] = new_weight.astype(low)

    def rows_of(body, rows=64, step=16):
        def go(k, carry):
            body(pl.ds(pl.multiple_of(k * step, step), step))
            return carry
        lax.fori_loop(0, rows // step, go, 0)

    part = grads.shape[1]
    stores = []
    for n, (group, lead) in enumerate(units):
        for copy in loads[n]:
            copy.wait()
        if group == 1:
            for k in range(lead, lead + 3):
                t = where[k // 3, k % 3][0][0]
                rows_of(lambda rows: update(1, (k, rows), grads[t, rows, :].astype(wide)), part)
        elif group == 2:
            spots = where[lead, "back"]
            length = held[2][0].shape[2]

            def tiles(rows):
                done = 0
                for t, start, size in spots:
                    size = min(size, length - done)
                    update(2, (lead, rows, slice(done, done + size)), grads[t, rows, start : start + size].astype(wide))
                    done += size
            rows_of(tiles, part)
        else:
            target = first_g if group == 0 else fore_g
            rows_of(lambda rows: update(group, (rows,), target[rows, :]), part)
        for k in range(3):
            stores.append(
                pltpu.make_async_copy(view(held[group][k], group, lead), view(outs[group][k], group, lead), out_sem.at[n, k])
            )
        stores.append(
            pltpu.make_async_copy(view(copies[group], group, lead), view(outs[group][3], group, lead), out_sem.at[n, 3])
        )
        for copy in stores[-4:]:
            copy.start()
    for copy in stores:
        copy.wait()


def adamw_all(step_count, result, grads, states, where, pieces):
    low, wide = jnp.bfloat16, jnp.float32
    hbm = pl.BlockSpec(memory_space=pltpu.HBM)
    shape = jax.ShapeDtypeStruct
    shapes = [state[0].shape for state in states]
    dma = pltpu.SemaphoreType.DMA
    return pl.pallas_call(
        functools.partial(adamw_kernel, (where, pieces, grads.shape[0])),
        out_shape=tuple(shape(s, kind) for s in shapes for kind in (wide, wide, wide, low)),
        in_specs=[pl.BlockSpec(memory_space=pltpu.SMEM), pl.BlockSpec(memory_space=pltpu.VMEM)] + [hbm] * 13,
        out_specs=(hbm,) * 16,
        scratch_shapes=[pltpu.VMEM(s, wide) for s in shapes for _ in range(3)]
        + [pltpu.VMEM(s, low) for s in shapes]
        + [
            pltpu.VMEM(grads.shape, low),
            pltpu.VMEM(shapes[0], wide),
            pltpu.VMEM(shapes[3], wide),
            dma,
            dma((7, 3)),
            dma((7, 4)),
        ],
        compiler_params=pltpu.CompilerParams(vmem_limit_bytes=60 * 1024 * 1024),
        name="adamw",
    )(step_count, result, grads, *[array for state in states for array in state])


def fast_body(
    devices,
    windows,
    targets,
    horizon,
    step_count,
    first_w,
    first_w_avg,
    first_w_sq,
    hidden_w,
    hidden_w_avg,
    hidden_w_sq,
    back_w,
    back_w_avg,
    back_w_sq,
    fore_w,
    fore_w_avg,
    fore_w_sq,
    bias_vec,
    bias_avg,
    bias_sq,
):
    length, steps_ahead_total, hidden_size = windows.shape[1], targets.shape[1], hidden_w.shape[-1]
    part = hidden_w.shape[2]
    pieces, total = packing(length, steps_ahead_total, hidden_size)
    rows, row_count = row_plan(length, steps_ahead_total, hidden_size)
    row_count = -(-row_count // 8) * 8
    where, count = chunk_plan(length, steps_ahead_total, hidden_size)
    spans = {}
    cursor = 0
    for key in bias_order(length, steps_ahead_total, hidden_size):
        spans[key] = cursor
        cursor += rows[key][1]
    bias_count = bias_vec.shape[0]
    flat_rows = -(-bias_count // (8 * hidden_size)) * 8
    flat = jnp.pad(bias_vec, (0, flat_rows * hidden_size - bias_count)).reshape(flat_rows, hidden_size)
    ups = np.zeros((256, tiled(steps_ahead_total)), np.float32)
    for stack_id in range(2):
        knots = steps_ahead_total // RATIOS[stack_id]
        ups[128 * stack_id : 128 * stack_id + knots, :steps_ahead_total] = blend_coefficients(steps_ahead_total, knots)
    up_high = ups.astype(jnp.bfloat16)
    up_low = (ups - up_high.astype(np.float32)).astype(jnp.bfloat16)
    scale = 2.0 ** -int(np.ceil(np.log2(devices * windows.shape[0] * steps_ahead_total)))

    def lead(array):
        return array.reshape((-1,) + array.shape[2:]) if array.ndim == 4 else array

    states = (
        (first_w.T, first_w_avg.T, first_w_sq.T),
        (lead(hidden_w), lead(hidden_w_avg), lead(hidden_w_sq)),
        (back_w, back_w_avg, back_w_sq),
        (fore_w, fore_w_avg, fore_w_sq),
    )
    w, a, slope, p0, p1, x2, g, small = forward(
        states[0][0], states[1][0], back_w, fore_w, windows, targets, horizon, flat,
        jnp.asarray(up_high), jnp.asarray(up_low), pieces, rows, spans, scale, total,
    )
    owned, _, flat_grad, result = backward(
        w, a, slope, p0, p1, x2, g, small, pieces, rows, spans, scale, row_count, flat_rows, count
    )
    new = adamw_all(step_count, result, owned, states, where, pieces)
    first_new, hidden_new, back_new, fore_new = (new[4 * k : 4 * k + 4] for k in range(4))
    grad_bias = flat_grad.reshape(-1)[:bias_count] * result[2, 0]
    bias_new = adamw(bias_vec, bias_avg, bias_sq, grad_bias, step_count[0].astype(jnp.float32))
    shape = hidden_w.shape
    first_new = [array.T for array in first_new]
    hidden_new = [array.reshape(shape) for array in hidden_new]
    flat_out = [result[1, 0], result[0, 0]]
    for weight, avg, square, _ in (first_new, hidden_new, back_new, fore_new):
        flat_out += [avg, square, weight]
    flat_out += list(bias_new)
    flat_out += [group[3] for group in (first_new, hidden_new, back_new, fore_new)]
    return tuple(flat_out)


def solution(mesh):
    fast = mesh.shape["fsdp"] == 8 and mesh.shape["dp"] == 4
    step = functools.partial(fast_body, mesh.shape["dp"] * mesh.shape["fsdp"]) if fast else body
    placed = (
        P(("dp", "fsdp"), None),
        P(("dp", "fsdp"), None),
        P(("dp", "fsdp")),
        P(),
        P(None, "fsdp"),
        P(None, "fsdp"),
        P(None, "fsdp"),
        P(None, None, "fsdp", None),
        P(None, None, "fsdp", None),
        P(None, None, "fsdp", None),
        P(None, "fsdp", None),
        P(None, "fsdp", None),
        P(None, "fsdp", None),
        P("fsdp", None),
        P("fsdp", None),
        P("fsdp", None),
        P(),
        P(),
        P(),
    )
    return jax.shard_map(
        step,
        mesh=mesh,
        in_specs=placed,
        out_specs=(
            P(),
            P(),
            P(None, "fsdp"),
            P(None, "fsdp"),
            P(None, "fsdp"),
            P(None, None, "fsdp", None),
            P(None, None, "fsdp", None),
            P(None, None, "fsdp", None),
            P(None, "fsdp", None),
            P(None, "fsdp", None),
            P(None, "fsdp", None),
            P("fsdp", None),
            P("fsdp", None),
            P("fsdp", None),
            P(),
            P(),
            P(),
            P(None, "fsdp"),
            P(None, None, "fsdp", None),
            P(None, "fsdp", None),
            P("fsdp", None),
        ),
        check_vma=False,
    )
```

```python
import functools
import jax
import jax.numpy as jnp
import numpy as np
from jax import lax
from jax.experimental import pallas as pl
from jax.experimental.pallas import tpu as pltpu
from jax.sharding import PartitionSpec as P

KERNELS = (8, 4, 1)
RATIOS = (24, 12, 1)
CLIP_MAX = 0.01
RATE = 0.02
BETA_ONE = 0.9
BETA_TWO = 0.999
EPSILON = 1e-08
DECAY = 0.01
DOT_EXACTNESS = lax.Precision.HIGHEST


def blend_coefficients(fine, coarse):
    column = np.arange(fine)
    numer = np.maximum((2 * column + 1) * coarse - fine, 0)
    lower_idx = numer // (2 * fine)
    frac = (numer - lower_idx * 2 * fine) / (2.0 * fine)
    upper_idx = np.minimum(lower_idx + 1, coarse - 1)
    matrix = np.zeros((coarse, fine), np.float32)
    matrix[lower_idx, column] += 1.0 - frac
    matrix[upper_idx, column] += frac
    return matrix


def normalize(windows, targets):
    center = jnp.mean(windows, axis=1, keepdims=True)
    spread = jnp.sqrt(jnp.mean((windows - center) ** 2, axis=1, keepdims=True) + 1e-05)
    return ((windows - center) / spread, (targets - center) / spread)


def mean_pool(values, kernel):
    if kernel == 1:
        return values
    return jnp.mean(values.reshape(values.shape[0], values.shape[1] // kernel, kernel), axis=2)


def pool_back(d_pooled, kernel):
    if kernel == 1:
        return d_pooled
    spread_out = jnp.broadcast_to((d_pooled / kernel)[:, :, None], d_pooled.shape + (kernel,))
    return spread_out.reshape(d_pooled.shape[0], d_pooled.shape[1] * kernel)


def silu_slope(pre_act):
    gate = jax.nn.sigmoid(pre_act)
    return gate * (1.0 + pre_act * (1.0 - gate))


def stack_params(stack_id, gathered, bias_vec, length, steps_ahead_total):
    first_full, hidden_full, back_full, fore_full = gathered
    hidden_size = hidden_full.shape[-1]
    row_start = sum((length // KERNELS[earlier] for earlier in range(stack_id)))
    col_start = sum((steps_ahead_total // RATIOS[earlier] for earlier in range(stack_id)))
    pooled_len = length // KERNELS[stack_id]
    anchor_entries = steps_ahead_total // RATIOS[stack_id]
    layers = [
        (
            first_full[row_start : row_start + pooled_len],
            bias_vec[stack_id * hidden_size : (stack_id + 1) * hidden_size],
        )
    ]
    for layer_id in range(3):
        offset = (3 + 3 * stack_id + layer_id) * hidden_size
        layers.append((hidden_full[stack_id, layer_id], bias_vec[offset : offset + hidden_size]))
    fore_start = 12 * hidden_size + 2 * length + col_start
    fore_pair = (
        fore_full[:, col_start : col_start + anchor_entries],
        bias_vec[fore_start : fore_start + anchor_entries],
    )
    back_pair = None
    if stack_id < 2:
        back_start = 12 * hidden_size + stack_id * length
        back_pair = (back_full[stack_id], bias_vec[back_start : back_start + length])
    linear_upsample_anchors = jnp.asarray(blend_coefficients(steps_ahead_total, anchor_entries))
    return (layers, fore_pair, back_pair, linear_upsample_anchors)


def stack_forward(residual, stack_id, layers, fore_pair, back_pair, linear_upsample_anchors):
    inputs_kept = [mean_pool(residual, KERNELS[stack_id]).astype(jnp.bfloat16)]
    pre_kept = []
    for weight, bias in layers:
        pre_act = jnp.dot(inputs_kept[-1], weight, preferred_element_type=jnp.float32) + bias
        pre_kept.append(pre_act)
        inputs_kept.append(jax.nn.silu(pre_act).astype(jnp.bfloat16))
    anchor_result = (
        jnp.dot(inputs_kept[-1], fore_pair[0], preferred_element_type=jnp.float32) + fore_pair[1]
    )
    running_subtotal = jnp.dot(anchor_result, linear_upsample_anchors, precision=DOT_EXACTNESS)
    backcast = None
    if back_pair is not None:
        backcast = (
            jnp.dot(inputs_kept[-1], back_pair[0], preferred_element_type=jnp.float32)
            + back_pair[1]
        )
    return ((inputs_kept, pre_kept), running_subtotal, backcast)


def head_grads(last_act, d_low, weight):
    grad_w = jnp.dot(last_act.T, d_low, preferred_element_type=jnp.float32)
    grad_b = jnp.sum(d_low.astype(jnp.float32), axis=0)
    return ((grad_w, grad_b), jnp.dot(d_low, weight.T, preferred_element_type=jnp.float32))


def stack_backward(kept, anchor_cotangent, d_backcast, layers, fore_pair, back_pair, need_input):
    inputs_kept, pre_kept = kept
    last_act = inputs_kept[-1]
    fore_grads, d_hidden = head_grads(last_act, anchor_cotangent.astype(jnp.bfloat16), fore_pair[0])
    back_grads = None
    if back_pair is not None:
        back_grads, d_extra = head_grads(last_act, d_backcast.astype(jnp.bfloat16), back_pair[0])
        d_hidden = d_hidden + d_extra
    layer_grads = [None, None, None, None]
    for layer_id in (3, 2, 1, 0):
        d_pre = (d_hidden * silu_slope(pre_kept[layer_id])).astype(jnp.bfloat16)
        layer_grads[layer_id] = (
            jnp.dot(inputs_kept[layer_id].T, d_pre, preferred_element_type=jnp.float32),
            jnp.sum(d_pre.astype(jnp.float32), axis=0),
        )
        if layer_id > 0 or need_input:
            d_hidden = jnp.dot(d_pre, layers[layer_id][0].T, preferred_element_type=jnp.float32)
    return (layer_grads, fore_grads, back_grads, d_hidden)


def adamw(weight, avg, square, grad, step_float):
    new_avg = BETA_ONE * avg + (1.0 - BETA_ONE) * grad
    new_sq = BETA_TWO * square + (1.0 - BETA_TWO) * grad * grad
    avg_hat = new_avg / (1.0 - BETA_ONE**step_float)
    sq_hat = new_sq / (1.0 - BETA_TWO**step_float)
    new_weight = weight - RATE * (avg_hat / (jnp.sqrt(sq_hat) + EPSILON) + DECAY * weight)
    return (new_avg, new_sq, new_weight)


def body(
    windows,
    targets,
    horizon,
    step_count,
    first_w,
    first_w_avg,
    first_w_sq,
    hidden_w,
    hidden_w_avg,
    hidden_w_sq,
    back_w,
    back_w_avg,
    back_w_sq,
    fore_w,
    fore_w_avg,
    fore_w_sq,
    bias_vec,
    bias_avg,
    bias_sq,
):
    length = windows.shape[1]
    steps_ahead_total = targets.shape[1]
    normed, observed_future = normalize(windows, targets)
    future_usable_flags = (
        jnp.arange(steps_ahead_total, dtype=jnp.int32)[None, :] < horizon[:, None]
    ).astype(jnp.float32)
    usable_tally = lax.psum(jnp.sum(horizon.astype(jnp.float32)), ("dp", "fsdp"))
    shards = (
        first_w.astype(jnp.bfloat16),
        hidden_w.astype(jnp.bfloat16),
        back_w.astype(jnp.bfloat16),
        fore_w.astype(jnp.bfloat16),
    )
    gathered = (
        lax.all_gather(shards[0], "fsdp", axis=1, tiled=True),
        lax.all_gather(shards[1], "fsdp", axis=2, tiled=True),
        lax.all_gather(shards[2], "fsdp", axis=1, tiled=True),
        lax.all_gather(shards[3], "fsdp", axis=0, tiled=True),
    )
    residual = normed
    kept_stacks = []
    predicted_future = jnp.zeros(observed_future.shape, jnp.float32)
    for stack_id in range(3):
        layers, fore_pair, back_pair, linear_upsample_anchors = stack_params(
            stack_id, gathered, bias_vec, length, steps_ahead_total
        )
        kept, running_subtotal, backcast = stack_forward(
            residual, stack_id, layers, fore_pair, back_pair, linear_upsample_anchors
        )
        kept_stacks.append(kept)
        predicted_future = predicted_future + running_subtotal
        if backcast is not None:
            residual = residual - backcast
    residual_difference = predicted_future - observed_future
    loss_part = (
        jnp.sum(future_usable_flags * residual_difference * residual_difference) / usable_tally
    )
    future_slope_cotangent = 2.0 * future_usable_flags * residual_difference / usable_tally
    again = (
        lax.all_gather(shards[0], "fsdp", axis=1, tiled=True),
        lax.all_gather(shards[1], "fsdp", axis=2, tiled=True),
        lax.all_gather(shards[2], "fsdp", axis=1, tiled=True),
        lax.all_gather(shards[3], "fsdp", axis=0, tiled=True),
    )
    results = [None, None, None]
    d_residual = None
    for stack_id in (2, 1, 0):
        layers, fore_pair, back_pair, linear_upsample_anchors = stack_params(
            stack_id, again, bias_vec, length, steps_ahead_total
        )
        anchor_cotangent = jnp.dot(
            future_slope_cotangent, linear_upsample_anchors.T, precision=DOT_EXACTNESS
        )
        d_backcast = None if d_residual is None else -d_residual
        results[stack_id] = stack_backward(
            kept_stacks[stack_id],
            anchor_cotangent,
            d_backcast,
            layers,
            fore_pair,
            back_pair,
            stack_id > 0,
        )
        if stack_id > 0:
            spread_back = pool_back(results[stack_id][3], KERNELS[stack_id])
            d_residual = spread_back if d_residual is None else d_residual + spread_back
    grad_first = jnp.concatenate([results[stack_id][0][0][0] for stack_id in range(3)], axis=0)
    grad_hidden = jnp.stack(
        [
            jnp.stack([results[stack_id][0][layer_id][0] for layer_id in (1, 2, 3)])
            for stack_id in range(3)
        ]
    )
    grad_back = jnp.stack([results[stack_id][2][0] for stack_id in range(2)])
    grad_fore = jnp.concatenate([results[stack_id][1][0] for stack_id in range(3)], axis=1)
    bias_pieces = [results[stack_id][0][0][1] for stack_id in range(3)]
    bias_pieces += [
        results[stack_id][0][layer_id][1] for stack_id in range(3) for layer_id in (1, 2, 3)
    ]
    bias_pieces += [results[stack_id][2][1] for stack_id in range(2)]
    bias_pieces += [results[stack_id][1][1] for stack_id in range(3)]
    grad_bias = jnp.concatenate(bias_pieces)
    owned = (
        lax.psum_scatter(grad_first, "fsdp", scatter_dimension=1, tiled=True),
        lax.psum_scatter(grad_hidden, "fsdp", scatter_dimension=2, tiled=True),
        lax.psum_scatter(grad_back, "fsdp", scatter_dimension=1, tiled=True),
        lax.psum_scatter(grad_fore, "fsdp", scatter_dimension=0, tiled=True),
    )
    owned = lax.psum((owned[0], owned[1], owned[2], owned[3]), "dp")
    grad_bias, loss = lax.psum((grad_bias, loss_part), ("dp", "fsdp"))
    local_sq = sum((jnp.sum(grad * grad) for grad in owned))
    total_sq = lax.psum(local_sq, "fsdp") + jnp.sum(grad_bias * grad_bias)
    grad_norm = jnp.sqrt(total_sq)
    clip_factor = jnp.minimum(1.0, CLIP_MAX / grad_norm)
    step_float = step_count[0].astype(jnp.float32)
    states = (
        (first_w, first_w_avg, first_w_sq),
        (hidden_w, hidden_w_avg, hidden_w_sq),
        (back_w, back_w_avg, back_w_sq),
        (fore_w, fore_w_avg, fore_w_sq),
        (bias_vec, bias_avg, bias_sq),
    )
    grads_all = (owned[0], owned[1], owned[2], owned[3], grad_bias)
    updated = []
    for state, grad in zip(states, grads_all):
        updated.append(adamw(state[0], state[1], state[2], grad * clip_factor, step_float))
    return (
        loss,
        grad_norm,
        updated[0][0],
        updated[0][1],
        updated[0][2],
        updated[1][0],
        updated[1][1],
        updated[1][2],
        updated[2][0],
        updated[2][1],
        updated[2][2],
        updated[3][0],
        updated[3][1],
        updated[3][2],
        updated[4][0],
        updated[4][1],
        updated[4][2],
        updated[0][2].astype(jnp.bfloat16),
        updated[1][2].astype(jnp.bfloat16),
        updated[2][2].astype(jnp.bfloat16),
        updated[3][2].astype(jnp.bfloat16),
    )


MESH = pl.DeviceIdType.MESH
CHUNK = 1024


def tiled(width):
    return -(-width // 128) * 128


def packing(length, steps_ahead_total, hidden_size):
    pieces = {}
    cursor = 0
    for stack_id in range(3):
        widths = [("first", length // KERNELS[stack_id])]
        widths += [(layer_id, hidden_size) for layer_id in range(3)]
        if stack_id < 2:
            widths.append(("back", length))
        widths.append(("fore", steps_ahead_total // RATIOS[stack_id]))
        for name, width in widths:
            pieces[stack_id, name] = (cursor, width)
            cursor += tiled(width)
    total = -(-cursor // CHUNK) * CHUNK
    return pieces, total


def pack(parts, pieces, total):
    out = []
    cursor = 0
    for key, (start, width) in pieces.items():
        part = parts[key]
        out.append(jnp.pad(part, ((0, 0), (0, tiled(width) - width))))
        cursor = start + tiled(width)
    rows, dtype = out[0].shape[0], out[0].dtype
    if total > cursor:
        out.append(jnp.zeros((rows, total - cursor), dtype))
    return jnp.concatenate(out, axis=1)


def places():
    row = lax.axis_index("dp")
    me = lax.axis_index("fsdp")
    core = me % 2
    across_x = (me // 2) % 2
    across_y = me // 4
    other = me + 1 - 2 * core
    over_x = me + 2 - 4 * across_x
    over_y = me + 4 - 8 * across_y
    return row, me, core, other, over_x, over_y


def remote(src, dst, send_sem, recv_sem, device):
    return pltpu.make_async_remote_copy(
        src_ref=src, dst_ref=dst, send_sem=send_sem, recv_sem=recv_sem, device_id=device, device_id_type=MESH
    )


HALF_LOW = 2


def row_plan(length, steps_ahead_total, hidden_size):
    rows = {}
    cursor = 0
    for stack_id in range(3):
        for name in ("first", 0, 1, 2):
            rows[stack_id, name] = (cursor, hidden_size)
            cursor += 1
    for stack_id in range(2):
        rows[stack_id, "back"] = (cursor, length)
        cursor += -(-length // hidden_size)
    for stack_id in range(3):
        width = steps_ahead_total // RATIOS[stack_id]
        rows[stack_id, "fore"] = (cursor, width)
        cursor += -(-width // hidden_size)
    return rows, cursor


def bias_order(length, steps_ahead_total, hidden_size):
    keys = [(stack_id, "first") for stack_id in range(3)]
    keys += [(stack_id, layer_id) for stack_id in range(3) for layer_id in range(3)]
    keys += [(stack_id, "back") for stack_id in range(2)]
    keys += [(stack_id, "fore") for stack_id in range(3)]
    return keys


def parts_low(value):
    high = value.astype(jnp.bfloat16)
    return high, (value - high.astype(jnp.float32)).astype(jnp.bfloat16)


NN = (((1,), (0,)), ((), ()))
NT = (((1,), (1,)), ((), ()))
TN = (((0,), (0,)), ((), ()))


def mul(left, right, dims=NN):
    return lax.dot_general(left, right, dims, preferred_element_type=jnp.float32)


def cut_classes(count):
    pattern = "eoeo" + "eob" * count
    return (pattern[: count - 2] + "bb")[:count]


def forward_kernel(
    plan,
    first_ref, hidden_ref, back_ref, fore_ref, windows_ref, targets_ref, horizon_ref, flat_ref, up_high_ref, up_low_ref,
    w_out, a_out, slope_out, p0_out, p1_out, x2_out, g_out, small_ref,
    w, x, stage, a, slope, p0, p1, x2, fc, tt, g, dk, center_s, scale_s, pool8, pool4,
    bias_ref, first_s, hidden_s, back_s, fore_s,
    raw_sem, send_sem, recv_sem, win_sem, tt_sem, out_sem, w_sem,
):
    pieces, bias_rows, spans, cut_width, count, scale = plan
    row, me, core, other, over_x, over_y = places()
    diag = over_x + over_y - me
    total_rows = windows_ref.shape[0]
    length = windows_ref.shape[1]
    hidden_size = a.shape[-1]
    steps_ahead = targets_ref.shape[0]
    block = total_rows // 2
    wide, low = jnp.float32, jnp.bfloat16
    wide_length = x.shape[1]
    tiles = [(k, min(hidden_size, wide_length - k)) for k in range(0, wide_length, hidden_size)]
    whole = wide_length // 128 * 128 - 128

    barrier = pltpu.get_barrier_semaphore()
    for peer in (other, over_x, over_y):
        pl.semaphore_signal(barrier, inc=1, device_id=(row, peer), device_id_type=MESH)
    pl.semaphore_signal(barrier, inc=1, device_id=(row + 1 - 2 * (row % 2), me), device_id_type=MESH)

    classes = cut_classes(count)
    turn_of = [classes[:cut].count(classes[cut]) % 2 for cut in range(count)]
    even_plane = row % 2 == 0
    z_pair = row + 1 - 2 * (row % 2)

    def copy_of(kind, cut, src, holder, device):
        cols = slice(cut * cut_width, (cut + 1) * cut_width)
        return remote(src.at[:, cols], w.at[holder, :, cols], send_sem.at[kind, cut], recv_sem.at[kind, cut], device)

    def to_x(cut):
        return copy_of(0, cut, w.at[me], me, (row, over_x))

    def to_y(cut):
        return copy_of(1, cut, w.at[me], me, (row, over_y))

    def onward(cut):
        if turn_of[cut] == 0:
            return copy_of(2, cut, w.at[over_x], over_x, (row, over_y))
        return copy_of(2, cut, w.at[over_y], over_y, (row, over_x))

    def to_core(kind, cut):
        holder = (me, over_x, over_y, diag)[kind]
        return copy_of(3 + kind, cut, w.at[holder], holder, (row, other))

    def to_z(kind, cut):
        holder = (None, over_x, over_y, diag)[kind]
        return copy_of(6 + kind, cut, w.at[holder], holder, (z_pair, me))

    def gathers(cut, body):
        if classes[cut] == "b":
            body()
        else:
            pl.when(even_plane if classes[cut] == "e" else jnp.logical_not(even_plane))(body)

    def receives(cut, body):
        if classes[cut] != "b":
            pl.when(jnp.logical_not(even_plane) if classes[cut] == "e" else even_plane)(body)

    def own_sends(cut):
        def body():
            to_x(cut).start()
            to_y(cut).start()
        gathers(cut, body)
        to_core(0, cut).start()

    def w_copy(cut):
        cols = slice(cut * cut_width, (cut + 1) * cut_width)
        return pltpu.make_async_copy(w.at[:, :, cols], w_out.at[:, :, cols], w_sem.at[cut])

    look, lag_diag, lag_z = 4, 2, 6
    arrived = set()

    def pump(cut):
        if cut < count:
            def body():
                to_x(cut).wait_recv()
                if turn_of[cut] == 0:
                    onward(cut).start()
                if classes[cut] != "b":
                    to_z(1, cut).start()
                to_core(1, cut).start()
                to_y(cut).wait_recv()
                if turn_of[cut] == 1:
                    onward(cut).start()
                if classes[cut] != "b":
                    to_z(2, cut).start()
                to_core(2, cut).start()
            gathers(cut, body)
            if cut + look < count:
                own_sends(cut + look)
        past = cut - lag_diag
        if 0 <= past < count:
            def body():
                onward(past).wait_recv()
                if classes[past] != "b":
                    to_z(3, past).start()
                to_core(3, past).start()
            gathers(past, body)
        gone = cut - lag_z
        if 0 <= gone < count:
            def body():
                for kind in (1, 2, 3):
                    to_z(kind, gone).wait_recv()
                    to_core(kind, gone).start()
            receives(gone, body)
        for done in range(count):
            if done not in arrived and cut - done >= (lag_diag + 1 if classes[done] == "b" else lag_z + 1):
                for kind in range(4):
                    to_core(kind, done).wait_recv()
                w_copy(done).start()
                arrived.add(done)

    tasks = []

    def task(need, cost):
        def keep(body):
            tasks.append((need, cost, body))
            return body
        return keep

    def cut_of(key):
        start, width = pieces[key]
        return (start + tiled(width) - 1) // cut_width

    def weights(key, start=0, width=None):
        at, full_width = pieces[key]
        width = tiled(full_width) if width is None else width
        return w[:, :, at + start : at + start + width].reshape(hidden_size, width)

    def bias(key, start=0, width=None):
        at, full_width = bias_rows[key]
        width = hidden_size if width is None else width
        return bias_ref[at + start // hidden_size : at + start // hidden_size + 1, 0:width]

    def over_rows(body):
        def step(k, carry):
            body(pl.ds(pl.multiple_of(k * block, block), block))
            return carry
        lax.fori_loop(0, 2, step, 0)

    def outgoing(src, dst, slot):
        return pltpu.make_async_copy(src, dst, out_sem.at[slot])

    slots = stage.shape[0]
    strip = stage.shape[1]
    strips = total_rows // strip

    def window_copy(k):
        rows = pl.ds(pl.multiple_of(k * strip, strip), strip)
        return pltpu.make_async_copy(windows_ref.at[rows], stage.at[k % slots], win_sem.at[k % slots])

    raw = [
        pltpu.make_async_copy(src, dst, raw_sem.at[k])
        for k, (src, dst) in enumerate(
            ((first_ref, first_s), (hidden_ref, hidden_s), (back_ref, back_s), (fore_ref, fore_s))
        )
    ]
    for copy in raw:
        copy.start()
    for k in range(slots):
        window_copy(k).start()
    targets_copy = pltpu.make_async_copy(targets_ref, tt.at[0:steps_ahead], tt_sem)
    targets_copy.start()

    def pack_piece(key, value):
        start, width = pieces[key]
        if width % 128:
            edge = start + width // 128 * 128
            w[me, :, edge : edge + 128] = jnp.zeros((value.shape[0], 128), low)
        w[me, :, start : start + width] = value.astype(low)

    def pack_stack(stack_id):
        width = pieces[stack_id, "first"][1]
        begin = sum(pieces[earlier, "first"][1] for earlier in range(stack_id))
        pack_piece((stack_id, "first"), first_s[:, begin : begin + width])
        for layer_id in range(3):
            pack_piece((stack_id, layer_id), hidden_s[3 * stack_id + layer_id])
        if stack_id < 2:
            pack_piece((stack_id, "back"), back_s[stack_id])
        width = pieces[stack_id, "fore"][1]
        begin = sum(pieces[earlier, "fore"][1] for earlier in range(stack_id))
        pack_piece((stack_id, "fore"), fore_s[:, begin : begin + width])

    raw[0].wait()
    raw[1].wait()
    raw[2].wait()
    raw[3].wait()
    pack_stack(0)
    pl.semaphore_wait(barrier, 4)
    for cut in range(look):
        own_sends(cut)
    pack_stack(1)
    pack_stack(2)
    packed = max(start + tiled(width) for start, width in pieces.values())
    if packed < w.shape[2]:
        w[me, :, packed:] = jnp.zeros((w.shape[1], w.shape[2] - packed), low)
    bias_ref[...] = jnp.zeros_like(bias_ref)
    for key, (at, width) in bias_rows.items():
        for k in range(0, width, hidden_size):
            flat = spans[key] + k
            todo = min(hidden_size, width - k)
            r, o = flat // hidden_size, flat % hidden_size
            here = min(todo, hidden_size - o)
            bias_ref[at + k // hidden_size : at + k // hidden_size + 1, 0:here] = flat_ref[r : r + 1, o : o + here]
            if here < todo:
                bias_ref[at + k // hidden_size : at + k // hidden_size + 1, here:todo] = flat_ref[r + 1 : r + 2, 0 : todo - here]

    @task(-1, 1.0)
    def _():
        ids = lax.broadcasted_iota(jnp.int32, pool8.shape, 0)
        col = lax.broadcasted_iota(jnp.int32, pool8.shape, 1) * KERNELS[0]
        pool8[...] = jnp.where((ids >= col) & (ids < col + KERNELS[0]), 1.0 / KERNELS[0], 0.0).astype(low)
        ids = lax.broadcasted_iota(jnp.int32, pool4.shape, 0)
        col = lax.broadcasted_iota(jnp.int32, pool4.shape, 1) * KERNELS[1]
        pool4[...] = jnp.where((ids >= col) & (ids < col + KERNELS[1]), 1.0 / KERNELS[1], 0.0).astype(low)
        x[:, whole:] = jnp.zeros((total_rows, wide_length - whole), wide)

    groups = 3
    for group in range(groups):
        @task(-1, 3.0)
        def _(group=group):
            def step(k, carry):
                window_copy(k).wait()
                rows = pl.ds(pl.multiple_of(k * strip, strip), strip)
                value = stage[k % slots]
                center = jnp.sum(value, axis=1, keepdims=True) * (1.0 / length)
                value = value - center
                spread = jnp.sqrt(jnp.sum(value * value, axis=1, keepdims=True) * (1.0 / length) + 1e-05)
                factor = 1.0 / spread
                center_s[rows, :] = center
                scale_s[rows, :] = factor
                value = value * factor
                x[rows, 0:length] = value

                @pl.when(k + slots < strips)
                def _():
                    window_copy(k + slots).start()
                return carry
            lax.fori_loop(group * strips // groups, (group + 1) * strips // groups, step, 0)

    @task(-1, 3.0)
    def _():
        def body(rows):
            for k in range(0, wide_length, 1024):
                width = min(1024, wide_length - k)
                high, rest = parts_low(x[rows, k : k + width])
                pooled = mul(high, pool8[0:width]) + mul(rest, pool8[0:width])
                p0[rows, k // 8 : k // 8 + 128] = pooled.astype(low)
        over_rows(body)
        outgoing(p0, p0_out, 0).start()

    def activate(z, stack_id, j, rows):
        gate = jax.nn.sigmoid(z)
        act = z * gate
        a[j, rows, :] = act.astype(low)
        slope[j % 2, rows, :] = (gate + act * (1.0 - gate)).astype(low)

    def a_copy(stack_id, j):
        return outgoing(a.at[j], a_out.at[stack_id, j], 8 + j)

    def slope_copy(stack_id, j):
        return outgoing(slope.at[j % 2], slope_out.at[stack_id, j], 12 + j % 2)

    def send_layer(stack_id, j):
        a_copy(stack_id, j).start()
        slope_copy(stack_id, j).start()

    def settle_layer(stack_id, j):
        if stack_id > 0:
            a_copy(stack_id - 1, j).wait()
        n = 4 * stack_id + j - 2
        if n >= 0:
            slope_copy(n // 4, n % 4).wait()

    for stack_id in range(3):
        inputs = (p0, p1, x2)[stack_id]

        @task(cut_of((stack_id, "first")), (1.3, 2.2, 6.0)[stack_id])
        def _(stack_id=stack_id, inputs=inputs):
            settle_layer(stack_id, 0)

            def body(rows):
                z = mul(inputs[rows, :], weights((stack_id, "first")), NT) + bias((stack_id, "first"))
                activate(z, stack_id, 0, rows)
            over_rows(body)
            send_layer(stack_id, 0)

        for layer_id in range(3):
            @task(cut_of((stack_id, layer_id)), 1.3)
            def _(stack_id=stack_id, layer_id=layer_id):
                settle_layer(stack_id, layer_id + 1)

                def body(rows):
                    z = mul(a[layer_id, rows, :], weights((stack_id, layer_id))) + bias((stack_id, layer_id))
                    activate(z, stack_id, layer_id + 1, rows)
                over_rows(body)
                send_layer(stack_id, layer_id + 1)

        if stack_id < 2:
            for start, width in tiles:
                need = (pieces[stack_id, "back"][0] + start + width - 1) // cut_width

                @task(need, 1.4 if stack_id else 1.7)
                def _(stack_id=stack_id, start=start, width=width):
                    def body(rows):
                        cols = slice(start, start + width)
                        head = mul(a[3, rows, :], weights((stack_id, "back"), start, width))
                        rest = x[rows, cols] - (head + bias((stack_id, "back"), start, width))
                        if stack_id == 0:
                            x[rows, cols] = rest
                            high, tail = parts_low(rest)
                            pooled = mul(high, pool4[0:width]) + mul(tail, pool4[0:width])
                            p1[rows, start // 4 : start // 4 + 128] = pooled.astype(low)
                        else:
                            x2[rows, cols] = rest.astype(low)
                    over_rows(body)
                    if start + width == wide_length:
                        if stack_id == 0:
                            outgoing(p1, p1_out, 1).start()
                        else:
                            outgoing(x2, x2_out, 2).start()

            @task(cut_of((stack_id, "fore")), 1.5)
            def _(stack_id=stack_id):
                def body(rows):
                    knots = mul(a[3, rows, :], weights((stack_id, "fore"))) + bias((stack_id, "fore"), 0, 128)
                    high, rest = parts_low(knots)
                    ups = slice(128 * stack_id, 128 * stack_id + 128)
                    part = (
                        mul(high, up_high_ref[ups, :]) + mul(rest, up_high_ref[ups, :]) + mul(high, up_low_ref[ups, :])
                    )
                    fc[rows, :] = part if stack_id == 0 else fc[rows, :] + part
                over_rows(body)

    wide_steps = fc.shape[1]
    for start in range(0, wide_steps, 256):
        @task(cut_of((2, "fore")), 2.5)
        def _(start=start):
            if start == 0:
                targets_copy.wait()
                small_ref[...] = jnp.zeros_like(small_ref)
                small_ref[2:3, 0:128] = jnp.broadcast_to(jnp.sum(horizon_ref[...].astype(wide)), (1, 128))
            cols = slice(start, start + 256)
            head = mul(a[3], weights((2, "fore"), start, 256)) + bias_ref[
                bias_rows[2, "fore"][0] + start // hidden_size : bias_rows[2, "fore"][0] + start // hidden_size + 1,
                start % hidden_size : start % hidden_size + 256,
            ]
            goal = jnp.concatenate([tt[start : start + 128, :].T, tt[start + 128 : start + 256, :].T], axis=1)
            goal = (goal - center_s[...]) * scale_s[...]
            step = lax.broadcasted_iota(jnp.int32, (total_rows, 256), 1) + start
            diff = jnp.where(step < horizon_ref[...], fc[:, cols] + head - goal, 0.0)
            losses = jnp.sum(diff * diff, axis=0, keepdims=True)
            r = start // hidden_size
            small_ref[r : r + 1, start % hidden_size : start % hidden_size + 256] = losses
            diff = diff * (2.0 * scale)
            high, rest = parts_low(diff)
            g[:, cols] = high
            back = (
                mul(high, up_high_ref[:, cols], NT) + mul(rest, up_high_ref[:, cols], NT) + mul(high, up_low_ref[:, cols], NT)
            )
            dk[...] = back if start == 0 else dk[...] + back
            if start + 256 == wide_steps:
                g[:, wide_steps : wide_steps + 256] = dk[...].astype(low)
                outgoing(g, g_out, 3).start()

    queue = list(tasks)
    last = count + lag_z
    for cut in range(-1, last + 1):
        if cut >= 0:
            pump(cut)
        ready = min((done for done in range(count) if done not in arrived), default=count) - 1
        spent = 0.0
        while queue and queue[0][0] <= ready and (spent < 4.0 or cut == last):
            _, cost, body = queue.pop(0)
            body()
            spent += cost
    for cut in range(count):
        def body():
            to_x(cut).wait_send()
            to_y(cut).wait_send()
            onward(cut).wait_send()
            if classes[cut] != "b":
                for kind in (1, 2, 3):
                    to_z(kind, cut).wait_send()
        gathers(cut, body)
        for kind in range(4):
            to_core(kind, cut).wait_send()
        w_copy(cut).wait()
    outgoing(p0, p0_out, 0).wait()
    outgoing(p1, p1_out, 1).wait()
    outgoing(x2, x2_out, 2).wait()
    outgoing(g, g_out, 3).wait()
    for j in range(4):
        a_copy(2, j).wait()
    for j in (2, 3):
        slope_copy(2, j).wait()


def forward(first, hidden, back, fore, windows, targets, horizon, flat, up_high, up_low, pieces, bias_rows, spans, scale, total):
    low, wide = jnp.bfloat16, jnp.float32
    rows, length = windows.shape
    part, hidden_size = hidden.shape[1:]
    count = total // CHUNK
    wide_length = tiled(length)
    wide_steps = up_high.shape[1]
    p0_width, p1_width = tiled(length // KERNELS[0]), tiled(wide_length // KERNELS[1])
    row_count = -(-max(at - (-width // hidden_size) for at, width in bias_rows.values()) // 8) * 8
    strip = rows // 36
    hbm = pl.BlockSpec(memory_space=pltpu.HBM)
    vmem = pl.BlockSpec(memory_space=pltpu.VMEM)
    dma = pltpu.SemaphoreType.DMA
    shape = jax.ShapeDtypeStruct
    return pl.pallas_call(
        functools.partial(forward_kernel, (pieces, bias_rows, spans, CHUNK, count, scale)),
        out_shape=(
            shape((8, part, total), low),
            shape((3, 4, rows, hidden_size), low),
            shape((3, 4, rows, hidden_size), low),
            shape((rows, p0_width), low),
            shape((rows, p1_width), low),
            shape((rows, wide_length), low),
            shape((rows, wide_steps + 256), low),
            shape((8, hidden_size), wide),
        ),
        in_specs=[hbm] * 6 + [vmem] * 4,
        out_specs=(hbm,) * 7 + (vmem,),
        scratch_shapes=[
            pltpu.VMEM((8, part, total), low),
            pltpu.VMEM((rows, wide_length), wide),
            pltpu.VMEM((3, strip, length), wide),
            pltpu.VMEM((4, rows, hidden_size), low),
            pltpu.VMEM((2, rows, hidden_size), low),
            pltpu.VMEM((rows, p0_width), low),
            pltpu.VMEM((rows, p1_width), low),
            pltpu.VMEM((rows, wide_length), low),
            pltpu.VMEM((rows, wide_steps), wide),
            pltpu.VMEM((wide_steps, rows), wide),
            pltpu.VMEM((rows, wide_steps + 256), low),
            pltpu.VMEM((rows, 256), wide),
            pltpu.VMEM((rows, 1), wide),
            pltpu.VMEM((rows, 1), wide),
            pltpu.VMEM((1024, 128), low),
            pltpu.VMEM((512, 128), low),
            pltpu.VMEM((row_count, hidden_size), wide),
            pltpu.VMEM(first.shape, wide),
            pltpu.VMEM(hidden.shape, wide),
            pltpu.VMEM(back.shape, wide),
            pltpu.VMEM(fore.shape, wide),
            dma((4,)),
            dma((10, count)),
            dma((10, count)),
            dma((3,)),
            dma,
            dma((16,)),
            dma((count,)),
        ],
        compiler_params=pltpu.CompilerParams(
            collective_id=0, has_side_effects=True, vmem_limit_bytes=63 * 1024 * 1024
        ),
        name="forward",
    )(first, hidden, back, fore, windows, targets.T, horizon.reshape(rows, 1), flat, up_high, up_low)


def chunk_plan(length, steps_ahead_total, hidden_size):
    where = {}
    tile = hidden_size
    full, rest = tiled(length) // tile, tiled(length) % tile
    steps = tiled(steps_ahead_total)
    where[2, "fore"] = [(0, 0, tile), (1, 0, steps - tile)]
    where[1, "fore"] = [(1, steps - tile, 128)]
    for i in range(3):
        where[2, 2 - i] = [(2 + i, 0, tile)]
    t = 5
    last = t + 2 * full + 3 + 2 + full
    where[2, "first"] = [(t + 2 * k, 0, tile) for k in range(full)] + [(last, 0, rest)]
    where[1, "back"] = [(t + 2 * k + 1, 0, tile) for k in range(full)] + [(last, rest, rest)]
    t += 2 * full
    for i in range(3):
        where[1, 2 - i] = [(t + i, 0, tile)]
    where[1, "first"] = [(t + 3, 0, tile), (t + 4, 0, tile)]
    t += 5
    where[0, "back"] = [(t + k, 0, tile) for k in range(full)] + [(last, 2 * rest, rest)]
    where[0, "fore"] = [(last, 3 * rest, 128)]
    for i in range(3):
        where[0, 2 - i] = [(last + 1 + i, 0, tile)]
    where[0, "first"] = [(last + 4, 0, tile)]
    return where, last + 5


LAGS = (1, 3, 5, 7, 9, 11)


def backward_kernel(
    plan,
    w_ref, a_ref, slope_ref, p0_ref, p1_ref, x2_ref, g_ref, forward_small_ref,
    out_ref, dx_ref, flat_ref, result_ref,
    wh, wf2, wf, w1, wtile, wtail, a4, ah, sl, ytile, x2tail, g, dz, gb, dxb, dxt, da, spread, hold,
    gbuf, from_core, s1, r1, keep, s2, r2, plane, zs, zr, zp_s, zp_r, zl_s, zl_r, final,
    small_s, small_r, small_sum, square_s, square_r,
    wh_sem, wf_sem, wtile_sem, wtail_sem, a4_sem, ah_sem, sl_sem, y_sem, misc_sem, dx_sem,
    core_ss, core_rs, credit, ss1, rs1, ss2, rs2, zss, zrs, pss, prs, lss, lrs, fss, frs, small_ss, small_rs, sq_ss, sq_rs, out_sem,
):
    pieces, bias_rows, spans, scale, count, full = plan
    row, me, core, other, over_x, over_y = places()
    lane = core
    chip, chip_x, chip_y = me // 2, over_x // 2, over_y // 2
    chip_d = chip_x + chip_y - chip
    wide, low = jnp.float32, jnp.bfloat16
    total_rows = a_ref.shape[2]
    tile = a_ref.shape[3]
    rest = x2tail.shape[1]
    upper = row // 2
    z_in = row + 1 - 2 * upper
    is_edge = (row == 0) | (row == 3)
    z_out = (row + 3 + 2 * upper) % 4
    t_hidden1 = 5 + 2 * full
    t_first1 = t_hidden1 + 3
    t_back0 = t_first1 + 2
    t_tail0 = t_back0 + full

    barrier = pltpu.get_barrier_semaphore()
    for peer in range(1, 8):
        pl.semaphore_signal(barrier, inc=1, device_id=(row, (me + peer) % 8), device_id_type=MESH)
    for peer in range(1, 4):
        pl.semaphore_signal(barrier, inc=1, device_id=((row + peer) % 4, me), device_id_type=MESH)

    def local(src, dst, sem):
        return pltpu.make_async_copy(src, dst, sem)

    def w_cols(start, width):
        return w_ref.at[:, :, pl.ds(start, width)]

    def load_g():
        return local(g_ref, g, misc_sem.at[0])

    def load_x2tail():
        return local(x2_ref.at[:, full * tile : full * tile + rest], x2tail, misc_sem.at[1])

    def load_w1():
        return local(w_cols(pieces[1, "first"][0], w1.shape[2]), w1, misc_sem.at[2])

    def load_wf2():
        return local(w_cols(pieces[2, "fore"][0], wf2.shape[2]), wf2, misc_sem.at[3])

    def load_wf(stack_id):
        return local(w_cols(pieces[stack_id, "fore"][0], 128), wf.at[stack_id], wf_sem.at[stack_id])

    tails = ((2, "first"), (1, "back"), (0, "back"))

    def load_wtail(k):
        return local(w_cols(pieces[tails[k]][0] + full * tile, rest), wtail.at[k], wtail_sem.at[k])

    def load_a4(stack_id):
        return local(a_ref.at[stack_id, 3], a4.at[stack_id % 2], a4_sem.at[stack_id])

    def load_wh(i):
        return local(w_cols(pieces[2 - i // 3, 2 - i % 3][0], tile), wh.at[i], wh_sem.at[i])

    def wait_wh(i):
        local(w_cols(0, tile), wh.at[i], wh_sem.at[i]).wait()

    def load_ah(i):
        return local(a_ref.at[2 - i // 3, 2 - i % 3], ah.at[i % 3], ah_sem.at[i % 3])

    def load_sl(q):
        return local(slope_ref.at[2 - q // 4, 3 - q % 4], sl.at[q % 3], sl_sem.at[q % 3])

    def start_y(n):
        @pl.when(n < full)
        def _():
            cols = pl.ds(pl.multiple_of(n * tile, tile), tile)
            local(x2_ref.at[:, cols], ytile.at[n % 2], y_sem.at[n % 2]).start()

        @pl.when((n >= full) & (n < full + 2))
        def _():
            cols = pl.ds(pl.multiple_of((n - full) * tile, tile), tile)
            local(p1_ref.at[:, cols], ytile.at[n % 2], y_sem.at[n % 2]).start()

        @pl.when(n == full + 2)
        def _():
            local(p0_ref, ytile.at[n % 2], y_sem.at[n % 2]).start()

    def wait_y(n):
        local(p0_ref, ytile.at[n % 2], y_sem.at[n % 2]).wait()

    def start_wtile(m):
        def go(key, k):
            cols = pl.multiple_of(pieces[key][0] + k * tile, 128)
            local(w_cols(cols, tile), wtile.at[m % 3], wtile_sem.at[m % 3]).start()

        @pl.when((m < 2 * full) & (m % 2 == 0))
        def _():
            go((2, "first"), m // 2)

        @pl.when((m < 2 * full) & (m % 2 == 1))
        def _():
            go((1, "back"), m // 2)

        @pl.when((m >= 2 * full) & (m < 3 * full))
        def _():
            go((0, "back"), m - 2 * full)

    def wait_wtile(m):
        local(w_cols(0, tile), wtile.at[m % 3], wtile_sem.at[m % 3]).wait()

    def dx_cols(k):
        return dx_ref.at[:, pl.ds(pl.multiple_of(k * tile, tile), tile)]

    def dx_store(k):
        return local(dxb.at[k % 2], dx_cols(k), dx_sem.at[k % 2])

    def dx_load(k):
        return local(dx_cols(k), dxb.at[k % 2], dx_sem.at[k % 2])

    load_g().start()
    load_a4(2).start()
    load_wf2().start()
    for q in range(3):
        load_sl(q).start()
        load_ah(q).start()
        load_wh(q).start()
    for n in range(2):
        start_y(jnp.int32(n))
    for m in range(3):
        start_wtile(jnp.int32(m))
    load_a4(1).start()
    load_x2tail().start()
    for k in range(3):
        load_wtail(k).start()
    load_wf(1).start()
    load_wf(0).start()
    load_w1().start()
    for i in range(3, 9):
        load_wh(i).start()

    def core_copy(t):
        return remote(gbuf.at[t % 3, :, 1 - lane], from_core.at[t % 4], core_ss.at[t % 3], core_rs.at[t % 4], (row, other))

    def first_to(t):
        peer = over_x + t % 2 * (over_y - over_x)
        return remote(s1.at[t % 4], r1.at[t], ss1.at[t % 4], rs1.at[t], (row, peer))

    def second_to(t):
        peer = over_y + t % 2 * (over_x - over_y)
        return remote(s2.at[t % 4], r2.at[t], ss2.at[t % 4], rs2.at[t], (row, peer))

    def z_all(t):
        return remote(zs.at[t % 4], zr.at[t], zss.at[t % 4], zrs.at[t], (z_in, me))

    def z_swap(t):
        return remote(zp_s.at[t % 4], zp_r.at[t], pss.at[t % 4], prs.at[t], (z_in, me))

    def z_low(t):
        return remote(zl_s.at[t % 2], zl_r.at[t % 2], lss.at[t % 2], lrs.at[t % 2], (z_in, me))

    def precise(t):
        return t < 2

    def save_low(t, total, high):
        zl_s[t % 2] = (total - high.astype(wide)).astype(low)

    def z_final(t):
        return remote(final.at[t], final.at[t], fss.at[t], frs.at[t], (z_out, me))

    def emit(t):
        @pl.when(t >= 4)
        def _():
            pl.semaphore_wait(credit, 1)
        core_copy(t).start()

    def guarded(sure, condition, body):
        if sure:
            body()
        else:
            pl.when(condition)(body)

    def stage_one(t, sure):
        core_copy(t).wait_recv()
        guarded(sure, t >= 4, lambda: first_to(t - 4).wait_send())
        odd = t % 2
        for k, c in enumerate((chip_x + odd * (chip_y - chip_x), chip_d)):
            s1[t % 4, k] = (gbuf[t % 3, c, lane] + from_core[t % 4, c]).astype(low)
        first_to(t).start()
        for k, c in enumerate((chip, chip_y + odd * (chip_x - chip_y))):
            keep[t % 6, k] = gbuf[t % 3, c, lane] + from_core[t % 4, c]
        guarded(
            sure,
            t + 4 < count,
            lambda: pl.semaphore_signal(credit, inc=1, device_id=(row, other), device_id_type=MESH),
        )

    def stage_two(t, sure):
        first_to(t).wait_recv()
        guarded(sure, t >= 4, lambda: second_to(t - 4).wait_send())
        s2[t % 4] = (keep[t % 6, 1] + r1[t, 1].astype(wide)).astype(low)
        second_to(t).start()

    def stage_three(t, sure):
        second_to(t).wait_recv()
        plane[t % 6] = keep[t % 6, 0] + r1[t, 0].astype(wide) + r2[t].astype(wide)

    def outer_send(t, sure):
        guarded(sure, t >= 4, lambda: z_all(t - 4).wait_send())
        zs[t % 4] = plane[t % 6].astype(low)
        z_all(t).start()

    def inner_swap(t, sure):
        z_all(t).wait_recv()
        guarded(sure, t >= 4, lambda: z_swap(t - 4).wait_send())
        total = plane[t % 6] + zr[t].astype(wide)
        high = total.astype(low)
        zp_s[t % 4] = high
        pl.when(precise(t))(lambda: save_low(t, total, high))
        z_swap(t).start()
        pl.when(precise(t))(lambda: z_low(t).start())

    def inner_total(t, sure):
        z_swap(t).wait_recv()

        @pl.when(precise(t))
        def _():
            z_low(t).wait_recv()
            here = zp_s[t % 4].astype(wide) + zl_s[t % 2].astype(wide)
            there = zp_r[t].astype(wide) + zl_r[t % 2].astype(wide)
            final[t] = (here + there).astype(low)

        @pl.when(jnp.logical_not(precise(t)))
        def _():
            final[t] = (zp_s[t % 4].astype(wide) + zp_r[t].astype(wide)).astype(low)
        z_final(t).start()

    def outer_total(t, sure):
        z_final(t).wait_recv()

    def stage_last(t, sure):
        local(final.at[t], out_ref.at[t], out_sem.at[t]).start()
        got = final[t].astype(wide)
        got = got * got
        acc = square_s[...]
        for k in range(0, got.shape[0], 8):
            for j in range(0, tile, 128):
                acc = acc + got[k : k + 8, j : j + 128]
        square_s[...] = acc

    def reduce_turn(t, sure):
        def at(lag, stage):
            guarded(sure, (t >= lag) & (t < count + lag), lambda: stage(t - lag, sure))
        at(LAGS[0], stage_one)
        at(LAGS[1], stage_two)
        at(LAGS[2], stage_three)

        @pl.when(is_edge)
        def _():
            at(LAGS[2], outer_send)
            at(LAGS[5], outer_total)

        @pl.when(jnp.logical_not(is_edge))
        def _():
            at(LAGS[3], inner_swap)
            at(LAGS[4], inner_total)
        at(LAGS[5], stage_last)

    def over_rows(body):
        body(slice(None), 0)

    def add_row(r, value, k):
        small_s[0, pl.ds(r, 1), 0 : value.shape[1]] = value

    def column_sums(value):
        return jnp.sum(value.astype(wide), axis=0, keepdims=True)

    def put(t, start, value):
        width = value.shape[1]
        gbuf[t % 3, :, :, :, start : start + width] = value.reshape(4, 2, tile // 8, width)

    def slot_free(t):
        @pl.when(t >= 3)
        def _():
            core_copy(t - 3).wait_send()

    def flat(value):
        return value.reshape(tile, value.shape[-1])

    def settle(q, r):
        load_sl(q).wait()

        def body(rows, k):
            low_dz = (da[rows, :] * sl[q % 3, rows, :].astype(wide)).astype(low)
            dz[rows, :] = low_dz
            add_row(r, column_sums(low_dz), k)
        over_rows(body)

        @pl.when(q + 3 < 12)
        def _():
            load_sl(q + 3).start()

    def fore_two_a(t):
        load_g().wait()
        load_a4(2).wait()
        put(t, 0, mul(a4[0], g[:, 0:tile], TN))
        emit(t)
        r = bias_rows[2, "fore"][0]
        small_s[0, r : r + 1, :] = column_sums(g[:, 0:tile])

    def fore_two_b(t):
        width = wf2.shape[2]
        put(t, 0, mul(a4[0], g[:, tile:width], TN))
        load_a4(0).start()
        load_a4(1).wait()
        put(t, width - tile, mul(a4[1], g[:, 896:1024], TN))
        done = width - tile + 128
        gbuf[t % 3, :, :, :, done:] = jnp.zeros((4, 2, tile // 8, tile - done), wide)
        emit(t)
        r = bias_rows[2, "fore"][0]
        small_s[0, r + 1 : r + 2, 0 : width - tile] = column_sums(g[:, tile:width])
        load_wf2().wait()

        def body(rows, k):
            da[rows, :] = mul(g[rows, 0:width], flat(wf2[...]), NT)
        over_rows(body)
        settle(jnp.int32(0), bias_rows[2, 2][0])

    def hidden(t, i):
        load_ah(i).wait()
        slot_free(t)
        wait_wh(i)
        q = i + 1 + i // 3
        load_sl(q).wait()
        r = 4 * (2 - i // 3) + 2 - i % 3
        put(t, 0, mul(ah[i % 3], dz[...], TN))

        def body(rows, k):
            d = mul(dz[rows, :], flat(wh[i]), NT)
            low_dz = (d * sl[q % 3, rows, :].astype(wide)).astype(low)
            dz[rows, :] = low_dz
            add_row(r, column_sums(low_dz), k)
        over_rows(body)
        emit(t)

        @pl.when(i + 3 < 9)
        def _():
            load_ah(i + 3).start()

        @pl.when(q + 3 < 12)
        def _():
            load_sl(q + 3).start()

    def first_two(t, k):
        wait_y(k)
        slot_free(t)
        m = 2 * k
        wait_wtile(m)

        @pl.when(k >= 2)
        def _():
            dx_store(k - 2).wait()
        r = bias_rows[1, "back"][0] + k
        put(t, 0, mul(dz[...], ytile[k % 2], TN))

        def body(rows, b):
            dx = mul(dz[rows, :], flat(wtile[m % 3]))
            dxb[k % 2, rows, :] = dx
            low_gb = (-dx).astype(low)
            gb[rows, :] = low_gb
            add_row(r, column_sums(low_gb), b)
        over_rows(body)
        emit(t)
        start_y(k + 2)
        dx_store(k).start()
        start_wtile(m + 3)

    def back_head(m):
        da[...] = da[...] + mul(gb[...], flat(wtile[m % 3]), NT)

    def clear_da(k):
        @pl.when(k == 0)
        def _():
            da[...] = jnp.zeros(da.shape, wide)

    def back_one(t, k):
        clear_da(k)
        slot_free(t)
        m = 2 * k + 1
        wait_wtile(m)
        put(t, 0, mul(a4[1], gb[...], TN))
        back_head(m)
        emit(t)
        start_wtile(m + 3)
        pl.when(k == full - 1)(tail_one)

    def tail_one():
        load_x2tail().wait()
        for k in range(3):
            load_wtail(k).wait()
        load_wf(1).wait()

        def body(rows, k):
            dx = mul(dz[rows, :], flat(wtail[0]))
            dxt[rows, :] = dx
            low_gb = (-dx).astype(low)
            gb[rows, 0:rest] = low_gb
            add_row(bias_rows[1, "back"][0] + full, column_sums(low_gb), k)
            add_row(bias_rows[1, "fore"][0], column_sums(g[rows, 896:1024]), k)
            da[rows, :] = (
                da[rows, :] + mul(low_gb, flat(wtail[1]), NT) + mul(g[rows, 896:1024], flat(wf[1]), NT)
            )
        over_rows(body)
        hold[:, 0:rest] = mul(dz[...], x2tail[...], TN)
        hold[:, rest : 2 * rest] = mul(a4[1], gb[:, 0:rest], TN)
        for k in (full - 2, full - 1):
            dx_store(jnp.int32(k)).wait()
        for k in range(2):
            dx_load(jnp.int32(k)).start()
        settle(jnp.int32(4), bias_rows[1, 2][0])

    def first_one(t, k):
        wait_y(k)
        slot_free(t)
        put(t, 0, mul(dz[...], ytile[k % 2], TN))
        emit(t)
        start_y(k + 2)

    def pooled_back(rows, cols, width):
        high, tail = parts_low(mul(dz[rows, :], flat(w1[:, :, cols])))
        return mul(high, spread[:, 0:width]) + mul(tail, spread[:, 0:width])

    def back_zero(t, k):
        @pl.when(k == 0)
        def _():
            load_w1().wait()
            load_a4(0).wait()
        dx_load(k).wait()
        clear_da(k)
        slot_free(t)
        m = 2 * full + k
        wait_wtile(m)
        r = bias_rows[0, "back"][0] + k

        def body(rows, b):
            cols = pl.ds(pl.multiple_of(k * 128, 128), 128)
            low_gb = (-(dxb[k % 2, rows, :] + pooled_back(rows, cols, tile))).astype(low)
            gb[rows, :] = low_gb
            add_row(r, column_sums(low_gb), b)
        over_rows(body)
        put(t, 0, mul(a4[0], gb[...], TN))
        back_head(m)
        emit(t)
        start_wtile(m + 3)

        @pl.when(k + 2 < full)
        def _():
            dx_load(k + 2).start()

    def tail_zero(t):
        load_wf(0).wait()

        def body(rows, k):
            low_gb = (-(dxt[rows, :] + pooled_back(rows, slice(full * 128, full * 128 + 128), rest))).astype(low)
            gb[rows, 0:rest] = low_gb
            gb[rows, rest : rest + 128] = g[rows, 768:896]
            add_row(bias_rows[0, "back"][0] + full, column_sums(low_gb), k)
            add_row(bias_rows[0, "fore"][0], column_sums(g[rows, 768:896]), k)
            da[rows, :] = (
                da[rows, :] + mul(low_gb, flat(wtail[2]), NT) + mul(g[rows, 768:896], flat(wf[0]), NT)
            )
        over_rows(body)
        slot_free(t)
        put(t, 0, hold[...])
        put(t, 2 * rest, mul(a4[0], gb[:, 0 : rest + 128], TN))
        emit(t)
        settle(jnp.int32(8), bias_rows[0, 2][0])

    row_pair = row + 1 - 2 * (row % 2)
    row_far = row + 2 - 4 * (row // 2)
    hops = ((row, other), (row, over_x), (row, over_y), (row_pair, me), (row_far, me))

    def small_step(k):
        return remote(small_s.at[k], small_r.at[k], small_ss.at[k], small_rs.at[k], hops[k])

    def small_stage(k):
        if k > 0:
            small_step(k - 1).wait_recv()
            total = small_s[k - 1] + small_r[k - 1]
            if k < len(hops):
                small_s[k] = total
            else:
                small_sum[...] = total
        if k < len(hops):
            small_step(k).start()

    square_s[...] = jnp.zeros_like(square_s)
    small_s[0] = jnp.zeros(small_s.shape[1:], wide)
    extra = small_s.shape[1] - 8
    small_s[0, extra:, :] = forward_small_ref[...]
    ids = lax.broadcasted_iota(jnp.int32, spread.shape, 0) * KERNELS[1]
    col = lax.broadcasted_iota(jnp.int32, spread.shape, 1)
    spread[...] = jnp.where((col >= ids) & (col < ids + KERNELS[1]), 1.0 / KERNELS[1], 0.0).astype(low)

    pl.semaphore_wait(barrier, 10)

    def compute(t):
        @pl.when(t < 2)
        def _():
            pl.when(t == 0)(lambda: fore_two_a(t))
            pl.when(t == 1)(lambda: fore_two_b(t))

        in_pair = (t >= 5) & (t < t_hidden1)
        in_back = (t >= t_back0) & (t < t_tail0)

        @pl.when(in_pair)
        def _():
            pl.when(t % 2 == 1)(lambda: first_two(t, (t - 5) // 2))
            pl.when(t % 2 == 0)(lambda: back_one(t, (t - 6) // 2))

        pl.when(in_back)(lambda: back_zero(t, t - t_back0))

        @pl.when((t >= 2) & jnp.logical_not(in_pair) & jnp.logical_not(in_back))
        def _():
            @pl.when((t < 5) | ((t >= t_hidden1) & (t < t_first1)) | ((t > t_tail0) & (t < t_tail0 + 4)))
            def _():
                past_one = (t + count - t_hidden1) // count
                past_zero = (t + count - t_tail0) // count
                hidden(t, t - 2 - past_one * (t_hidden1 - 5) - past_zero * (t_tail0 - t_hidden1 - 2))

            pl.when((t >= t_first1) & (t < t_back0))(lambda: first_one(t, t - t_first1 + full))
            pl.when(t == t_tail0)(lambda: tail_zero(t))
            pl.when(t == t_tail0 + 4)(lambda: first_one(t, t - t_tail0 - 4 + full + 2))

    def turn(t, carry):
        pl.when(t < count)(lambda: compute(t))

        @pl.when(t >= count)
        def _():
            for k in range(len(hops) + 1):
                pl.when(t == count + 2 * k)(functools.partial(small_stage, k))
        steady = (t >= LAGS[-1]) & (t < count - 3)
        pl.when(steady)(lambda: reduce_turn(t, True))
        pl.when(jnp.logical_not(steady))(lambda: reduce_turn(t, False))
        return carry

    lax.fori_loop(0, count + LAGS[-1], turn, 0)

    def square_copy(peer):
        return remote(square_s, square_r.at[me], sq_ss.at[peer], sq_rs.at[peer], (row, (me + peer) % 8))

    def square_wait(peer):
        return remote(square_s, square_r.at[(me - peer + 8) % 8], sq_ss.at[peer], sq_rs.at[peer], (row, (me + peer) % 8))

    for peer in range(1, 8):
        square_copy(peer).start()
    square_r[me] = square_s[...]
    for peer in range(1, 8):
        square_wait(peer).wait_recv()
    acc = square_r[0]
    for k in range(1, 8):
        acc = acc + square_r[k]
    tile_rows = small_s.shape[1] - 8
    biases = small_sum[0:tile_rows, :]
    total = jnp.sum(acc, keepdims=True) + jnp.sum(biases * biases, keepdims=True)
    tally = small_sum[tile_rows + 2 : tile_rows + 3, 0:1]
    factor = (1.0 / scale) / tally
    norm = jnp.sqrt(total) * factor
    result_ref[0:1, :] = jnp.broadcast_to(norm, (1, 128))
    loss = jnp.sum(small_sum[tile_rows : tile_rows + 2, :], keepdims=True) / tally
    result_ref[1:2, :] = jnp.broadcast_to(loss, (1, 128))
    result_ref[2:3, :] = jnp.broadcast_to(jnp.minimum(1.0, CLIP_MAX / norm) * factor, (1, 128))
    flat_ref[...] = jnp.zeros_like(flat_ref)
    for key, (at, width) in bias_rows.items():
        for k in range(0, width, tile):
            begin = spans[key] + k
            todo = min(tile, width - k)
            r, o = begin // tile, begin % tile
            here = min(todo, tile - o)
            line = slice(at + k // tile, at + k // tile + 1)
            flat_ref[r : r + 1, o : o + here] = small_sum[line, 0:here]
            if here < todo:
                flat_ref[r + 1 : r + 2, 0 : todo - here] = small_sum[line, here:todo]

    def finish(t, carry):
        @pl.when(t >= count - 3)
        def _():
            core_copy(t).wait_send()

        @pl.when(t >= count - 4)
        def _():
            first_to(t).wait_send()
            second_to(t).wait_send()

            @pl.when(is_edge)
            def _():
                z_all(t).wait_send()

            @pl.when(jnp.logical_not(is_edge))
            def _():
                z_swap(t).wait_send()

        @pl.when(jnp.logical_not(is_edge))
        def _():
            z_final(t).wait_send()
            pl.when(precise(t))(lambda: z_low(t).wait_send())
        local(final.at[t], out_ref.at[t], out_sem.at[t]).wait()
        return carry

    lax.fori_loop(0, count, finish, 0)
    for k in range(len(hops)):
        small_step(k).wait_send()
    for peer in range(1, 8):
        square_copy(peer).wait_send()


def backward(w, a, slope, p0, p1, x2, g, small, pieces, bias_rows, spans, scale, row_count, flat_rows, count):
    low, wide = jnp.bfloat16, jnp.float32
    rows, tile = a.shape[2], a.shape[3]
    part = tile // 8
    full, rest = x2.shape[1] // tile, x2.shape[1] % tile
    wide_steps = g.shape[1] - 256
    small_rows = row_count + 8
    hbm = pl.BlockSpec(memory_space=pltpu.HBM)
    vmem = pl.BlockSpec(memory_space=pltpu.VMEM)
    dma = pltpu.SemaphoreType.DMA
    shape = jax.ShapeDtypeStruct
    return pl.pallas_call(
        functools.partial(backward_kernel, (pieces, bias_rows, spans, scale, count, full)),
        out_shape=(
            shape((count, part, tile), low),
            shape((rows, full * tile), wide),
            shape((flat_rows, tile), wide),
            shape((8, 128), wide),
        ),
        in_specs=[hbm] * 7 + [vmem],
        out_specs=(hbm, hbm, vmem, vmem),
        scratch_shapes=[
            pltpu.VMEM((9, 8, part, tile), low),
            pltpu.VMEM((8, part, wide_steps), low),
            pltpu.VMEM((2, 8, part, 128), low),
            pltpu.VMEM((8, part, p1.shape[1]), low),
            pltpu.VMEM((3, 8, part, tile), low),
            pltpu.VMEM((3, 8, part, rest), low),
            pltpu.VMEM((2, rows, tile), low),
            pltpu.VMEM((3, rows, tile), low),
            pltpu.VMEM((3, rows, tile), low),
            pltpu.VMEM((2, rows, tile), low),
            pltpu.VMEM((rows, rest), low),
            pltpu.VMEM(g.shape, low),
            pltpu.VMEM((rows, tile), low),
            pltpu.VMEM((rows, tile), low),
            pltpu.VMEM((2, rows, tile), wide),
            pltpu.VMEM((rows, rest), wide),
            pltpu.VMEM((rows, tile), wide),
            pltpu.VMEM((128, tile), low),
            pltpu.VMEM((tile, 2 * rest), wide),
            pltpu.VMEM((3, 4, 2, part, tile), wide),
            pltpu.VMEM((4, 4, part, tile), wide),
            pltpu.VMEM((4, 2, part, tile), low),
            pltpu.VMEM((count, 2, part, tile), low),
            pltpu.VMEM((6, 2, part, tile), wide),
            pltpu.VMEM((4, part, tile), low),
            pltpu.VMEM((count, part, tile), low),
            pltpu.VMEM((6, part, tile), wide),
            pltpu.VMEM((4, part, tile), low),
            pltpu.VMEM((count, part, tile), low),
            pltpu.VMEM((4, part, tile), low),
            pltpu.VMEM((count, part, tile), low),
            pltpu.VMEM((2, part, tile), low),
            pltpu.VMEM((2, part, tile), low),
            pltpu.VMEM((count, part, tile), low),
            pltpu.VMEM((5, small_rows, tile), wide),
            pltpu.VMEM((5, small_rows, tile), wide),
            pltpu.VMEM((small_rows, tile), wide),
            pltpu.VMEM((8, 128), wide),
            pltpu.VMEM((8, 8, 128), wide),
            dma((9,)),
            dma((2,)),
            dma((3,)),
            dma((3,)),
            dma((3,)),
            dma((3,)),
            dma((3,)),
            dma((2,)),
            dma((4,)),
            dma((2,)),
            dma((3,)),
            dma((4,)),
            pltpu.SemaphoreType.REGULAR,
            dma((4,)),
            dma((count,)),
            dma((4,)),
            dma((count,)),
            dma((4,)),
            dma((count,)),
            dma((4,)),
            dma((count,)),
            dma((2,)),
            dma((2,)),
            dma((count,)),
            dma((count,)),
            dma((5,)),
            dma((5,)),
            dma((8,)),
            dma((8,)),
            dma((count,)),
        ],
        compiler_params=pltpu.CompilerParams(
            collective_id=1, has_side_effects=True, vmem_limit_bytes=63 * 1024 * 1024
        ),
        name="backward",
    )(w, a, slope, p0, p1, x2, g, small)


def adamw_kernel(
    plan, step_ref, result_ref, grad_ref, *refs,
):
    where, pieces, count = plan
    groups = [refs[3 * k : 3 * k + 3] for k in range(4)]
    outs = [refs[12 + 4 * k : 16 + 4 * k] for k in range(4)]
    held = [refs[28 + 3 * k : 31 + 3 * k] for k in range(4)]
    copies = refs[40:44]
    grads, first_g, fore_g, grad_sem, in_sem, out_sem = refs[44:]
    wide, low = jnp.float32, jnp.bfloat16
    clip = result_ref[2:3, 0:1]
    steps = jnp.full((1, 1), 1.0, wide) * step_ref[0].astype(wide)
    mean_fix = 1.0 / (1.0 - jnp.exp(steps * float(np.log(BETA_ONE))))
    square_fix = 1.0 / (1.0 - jnp.exp(steps * float(np.log(BETA_TWO))))
    tile = grads.shape[2]

    units = [(1, k) for k in range(0, 9, 3)] + [(2, 0), (2, 1), (3, None), (0, None)]

    def view(ref, group, lead):
        if lead is None:
            return ref
        return ref.at[lead : lead + 3] if group == 1 else ref.at[lead]

    loads = []
    for n, (group, lead) in enumerate(units):
        loads.append(
            [
                pltpu.make_async_copy(view(groups[group][k], group, lead), view(held[group][k], group, lead), in_sem.at[n, k])
                for k in range(3)
            ]
        )
    whole = pltpu.make_async_copy(grad_ref, grads, grad_sem)
    whole.start()
    for unit in loads:
        for copy in unit:
            copy.start()
    whole.wait()

    for key_group, target in (("first", first_g), ("fore", fore_g)):
        begin = 0
        for stack_id in range(3):
            done = 0
            width = pieces[stack_id, key_group][1]
            for t, start, size in where[stack_id, key_group]:
                size = min(size, width - done)
                if size > 0:
                    target[:, begin + done : begin + done + size] = grads[t, :, start : start + size].astype(wide)
                done += size
            begin += width

    def update(group, index, grad):
        weight, avg, square = (held[group][k][index] for k in range(3))
        grad = grad * clip
        new_avg = BETA_ONE * avg + (1.0 - BETA_ONE) * grad
        new_sq = BETA_TWO * square + (1.0 - BETA_TWO) * grad * grad
        step = (new_avg * mean_fix) / (jnp.sqrt(new_sq * square_fix) + EPSILON) + DECAY * weight
        new_weight = weight - RATE * step
        held[group][0][index] = new_weight
        held[group][1][index] = new_avg
        held[group][2][index] = new_sq
        copies[group][index] = new_weight.astype(low)

    def rows_of(body, rows=64, step=16):
        def go(k, carry):
            body(pl.ds(pl.multiple_of(k * step, step), step))
            return carry
        lax.fori_loop(0, rows // step, go, 0)

    part = grads.shape[1]
    stores = []
    for n, (group, lead) in enumerate(units):
        for copy in loads[n]:
            copy.wait()
        if group == 1:
            for k in range(lead, lead + 3):
                t = where[k // 3, k % 3][0][0]
                rows_of(lambda rows: update(1, (k, rows), grads[t, rows, :].astype(wide)), part)
        elif group == 2:
            spots = where[lead, "back"]
            length = held[2][0].shape[2]

            def tiles(rows):
                done = 0
                for t, start, size in spots:
                    size = min(size, length - done)
                    update(2, (lead, rows, slice(done, done + size)), grads[t, rows, start : start + size].astype(wide))
                    done += size
            rows_of(tiles, part)
        else:
            target = first_g if group == 0 else fore_g
            rows_of(lambda rows: update(group, (rows,), target[rows, :]), part)
        for k in range(3):
            stores.append(
                pltpu.make_async_copy(view(held[group][k], group, lead), view(outs[group][k], group, lead), out_sem.at[n, k])
            )
        stores.append(
            pltpu.make_async_copy(view(copies[group], group, lead), view(outs[group][3], group, lead), out_sem.at[n, 3])
        )
        for copy in stores[-4:]:
            copy.start()
    for copy in stores:
        copy.wait()


def adamw_all(step_count, result, grads, states, where, pieces):
    low, wide = jnp.bfloat16, jnp.float32
    hbm = pl.BlockSpec(memory_space=pltpu.HBM)
    shape = jax.ShapeDtypeStruct
    shapes = [state[0].shape for state in states]
    dma = pltpu.SemaphoreType.DMA
    return pl.pallas_call(
        functools.partial(adamw_kernel, (where, pieces, grads.shape[0])),
        out_shape=tuple(shape(s, kind) for s in shapes for kind in (wide, wide, wide, low)),
        in_specs=[pl.BlockSpec(memory_space=pltpu.SMEM), pl.BlockSpec(memory_space=pltpu.VMEM)] + [hbm] * 13,
        out_specs=(hbm,) * 16,
        scratch_shapes=[pltpu.VMEM(s, wide) for s in shapes for _ in range(3)]
        + [pltpu.VMEM(s, low) for s in shapes]
        + [
            pltpu.VMEM(grads.shape, low),
            pltpu.VMEM(shapes[0], wide),
            pltpu.VMEM(shapes[3], wide),
            dma,
            dma((7, 3)),
            dma((7, 4)),
        ],
        compiler_params=pltpu.CompilerParams(vmem_limit_bytes=60 * 1024 * 1024),
        name="adamw",
    )(step_count, result, grads, *[array for state in states for array in state])


def fast_body(
    devices,
    windows,
    targets,
    horizon,
    step_count,
    first_w,
    first_w_avg,
    first_w_sq,
    hidden_w,
    hidden_w_avg,
    hidden_w_sq,
    back_w,
    back_w_avg,
    back_w_sq,
    fore_w,
    fore_w_avg,
    fore_w_sq,
    bias_vec,
    bias_avg,
    bias_sq,
):
    length, steps_ahead_total, hidden_size = windows.shape[1], targets.shape[1], hidden_w.shape[-1]
    part = hidden_w.shape[2]
    pieces, total = packing(length, steps_ahead_total, hidden_size)
    rows, row_count = row_plan(length, steps_ahead_total, hidden_size)
    row_count = -(-row_count // 8) * 8
    where, count = chunk_plan(length, steps_ahead_total, hidden_size)
    spans = {}
    cursor = 0
    for key in bias_order(length, steps_ahead_total, hidden_size):
        spans[key] = cursor
        cursor += rows[key][1]
    bias_count = bias_vec.shape[0]
    flat_rows = -(-bias_count // (8 * hidden_size)) * 8
    flat = jnp.pad(bias_vec, (0, flat_rows * hidden_size - bias_count)).reshape(flat_rows, hidden_size)
    ups = np.zeros((256, tiled(steps_ahead_total)), np.float32)
    for stack_id in range(2):
        knots = steps_ahead_total // RATIOS[stack_id]
        ups[128 * stack_id : 128 * stack_id + knots, :steps_ahead_total] = blend_coefficients(steps_ahead_total, knots)
    up_high = ups.astype(jnp.bfloat16)
    up_low = (ups - up_high.astype(np.float32)).astype(jnp.bfloat16)
    scale = 2.0 ** -int(np.ceil(np.log2(devices * windows.shape[0] * steps_ahead_total)))

    def lead(array):
        return array.reshape((-1,) + array.shape[2:]) if array.ndim == 4 else array

    states = (
        (first_w.T, first_w_avg.T, first_w_sq.T),
        (lead(hidden_w), lead(hidden_w_avg), lead(hidden_w_sq)),
        (back_w, back_w_avg, back_w_sq),
        (fore_w, fore_w_avg, fore_w_sq),
    )
    w, a, slope, p0, p1, x2, g, small = forward(
        states[0][0], states[1][0], back_w, fore_w, windows, targets, horizon, flat,
        jnp.asarray(up_high), jnp.asarray(up_low), pieces, rows, spans, scale, total,
    )
    owned, _, flat_grad, result = backward(
        w, a, slope, p0, p1, x2, g, small, pieces, rows, spans, scale, row_count, flat_rows, count
    )
    new = adamw_all(step_count, result, owned, states, where, pieces)
    first_new, hidden_new, back_new, fore_new = (new[4 * k : 4 * k + 4] for k in range(4))
    grad_bias = flat_grad.reshape(-1)[:bias_count] * result[2, 0]
    bias_new = adamw(bias_vec, bias_avg, bias_sq, grad_bias, step_count[0].astype(jnp.float32))
    shape = hidden_w.shape
    first_new = [array.T for array in first_new]
    hidden_new = [array.reshape(shape) for array in hidden_new]
    flat_out = [result[1, 0], result[0, 0]]
    for weight, avg, square, _ in (first_new, hidden_new, back_new, fore_new):
        flat_out += [avg, square, weight]
    flat_out += list(bias_new)
    flat_out += [group[3] for group in (first_new, hidden_new, back_new, fore_new)]
    return tuple(flat_out)


def solution(mesh):
    fast = mesh.shape["fsdp"] == 8 and mesh.shape["dp"] == 4
    step = functools.partial(fast_body, mesh.shape["dp"] * mesh.shape["fsdp"]) if fast else body
    placed = (
        P(("dp", "fsdp"), None),
        P(("dp", "fsdp"), None),
        P(("dp", "fsdp")),
        P(),
        P(None, "fsdp"),
        P(None, "fsdp"),
        P(None, "fsdp"),
        P(None, None, "fsdp", None),
        P(None, None, "fsdp", None),
        P(None, None, "fsdp", None),
        P(None, "fsdp", None),
        P(None, "fsdp", None),
        P(None, "fsdp", None),
        P("fsdp", None),
        P("fsdp", None),
        P("fsdp", None),
        P(),
        P(),
        P(),
    )
    return jax.shard_map(
        step,
        mesh=mesh,
        in_specs=placed,
        out_specs=(
            P(),
            P(),
            P(None, "fsdp"),
            P(None, "fsdp"),
            P(None, "fsdp"),
            P(None, None, "fsdp", None),
            P(None, None, "fsdp", None),
            P(None, None, "fsdp", None),
            P(None, "fsdp", None),
            P(None, "fsdp", None),
            P(None, "fsdp", None),
            P("fsdp", None),
            P("fsdp", None),
            P("fsdp", None),
            P(),
            P(),
            P(),
            P(None, "fsdp"),
            P(None, None, "fsdp", None),
            P(None, "fsdp", None),
            P("fsdp", None),
        ),
        check_vma=False,
    )
```

```python
import functools
import jax
import jax.numpy as jnp
import numpy as np
from jax import lax
from jax.experimental import pallas as pl
from jax.experimental.pallas import tpu as pltpu
from jax.sharding import PartitionSpec as P

KERNELS = (8, 4, 1)
RATIOS = (24, 12, 1)
CLIP_MAX = 0.01
RATE = 0.02
BETA_ONE = 0.9
BETA_TWO = 0.999
EPSILON = 1e-08
DECAY = 0.01
DOT_EXACTNESS = lax.Precision.HIGHEST


def blend_coefficients(fine, coarse):
    column = np.arange(fine)
    numer = np.maximum((2 * column + 1) * coarse - fine, 0)
    lower_idx = numer // (2 * fine)
    frac = (numer - lower_idx * 2 * fine) / (2.0 * fine)
    upper_idx = np.minimum(lower_idx + 1, coarse - 1)
    matrix = np.zeros((coarse, fine), np.float32)
    matrix[lower_idx, column] += 1.0 - frac
    matrix[upper_idx, column] += frac
    return matrix


def normalize(windows, targets):
    center = jnp.mean(windows, axis=1, keepdims=True)
    spread = jnp.sqrt(jnp.mean((windows - center) ** 2, axis=1, keepdims=True) + 1e-05)
    return ((windows - center) / spread, (targets - center) / spread)


def mean_pool(values, kernel):
    if kernel == 1:
        return values
    return jnp.mean(values.reshape(values.shape[0], values.shape[1] // kernel, kernel), axis=2)


def pool_back(d_pooled, kernel):
    if kernel == 1:
        return d_pooled
    spread_out = jnp.broadcast_to((d_pooled / kernel)[:, :, None], d_pooled.shape + (kernel,))
    return spread_out.reshape(d_pooled.shape[0], d_pooled.shape[1] * kernel)


def silu_slope(pre_act):
    gate = jax.nn.sigmoid(pre_act)
    return gate * (1.0 + pre_act * (1.0 - gate))


def stack_params(stack_id, gathered, bias_vec, length, steps_ahead_total):
    first_full, hidden_full, back_full, fore_full = gathered
    hidden_size = hidden_full.shape[-1]
    row_start = sum((length // KERNELS[earlier] for earlier in range(stack_id)))
    col_start = sum((steps_ahead_total // RATIOS[earlier] for earlier in range(stack_id)))
    pooled_len = length // KERNELS[stack_id]
    anchor_entries = steps_ahead_total // RATIOS[stack_id]
    layers = [
        (
            first_full[row_start : row_start + pooled_len],
            bias_vec[stack_id * hidden_size : (stack_id + 1) * hidden_size],
        )
    ]
    for layer_id in range(3):
        offset = (3 + 3 * stack_id + layer_id) * hidden_size
        layers.append((hidden_full[stack_id, layer_id], bias_vec[offset : offset + hidden_size]))
    fore_start = 12 * hidden_size + 2 * length + col_start
    fore_pair = (
        fore_full[:, col_start : col_start + anchor_entries],
        bias_vec[fore_start : fore_start + anchor_entries],
    )
    back_pair = None
    if stack_id < 2:
        back_start = 12 * hidden_size + stack_id * length
        back_pair = (back_full[stack_id], bias_vec[back_start : back_start + length])
    linear_upsample_anchors = jnp.asarray(blend_coefficients(steps_ahead_total, anchor_entries))
    return (layers, fore_pair, back_pair, linear_upsample_anchors)


def stack_forward(residual, stack_id, layers, fore_pair, back_pair, linear_upsample_anchors):
    inputs_kept = [mean_pool(residual, KERNELS[stack_id]).astype(jnp.bfloat16)]
    pre_kept = []
    for weight, bias in layers:
        pre_act = jnp.dot(inputs_kept[-1], weight, preferred_element_type=jnp.float32) + bias
        pre_kept.append(pre_act)
        inputs_kept.append(jax.nn.silu(pre_act).astype(jnp.bfloat16))
    anchor_result = (
        jnp.dot(inputs_kept[-1], fore_pair[0], preferred_element_type=jnp.float32) + fore_pair[1]
    )
    running_subtotal = jnp.dot(anchor_result, linear_upsample_anchors, precision=DOT_EXACTNESS)
    backcast = None
    if back_pair is not None:
        backcast = (
            jnp.dot(inputs_kept[-1], back_pair[0], preferred_element_type=jnp.float32)
            + back_pair[1]
        )
    return ((inputs_kept, pre_kept), running_subtotal, backcast)


def head_grads(last_act, d_low, weight):
    grad_w = jnp.dot(last_act.T, d_low, preferred_element_type=jnp.float32)
    grad_b = jnp.sum(d_low.astype(jnp.float32), axis=0)
    return ((grad_w, grad_b), jnp.dot(d_low, weight.T, preferred_element_type=jnp.float32))


def stack_backward(kept, anchor_cotangent, d_backcast, layers, fore_pair, back_pair, need_input):
    inputs_kept, pre_kept = kept
    last_act = inputs_kept[-1]
    fore_grads, d_hidden = head_grads(last_act, anchor_cotangent.astype(jnp.bfloat16), fore_pair[0])
    back_grads = None
    if back_pair is not None:
        back_grads, d_extra = head_grads(last_act, d_backcast.astype(jnp.bfloat16), back_pair[0])
        d_hidden = d_hidden + d_extra
    layer_grads = [None, None, None, None]
    for layer_id in (3, 2, 1, 0):
        d_pre = (d_hidden * silu_slope(pre_kept[layer_id])).astype(jnp.bfloat16)
        layer_grads[layer_id] = (
            jnp.dot(inputs_kept[layer_id].T, d_pre, preferred_element_type=jnp.float32),
            jnp.sum(d_pre.astype(jnp.float32), axis=0),
        )
        if layer_id > 0 or need_input:
            d_hidden = jnp.dot(d_pre, layers[layer_id][0].T, preferred_element_type=jnp.float32)
    return (layer_grads, fore_grads, back_grads, d_hidden)


def adamw(weight, avg, square, grad, step_float):
    new_avg = BETA_ONE * avg + (1.0 - BETA_ONE) * grad
    new_sq = BETA_TWO * square + (1.0 - BETA_TWO) * grad * grad
    avg_hat = new_avg / (1.0 - BETA_ONE**step_float)
    sq_hat = new_sq / (1.0 - BETA_TWO**step_float)
    new_weight = weight - RATE * (avg_hat / (jnp.sqrt(sq_hat) + EPSILON) + DECAY * weight)
    return (new_avg, new_sq, new_weight)


def body(
    windows,
    targets,
    horizon,
    step_count,
    first_w,
    first_w_avg,
    first_w_sq,
    hidden_w,
    hidden_w_avg,
    hidden_w_sq,
    back_w,
    back_w_avg,
    back_w_sq,
    fore_w,
    fore_w_avg,
    fore_w_sq,
    bias_vec,
    bias_avg,
    bias_sq,
):
    length = windows.shape[1]
    steps_ahead_total = targets.shape[1]
    normed, observed_future = normalize(windows, targets)
    future_usable_flags = (
        jnp.arange(steps_ahead_total, dtype=jnp.int32)[None, :] < horizon[:, None]
    ).astype(jnp.float32)
    usable_tally = lax.psum(jnp.sum(horizon.astype(jnp.float32)), ("dp", "fsdp"))
    shards = (
        first_w.astype(jnp.bfloat16),
        hidden_w.astype(jnp.bfloat16),
        back_w.astype(jnp.bfloat16),
        fore_w.astype(jnp.bfloat16),
    )
    gathered = (
        lax.all_gather(shards[0], "fsdp", axis=1, tiled=True),
        lax.all_gather(shards[1], "fsdp", axis=2, tiled=True),
        lax.all_gather(shards[2], "fsdp", axis=1, tiled=True),
        lax.all_gather(shards[3], "fsdp", axis=0, tiled=True),
    )
    residual = normed
    kept_stacks = []
    predicted_future = jnp.zeros(observed_future.shape, jnp.float32)
    for stack_id in range(3):
        layers, fore_pair, back_pair, linear_upsample_anchors = stack_params(
            stack_id, gathered, bias_vec, length, steps_ahead_total
        )
        kept, running_subtotal, backcast = stack_forward(
            residual, stack_id, layers, fore_pair, back_pair, linear_upsample_anchors
        )
        kept_stacks.append(kept)
        predicted_future = predicted_future + running_subtotal
        if backcast is not None:
            residual = residual - backcast
    residual_difference = predicted_future - observed_future
    loss_part = (
        jnp.sum(future_usable_flags * residual_difference * residual_difference) / usable_tally
    )
    future_slope_cotangent = 2.0 * future_usable_flags * residual_difference / usable_tally
    again = (
        lax.all_gather(shards[0], "fsdp", axis=1, tiled=True),
        lax.all_gather(shards[1], "fsdp", axis=2, tiled=True),
        lax.all_gather(shards[2], "fsdp", axis=1, tiled=True),
        lax.all_gather(shards[3], "fsdp", axis=0, tiled=True),
    )
    results = [None, None, None]
    d_residual = None
    for stack_id in (2, 1, 0):
        layers, fore_pair, back_pair, linear_upsample_anchors = stack_params(
            stack_id, again, bias_vec, length, steps_ahead_total
        )
        anchor_cotangent = jnp.dot(
            future_slope_cotangent, linear_upsample_anchors.T, precision=DOT_EXACTNESS
        )
        d_backcast = None if d_residual is None else -d_residual
        results[stack_id] = stack_backward(
            kept_stacks[stack_id],
            anchor_cotangent,
            d_backcast,
            layers,
            fore_pair,
            back_pair,
            stack_id > 0,
        )
        if stack_id > 0:
            spread_back = pool_back(results[stack_id][3], KERNELS[stack_id])
            d_residual = spread_back if d_residual is None else d_residual + spread_back
    grad_first = jnp.concatenate([results[stack_id][0][0][0] for stack_id in range(3)], axis=0)
    grad_hidden = jnp.stack(
        [
            jnp.stack([results[stack_id][0][layer_id][0] for layer_id in (1, 2, 3)])
            for stack_id in range(3)
        ]
    )
    grad_back = jnp.stack([results[stack_id][2][0] for stack_id in range(2)])
    grad_fore = jnp.concatenate([results[stack_id][1][0] for stack_id in range(3)], axis=1)
    bias_pieces = [results[stack_id][0][0][1] for stack_id in range(3)]
    bias_pieces += [
        results[stack_id][0][layer_id][1] for stack_id in range(3) for layer_id in (1, 2, 3)
    ]
    bias_pieces += [results[stack_id][2][1] for stack_id in range(2)]
    bias_pieces += [results[stack_id][1][1] for stack_id in range(3)]
    grad_bias = jnp.concatenate(bias_pieces)
    owned = (
        lax.psum_scatter(grad_first, "fsdp", scatter_dimension=1, tiled=True),
        lax.psum_scatter(grad_hidden, "fsdp", scatter_dimension=2, tiled=True),
        lax.psum_scatter(grad_back, "fsdp", scatter_dimension=1, tiled=True),
        lax.psum_scatter(grad_fore, "fsdp", scatter_dimension=0, tiled=True),
    )
    owned = lax.psum((owned[0], owned[1], owned[2], owned[3]), "dp")
    grad_bias, loss = lax.psum((grad_bias, loss_part), ("dp", "fsdp"))
    local_sq = sum((jnp.sum(grad * grad) for grad in owned))
    total_sq = lax.psum(local_sq, "fsdp") + jnp.sum(grad_bias * grad_bias)
    grad_norm = jnp.sqrt(total_sq)
    clip_factor = jnp.minimum(1.0, CLIP_MAX / grad_norm)
    step_float = step_count[0].astype(jnp.float32)
    states = (
        (first_w, first_w_avg, first_w_sq),
        (hidden_w, hidden_w_avg, hidden_w_sq),
        (back_w, back_w_avg, back_w_sq),
        (fore_w, fore_w_avg, fore_w_sq),
        (bias_vec, bias_avg, bias_sq),
    )
    grads_all = (owned[0], owned[1], owned[2], owned[3], grad_bias)
    updated = []
    for state, grad in zip(states, grads_all):
        updated.append(adamw(state[0], state[1], state[2], grad * clip_factor, step_float))
    return (
        loss,
        grad_norm,
        updated[0][0],
        updated[0][1],
        updated[0][2],
        updated[1][0],
        updated[1][1],
        updated[1][2],
        updated[2][0],
        updated[2][1],
        updated[2][2],
        updated[3][0],
        updated[3][1],
        updated[3][2],
        updated[4][0],
        updated[4][1],
        updated[4][2],
        updated[0][2].astype(jnp.bfloat16),
        updated[1][2].astype(jnp.bfloat16),
        updated[2][2].astype(jnp.bfloat16),
        updated[3][2].astype(jnp.bfloat16),
    )


MESH = pl.DeviceIdType.MESH
CHUNK = 1024


def tiled(width):
    return -(-width // 128) * 128


def packing(length, steps_ahead_total, hidden_size):
    pieces = {}
    cursor = 0
    for stack_id in range(3):
        widths = [("first", length // KERNELS[stack_id])]
        widths += [(layer_id, hidden_size) for layer_id in range(3)]
        if stack_id < 2:
            widths.append(("back", length))
        widths.append(("fore", steps_ahead_total // RATIOS[stack_id]))
        for name, width in widths:
            pieces[stack_id, name] = (cursor, width)
            cursor += tiled(width)
    total = -(-cursor // CHUNK) * CHUNK
    return pieces, total


def pack(parts, pieces, total):
    out = []
    cursor = 0
    for key, (start, width) in pieces.items():
        part = parts[key]
        out.append(jnp.pad(part, ((0, 0), (0, tiled(width) - width))))
        cursor = start + tiled(width)
    rows, dtype = out[0].shape[0], out[0].dtype
    if total > cursor:
        out.append(jnp.zeros((rows, total - cursor), dtype))
    return jnp.concatenate(out, axis=1)


def places():
    row = lax.axis_index("dp")
    me = lax.axis_index("fsdp")
    core = me % 2
    across_x = (me // 2) % 2
    across_y = me // 4
    other = me + 1 - 2 * core
    over_x = me + 2 - 4 * across_x
    over_y = me + 4 - 8 * across_y
    return row, me, core, other, over_x, over_y


def remote(src, dst, send_sem, recv_sem, device):
    return pltpu.make_async_remote_copy(
        src_ref=src, dst_ref=dst, send_sem=send_sem, recv_sem=recv_sem, device_id=device, device_id_type=MESH
    )


HALF_LOW = 2


def row_plan(length, steps_ahead_total, hidden_size):
    rows = {}
    cursor = 0
    for stack_id in range(3):
        for name in ("first", 0, 1, 2):
            rows[stack_id, name] = (cursor, hidden_size)
            cursor += 1
    for stack_id in range(2):
        rows[stack_id, "back"] = (cursor, length)
        cursor += -(-length // hidden_size)
    for stack_id in range(3):
        width = steps_ahead_total // RATIOS[stack_id]
        rows[stack_id, "fore"] = (cursor, width)
        cursor += -(-width // hidden_size)
    return rows, cursor


def bias_order(length, steps_ahead_total, hidden_size):
    keys = [(stack_id, "first") for stack_id in range(3)]
    keys += [(stack_id, layer_id) for stack_id in range(3) for layer_id in range(3)]
    keys += [(stack_id, "back") for stack_id in range(2)]
    keys += [(stack_id, "fore") for stack_id in range(3)]
    return keys


def parts_low(value):
    high = value.astype(jnp.bfloat16)
    return high, (value - high.astype(jnp.float32)).astype(jnp.bfloat16)


NN = (((1,), (0,)), ((), ()))
NT = (((1,), (1,)), ((), ()))
TN = (((0,), (0,)), ((), ()))


def mul(left, right, dims=NN):
    return lax.dot_general(left, right, dims, preferred_element_type=jnp.float32)


def cut_classes(count):
    pattern = "eoeo" + "eob" * count
    return (pattern[: count - 2] + "bb")[:count]


def forward_kernel(
    plan,
    first_ref, hidden_ref, back_ref, fore_ref, windows_ref, targets_ref, horizon_ref, flat_ref, up_high_ref, up_low_ref,
    w_out, a_out, slope_out, p0_out, p1_out, x2_out, g_out, small_ref,
    w, x, stage, a, slope, p0, p1, x2, fc, tt, g, dk, center_s, scale_s, pool8, pool4,
    bias_ref, horizon_s, first_s, hidden_s, back_s, fore_s,
    raw_sem, send_sem, recv_sem, win_sem, tt_sem, out_sem, w_sem,
):
    pieces, bias_rows, spans, cut_width, count, scale = plan
    row, me, core, other, over_x, over_y = places()
    diag = over_x + over_y - me
    total_rows = windows_ref.shape[0]
    length = windows_ref.shape[1]
    hidden_size = a.shape[-1]
    steps_ahead = targets_ref.shape[0]
    block = total_rows // 2
    wide, low = jnp.float32, jnp.bfloat16
    wide_length = x.shape[1]
    tiles = [(k, min(hidden_size, wide_length - k)) for k in range(0, wide_length, hidden_size)]
    whole = wide_length // 128 * 128 - 128

    barrier = pltpu.get_barrier_semaphore()
    for peer in (other, over_x, over_y):
        pl.semaphore_signal(barrier, inc=1, device_id=(row, peer), device_id_type=MESH)
    pl.semaphore_signal(barrier, inc=1, device_id=(row + 1 - 2 * (row % 2), me), device_id_type=MESH)

    classes = cut_classes(count)
    turn_of = [classes[:cut].count(classes[cut]) % 2 for cut in range(count)]
    even_plane = row % 2 == 0
    z_pair = row + 1 - 2 * (row % 2)

    def copy_of(kind, cut, src, holder, device):
        cols = slice(cut * cut_width, (cut + 1) * cut_width)
        return remote(src.at[:, cols], w.at[holder, :, cols], send_sem.at[kind, cut], recv_sem.at[kind, cut], device)

    def to_x(cut):
        return copy_of(0, cut, w.at[me], me, (row, over_x))

    def to_y(cut):
        return copy_of(1, cut, w.at[me], me, (row, over_y))

    def onward(cut):
        if turn_of[cut] == 0:
            return copy_of(2, cut, w.at[over_x], over_x, (row, over_y))
        return copy_of(2, cut, w.at[over_y], over_y, (row, over_x))

    def to_core(kind, cut):
        holder = (me, over_x, over_y, diag)[kind]
        return copy_of(3 + kind, cut, w.at[holder], holder, (row, other))

    def to_z(kind, cut):
        holder = (None, over_x, over_y, diag)[kind]
        return copy_of(6 + kind, cut, w.at[holder], holder, (z_pair, me))

    def gathers(cut, body):
        if classes[cut] == "b":
            body()
        else:
            pl.when(even_plane if classes[cut] == "e" else jnp.logical_not(even_plane))(body)

    def receives(cut, body):
        if classes[cut] != "b":
            pl.when(jnp.logical_not(even_plane) if classes[cut] == "e" else even_plane)(body)

    def own_sends(cut):
        def body():
            to_x(cut).start()
            to_y(cut).start()
        gathers(cut, body)
        to_core(0, cut).start()

    def w_copy(cut):
        cols = slice(cut * cut_width, (cut + 1) * cut_width)
        return pltpu.make_async_copy(w.at[:, :, cols], w_out.at[:, :, cols], w_sem.at[cut])

    look, lag_diag, lag_z = 6, 2, 6
    arrived = set()

    def pump(cut):
        if cut < count:
            def body():
                to_x(cut).wait_recv()
                if turn_of[cut] == 0:
                    onward(cut).start()
                if classes[cut] != "b":
                    to_z(1, cut).start()
                to_core(1, cut).start()
                to_y(cut).wait_recv()
                if turn_of[cut] == 1:
                    onward(cut).start()
                if classes[cut] != "b":
                    to_z(2, cut).start()
                to_core(2, cut).start()
            gathers(cut, body)
            if cut + look < count:
                own_sends(cut + look)
        past = cut - lag_diag
        if 0 <= past < count:
            def body():
                onward(past).wait_recv()
                if classes[past] != "b":
                    to_z(3, past).start()
                to_core(3, past).start()
            gathers(past, body)
        gone = cut - lag_z
        if 0 <= gone < count:
            def body():
                for kind in (1, 2, 3):
                    to_z(kind, gone).wait_recv()
                    to_core(kind, gone).start()
            receives(gone, body)
        for done in range(count):
            if done not in arrived and cut - done >= (lag_diag + 1 if classes[done] == "b" else lag_z + 1):
                for kind in range(4):
                    to_core(kind, done).wait_recv()
                w_copy(done).start()
                arrived.add(done)

    tasks = []

    def task(need, cost):
        def keep(body):
            tasks.append((need, cost, body))
            return body
        return keep

    def cut_of(key):
        start, width = pieces[key]
        return (start + tiled(width) - 1) // cut_width

    def weights(key, start=0, width=None):
        at, full_width = pieces[key]
        width = tiled(full_width) if width is None else width
        return w[:, :, at + start : at + start + width].reshape(hidden_size, width)

    def bias(key, start=0, width=None):
        at, full_width = bias_rows[key]
        width = hidden_size if width is None else width
        return bias_ref[at + start // hidden_size : at + start // hidden_size + 1, 0:width]

    def over_rows(body):
        def step(k, carry):
            body(pl.ds(pl.multiple_of(k * block, block), block))
            return carry
        lax.fori_loop(0, 2, step, 0)

    def outgoing(src, dst, slot):
        return pltpu.make_async_copy(src, dst, out_sem.at[slot])

    slots = stage.shape[0]
    strip = stage.shape[1]
    strips = total_rows // strip

    def window_copy(k):
        rows = pl.ds(pl.multiple_of(k * strip, strip), strip)
        return pltpu.make_async_copy(windows_ref.at[rows], stage.at[k % slots], win_sem.at[k % slots])

    raw = [
        pltpu.make_async_copy(src, dst, raw_sem.at[k])
        for k, (src, dst) in enumerate(
            ((first_ref, first_s), (hidden_ref, hidden_s), (back_ref, back_s), (fore_ref, fore_s))
        )
    ]
    for copy in raw:
        copy.start()
    for k in range(slots):
        window_copy(k).start()
    targets_copy = pltpu.make_async_copy(targets_ref, tt.at[0:steps_ahead], tt_sem)
    targets_copy.start()

    def pack_piece(key, value):
        start, width = pieces[key]
        if width % 128:
            edge = start + width // 128 * 128
            w[me, :, edge : edge + 128] = jnp.zeros((value.shape[0], 128), low)
        w[me, :, start : start + width] = value.astype(low)

    def pack_stack(stack_id):
        width = pieces[stack_id, "first"][1]
        begin = sum(pieces[earlier, "first"][1] for earlier in range(stack_id))
        pack_piece((stack_id, "first"), first_s[:, begin : begin + width])
        for layer_id in range(3):
            pack_piece((stack_id, layer_id), hidden_s[3 * stack_id + layer_id])
        if stack_id < 2:
            pack_piece((stack_id, "back"), back_s[stack_id])
        width = pieces[stack_id, "fore"][1]
        begin = sum(pieces[earlier, "fore"][1] for earlier in range(stack_id))
        pack_piece((stack_id, "fore"), fore_s[:, begin : begin + width])

    raw[0].wait()
    raw[1].wait()
    raw[2].wait()
    raw[3].wait()
    pack_stack(0)
    pl.semaphore_wait(barrier, 4)
    early = min(look, pieces[1, "first"][0] // cut_width)
    for cut in range(early):
        own_sends(cut)
    pack_stack(1)
    pack_stack(2)
    packed = max(start + tiled(width) for start, width in pieces.values())
    if packed < w.shape[2]:
        w[me, :, packed:] = jnp.zeros((w.shape[1], w.shape[2] - packed), low)
    for cut in range(early, look):
        own_sends(cut)
    bias_ref[...] = jnp.zeros_like(bias_ref)
    for key, (at, width) in bias_rows.items():
        for k in range(0, width, hidden_size):
            flat = spans[key] + k
            todo = min(hidden_size, width - k)
            r, o = flat // hidden_size, flat % hidden_size
            here = min(todo, hidden_size - o)
            bias_ref[at + k // hidden_size : at + k // hidden_size + 1, 0:here] = flat_ref[r : r + 1, o : o + here]
            if here < todo:
                bias_ref[at + k // hidden_size : at + k // hidden_size + 1, here:todo] = flat_ref[r + 1 : r + 2, 0 : todo - here]

    @task(-1, 1.0)
    def _():
        ids = lax.broadcasted_iota(jnp.int32, pool8.shape, 0)
        col = lax.broadcasted_iota(jnp.int32, pool8.shape, 1) * KERNELS[0]
        pool8[...] = jnp.where((ids >= col) & (ids < col + KERNELS[0]), 1.0 / KERNELS[0], 0.0).astype(low)
        ids = lax.broadcasted_iota(jnp.int32, pool4.shape, 0)
        col = lax.broadcasted_iota(jnp.int32, pool4.shape, 1) * KERNELS[1]
        pool4[...] = jnp.where((ids >= col) & (ids < col + KERNELS[1]), 1.0 / KERNELS[1], 0.0).astype(low)
        x[:, whole:] = jnp.zeros((total_rows, wide_length - whole), wide)

    groups = 3
    for group in range(groups):
        @task(-1, 3.0)
        def _(group=group):
            def step(k, carry):
                window_copy(k).wait()
                rows = pl.ds(pl.multiple_of(k * strip, strip), strip)
                value = stage[k % slots]
                center = jnp.sum(value, axis=1, keepdims=True) * (1.0 / length)
                value = value - center
                spread = jnp.sqrt(jnp.sum(value * value, axis=1, keepdims=True) * (1.0 / length) + 1e-05)
                factor = 1.0 / spread
                center_s[rows, :] = center
                scale_s[rows, :] = factor
                value = value * factor
                x[rows, 0:length] = value

                @pl.when(k + slots < strips)
                def _():
                    window_copy(k + slots).start()
                return carry
            lax.fori_loop(group * strips // groups, (group + 1) * strips // groups, step, 0)

    @task(-1, 3.0)
    def _():
        def body(rows):
            for k in range(0, wide_length, 1024):
                width = min(1024, wide_length - k)
                high, rest = parts_low(x[rows, k : k + width])
                pooled = mul(high, pool8[0:width]) + mul(rest, pool8[0:width])
                p0[rows, k // 8 : k // 8 + 128] = pooled.astype(low)
        over_rows(body)
        outgoing(p0, p0_out, 0).start()

    def activate(z, stack_id, j, rows):
        gate = jax.nn.sigmoid(z)
        act = z * gate
        a[j, rows, :] = act.astype(low)
        slope[j % 2, rows, :] = (gate + act * (1.0 - gate)).astype(low)

    def a_copy(stack_id, j):
        return outgoing(a.at[j], a_out.at[stack_id, j], 8 + j)

    def slope_copy(stack_id, j):
        return outgoing(slope.at[j % 2], slope_out.at[stack_id, j], 12 + j % 2)

    def send_layer(stack_id, j):
        a_copy(stack_id, j).start()
        slope_copy(stack_id, j).start()

    def settle_layer(stack_id, j):
        if stack_id > 0:
            a_copy(stack_id - 1, j).wait()
        n = 4 * stack_id + j - 2
        if n >= 0:
            slope_copy(n // 4, n % 4).wait()

    for stack_id in range(3):
        inputs = (p0, p1, x2)[stack_id]

        @task(cut_of((stack_id, "first")), (1.3, 2.2, 6.0)[stack_id])
        def _(stack_id=stack_id, inputs=inputs):
            settle_layer(stack_id, 0)

            def body(rows):
                z = mul(inputs[rows, :], weights((stack_id, "first")), NT) + bias((stack_id, "first"))
                activate(z, stack_id, 0, rows)
            over_rows(body)
            send_layer(stack_id, 0)

        for layer_id in range(3):
            @task(cut_of((stack_id, layer_id)), 1.3)
            def _(stack_id=stack_id, layer_id=layer_id):
                settle_layer(stack_id, layer_id + 1)

                def body(rows):
                    z = mul(a[layer_id, rows, :], weights((stack_id, layer_id))) + bias((stack_id, layer_id))
                    activate(z, stack_id, layer_id + 1, rows)
                over_rows(body)
                send_layer(stack_id, layer_id + 1)

        if stack_id < 2:
            for start, width in tiles:
                need = (pieces[stack_id, "back"][0] + start + width - 1) // cut_width

                @task(need, 1.4 if stack_id else 1.7)
                def _(stack_id=stack_id, start=start, width=width):
                    def body(rows):
                        cols = slice(start, start + width)
                        head = mul(a[3, rows, :], weights((stack_id, "back"), start, width))
                        rest = x[rows, cols] - (head + bias((stack_id, "back"), start, width))
                        if stack_id == 0:
                            x[rows, cols] = rest
                            high, tail = parts_low(rest)
                            pooled = mul(high, pool4[0:width]) + mul(tail, pool4[0:width])
                            p1[rows, start // 4 : start // 4 + 128] = pooled.astype(low)
                        else:
                            x2[rows, cols] = rest.astype(low)
                    over_rows(body)
                    if start + width == wide_length:
                        if stack_id == 0:
                            outgoing(p1, p1_out, 1).start()
                        else:
                            outgoing(x2, x2_out, 2).start()

            @task(cut_of((stack_id, "fore")), 1.5)
            def _(stack_id=stack_id):
                def body(rows):
                    knots = mul(a[3, rows, :], weights((stack_id, "fore"))) + bias((stack_id, "fore"), 0, 128)
                    high, rest = parts_low(knots)
                    ups = slice(128 * stack_id, 128 * stack_id + 128)
                    part = (
                        mul(high, up_high_ref[ups, :]) + mul(rest, up_high_ref[ups, :]) + mul(high, up_low_ref[ups, :])
                    )
                    fc[rows, :] = part if stack_id == 0 else fc[rows, :] + part
                over_rows(body)

    wide_steps = fc.shape[1]
    for start in range(0, wide_steps, 256):
        @task(cut_of((2, "fore")), 2.5)
        def _(start=start):
            if start == 0:
                targets_copy.wait()
                small_ref[...] = jnp.zeros_like(small_ref)
                lines = horizon_ref[...].astype(wide)
                small_ref[2:3, 0:128] = jnp.broadcast_to(jnp.sum(lines, axis=1, keepdims=True), (1, 128))
                horizon_s[...] = jnp.broadcast_to(lines, (8, total_rows)).T
            cols = slice(start, start + 256)
            head = mul(a[3], weights((2, "fore"), start, 256)) + bias_ref[
                bias_rows[2, "fore"][0] + start // hidden_size : bias_rows[2, "fore"][0] + start // hidden_size + 1,
                start % hidden_size : start % hidden_size + 256,
            ]
            goal = jnp.concatenate([tt[start : start + 128, :].T, tt[start + 128 : start + 256, :].T], axis=1)
            goal = (goal - center_s[...]) * scale_s[...]
            step = lax.broadcasted_iota(jnp.int32, (total_rows, 256), 1) + start
            diff = jnp.where(step.astype(wide) < horizon_s[:, 0:1], fc[:, cols] + head - goal, 0.0)
            losses = jnp.sum(diff * diff, axis=0, keepdims=True)
            r = start // hidden_size
            small_ref[r : r + 1, start % hidden_size : start % hidden_size + 256] = losses
            diff = diff * (2.0 * scale)
            high, rest = parts_low(diff)
            g[:, cols] = high
            back = (
                mul(high, up_high_ref[:, cols], NT) + mul(rest, up_high_ref[:, cols], NT) + mul(high, up_low_ref[:, cols], NT)
            )
            dk[...] = back if start == 0 else dk[...] + back
            if start + 256 == wide_steps:
                g[:, wide_steps : wide_steps + 256] = dk[...].astype(low)
                outgoing(g, g_out, 3).start()

    queue = list(tasks)
    last = count + lag_z
    for cut in range(-1, last + 1):
        if cut >= 0:
            pump(cut)
        ready = min((done for done in range(count) if done not in arrived), default=count) - 1
        spent = 0.0
        while queue and queue[0][0] <= ready and (spent < 2.0 or cut == last):
            _, cost, body = queue.pop(0)
            body()
            spent += cost
    for cut in range(count):
        def body():
            to_x(cut).wait_send()
            to_y(cut).wait_send()
            onward(cut).wait_send()
            if classes[cut] != "b":
                for kind in (1, 2, 3):
                    to_z(kind, cut).wait_send()
        gathers(cut, body)
        for kind in range(4):
            to_core(kind, cut).wait_send()
        w_copy(cut).wait()
    outgoing(p0, p0_out, 0).wait()
    outgoing(p1, p1_out, 1).wait()
    outgoing(x2, x2_out, 2).wait()
    outgoing(g, g_out, 3).wait()
    for j in range(4):
        a_copy(2, j).wait()
    for j in (2, 3):
        slope_copy(2, j).wait()


def forward(first, hidden, back, fore, windows, targets, horizon, flat, up_high, up_low, pieces, bias_rows, spans, scale, total):
    low, wide = jnp.bfloat16, jnp.float32
    rows, length = windows.shape
    part, hidden_size = hidden.shape[1:]
    count = total // CHUNK
    wide_length = tiled(length)
    wide_steps = up_high.shape[1]
    p0_width, p1_width = tiled(length // KERNELS[0]), tiled(wide_length // KERNELS[1])
    row_count = -(-max(at - (-width // hidden_size) for at, width in bias_rows.values()) // 8) * 8
    strip = rows // 36
    hbm = pl.BlockSpec(memory_space=pltpu.HBM)
    vmem = pl.BlockSpec(memory_space=pltpu.VMEM)
    dma = pltpu.SemaphoreType.DMA
    shape = jax.ShapeDtypeStruct
    return pl.pallas_call(
        functools.partial(forward_kernel, (pieces, bias_rows, spans, CHUNK, count, scale)),
        out_shape=(
            shape((8, part, total), low),
            shape((3, 4, rows, hidden_size), low),
            shape((3, 4, rows, hidden_size), low),
            shape((rows, p0_width), low),
            shape((rows, p1_width), low),
            shape((rows, wide_length), low),
            shape((rows, wide_steps + 256), low),
            shape((8, hidden_size), wide),
        ),
        in_specs=[hbm] * 6 + [vmem] * 4,
        out_specs=(hbm,) * 7 + (vmem,),
        scratch_shapes=[
            pltpu.VMEM((8, part, total), low),
            pltpu.VMEM((rows, wide_length), wide),
            pltpu.VMEM((3, strip, length), wide),
            pltpu.VMEM((4, rows, hidden_size), low),
            pltpu.VMEM((2, rows, hidden_size), low),
            pltpu.VMEM((rows, p0_width), low),
            pltpu.VMEM((rows, p1_width), low),
            pltpu.VMEM((rows, wide_length), low),
            pltpu.VMEM((rows, wide_steps), wide),
            pltpu.VMEM((wide_steps, rows), wide),
            pltpu.VMEM((rows, wide_steps + 256), low),
            pltpu.VMEM((rows, 256), wide),
            pltpu.VMEM((rows, 1), wide),
            pltpu.VMEM((rows, 1), wide),
            pltpu.VMEM((1024, 128), low),
            pltpu.VMEM((512, 128), low),
            pltpu.VMEM((row_count, hidden_size), wide),
            pltpu.VMEM((rows, 8), wide),
            pltpu.VMEM(first.shape, wide),
            pltpu.VMEM(hidden.shape, wide),
            pltpu.VMEM(back.shape, wide),
            pltpu.VMEM(fore.shape, wide),
            dma((4,)),
            dma((10, count)),
            dma((10, count)),
            dma((3,)),
            dma,
            dma((16,)),
            dma((count,)),
        ],
        compiler_params=pltpu.CompilerParams(
            collective_id=0, has_side_effects=True, vmem_limit_bytes=63 * 1024 * 1024
        ),
        name="forward",
    )(first, hidden, back, fore, windows, targets.T, horizon.reshape(1, rows), flat, up_high, up_low)


def chunk_plan(length, steps_ahead_total, hidden_size):
    where = {}
    tile = hidden_size
    full, rest = tiled(length) // tile, tiled(length) % tile
    steps = tiled(steps_ahead_total)
    where[2, "fore"] = [(0, 0, tile), (1, 0, steps - tile)]
    where[1, "fore"] = [(1, steps - tile, 128)]
    for i in range(3):
        where[2, 2 - i] = [(2 + i, 0, tile)]
    t = 5
    last = t + 2 * full + 3 + 2 + full
    where[2, "first"] = [(t + 2 * k, 0, tile) for k in range(full)] + [(last, 0, rest)]
    where[1, "back"] = [(t + 2 * k + 1, 0, tile) for k in range(full)] + [(last, rest, rest)]
    t += 2 * full
    for i in range(3):
        where[1, 2 - i] = [(t + i, 0, tile)]
    where[1, "first"] = [(t + 3, 0, tile), (t + 4, 0, tile)]
    t += 5
    where[0, "back"] = [(t + k, 0, tile) for k in range(full)] + [(last, 2 * rest, rest)]
    where[0, "fore"] = [(last, 3 * rest, 128)]
    for i in range(3):
        where[0, 2 - i] = [(last + 1 + i, 0, tile)]
    where[0, "first"] = [(last + 4, 0, tile)]
    return where, last + 5


LAGS = (1, 4, 7, 9, 11, 13)


def backward_kernel(
    plan,
    w_ref, a_ref, slope_ref, p0_ref, p1_ref, x2_ref, g_ref, forward_small_ref,
    out_ref, dx_ref, flat_ref, result_ref,
    wh, wf2, wf, w1, wtile, wtail, a4, ah, sl, ytile, x2tail, g, dz, gb, dxb, dxt, da, spread, hold,
    gbuf, from_core, s1, r1, keep, s2, r2, plane, zs, zr, zp_s, zp_r, zl_s, zl_r, final,
    small_s, small_r, small_sum, square_s, square_r,
    wh_sem, wf_sem, wtile_sem, wtail_sem, a4_sem, ah_sem, sl_sem, y_sem, misc_sem, dx_sem,
    core_ss, core_rs, credit, ss1, rs1, ss2, rs2, zss, zrs, pss, prs, lss, lrs, fss, frs, small_ss, small_rs, sq_ss, sq_rs, out_sem,
):
    pieces, bias_rows, spans, scale, count, full = plan
    row, me, core, other, over_x, over_y = places()
    lane = core
    chip, chip_x, chip_y = me // 2, over_x // 2, over_y // 2
    chip_d = chip_x + chip_y - chip
    wide, low = jnp.float32, jnp.bfloat16
    total_rows = a_ref.shape[2]
    tile = a_ref.shape[3]
    rest = x2tail.shape[1]
    upper = row // 2
    z_in = row + 1 - 2 * upper
    is_edge = (row == 0) | (row == 3)
    z_out = (row + 3 + 2 * upper) % 4
    t_hidden1 = 5 + 2 * full
    t_first1 = t_hidden1 + 3
    t_back0 = t_first1 + 2
    t_tail0 = t_back0 + full

    barrier = pltpu.get_barrier_semaphore()
    for peer in range(1, 8):
        pl.semaphore_signal(barrier, inc=1, device_id=(row, (me + peer) % 8), device_id_type=MESH)
    for peer in range(1, 4):
        pl.semaphore_signal(barrier, inc=1, device_id=((row + peer) % 4, me), device_id_type=MESH)

    def local(src, dst, sem):
        return pltpu.make_async_copy(src, dst, sem)

    def w_cols(start, width):
        return w_ref.at[:, :, pl.ds(start, width)]

    def load_g():
        return local(g_ref, g, misc_sem.at[0])

    def load_x2tail():
        return local(x2_ref.at[:, full * tile : full * tile + rest], x2tail, misc_sem.at[1])

    def load_w1():
        return local(w_cols(pieces[1, "first"][0], w1.shape[2]), w1, misc_sem.at[2])

    def load_wf2():
        return local(w_cols(pieces[2, "fore"][0], wf2.shape[2]), wf2, misc_sem.at[3])

    def load_wf(stack_id):
        return local(w_cols(pieces[stack_id, "fore"][0], 128), wf.at[stack_id], wf_sem.at[stack_id])

    tails = ((2, "first"), (1, "back"), (0, "back"))

    def load_wtail(k):
        return local(w_cols(pieces[tails[k]][0] + full * tile, rest), wtail.at[k], wtail_sem.at[k])

    def load_a4(stack_id):
        return local(a_ref.at[stack_id, 3], a4.at[stack_id % 2], a4_sem.at[stack_id])

    def load_wh(i):
        return local(w_cols(pieces[2 - i // 3, 2 - i % 3][0], tile), wh.at[i], wh_sem.at[i])

    def wait_wh(i):
        local(w_cols(0, tile), wh.at[i], wh_sem.at[i]).wait()

    def load_ah(i):
        return local(a_ref.at[2 - i // 3, 2 - i % 3], ah.at[i % 3], ah_sem.at[i % 3])

    def load_sl(q):
        return local(slope_ref.at[2 - q // 4, 3 - q % 4], sl.at[q % 3], sl_sem.at[q % 3])

    def start_y(n):
        @pl.when(n < full)
        def _():
            cols = pl.ds(pl.multiple_of(n * tile, tile), tile)
            local(x2_ref.at[:, cols], ytile.at[n % 2], y_sem.at[n % 2]).start()

        @pl.when((n >= full) & (n < full + 2))
        def _():
            cols = pl.ds(pl.multiple_of((n - full) * tile, tile), tile)
            local(p1_ref.at[:, cols], ytile.at[n % 2], y_sem.at[n % 2]).start()

        @pl.when(n == full + 2)
        def _():
            local(p0_ref, ytile.at[n % 2], y_sem.at[n % 2]).start()

    def wait_y(n):
        local(p0_ref, ytile.at[n % 2], y_sem.at[n % 2]).wait()

    def start_wtile(m):
        def go(key, k):
            cols = pl.multiple_of(pieces[key][0] + k * tile, 128)
            local(w_cols(cols, tile), wtile.at[m % 3], wtile_sem.at[m % 3]).start()

        @pl.when((m < 2 * full) & (m % 2 == 0))
        def _():
            go((2, "first"), m // 2)

        @pl.when((m < 2 * full) & (m % 2 == 1))
        def _():
            go((1, "back"), m // 2)

        @pl.when((m >= 2 * full) & (m < 3 * full))
        def _():
            go((0, "back"), m - 2 * full)

    def wait_wtile(m):
        local(w_cols(0, tile), wtile.at[m % 3], wtile_sem.at[m % 3]).wait()

    def dx_cols(k):
        return dx_ref.at[:, pl.ds(pl.multiple_of(k * tile, tile), tile)]

    def dx_store(k):
        return local(dxb.at[k % 2], dx_cols(k), dx_sem.at[k % 2])

    def dx_load(k):
        return local(dx_cols(k), dxb.at[k % 2], dx_sem.at[k % 2])

    load_g().start()
    load_a4(2).start()
    load_wf2().start()
    for q in range(3):
        load_sl(q).start()
        load_ah(q).start()
        load_wh(q).start()
    for n in range(2):
        start_y(jnp.int32(n))
    for m in range(3):
        start_wtile(jnp.int32(m))
    load_a4(1).start()
    load_x2tail().start()
    for k in range(3):
        load_wtail(k).start()
    load_wf(1).start()
    load_wf(0).start()
    load_w1().start()
    for i in range(3, 9):
        load_wh(i).start()

    def core_copy(t):
        return remote(gbuf.at[t % 3, :, 1 - lane], from_core.at[t % 4], core_ss.at[t % 3], core_rs.at[t % 4], (row, other))

    def first_to(t):
        peer = over_x + t % 2 * (over_y - over_x)
        return remote(s1.at[t % 4], r1.at[t], ss1.at[t % 4], rs1.at[t], (row, peer))

    def second_to(t):
        peer = over_y + t % 2 * (over_x - over_y)
        return remote(s2.at[t % 4], r2.at[t], ss2.at[t % 4], rs2.at[t], (row, peer))

    def z_all(t):
        return remote(zs.at[t % 4], zr.at[t], zss.at[t % 4], zrs.at[t], (z_in, me))

    def z_swap(t):
        return remote(zp_s.at[t % 4], zp_r.at[t], pss.at[t % 4], prs.at[t], (z_in, me))

    def z_low(t):
        return remote(zl_s.at[t % 2], zl_r.at[t % 2], lss.at[t % 2], lrs.at[t % 2], (z_in, me))

    def precise(t):
        return t < 2

    def save_low(t, total, high):
        zl_s[t % 2] = (total - high.astype(wide)).astype(low)

    def z_final(t):
        return remote(final.at[t], final.at[t], fss.at[t], frs.at[t], (z_out, me))

    def emit(t):
        @pl.when(t >= 4)
        def _():
            pl.semaphore_wait(credit, 1)
        core_copy(t).start()

    def guarded(sure, condition, body):
        if sure:
            body()
        else:
            pl.when(condition)(body)

    def stage_one(t, sure):
        core_copy(t).wait_recv()
        guarded(sure, t >= 4, lambda: first_to(t - 4).wait_send())
        odd = t % 2
        for k, c in enumerate((chip_x + odd * (chip_y - chip_x), chip_d)):
            s1[t % 4, k] = (gbuf[t % 3, c, lane] + from_core[t % 4, c]).astype(low)
        first_to(t).start()
        for k, c in enumerate((chip, chip_y + odd * (chip_x - chip_y))):
            keep[t % 8, k] = gbuf[t % 3, c, lane] + from_core[t % 4, c]
        guarded(
            sure,
            t + 4 < count,
            lambda: pl.semaphore_signal(credit, inc=1, device_id=(row, other), device_id_type=MESH),
        )

    def stage_two(t, sure):
        first_to(t).wait_recv()
        guarded(sure, t >= 4, lambda: second_to(t - 4).wait_send())
        s2[t % 4] = (keep[t % 8, 1] + r1[t, 1].astype(wide)).astype(low)
        second_to(t).start()

    def stage_three(t, sure):
        second_to(t).wait_recv()
        plane[t % 6] = keep[t % 8, 0] + r1[t, 0].astype(wide) + r2[t].astype(wide)

    def outer_send(t, sure):
        guarded(sure, t >= 4, lambda: z_all(t - 4).wait_send())
        zs[t % 4] = plane[t % 6].astype(low)
        z_all(t).start()

    def inner_swap(t, sure):
        z_all(t).wait_recv()
        guarded(sure, t >= 4, lambda: z_swap(t - 4).wait_send())
        total = plane[t % 6] + zr[t].astype(wide)
        high = total.astype(low)
        zp_s[t % 4] = high
        pl.when(precise(t))(lambda: save_low(t, total, high))
        z_swap(t).start()
        pl.when(precise(t))(lambda: z_low(t).start())

    def inner_total(t, sure):
        z_swap(t).wait_recv()

        @pl.when(precise(t))
        def _():
            z_low(t).wait_recv()
            here = zp_s[t % 4].astype(wide) + zl_s[t % 2].astype(wide)
            there = zp_r[t].astype(wide) + zl_r[t % 2].astype(wide)
            final[t] = (here + there).astype(low)

        @pl.when(jnp.logical_not(precise(t)))
        def _():
            final[t] = (zp_s[t % 4].astype(wide) + zp_r[t].astype(wide)).astype(low)
        z_final(t).start()

    def outer_total(t, sure):
        z_final(t).wait_recv()

    def stage_last(t, sure):
        local(final.at[t], out_ref.at[t], out_sem.at[t]).start()
        got = final[t].astype(wide)
        got = got * got
        acc = square_s[...]
        for k in range(0, got.shape[0], 8):
            for j in range(0, tile, 128):
                acc = acc + got[k : k + 8, j : j + 128]
        square_s[...] = acc

    def reduce_turn(t, sure):
        def at(lag, stage):
            guarded(sure, (t >= lag) & (t < count + lag), lambda: stage(t - lag, sure))
        at(LAGS[0], stage_one)
        at(LAGS[1], stage_two)
        at(LAGS[2], stage_three)

        @pl.when(is_edge)
        def _():
            at(LAGS[2], outer_send)
            at(LAGS[5], outer_total)

        @pl.when(jnp.logical_not(is_edge))
        def _():
            at(LAGS[3], inner_swap)
            at(LAGS[4], inner_total)
        at(LAGS[5], stage_last)

    def over_rows(body):
        body(slice(None), 0)

    def add_row(r, value, k):
        small_s[0, pl.ds(r, 1), 0 : value.shape[1]] = value

    def column_sums(value):
        return jnp.sum(value.astype(wide), axis=0, keepdims=True)

    def put(t, start, value):
        width = value.shape[1]
        gbuf[t % 3, :, :, :, start : start + width] = value.reshape(4, 2, tile // 8, width)

    def slot_free(t):
        @pl.when(t >= 3)
        def _():
            core_copy(t - 3).wait_send()

    def flat(value):
        return value.reshape(tile, value.shape[-1])

    def settle(q, r):
        load_sl(q).wait()

        def body(rows, k):
            low_dz = (da[rows, :] * sl[q % 3, rows, :].astype(wide)).astype(low)
            dz[rows, :] = low_dz
            add_row(r, column_sums(low_dz), k)
        over_rows(body)

        @pl.when(q + 3 < 12)
        def _():
            load_sl(q + 3).start()

    def fore_two_a(t):
        load_g().wait()
        load_a4(2).wait()
        put(t, 0, mul(a4[0], g[:, 0:tile], TN))
        emit(t)
        r = bias_rows[2, "fore"][0]
        small_s[0, r : r + 1, :] = column_sums(g[:, 0:tile])

    def fore_two_b(t):
        width = wf2.shape[2]
        put(t, 0, mul(a4[0], g[:, tile:width], TN))
        load_a4(0).start()
        load_a4(1).wait()
        put(t, width - tile, mul(a4[1], g[:, 896:1024], TN))
        done = width - tile + 128
        gbuf[t % 3, :, :, :, done:] = jnp.zeros((4, 2, tile // 8, tile - done), wide)
        emit(t)
        r = bias_rows[2, "fore"][0]
        small_s[0, r + 1 : r + 2, 0 : width - tile] = column_sums(g[:, tile:width])
        load_wf2().wait()

        def body(rows, k):
            da[rows, :] = mul(g[rows, 0:width], flat(wf2[...]), NT)
        over_rows(body)
        settle(jnp.int32(0), bias_rows[2, 2][0])

    def hidden(t, i):
        load_ah(i).wait()
        slot_free(t)
        wait_wh(i)
        q = i + 1 + i // 3
        load_sl(q).wait()
        r = 4 * (2 - i // 3) + 2 - i % 3
        put(t, 0, mul(ah[i % 3], dz[...], TN))

        def body(rows, k):
            d = mul(dz[rows, :], flat(wh[i]), NT)
            low_dz = (d * sl[q % 3, rows, :].astype(wide)).astype(low)
            dz[rows, :] = low_dz
            add_row(r, column_sums(low_dz), k)
        over_rows(body)
        emit(t)

        @pl.when(i + 3 < 9)
        def _():
            load_ah(i + 3).start()

        @pl.when(q + 3 < 12)
        def _():
            load_sl(q + 3).start()

    def first_two(t, k):
        wait_y(k)
        slot_free(t)
        m = 2 * k
        wait_wtile(m)

        @pl.when(k >= 2)
        def _():
            dx_store(k - 2).wait()
        r = bias_rows[1, "back"][0] + k
        put(t, 0, mul(dz[...], ytile[k % 2], TN))

        def body(rows, b):
            dx = mul(dz[rows, :], flat(wtile[m % 3]))
            dxb[k % 2, rows, :] = dx
            low_gb = (-dx).astype(low)
            gb[rows, :] = low_gb
            add_row(r, column_sums(low_gb), b)
        over_rows(body)
        emit(t)
        start_y(k + 2)
        dx_store(k).start()
        start_wtile(m + 3)

    def back_head(m):
        da[...] = da[...] + mul(gb[...], flat(wtile[m % 3]), NT)

    def clear_da(k):
        @pl.when(k == 0)
        def _():
            da[...] = jnp.zeros(da.shape, wide)

    def back_one(t, k):
        clear_da(k)
        slot_free(t)
        m = 2 * k + 1
        wait_wtile(m)
        put(t, 0, mul(a4[1], gb[...], TN))
        back_head(m)
        emit(t)
        start_wtile(m + 3)
        pl.when(k == full - 1)(tail_one)

    def tail_one():
        load_x2tail().wait()
        for k in range(3):
            load_wtail(k).wait()
        load_wf(1).wait()

        def body(rows, k):
            dx = mul(dz[rows, :], flat(wtail[0]))
            dxt[rows, :] = dx
            low_gb = (-dx).astype(low)
            gb[rows, 0:rest] = low_gb
            add_row(bias_rows[1, "back"][0] + full, column_sums(low_gb), k)
            add_row(bias_rows[1, "fore"][0], column_sums(g[rows, 896:1024]), k)
            da[rows, :] = (
                da[rows, :] + mul(low_gb, flat(wtail[1]), NT) + mul(g[rows, 896:1024], flat(wf[1]), NT)
            )
        over_rows(body)
        hold[:, 0:rest] = mul(dz[...], x2tail[...], TN)
        hold[:, rest : 2 * rest] = mul(a4[1], gb[:, 0:rest], TN)
        for k in (full - 2, full - 1):
            dx_store(jnp.int32(k)).wait()
        for k in range(2):
            dx_load(jnp.int32(k)).start()
        settle(jnp.int32(4), bias_rows[1, 2][0])

    def first_one(t, k):
        wait_y(k)
        slot_free(t)
        put(t, 0, mul(dz[...], ytile[k % 2], TN))
        emit(t)
        start_y(k + 2)

    def pooled_back(rows, cols, width):
        high, tail = parts_low(mul(dz[rows, :], flat(w1[:, :, cols])))
        return mul(high, spread[:, 0:width]) + mul(tail, spread[:, 0:width])

    def back_zero(t, k):
        @pl.when(k == 0)
        def _():
            load_w1().wait()
            load_a4(0).wait()
        dx_load(k).wait()
        clear_da(k)
        slot_free(t)
        m = 2 * full + k
        wait_wtile(m)
        r = bias_rows[0, "back"][0] + k

        def body(rows, b):
            cols = pl.ds(pl.multiple_of(k * 128, 128), 128)
            low_gb = (-(dxb[k % 2, rows, :] + pooled_back(rows, cols, tile))).astype(low)
            gb[rows, :] = low_gb
            add_row(r, column_sums(low_gb), b)
        over_rows(body)
        put(t, 0, mul(a4[0], gb[...], TN))
        back_head(m)
        emit(t)
        start_wtile(m + 3)

        @pl.when(k + 2 < full)
        def _():
            dx_load(k + 2).start()

    def tail_zero(t):
        load_wf(0).wait()

        def body(rows, k):
            low_gb = (-(dxt[rows, :] + pooled_back(rows, slice(full * 128, full * 128 + 128), rest))).astype(low)
            gb[rows, 0:rest] = low_gb
            gb[rows, rest : rest + 128] = g[rows, 768:896]
            add_row(bias_rows[0, "back"][0] + full, column_sums(low_gb), k)
            add_row(bias_rows[0, "fore"][0], column_sums(g[rows, 768:896]), k)
            da[rows, :] = (
                da[rows, :] + mul(low_gb, flat(wtail[2]), NT) + mul(g[rows, 768:896], flat(wf[0]), NT)
            )
        over_rows(body)
        slot_free(t)
        put(t, 0, hold[...])
        put(t, 2 * rest, mul(a4[0], gb[:, 0 : rest + 128], TN))
        emit(t)
        settle(jnp.int32(8), bias_rows[0, 2][0])

    row_pair = row + 1 - 2 * (row % 2)
    row_far = row + 2 - 4 * (row // 2)
    hops = ((row, other), (row, over_x), (row, over_y), (row_pair, me), (row_far, me))

    def small_step(k):
        return remote(small_s.at[k], small_r.at[k], small_ss.at[k], small_rs.at[k], hops[k])

    def small_stage(k):
        if k > 0:
            small_step(k - 1).wait_recv()
            total = small_s[k - 1] + small_r[k - 1]
            if k < len(hops):
                small_s[k] = total
            else:
                small_sum[...] = total
        if k < len(hops):
            small_step(k).start()

    square_s[...] = jnp.zeros_like(square_s)
    small_s[0] = jnp.zeros(small_s.shape[1:], wide)
    extra = small_s.shape[1] - 8
    small_s[0, extra:, :] = forward_small_ref[...]
    ids = lax.broadcasted_iota(jnp.int32, spread.shape, 0) * KERNELS[1]
    col = lax.broadcasted_iota(jnp.int32, spread.shape, 1)
    spread[...] = jnp.where((col >= ids) & (col < ids + KERNELS[1]), 1.0 / KERNELS[1], 0.0).astype(low)

    pl.semaphore_wait(barrier, 10)

    def compute(t):
        @pl.when(t < 2)
        def _():
            pl.when(t == 0)(lambda: fore_two_a(t))
            pl.when(t == 1)(lambda: fore_two_b(t))

        in_pair = (t >= 5) & (t < t_hidden1)
        in_back = (t >= t_back0) & (t < t_tail0)

        @pl.when(in_pair)
        def _():
            pl.when(t % 2 == 1)(lambda: first_two(t, (t - 5) // 2))
            pl.when(t % 2 == 0)(lambda: back_one(t, (t - 6) // 2))

        pl.when(in_back)(lambda: back_zero(t, t - t_back0))

        @pl.when((t >= 2) & jnp.logical_not(in_pair) & jnp.logical_not(in_back))
        def _():
            @pl.when((t < 5) | ((t >= t_hidden1) & (t < t_first1)) | ((t > t_tail0) & (t < t_tail0 + 4)))
            def _():
                past_one = (t + count - t_hidden1) // count
                past_zero = (t + count - t_tail0) // count
                hidden(t, t - 2 - past_one * (t_hidden1 - 5) - past_zero * (t_tail0 - t_hidden1 - 2))

            pl.when((t >= t_first1) & (t < t_back0))(lambda: first_one(t, t - t_first1 + full))
            pl.when(t == t_tail0)(lambda: tail_zero(t))
            pl.when(t == t_tail0 + 4)(lambda: first_one(t, t - t_tail0 - 4 + full + 2))

    def turn(t, carry):
        pl.when(t < count)(lambda: compute(t))

        @pl.when(t >= count)
        def _():
            for k in range(len(hops) + 1):
                pl.when(t == count + 2 * k)(functools.partial(small_stage, k))
        steady = (t >= LAGS[-1]) & (t < count - 3)
        pl.when(steady)(lambda: reduce_turn(t, True))
        pl.when(jnp.logical_not(steady))(lambda: reduce_turn(t, False))
        return carry

    lax.fori_loop(0, count + LAGS[-1], turn, 0)

    def square_copy(peer):
        return remote(square_s, square_r.at[me], sq_ss.at[peer], sq_rs.at[peer], (row, (me + peer) % 8))

    def square_wait(peer):
        return remote(square_s, square_r.at[(me - peer + 8) % 8], sq_ss.at[peer], sq_rs.at[peer], (row, (me + peer) % 8))

    for peer in range(1, 8):
        square_copy(peer).start()
    square_r[me] = square_s[...]
    for peer in range(1, 8):
        square_wait(peer).wait_recv()
    acc = square_r[0]
    for k in range(1, 8):
        acc = acc + square_r[k]
    tile_rows = small_s.shape[1] - 8
    biases = small_sum[0:tile_rows, :]
    total = jnp.sum(acc, keepdims=True) + jnp.sum(biases * biases, keepdims=True)
    tally = small_sum[tile_rows + 2 : tile_rows + 3, 0:1]
    factor = (1.0 / scale) / tally
    norm = jnp.sqrt(total) * factor
    result_ref[0:1, :] = jnp.broadcast_to(norm, (1, 128))
    loss = jnp.sum(small_sum[tile_rows : tile_rows + 2, :], keepdims=True) / tally
    result_ref[1:2, :] = jnp.broadcast_to(loss, (1, 128))
    result_ref[2:3, :] = jnp.broadcast_to(jnp.minimum(1.0, CLIP_MAX / norm) * factor, (1, 128))
    flat_ref[...] = jnp.zeros_like(flat_ref)
    for key, (at, width) in bias_rows.items():
        for k in range(0, width, tile):
            begin = spans[key] + k
            todo = min(tile, width - k)
            r, o = begin // tile, begin % tile
            here = min(todo, tile - o)
            line = slice(at + k // tile, at + k // tile + 1)
            flat_ref[r : r + 1, o : o + here] = small_sum[line, 0:here]
            if here < todo:
                flat_ref[r + 1 : r + 2, 0 : todo - here] = small_sum[line, here:todo]

    def finish(t, carry):
        @pl.when(t >= count - 3)
        def _():
            core_copy(t).wait_send()

        @pl.when(t >= count - 4)
        def _():
            first_to(t).wait_send()
            second_to(t).wait_send()

            @pl.when(is_edge)
            def _():
                z_all(t).wait_send()

            @pl.when(jnp.logical_not(is_edge))
            def _():
                z_swap(t).wait_send()

        @pl.when(jnp.logical_not(is_edge))
        def _():
            z_final(t).wait_send()
            pl.when(precise(t))(lambda: z_low(t).wait_send())
        local(final.at[t], out_ref.at[t], out_sem.at[t]).wait()
        return carry

    lax.fori_loop(0, count, finish, 0)
    for k in range(len(hops)):
        small_step(k).wait_send()
    for peer in range(1, 8):
        square_copy(peer).wait_send()


def backward(w, a, slope, p0, p1, x2, g, small, pieces, bias_rows, spans, scale, row_count, flat_rows, count):
    low, wide = jnp.bfloat16, jnp.float32
    rows, tile = a.shape[2], a.shape[3]
    part = tile // 8
    full, rest = x2.shape[1] // tile, x2.shape[1] % tile
    wide_steps = g.shape[1] - 256
    small_rows = row_count + 8
    hbm = pl.BlockSpec(memory_space=pltpu.HBM)
    vmem = pl.BlockSpec(memory_space=pltpu.VMEM)
    dma = pltpu.SemaphoreType.DMA
    shape = jax.ShapeDtypeStruct
    return pl.pallas_call(
        functools.partial(backward_kernel, (pieces, bias_rows, spans, scale, count, full)),
        out_shape=(
            shape((count, part, tile), low),
            shape((rows, full * tile), wide),
            shape((flat_rows, tile), wide),
            shape((8, 128), wide),
        ),
        in_specs=[hbm] * 7 + [vmem],
        out_specs=(hbm, hbm, vmem, vmem),
        scratch_shapes=[
            pltpu.VMEM((9, 8, part, tile), low),
            pltpu.VMEM((8, part, wide_steps), low),
            pltpu.VMEM((2, 8, part, 128), low),
            pltpu.VMEM((8, part, p1.shape[1]), low),
            pltpu.VMEM((3, 8, part, tile), low),
            pltpu.VMEM((3, 8, part, rest), low),
            pltpu.VMEM((2, rows, tile), low),
            pltpu.VMEM((3, rows, tile), low),
            pltpu.VMEM((3, rows, tile), low),
            pltpu.VMEM((2, rows, tile), low),
            pltpu.VMEM((rows, rest), low),
            pltpu.VMEM(g.shape, low),
            pltpu.VMEM((rows, tile), low),
            pltpu.VMEM((rows, tile), low),
            pltpu.VMEM((2, rows, tile), wide),
            pltpu.VMEM((rows, rest), wide),
            pltpu.VMEM((rows, tile), wide),
            pltpu.VMEM((128, tile), low),
            pltpu.VMEM((tile, 2 * rest), wide),
            pltpu.VMEM((3, 4, 2, part, tile), wide),
            pltpu.VMEM((4, 4, part, tile), wide),
            pltpu.VMEM((4, 2, part, tile), low),
            pltpu.VMEM((count, 2, part, tile), low),
            pltpu.VMEM((8, 2, part, tile), wide),
            pltpu.VMEM((4, part, tile), low),
            pltpu.VMEM((count, part, tile), low),
            pltpu.VMEM((6, part, tile), wide),
            pltpu.VMEM((4, part, tile), low),
            pltpu.VMEM((count, part, tile), low),
            pltpu.VMEM((4, part, tile), low),
            pltpu.VMEM((count, part, tile), low),
            pltpu.VMEM((2, part, tile), low),
            pltpu.VMEM((2, part, tile), low),
            pltpu.VMEM((count, part, tile), low),
            pltpu.VMEM((5, small_rows, tile), wide),
            pltpu.VMEM((5, small_rows, tile), wide),
            pltpu.VMEM((small_rows, tile), wide),
            pltpu.VMEM((8, 128), wide),
            pltpu.VMEM((8, 8, 128), wide),
            dma((9,)),
            dma((2,)),
            dma((3,)),
            dma((3,)),
            dma((3,)),
            dma((3,)),
            dma((3,)),
            dma((2,)),
            dma((4,)),
            dma((2,)),
            dma((3,)),
            dma((4,)),
            pltpu.SemaphoreType.REGULAR,
            dma((4,)),
            dma((count,)),
            dma((4,)),
            dma((count,)),
            dma((4,)),
            dma((count,)),
            dma((4,)),
            dma((count,)),
            dma((2,)),
            dma((2,)),
            dma((count,)),
            dma((count,)),
            dma((5,)),
            dma((5,)),
            dma((8,)),
            dma((8,)),
            dma((count,)),
        ],
        compiler_params=pltpu.CompilerParams(
            collective_id=1, has_side_effects=True, vmem_limit_bytes=63 * 1024 * 1024
        ),
        name="backward",
    )(w, a, slope, p0, p1, x2, g, small)


def adamw_kernel(
    plan, step_ref, result_ref, grad_ref, *refs,
):
    where, pieces, count = plan
    groups = [refs[3 * k : 3 * k + 3] for k in range(4)]
    outs = [refs[12 + 4 * k : 16 + 4 * k] for k in range(4)]
    held = [refs[28 + 3 * k : 31 + 3 * k] for k in range(4)]
    copies = refs[40:44]
    grads, first_g, fore_g, grad_sem, in_sem, out_sem = refs[44:]
    wide, low = jnp.float32, jnp.bfloat16
    clip = result_ref[2:3, 0:1]
    steps = jnp.full((1, 1), 1.0, wide) * step_ref[0].astype(wide)
    mean_fix = 1.0 / (1.0 - jnp.exp(steps * float(np.log(BETA_ONE))))
    square_fix = 1.0 / (1.0 - jnp.exp(steps * float(np.log(BETA_TWO))))
    tile = grads.shape[2]

    units = [(1, k) for k in range(0, 9, 3)] + [(2, 0), (2, 1), (3, None), (0, None)]

    def view(ref, group, lead):
        if lead is None:
            return ref
        return ref.at[lead : lead + 3] if group == 1 else ref.at[lead]

    loads = []
    for n, (group, lead) in enumerate(units):
        loads.append(
            [
                pltpu.make_async_copy(view(groups[group][k], group, lead), view(held[group][k], group, lead), in_sem.at[n, k])
                for k in range(3)
            ]
        )
    whole = pltpu.make_async_copy(grad_ref, grads, grad_sem)
    whole.start()
    for unit in loads:
        for copy in unit:
            copy.start()
    whole.wait()

    for key_group, target in (("first", first_g), ("fore", fore_g)):
        begin = 0
        for stack_id in range(3):
            done = 0
            width = pieces[stack_id, key_group][1]
            for t, start, size in where[stack_id, key_group]:
                size = min(size, width - done)
                if size > 0:
                    target[:, begin + done : begin + done + size] = grads[t, :, start : start + size].astype(wide)
                done += size
            begin += width

    def update(group, index, grad):
        weight, avg, square = (held[group][k][index] for k in range(3))
        grad = grad * clip
        new_avg = BETA_ONE * avg + (1.0 - BETA_ONE) * grad
        new_sq = BETA_TWO * square + (1.0 - BETA_TWO) * grad * grad
        step = (new_avg * mean_fix) / (jnp.sqrt(new_sq * square_fix) + EPSILON) + DECAY * weight
        new_weight = weight - RATE * step
        held[group][0][index] = new_weight
        held[group][1][index] = new_avg
        held[group][2][index] = new_sq
        copies[group][index] = new_weight.astype(low)

    def rows_of(body, rows=64, step=16):
        def go(k, carry):
            body(pl.ds(pl.multiple_of(k * step, step), step))
            return carry
        lax.fori_loop(0, rows // step, go, 0)

    part = grads.shape[1]
    stores = []
    for n, (group, lead) in enumerate(units):
        for copy in loads[n]:
            copy.wait()
        if group == 1:
            for k in range(lead, lead + 3):
                t = where[k // 3, k % 3][0][0]
                rows_of(lambda rows: update(1, (k, rows), grads[t, rows, :].astype(wide)), part)
        elif group == 2:
            spots = where[lead, "back"]
            length = held[2][0].shape[2]

            def tiles(rows):
                done = 0
                for t, start, size in spots:
                    size = min(size, length - done)
                    update(2, (lead, rows, slice(done, done + size)), grads[t, rows, start : start + size].astype(wide))
                    done += size
            rows_of(tiles, part)
        else:
            target = first_g if group == 0 else fore_g
            rows_of(lambda rows: update(group, (rows,), target[rows, :]), part)
        for k in range(3):
            stores.append(
                pltpu.make_async_copy(view(held[group][k], group, lead), view(outs[group][k], group, lead), out_sem.at[n, k])
            )
        stores.append(
            pltpu.make_async_copy(view(copies[group], group, lead), view(outs[group][3], group, lead), out_sem.at[n, 3])
        )
        for copy in stores[-4:]:
            copy.start()
    for copy in stores:
        copy.wait()


def adamw_all(step_count, result, grads, states, where, pieces):
    low, wide = jnp.bfloat16, jnp.float32
    hbm = pl.BlockSpec(memory_space=pltpu.HBM)
    shape = jax.ShapeDtypeStruct
    shapes = [state[0].shape for state in states]
    dma = pltpu.SemaphoreType.DMA
    return pl.pallas_call(
        functools.partial(adamw_kernel, (where, pieces, grads.shape[0])),
        out_shape=tuple(shape(s, kind) for s in shapes for kind in (wide, wide, wide, low)),
        in_specs=[pl.BlockSpec(memory_space=pltpu.SMEM), pl.BlockSpec(memory_space=pltpu.VMEM)] + [hbm] * 13,
        out_specs=(hbm,) * 16,
        scratch_shapes=[pltpu.VMEM(s, wide) for s in shapes for _ in range(3)]
        + [pltpu.VMEM(s, low) for s in shapes]
        + [
            pltpu.VMEM(grads.shape, low),
            pltpu.VMEM(shapes[0], wide),
            pltpu.VMEM(shapes[3], wide),
            dma,
            dma((7, 3)),
            dma((7, 4)),
        ],
        compiler_params=pltpu.CompilerParams(vmem_limit_bytes=60 * 1024 * 1024),
        name="adamw",
    )(step_count, result, grads, *[array for state in states for array in state])


def fast_body(
    devices,
    windows,
    targets,
    horizon,
    step_count,
    first_w,
    first_w_avg,
    first_w_sq,
    hidden_w,
    hidden_w_avg,
    hidden_w_sq,
    back_w,
    back_w_avg,
    back_w_sq,
    fore_w,
    fore_w_avg,
    fore_w_sq,
    bias_vec,
    bias_avg,
    bias_sq,
):
    length, steps_ahead_total, hidden_size = windows.shape[1], targets.shape[1], hidden_w.shape[-1]
    part = hidden_w.shape[2]
    pieces, total = packing(length, steps_ahead_total, hidden_size)
    rows, row_count = row_plan(length, steps_ahead_total, hidden_size)
    row_count = -(-row_count // 8) * 8
    where, count = chunk_plan(length, steps_ahead_total, hidden_size)
    spans = {}
    cursor = 0
    for key in bias_order(length, steps_ahead_total, hidden_size):
        spans[key] = cursor
        cursor += rows[key][1]
    bias_count = bias_vec.shape[0]
    flat_rows = -(-bias_count // (8 * hidden_size)) * 8
    flat = jnp.pad(bias_vec, (0, flat_rows * hidden_size - bias_count)).reshape(flat_rows, hidden_size)
    ups = np.zeros((256, tiled(steps_ahead_total)), np.float32)
    for stack_id in range(2):
        knots = steps_ahead_total // RATIOS[stack_id]
        ups[128 * stack_id : 128 * stack_id + knots, :steps_ahead_total] = blend_coefficients(steps_ahead_total, knots)
    up_high = ups.astype(jnp.bfloat16)
    up_low = (ups - up_high.astype(np.float32)).astype(jnp.bfloat16)
    scale = 2.0 ** -int(np.ceil(np.log2(devices * windows.shape[0] * steps_ahead_total)))

    def lead(array):
        return array.reshape((-1,) + array.shape[2:]) if array.ndim == 4 else array

    states = (
        (first_w.T, first_w_avg.T, first_w_sq.T),
        (lead(hidden_w), lead(hidden_w_avg), lead(hidden_w_sq)),
        (back_w, back_w_avg, back_w_sq),
        (fore_w, fore_w_avg, fore_w_sq),
    )
    w, a, slope, p0, p1, x2, g, small = forward(
        states[0][0], states[1][0], back_w, fore_w, windows, targets, horizon, flat,
        jnp.asarray(up_high), jnp.asarray(up_low), pieces, rows, spans, scale, total,
    )
    owned, _, flat_grad, result = backward(
        w, a, slope, p0, p1, x2, g, small, pieces, rows, spans, scale, row_count, flat_rows, count
    )
    new = adamw_all(step_count, result, owned, states, where, pieces)
    first_new, hidden_new, back_new, fore_new = (new[4 * k : 4 * k + 4] for k in range(4))
    grad_bias = flat_grad.reshape(-1)[:bias_count] * result[2, 0]
    bias_new = adamw(bias_vec, bias_avg, bias_sq, grad_bias, step_count[0].astype(jnp.float32))
    shape = hidden_w.shape
    first_new = [array.T for array in first_new]
    hidden_new = [array.reshape(shape) for array in hidden_new]
    flat_out = [result[1, 0], result[0, 0]]
    for weight, avg, square, _ in (first_new, hidden_new, back_new, fore_new):
        flat_out += [avg, square, weight]
    flat_out += list(bias_new)
    flat_out += [group[3] for group in (first_new, hidden_new, back_new, fore_new)]
    return tuple(flat_out)


def solution(mesh):
    fast = mesh.shape["fsdp"] == 8 and mesh.shape["dp"] == 4
    step = functools.partial(fast_body, mesh.shape["dp"] * mesh.shape["fsdp"]) if fast else body
    placed = (
        P(("dp", "fsdp"), None),
        P(("dp", "fsdp"), None),
        P(("dp", "fsdp")),
        P(),
        P(None, "fsdp"),
        P(None, "fsdp"),
        P(None, "fsdp"),
        P(None, None, "fsdp", None),
        P(None, None, "fsdp", None),
        P(None, None, "fsdp", None),
        P(None, "fsdp", None),
        P(None, "fsdp", None),
        P(None, "fsdp", None),
        P("fsdp", None),
        P("fsdp", None),
        P("fsdp", None),
        P(),
        P(),
        P(),
    )
    return jax.shard_map(
        step,
        mesh=mesh,
        in_specs=placed,
        out_specs=(
            P(),
            P(),
            P(None, "fsdp"),
            P(None, "fsdp"),
            P(None, "fsdp"),
            P(None, None, "fsdp", None),
            P(None, None, "fsdp", None),
            P(None, None, "fsdp", None),
            P(None, "fsdp", None),
            P(None, "fsdp", None),
            P(None, "fsdp", None),
            P("fsdp", None),
            P("fsdp", None),
            P("fsdp", None),
            P(),
            P(),
            P(),
            P(None, "fsdp"),
            P(None, None, "fsdp", None),
            P(None, "fsdp", None),
            P("fsdp", None),
        ),
        check_vma=False,
    )
```

```python
import functools
import jax
import jax.numpy as jnp
import numpy as np
from jax import lax
from jax.experimental import pallas as pl
from jax.experimental.pallas import tpu as pltpu
from jax.sharding import PartitionSpec as P

KERNELS = (8, 4, 1)
RATIOS = (24, 12, 1)
CLIP_MAX = 0.01
RATE = 0.02
BETA_ONE = 0.9
BETA_TWO = 0.999
EPSILON = 1e-08
DECAY = 0.01
DOT_EXACTNESS = lax.Precision.HIGHEST


def blend_coefficients(fine, coarse):
    column = np.arange(fine)
    numer = np.maximum((2 * column + 1) * coarse - fine, 0)
    lower_idx = numer // (2 * fine)
    frac = (numer - lower_idx * 2 * fine) / (2.0 * fine)
    upper_idx = np.minimum(lower_idx + 1, coarse - 1)
    matrix = np.zeros((coarse, fine), np.float32)
    matrix[lower_idx, column] += 1.0 - frac
    matrix[upper_idx, column] += frac
    return matrix


def normalize(windows, targets):
    center = jnp.mean(windows, axis=1, keepdims=True)
    spread = jnp.sqrt(jnp.mean((windows - center) ** 2, axis=1, keepdims=True) + 1e-05)
    return ((windows - center) / spread, (targets - center) / spread)


def mean_pool(values, kernel):
    if kernel == 1:
        return values
    return jnp.mean(values.reshape(values.shape[0], values.shape[1] // kernel, kernel), axis=2)


def pool_back(d_pooled, kernel):
    if kernel == 1:
        return d_pooled
    spread_out = jnp.broadcast_to((d_pooled / kernel)[:, :, None], d_pooled.shape + (kernel,))
    return spread_out.reshape(d_pooled.shape[0], d_pooled.shape[1] * kernel)


def silu_slope(pre_act):
    gate = jax.nn.sigmoid(pre_act)
    return gate * (1.0 + pre_act * (1.0 - gate))


def stack_params(stack_id, gathered, bias_vec, length, steps_ahead_total):
    first_full, hidden_full, back_full, fore_full = gathered
    hidden_size = hidden_full.shape[-1]
    row_start = sum((length // KERNELS[earlier] for earlier in range(stack_id)))
    col_start = sum((steps_ahead_total // RATIOS[earlier] for earlier in range(stack_id)))
    pooled_len = length // KERNELS[stack_id]
    anchor_entries = steps_ahead_total // RATIOS[stack_id]
    layers = [
        (
            first_full[row_start : row_start + pooled_len],
            bias_vec[stack_id * hidden_size : (stack_id + 1) * hidden_size],
        )
    ]
    for layer_id in range(3):
        offset = (3 + 3 * stack_id + layer_id) * hidden_size
        layers.append((hidden_full[stack_id, layer_id], bias_vec[offset : offset + hidden_size]))
    fore_start = 12 * hidden_size + 2 * length + col_start
    fore_pair = (
        fore_full[:, col_start : col_start + anchor_entries],
        bias_vec[fore_start : fore_start + anchor_entries],
    )
    back_pair = None
    if stack_id < 2:
        back_start = 12 * hidden_size + stack_id * length
        back_pair = (back_full[stack_id], bias_vec[back_start : back_start + length])
    linear_upsample_anchors = jnp.asarray(blend_coefficients(steps_ahead_total, anchor_entries))
    return (layers, fore_pair, back_pair, linear_upsample_anchors)


def stack_forward(residual, stack_id, layers, fore_pair, back_pair, linear_upsample_anchors):
    inputs_kept = [mean_pool(residual, KERNELS[stack_id]).astype(jnp.bfloat16)]
    pre_kept = []
    for weight, bias in layers:
        pre_act = jnp.dot(inputs_kept[-1], weight, preferred_element_type=jnp.float32) + bias
        pre_kept.append(pre_act)
        inputs_kept.append(jax.nn.silu(pre_act).astype(jnp.bfloat16))
    anchor_result = (
        jnp.dot(inputs_kept[-1], fore_pair[0], preferred_element_type=jnp.float32) + fore_pair[1]
    )
    running_subtotal = jnp.dot(anchor_result, linear_upsample_anchors, precision=DOT_EXACTNESS)
    backcast = None
    if back_pair is not None:
        backcast = (
            jnp.dot(inputs_kept[-1], back_pair[0], preferred_element_type=jnp.float32)
            + back_pair[1]
        )
    return ((inputs_kept, pre_kept), running_subtotal, backcast)


def head_grads(last_act, d_low, weight):
    grad_w = jnp.dot(last_act.T, d_low, preferred_element_type=jnp.float32)
    grad_b = jnp.sum(d_low.astype(jnp.float32), axis=0)
    return ((grad_w, grad_b), jnp.dot(d_low, weight.T, preferred_element_type=jnp.float32))


def stack_backward(kept, anchor_cotangent, d_backcast, layers, fore_pair, back_pair, need_input):
    inputs_kept, pre_kept = kept
    last_act = inputs_kept[-1]
    fore_grads, d_hidden = head_grads(last_act, anchor_cotangent.astype(jnp.bfloat16), fore_pair[0])
    back_grads = None
    if back_pair is not None:
        back_grads, d_extra = head_grads(last_act, d_backcast.astype(jnp.bfloat16), back_pair[0])
        d_hidden = d_hidden + d_extra
    layer_grads = [None, None, None, None]
    for layer_id in (3, 2, 1, 0):
        d_pre = (d_hidden * silu_slope(pre_kept[layer_id])).astype(jnp.bfloat16)
        layer_grads[layer_id] = (
            jnp.dot(inputs_kept[layer_id].T, d_pre, preferred_element_type=jnp.float32),
            jnp.sum(d_pre.astype(jnp.float32), axis=0),
        )
        if layer_id > 0 or need_input:
            d_hidden = jnp.dot(d_pre, layers[layer_id][0].T, preferred_element_type=jnp.float32)
    return (layer_grads, fore_grads, back_grads, d_hidden)


def adamw(weight, avg, square, grad, step_float):
    new_avg = BETA_ONE * avg + (1.0 - BETA_ONE) * grad
    new_sq = BETA_TWO * square + (1.0 - BETA_TWO) * grad * grad
    avg_hat = new_avg / (1.0 - BETA_ONE**step_float)
    sq_hat = new_sq / (1.0 - BETA_TWO**step_float)
    new_weight = weight - RATE * (avg_hat / (jnp.sqrt(sq_hat) + EPSILON) + DECAY * weight)
    return (new_avg, new_sq, new_weight)


def body(
    windows,
    targets,
    horizon,
    step_count,
    first_w,
    first_w_avg,
    first_w_sq,
    hidden_w,
    hidden_w_avg,
    hidden_w_sq,
    back_w,
    back_w_avg,
    back_w_sq,
    fore_w,
    fore_w_avg,
    fore_w_sq,
    bias_vec,
    bias_avg,
    bias_sq,
):
    length = windows.shape[1]
    steps_ahead_total = targets.shape[1]
    normed, observed_future = normalize(windows, targets)
    future_usable_flags = (
        jnp.arange(steps_ahead_total, dtype=jnp.int32)[None, :] < horizon[:, None]
    ).astype(jnp.float32)
    usable_tally = lax.psum(jnp.sum(horizon.astype(jnp.float32)), ("dp", "fsdp"))
    shards = (
        first_w.astype(jnp.bfloat16),
        hidden_w.astype(jnp.bfloat16),
        back_w.astype(jnp.bfloat16),
        fore_w.astype(jnp.bfloat16),
    )
    gathered = (
        lax.all_gather(shards[0], "fsdp", axis=1, tiled=True),
        lax.all_gather(shards[1], "fsdp", axis=2, tiled=True),
        lax.all_gather(shards[2], "fsdp", axis=1, tiled=True),
        lax.all_gather(shards[3], "fsdp", axis=0, tiled=True),
    )
    residual = normed
    kept_stacks = []
    predicted_future = jnp.zeros(observed_future.shape, jnp.float32)
    for stack_id in range(3):
        layers, fore_pair, back_pair, linear_upsample_anchors = stack_params(
            stack_id, gathered, bias_vec, length, steps_ahead_total
        )
        kept, running_subtotal, backcast = stack_forward(
            residual, stack_id, layers, fore_pair, back_pair, linear_upsample_anchors
        )
        kept_stacks.append(kept)
        predicted_future = predicted_future + running_subtotal
        if backcast is not None:
            residual = residual - backcast
    residual_difference = predicted_future - observed_future
    loss_part = (
        jnp.sum(future_usable_flags * residual_difference * residual_difference) / usable_tally
    )
    future_slope_cotangent = 2.0 * future_usable_flags * residual_difference / usable_tally
    again = (
        lax.all_gather(shards[0], "fsdp", axis=1, tiled=True),
        lax.all_gather(shards[1], "fsdp", axis=2, tiled=True),
        lax.all_gather(shards[2], "fsdp", axis=1, tiled=True),
        lax.all_gather(shards[3], "fsdp", axis=0, tiled=True),
    )
    results = [None, None, None]
    d_residual = None
    for stack_id in (2, 1, 0):
        layers, fore_pair, back_pair, linear_upsample_anchors = stack_params(
            stack_id, again, bias_vec, length, steps_ahead_total
        )
        anchor_cotangent = jnp.dot(
            future_slope_cotangent, linear_upsample_anchors.T, precision=DOT_EXACTNESS
        )
        d_backcast = None if d_residual is None else -d_residual
        results[stack_id] = stack_backward(
            kept_stacks[stack_id],
            anchor_cotangent,
            d_backcast,
            layers,
            fore_pair,
            back_pair,
            stack_id > 0,
        )
        if stack_id > 0:
            spread_back = pool_back(results[stack_id][3], KERNELS[stack_id])
            d_residual = spread_back if d_residual is None else d_residual + spread_back
    grad_first = jnp.concatenate([results[stack_id][0][0][0] for stack_id in range(3)], axis=0)
    grad_hidden = jnp.stack(
        [
            jnp.stack([results[stack_id][0][layer_id][0] for layer_id in (1, 2, 3)])
            for stack_id in range(3)
        ]
    )
    grad_back = jnp.stack([results[stack_id][2][0] for stack_id in range(2)])
    grad_fore = jnp.concatenate([results[stack_id][1][0] for stack_id in range(3)], axis=1)
    bias_pieces = [results[stack_id][0][0][1] for stack_id in range(3)]
    bias_pieces += [
        results[stack_id][0][layer_id][1] for stack_id in range(3) for layer_id in (1, 2, 3)
    ]
    bias_pieces += [results[stack_id][2][1] for stack_id in range(2)]
    bias_pieces += [results[stack_id][1][1] for stack_id in range(3)]
    grad_bias = jnp.concatenate(bias_pieces)
    owned = (
        lax.psum_scatter(grad_first, "fsdp", scatter_dimension=1, tiled=True),
        lax.psum_scatter(grad_hidden, "fsdp", scatter_dimension=2, tiled=True),
        lax.psum_scatter(grad_back, "fsdp", scatter_dimension=1, tiled=True),
        lax.psum_scatter(grad_fore, "fsdp", scatter_dimension=0, tiled=True),
    )
    owned = lax.psum((owned[0], owned[1], owned[2], owned[3]), "dp")
    grad_bias, loss = lax.psum((grad_bias, loss_part), ("dp", "fsdp"))
    local_sq = sum((jnp.sum(grad * grad) for grad in owned))
    total_sq = lax.psum(local_sq, "fsdp") + jnp.sum(grad_bias * grad_bias)
    grad_norm = jnp.sqrt(total_sq)
    clip_factor = jnp.minimum(1.0, CLIP_MAX / grad_norm)
    step_float = step_count[0].astype(jnp.float32)
    states = (
        (first_w, first_w_avg, first_w_sq),
        (hidden_w, hidden_w_avg, hidden_w_sq),
        (back_w, back_w_avg, back_w_sq),
        (fore_w, fore_w_avg, fore_w_sq),
        (bias_vec, bias_avg, bias_sq),
    )
    grads_all = (owned[0], owned[1], owned[2], owned[3], grad_bias)
    updated = []
    for state, grad in zip(states, grads_all):
        updated.append(adamw(state[0], state[1], state[2], grad * clip_factor, step_float))
    return (
        loss,
        grad_norm,
        updated[0][0],
        updated[0][1],
        updated[0][2],
        updated[1][0],
        updated[1][1],
        updated[1][2],
        updated[2][0],
        updated[2][1],
        updated[2][2],
        updated[3][0],
        updated[3][1],
        updated[3][2],
        updated[4][0],
        updated[4][1],
        updated[4][2],
        updated[0][2].astype(jnp.bfloat16),
        updated[1][2].astype(jnp.bfloat16),
        updated[2][2].astype(jnp.bfloat16),
        updated[3][2].astype(jnp.bfloat16),
    )


MESH = pl.DeviceIdType.MESH
CHUNK = 1024


def tiled(width):
    return -(-width // 128) * 128


def packing(length, steps_ahead_total, hidden_size):
    pieces = {}
    cursor = 0
    for stack_id in range(3):
        widths = [("first", length // KERNELS[stack_id])]
        widths += [(layer_id, hidden_size) for layer_id in range(3)]
        if stack_id < 2:
            widths.append(("back", length))
        widths.append(("fore", steps_ahead_total // RATIOS[stack_id]))
        for name, width in widths:
            pieces[stack_id, name] = (cursor, width)
            cursor += tiled(width)
    total = -(-cursor // CHUNK) * CHUNK
    return pieces, total


def pack(parts, pieces, total):
    out = []
    cursor = 0
    for key, (start, width) in pieces.items():
        part = parts[key]
        out.append(jnp.pad(part, ((0, 0), (0, tiled(width) - width))))
        cursor = start + tiled(width)
    rows, dtype = out[0].shape[0], out[0].dtype
    if total > cursor:
        out.append(jnp.zeros((rows, total - cursor), dtype))
    return jnp.concatenate(out, axis=1)


def places():
    row = lax.axis_index("dp")
    me = lax.axis_index("fsdp")
    core = me % 2
    across_x = (me // 2) % 2
    across_y = me // 4
    other = me + 1 - 2 * core
    over_x = me + 2 - 4 * across_x
    over_y = me + 4 - 8 * across_y
    return row, me, core, other, over_x, over_y


def remote(src, dst, send_sem, recv_sem, device):
    return pltpu.make_async_remote_copy(
        src_ref=src, dst_ref=dst, send_sem=send_sem, recv_sem=recv_sem, device_id=device, device_id_type=MESH
    )


HALF_LOW = 2


def row_plan(length, steps_ahead_total, hidden_size):
    rows = {}
    cursor = 0
    for stack_id in range(3):
        for name in ("first", 0, 1, 2):
            rows[stack_id, name] = (cursor, hidden_size)
            cursor += 1
    for stack_id in range(2):
        rows[stack_id, "back"] = (cursor, length)
        cursor += -(-length // hidden_size)
    for stack_id in range(3):
        width = steps_ahead_total // RATIOS[stack_id]
        rows[stack_id, "fore"] = (cursor, width)
        cursor += -(-width // hidden_size)
    return rows, cursor


def bias_order(length, steps_ahead_total, hidden_size):
    keys = [(stack_id, "first") for stack_id in range(3)]
    keys += [(stack_id, layer_id) for stack_id in range(3) for layer_id in range(3)]
    keys += [(stack_id, "back") for stack_id in range(2)]
    keys += [(stack_id, "fore") for stack_id in range(3)]
    return keys


def parts_low(value):
    high = value.astype(jnp.bfloat16)
    return high, (value - high.astype(jnp.float32)).astype(jnp.bfloat16)


NN = (((1,), (0,)), ((), ()))
NT = (((1,), (1,)), ((), ()))
TN = (((0,), (0,)), ((), ()))


def mul(left, right, dims=NN):
    return lax.dot_general(left, right, dims, preferred_element_type=jnp.float32)


def cut_classes(count):
    pattern = "eoeo" + "eob" * count
    return (pattern[: count - 2] + "bb")[:count]


def forward_kernel(
    plan,
    first_ref, hidden_ref, back_ref, fore_ref, windows_ref, targets_ref, horizon_ref, flat_ref, up_high_ref, up_low_ref,
    w_out, a_out, slope_out, p0_out, p1_out, x2_out, g_out, small_ref,
    w, x, stage, a, slope, p0, p1, x2, fc, tt, g, dk, center_s, scale_s, pool8, pool4,
    bias_ref, horizon_s, first_s, hidden_s, back_s, fore_s,
    raw_sem, send_sem, recv_sem, win_sem, tt_sem, out_sem, w_sem,
):
    pieces, bias_rows, spans, cut_width, count, scale = plan
    row, me, core, other, over_x, over_y = places()
    diag = over_x + over_y - me
    total_rows = windows_ref.shape[0]
    length = windows_ref.shape[1]
    hidden_size = a.shape[-1]
    steps_ahead = targets_ref.shape[0]
    block = total_rows // 2
    wide, low = jnp.float32, jnp.bfloat16
    wide_length = x.shape[1]
    tiles = [(k, min(hidden_size, wide_length - k)) for k in range(0, wide_length, hidden_size)]
    whole = wide_length // 128 * 128 - 128

    barrier = pltpu.get_barrier_semaphore()
    for peer in (other, over_x, over_y):
        pl.semaphore_signal(barrier, inc=1, device_id=(row, peer), device_id_type=MESH)
    pl.semaphore_signal(barrier, inc=1, device_id=(row + 1 - 2 * (row % 2), me), device_id_type=MESH)

    classes = cut_classes(count)
    turn_of = [classes[:cut].count(classes[cut]) % 2 for cut in range(count)]
    even_plane = row % 2 == 0
    z_pair = row + 1 - 2 * (row % 2)

    def copy_of(kind, cut, src, holder, device):
        cols = slice(cut * cut_width, (cut + 1) * cut_width)
        return remote(src.at[:, cols], w.at[holder, :, cols], send_sem.at[kind, cut], recv_sem.at[kind, cut], device)

    def to_x(cut):
        return copy_of(0, cut, w.at[me], me, (row, over_x))

    def to_y(cut):
        return copy_of(1, cut, w.at[me], me, (row, over_y))

    def onward(cut):
        if turn_of[cut] == 0:
            return copy_of(2, cut, w.at[over_x], over_x, (row, over_y))
        return copy_of(2, cut, w.at[over_y], over_y, (row, over_x))

    def to_core(kind, cut):
        holder = (me, over_x, over_y, diag)[kind]
        return copy_of(3 + kind, cut, w.at[holder], holder, (row, other))

    def to_z(kind, cut):
        holder = (None, over_x, over_y, diag)[kind]
        return copy_of(6 + kind, cut, w.at[holder], holder, (z_pair, me))

    def gathers(cut, body):
        if classes[cut] == "b":
            body()
        else:
            pl.when(even_plane if classes[cut] == "e" else jnp.logical_not(even_plane))(body)

    def receives(cut, body):
        if classes[cut] != "b":
            pl.when(jnp.logical_not(even_plane) if classes[cut] == "e" else even_plane)(body)

    def own_sends(cut):
        def body():
            to_x(cut).start()
            to_y(cut).start()
        gathers(cut, body)
        to_core(0, cut).start()

    def w_copy(cut):
        cols = slice(cut * cut_width, (cut + 1) * cut_width)
        return pltpu.make_async_copy(w.at[:, :, cols], w_out.at[:, :, cols], w_sem.at[cut])

    look, lag_diag, lag_z = 6, 2, 6
    arrived = set()

    def pump(cut):
        if cut < count:
            def body():
                to_x(cut).wait_recv()
                if turn_of[cut] == 0:
                    onward(cut).start()
                if classes[cut] != "b":
                    to_z(1, cut).start()
                to_core(1, cut).start()
                to_y(cut).wait_recv()
                if turn_of[cut] == 1:
                    onward(cut).start()
                if classes[cut] != "b":
                    to_z(2, cut).start()
                to_core(2, cut).start()
            gathers(cut, body)
            if cut + look < count:
                own_sends(cut + look)
        past = cut - lag_diag
        if 0 <= past < count:
            def body():
                onward(past).wait_recv()
                if classes[past] != "b":
                    to_z(3, past).start()
                to_core(3, past).start()
            gathers(past, body)
        gone = cut - lag_z
        if 0 <= gone < count:
            def body():
                for kind in (1, 2, 3):
                    to_z(kind, gone).wait_recv()
                    to_core(kind, gone).start()
            receives(gone, body)
        for done in range(count):
            if done not in arrived and cut - done >= (lag_diag + 1 if classes[done] == "b" else lag_z + 1):
                for kind in range(4):
                    to_core(kind, done).wait_recv()
                w_copy(done).start()
                arrived.add(done)

    tasks = []

    def task(need, cost):
        def keep(body):
            tasks.append((need, cost, body))
            return body
        return keep

    def cut_of(key):
        start, width = pieces[key]
        return (start + tiled(width) - 1) // cut_width

    def weights(key, start=0, width=None):
        at, full_width = pieces[key]
        width = tiled(full_width) if width is None else width
        return w[:, :, at + start : at + start + width].reshape(hidden_size, width)

    def bias(key, start=0, width=None):
        at, full_width = bias_rows[key]
        width = hidden_size if width is None else width
        return bias_ref[at + start // hidden_size : at + start // hidden_size + 1, 0:width]

    def over_rows(body):
        def step(k, carry):
            body(pl.ds(pl.multiple_of(k * block, block), block))
            return carry
        lax.fori_loop(0, 2, step, 0)

    def outgoing(src, dst, slot):
        return pltpu.make_async_copy(src, dst, out_sem.at[slot])

    slots = stage.shape[0]
    strip = stage.shape[1]
    strips = total_rows // strip

    def window_copy(k):
        rows = pl.ds(pl.multiple_of(k * strip, strip), strip)
        return pltpu.make_async_copy(windows_ref.at[rows], stage.at[k % slots], win_sem.at[k % slots])

    raw = [
        pltpu.make_async_copy(src, dst, raw_sem.at[k])
        for k, (src, dst) in enumerate(
            ((first_ref, first_s), (hidden_ref, hidden_s), (back_ref, back_s), (fore_ref, fore_s))
        )
    ]
    for copy in raw:
        copy.start()
    for k in range(slots):
        window_copy(k).start()
    targets_copy = pltpu.make_async_copy(targets_ref, tt.at[0:steps_ahead], tt_sem)
    targets_copy.start()

    def pack_piece(key, value):
        start, width = pieces[key]
        if width % 128:
            edge = start + width // 128 * 128
            w[me, :, edge : edge + 128] = jnp.zeros((value.shape[0], 128), low)
        w[me, :, start : start + width] = value.astype(low)

    def pack_stack(stack_id):
        width = pieces[stack_id, "first"][1]
        begin = sum(pieces[earlier, "first"][1] for earlier in range(stack_id))
        pack_piece((stack_id, "first"), first_s[:, begin : begin + width])
        for layer_id in range(3):
            pack_piece((stack_id, layer_id), hidden_s[3 * stack_id + layer_id])
        if stack_id < 2:
            pack_piece((stack_id, "back"), back_s[stack_id])
        width = pieces[stack_id, "fore"][1]
        begin = sum(pieces[earlier, "fore"][1] for earlier in range(stack_id))
        pack_piece((stack_id, "fore"), fore_s[:, begin : begin + width])

    raw[0].wait()
    raw[1].wait()
    raw[2].wait()
    raw[3].wait()
    pack_stack(0)
    pl.semaphore_wait(barrier, 4)
    early = min(look, pieces[1, "first"][0] // cut_width)
    for cut in range(early):
        own_sends(cut)
    pack_stack(1)
    pack_stack(2)
    packed = max(start + tiled(width) for start, width in pieces.values())
    if packed < w.shape[2]:
        w[me, :, packed:] = jnp.zeros((w.shape[1], w.shape[2] - packed), low)
    for cut in range(early, look):
        own_sends(cut)
    bias_ref[...] = jnp.zeros_like(bias_ref)
    for key, (at, width) in bias_rows.items():
        for k in range(0, width, hidden_size):
            flat = spans[key] + k
            todo = min(hidden_size, width - k)
            r, o = flat // hidden_size, flat % hidden_size
            here = min(todo, hidden_size - o)
            bias_ref[at + k // hidden_size : at + k // hidden_size + 1, 0:here] = flat_ref[r : r + 1, o : o + here]
            if here < todo:
                bias_ref[at + k // hidden_size : at + k // hidden_size + 1, here:todo] = flat_ref[r + 1 : r + 2, 0 : todo - here]

    @task(-1, 1.0)
    def _():
        ids = lax.broadcasted_iota(jnp.int32, pool8.shape, 0)
        col = lax.broadcasted_iota(jnp.int32, pool8.shape, 1) * KERNELS[0]
        pool8[...] = jnp.where((ids >= col) & (ids < col + KERNELS[0]), 1.0 / KERNELS[0], 0.0).astype(low)
        ids = lax.broadcasted_iota(jnp.int32, pool4.shape, 0)
        col = lax.broadcasted_iota(jnp.int32, pool4.shape, 1) * KERNELS[1]
        pool4[...] = jnp.where((ids >= col) & (ids < col + KERNELS[1]), 1.0 / KERNELS[1], 0.0).astype(low)
        x[:, whole:] = jnp.zeros((total_rows, wide_length - whole), wide)

    groups = 3
    for group in range(groups):
        @task(-1, 3.0)
        def _(group=group):
            def step(k, carry):
                window_copy(k).wait()
                rows = pl.ds(pl.multiple_of(k * strip, strip), strip)
                value = stage[k % slots]
                center = jnp.sum(value, axis=1, keepdims=True) * (1.0 / length)
                value = value - center
                spread = jnp.sqrt(jnp.sum(value * value, axis=1, keepdims=True) * (1.0 / length) + 1e-05)
                factor = 1.0 / spread
                center_s[rows, :] = center
                scale_s[rows, :] = factor
                value = value * factor
                x[rows, 0:length] = value

                @pl.when(k + slots < strips)
                def _():
                    window_copy(k + slots).start()
                return carry
            lax.fori_loop(group * strips // groups, (group + 1) * strips // groups, step, 0)

    @task(-1, 3.0)
    def _():
        def body(rows):
            for k in range(0, wide_length, 1024):
                width = min(1024, wide_length - k)
                high, rest = parts_low(x[rows, k : k + width])
                pooled = mul(high, pool8[0:width]) + mul(rest, pool8[0:width])
                p0[rows, k // 8 : k // 8 + 128] = pooled.astype(low)
        over_rows(body)
        outgoing(p0, p0_out, 0).start()

    def activate(z, stack_id, j, rows):
        gate = jax.nn.sigmoid(z)
        act = z * gate
        a[j, rows, :] = act.astype(low)
        slope[j % 2, rows, :] = (gate + act * (1.0 - gate)).astype(low)

    def a_copy(stack_id, j):
        return outgoing(a.at[j], a_out.at[stack_id, j], 8 + j)

    def slope_copy(stack_id, j):
        return outgoing(slope.at[j % 2], slope_out.at[stack_id, j], 12 + j % 2)

    def send_layer(stack_id, j):
        a_copy(stack_id, j).start()
        slope_copy(stack_id, j).start()

    def settle_layer(stack_id, j):
        if stack_id > 0:
            a_copy(stack_id - 1, j).wait()
        n = 4 * stack_id + j - 2
        if n >= 0:
            slope_copy(n // 4, n % 4).wait()

    for stack_id in range(3):
        inputs = (p0, p1, x2)[stack_id]

        @task(cut_of((stack_id, "first")), (1.3, 2.2, 6.0)[stack_id])
        def _(stack_id=stack_id, inputs=inputs):
            settle_layer(stack_id, 0)

            def body(rows):
                z = mul(inputs[rows, :], weights((stack_id, "first")), NT) + bias((stack_id, "first"))
                activate(z, stack_id, 0, rows)
            over_rows(body)
            send_layer(stack_id, 0)

        for layer_id in range(3):
            @task(cut_of((stack_id, layer_id)), 1.3)
            def _(stack_id=stack_id, layer_id=layer_id):
                settle_layer(stack_id, layer_id + 1)

                def body(rows):
                    z = mul(a[layer_id, rows, :], weights((stack_id, layer_id))) + bias((stack_id, layer_id))
                    activate(z, stack_id, layer_id + 1, rows)
                over_rows(body)
                send_layer(stack_id, layer_id + 1)

        if stack_id < 2:
            for start, width in tiles:
                need = (pieces[stack_id, "back"][0] + start + width - 1) // cut_width

                @task(need, 1.4 if stack_id else 1.7)
                def _(stack_id=stack_id, start=start, width=width):
                    def body(rows):
                        cols = slice(start, start + width)
                        head = mul(a[3, rows, :], weights((stack_id, "back"), start, width))
                        rest = x[rows, cols] - (head + bias((stack_id, "back"), start, width))
                        if stack_id == 0:
                            x[rows, cols] = rest
                            high, tail = parts_low(rest)
                            pooled = mul(high, pool4[0:width]) + mul(tail, pool4[0:width])
                            p1[rows, start // 4 : start // 4 + 128] = pooled.astype(low)
                        else:
                            x2[rows, cols] = rest.astype(low)
                    over_rows(body)
                    if start + width == wide_length:
                        if stack_id == 0:
                            outgoing(p1, p1_out, 1).start()
                        else:
                            outgoing(x2, x2_out, 2).start()

            @task(cut_of((stack_id, "fore")), 1.5)
            def _(stack_id=stack_id):
                def body(rows):
                    knots = mul(a[3, rows, :], weights((stack_id, "fore"))) + bias((stack_id, "fore"), 0, 128)
                    high, rest = parts_low(knots)
                    ups = slice(128 * stack_id, 128 * stack_id + 128)
                    part = (
                        mul(high, up_high_ref[ups, :]) + mul(rest, up_high_ref[ups, :]) + mul(high, up_low_ref[ups, :])
                    )
                    fc[rows, :] = part if stack_id == 0 else fc[rows, :] + part
                over_rows(body)

    wide_steps = fc.shape[1]
    for start in range(0, wide_steps, 256):
        @task(cut_of((2, "fore")), 2.5)
        def _(start=start):
            if start == 0:
                targets_copy.wait()
                small_ref[...] = jnp.zeros_like(small_ref)
                lines = horizon_ref[...].astype(wide)
                small_ref[2:3, 0:128] = jnp.broadcast_to(jnp.sum(lines, axis=1, keepdims=True), (1, 128))
                horizon_s[...] = jnp.broadcast_to(lines, (8, total_rows)).T
            cols = slice(start, start + 256)
            head = mul(a[3], weights((2, "fore"), start, 256)) + bias_ref[
                bias_rows[2, "fore"][0] + start // hidden_size : bias_rows[2, "fore"][0] + start // hidden_size + 1,
                start % hidden_size : start % hidden_size + 256,
            ]
            goal = jnp.concatenate([tt[start : start + 128, :].T, tt[start + 128 : start + 256, :].T], axis=1)
            goal = (goal - center_s[...]) * scale_s[...]
            step = lax.broadcasted_iota(jnp.int32, (total_rows, 256), 1) + start
            diff = jnp.where(step.astype(wide) < horizon_s[:, 0:1], fc[:, cols] + head - goal, 0.0)
            losses = jnp.sum(diff * diff, axis=0, keepdims=True)
            r = start // hidden_size
            small_ref[r : r + 1, start % hidden_size : start % hidden_size + 256] = losses
            diff = diff * (2.0 * scale)
            high, rest = parts_low(diff)
            g[:, cols] = high
            back = (
                mul(high, up_high_ref[:, cols], NT) + mul(rest, up_high_ref[:, cols], NT) + mul(high, up_low_ref[:, cols], NT)
            )
            dk[...] = back if start == 0 else dk[...] + back
            if start + 256 == wide_steps:
                g[:, wide_steps : wide_steps + 256] = dk[...].astype(low)
                outgoing(g, g_out, 3).start()

    queue = list(tasks)
    last = count + lag_z
    for cut in range(-1, last + 1):
        if cut >= 0:
            pump(cut)
        ready = min((done for done in range(count) if done not in arrived), default=count) - 1
        spent = 0.0
        while queue and queue[0][0] <= ready and (spent < 2.0 or cut == last):
            _, cost, body = queue.pop(0)
            body()
            spent += cost
    for cut in range(count):
        def body():
            to_x(cut).wait_send()
            to_y(cut).wait_send()
            onward(cut).wait_send()
            if classes[cut] != "b":
                for kind in (1, 2, 3):
                    to_z(kind, cut).wait_send()
        gathers(cut, body)
        for kind in range(4):
            to_core(kind, cut).wait_send()
        w_copy(cut).wait()
    outgoing(p0, p0_out, 0).wait()
    outgoing(p1, p1_out, 1).wait()
    outgoing(x2, x2_out, 2).wait()
    outgoing(g, g_out, 3).wait()
    for j in range(4):
        a_copy(2, j).wait()
    for j in (2, 3):
        slope_copy(2, j).wait()


def forward(first, hidden, back, fore, windows, targets, horizon, flat, up_high, up_low, pieces, bias_rows, spans, scale, total):
    low, wide = jnp.bfloat16, jnp.float32
    rows, length = windows.shape
    part, hidden_size = hidden.shape[1:]
    count = total // CHUNK
    wide_length = tiled(length)
    wide_steps = up_high.shape[1]
    p0_width, p1_width = tiled(length // KERNELS[0]), tiled(wide_length // KERNELS[1])
    row_count = -(-max(at - (-width // hidden_size) for at, width in bias_rows.values()) // 8) * 8
    strip = rows // 36
    hbm = pl.BlockSpec(memory_space=pltpu.HBM)
    vmem = pl.BlockSpec(memory_space=pltpu.VMEM)
    dma = pltpu.SemaphoreType.DMA
    shape = jax.ShapeDtypeStruct
    return pl.pallas_call(
        functools.partial(forward_kernel, (pieces, bias_rows, spans, CHUNK, count, scale)),
        out_shape=(
            shape((8, part, total), low),
            shape((3, 4, rows, hidden_size), low),
            shape((3, 4, rows, hidden_size), low),
            shape((rows, p0_width), low),
            shape((rows, p1_width), low),
            shape((rows, wide_length), low),
            shape((rows, wide_steps + 256), low),
            shape((8, hidden_size), wide),
        ),
        in_specs=[hbm] * 6 + [vmem] * 4,
        out_specs=(hbm,) * 7 + (vmem,),
        scratch_shapes=[
            pltpu.VMEM((8, part, total), low),
            pltpu.VMEM((rows, wide_length), wide),
            pltpu.VMEM((3, strip, length), wide),
            pltpu.VMEM((4, rows, hidden_size), low),
            pltpu.VMEM((2, rows, hidden_size), low),
            pltpu.VMEM((rows, p0_width), low),
            pltpu.VMEM((rows, p1_width), low),
            pltpu.VMEM((rows, wide_length), low),
            pltpu.VMEM((rows, wide_steps), wide),
            pltpu.VMEM((wide_steps, rows), wide),
            pltpu.VMEM((rows, wide_steps + 256), low),
            pltpu.VMEM((rows, 256), wide),
            pltpu.VMEM((rows, 1), wide),
            pltpu.VMEM((rows, 1), wide),
            pltpu.VMEM((1024, 128), low),
            pltpu.VMEM((512, 128), low),
            pltpu.VMEM((row_count, hidden_size), wide),
            pltpu.VMEM((rows, 8), wide),
            pltpu.VMEM(first.shape, wide),
            pltpu.VMEM(hidden.shape, wide),
            pltpu.VMEM(back.shape, wide),
            pltpu.VMEM(fore.shape, wide),
            dma((4,)),
            dma((10, count)),
            dma((10, count)),
            dma((3,)),
            dma,
            dma((16,)),
            dma((count,)),
        ],
        compiler_params=pltpu.CompilerParams(
            collective_id=0, has_side_effects=True, vmem_limit_bytes=63 * 1024 * 1024
        ),
        name="forward",
    )(first, hidden, back, fore, windows, targets.T, horizon.reshape(1, rows), flat, up_high, up_low)


def chunk_plan(length, steps_ahead_total, hidden_size):
    where = {}
    tile = hidden_size
    full, rest = tiled(length) // tile, tiled(length) % tile
    steps = tiled(steps_ahead_total)
    where[2, "fore"] = [(0, 0, tile), (1, 0, steps - tile)]
    where[1, "fore"] = [(1, steps - tile, 128)]
    for i in range(3):
        where[2, 2 - i] = [(2 + i, 0, tile)]
    t = 5
    last = t + 2 * full + 3 + 2 + full
    where[2, "first"] = [(t + 2 * k, 0, tile) for k in range(full)] + [(last, 0, rest)]
    where[1, "back"] = [(t + 2 * k + 1, 0, tile) for k in range(full)] + [(last, rest, rest)]
    t += 2 * full
    for i in range(3):
        where[1, 2 - i] = [(t + i, 0, tile)]
    where[1, "first"] = [(t + 3, 0, tile), (t + 4, 0, tile)]
    t += 5
    where[0, "back"] = [(t + k, 0, tile) for k in range(full)] + [(last, 2 * rest, rest)]
    where[0, "fore"] = [(last, 3 * rest, 128)]
    for i in range(3):
        where[0, 2 - i] = [(last + 1 + i, 0, tile)]
    where[0, "first"] = [(last + 4, 0, tile)]
    return where, last + 5


LAGS = (1, 4, 7, 10, 13, 16)


def backward_kernel(
    plan,
    w_ref, a_ref, slope_ref, p0_ref, p1_ref, x2_ref, g_ref, forward_small_ref,
    out_ref, dx_ref, flat_ref, result_ref,
    wh, wf2, wf, w1, wtile, wtail, a4, ah, sl, ytile, x2tail, g, dz, gb, dxb, dxt, da, spread, hold,
    gbuf, from_core, s1, r1, keep, s2, r2, plane, zs, zr, zp_s, zp_r, zl_s, zl_r, final,
    small_s, small_r, small_sum, square_s, square_r,
    wh_sem, wf_sem, wtile_sem, wtail_sem, a4_sem, ah_sem, sl_sem, y_sem, misc_sem, dx_sem,
    core_ss, core_rs, credit, ss1, rs1, ss2, rs2, zss, zrs, pss, prs, lss, lrs, fss, frs, small_ss, small_rs, sq_ss, sq_rs, out_sem,
):
    pieces, bias_rows, spans, scale, count, full = plan
    row, me, core, other, over_x, over_y = places()
    lane = core
    chip, chip_x, chip_y = me // 2, over_x // 2, over_y // 2
    chip_d = chip_x + chip_y - chip
    wide, low = jnp.float32, jnp.bfloat16
    total_rows = a_ref.shape[2]
    tile = a_ref.shape[3]
    rest = x2tail.shape[1]
    upper = row // 2
    z_in = row + 1 - 2 * upper
    is_edge = (row == 0) | (row == 3)
    z_out = (row + 3 + 2 * upper) % 4
    t_hidden1 = 5 + 2 * full
    t_first1 = t_hidden1 + 3
    t_back0 = t_first1 + 2
    t_tail0 = t_back0 + full

    barrier = pltpu.get_barrier_semaphore()
    for peer in range(1, 8):
        pl.semaphore_signal(barrier, inc=1, device_id=(row, (me + peer) % 8), device_id_type=MESH)
    for peer in range(1, 4):
        pl.semaphore_signal(barrier, inc=1, device_id=((row + peer) % 4, me), device_id_type=MESH)

    def local(src, dst, sem):
        return pltpu.make_async_copy(src, dst, sem)

    def w_cols(start, width):
        return w_ref.at[:, :, pl.ds(start, width)]

    def load_g():
        return local(g_ref, g, misc_sem.at[0])

    def load_x2tail():
        return local(x2_ref.at[:, full * tile : full * tile + rest], x2tail, misc_sem.at[1])

    def load_w1():
        return local(w_cols(pieces[1, "first"][0], w1.shape[2]), w1, misc_sem.at[2])

    def load_wf2():
        return local(w_cols(pieces[2, "fore"][0], wf2.shape[2]), wf2, misc_sem.at[3])

    def load_wf(stack_id):
        return local(w_cols(pieces[stack_id, "fore"][0], 128), wf.at[stack_id], wf_sem.at[stack_id])

    tails = ((2, "first"), (1, "back"), (0, "back"))

    def load_wtail(k):
        return local(w_cols(pieces[tails[k]][0] + full * tile, rest), wtail.at[k], wtail_sem.at[k])

    def load_a4(stack_id):
        return local(a_ref.at[stack_id, 3], a4.at[stack_id % 2], a4_sem.at[stack_id])

    def load_wh(i):
        return local(w_cols(pieces[2 - i // 3, 2 - i % 3][0], tile), wh.at[i], wh_sem.at[i])

    def wait_wh(i):
        local(w_cols(0, tile), wh.at[i], wh_sem.at[i]).wait()

    def load_ah(i):
        return local(a_ref.at[2 - i // 3, 2 - i % 3], ah.at[i % 3], ah_sem.at[i % 3])

    def load_sl(q):
        return local(slope_ref.at[2 - q // 4, 3 - q % 4], sl.at[q % 3], sl_sem.at[q % 3])

    def start_y(n):
        @pl.when(n < full)
        def _():
            cols = pl.ds(pl.multiple_of(n * tile, tile), tile)
            local(x2_ref.at[:, cols], ytile.at[n % 2], y_sem.at[n % 2]).start()

        @pl.when((n >= full) & (n < full + 2))
        def _():
            cols = pl.ds(pl.multiple_of((n - full) * tile, tile), tile)
            local(p1_ref.at[:, cols], ytile.at[n % 2], y_sem.at[n % 2]).start()

        @pl.when(n == full + 2)
        def _():
            local(p0_ref, ytile.at[n % 2], y_sem.at[n % 2]).start()

    def wait_y(n):
        local(p0_ref, ytile.at[n % 2], y_sem.at[n % 2]).wait()

    def start_wtile(m):
        def go(key, k):
            cols = pl.multiple_of(pieces[key][0] + k * tile, 128)
            local(w_cols(cols, tile), wtile.at[m % 3], wtile_sem.at[m % 3]).start()

        @pl.when((m < 2 * full) & (m % 2 == 0))
        def _():
            go((2, "first"), m // 2)

        @pl.when((m < 2 * full) & (m % 2 == 1))
        def _():
            go((1, "back"), m // 2)

        @pl.when((m >= 2 * full) & (m < 3 * full))
        def _():
            go((0, "back"), m - 2 * full)

    def wait_wtile(m):
        local(w_cols(0, tile), wtile.at[m % 3], wtile_sem.at[m % 3]).wait()

    def dx_cols(k):
        return dx_ref.at[:, pl.ds(pl.multiple_of(k * tile, tile), tile)]

    def dx_store(k):
        return local(dxb.at[k % 2], dx_cols(k), dx_sem.at[k % 2])

    def dx_load(k):
        return local(dx_cols(k), dxb.at[k % 2], dx_sem.at[k % 2])

    load_g().start()
    load_a4(2).start()
    load_wf2().start()
    for q in range(3):
        load_sl(q).start()
        load_ah(q).start()
        load_wh(q).start()
    for n in range(2):
        start_y(jnp.int32(n))
    for m in range(3):
        start_wtile(jnp.int32(m))
    load_a4(1).start()
    load_x2tail().start()
    for k in range(3):
        load_wtail(k).start()
    load_wf(1).start()
    load_wf(0).start()
    load_w1().start()
    for i in range(3, 9):
        load_wh(i).start()

    def core_copy(t):
        return remote(gbuf.at[t % 3, :, 1 - lane], from_core.at[t % 4], core_ss.at[t % 3], core_rs.at[t % 4], (row, other))

    def first_to(t):
        peer = over_x + t % 2 * (over_y - over_x)
        return remote(s1.at[t % 4], r1.at[t], ss1.at[t % 4], rs1.at[t], (row, peer))

    def second_to(t):
        peer = over_y + t % 2 * (over_x - over_y)
        return remote(s2.at[t % 4], r2.at[t], ss2.at[t % 4], rs2.at[t], (row, peer))

    def z_all(t):
        return remote(zs.at[t % 4], zr.at[t], zss.at[t % 4], zrs.at[t], (z_in, me))

    def z_swap(t):
        return remote(zp_s.at[t % 4], zp_r.at[t], pss.at[t % 4], prs.at[t], (z_in, me))

    def z_low(t):
        return remote(zl_s.at[t % 2], zl_r.at[t % 2], lss.at[t % 2], lrs.at[t % 2], (z_in, me))

    def precise(t):
        return t < 2

    def save_low(t, total, high):
        zl_s[t % 2] = (total - high.astype(wide)).astype(low)

    def z_final(t):
        return remote(final.at[t], final.at[t], fss.at[t], frs.at[t], (z_out, me))

    def emit(t):
        @pl.when(t >= 4)
        def _():
            pl.semaphore_wait(credit, 1)
        core_copy(t).start()

    def guarded(sure, condition, body):
        if sure:
            body()
        else:
            pl.when(condition)(body)

    def stage_one(t, sure):
        core_copy(t).wait_recv()
        guarded(sure, t >= 4, lambda: first_to(t - 4).wait_send())
        odd = t % 2
        for k, c in enumerate((chip_x + odd * (chip_y - chip_x), chip_d)):
            s1[t % 4, k] = (gbuf[t % 3, c, lane] + from_core[t % 4, c]).astype(low)
        first_to(t).start()
        for k, c in enumerate((chip, chip_y + odd * (chip_x - chip_y))):
            keep[t % 8, k] = gbuf[t % 3, c, lane] + from_core[t % 4, c]
        guarded(
            sure,
            t + 4 < count,
            lambda: pl.semaphore_signal(credit, inc=1, device_id=(row, other), device_id_type=MESH),
        )

    def stage_two(t, sure):
        first_to(t).wait_recv()
        guarded(sure, t >= 4, lambda: second_to(t - 4).wait_send())
        s2[t % 4] = (keep[t % 8, 1] + r1[t, 1].astype(wide)).astype(low)
        second_to(t).start()

    def stage_three(t, sure):
        second_to(t).wait_recv()
        plane[t % 8] = keep[t % 8, 0] + r1[t, 0].astype(wide) + r2[t].astype(wide)

    def outer_send(t, sure):
        guarded(sure, t >= 4, lambda: z_all(t - 4).wait_send())
        zs[t % 4] = plane[t % 8].astype(low)
        z_all(t).start()

    def inner_swap(t, sure):
        z_all(t).wait_recv()
        guarded(sure, t >= 4, lambda: z_swap(t - 4).wait_send())
        total = plane[t % 8] + zr[t].astype(wide)
        high = total.astype(low)
        zp_s[t % 4] = high
        pl.when(precise(t))(lambda: save_low(t, total, high))
        z_swap(t).start()
        pl.when(precise(t))(lambda: z_low(t).start())

    def inner_total(t, sure):
        z_swap(t).wait_recv()

        @pl.when(precise(t))
        def _():
            z_low(t).wait_recv()
            here = zp_s[t % 4].astype(wide) + zl_s[t % 2].astype(wide)
            there = zp_r[t].astype(wide) + zl_r[t % 2].astype(wide)
            final[t] = (here + there).astype(low)

        @pl.when(jnp.logical_not(precise(t)))
        def _():
            final[t] = (zp_s[t % 4].astype(wide) + zp_r[t].astype(wide)).astype(low)
        z_final(t).start()

    def outer_total(t, sure):
        z_final(t).wait_recv()

    def stage_last(t, sure):
        local(final.at[t], out_ref.at[t], out_sem.at[t]).start()
        got = final[t].astype(wide)
        got = got * got
        acc = square_s[...]
        for k in range(0, got.shape[0], 8):
            for j in range(0, tile, 128):
                acc = acc + got[k : k + 8, j : j + 128]
        square_s[...] = acc

    def reduce_turn(t, sure):
        def at(lag, stage):
            guarded(sure, (t >= lag) & (t < count + lag), lambda: stage(t - lag, sure))
        at(LAGS[0], stage_one)
        at(LAGS[1], stage_two)
        at(LAGS[2], stage_three)

        @pl.when(is_edge)
        def _():
            at(LAGS[2], outer_send)
            at(LAGS[5], outer_total)

        @pl.when(jnp.logical_not(is_edge))
        def _():
            at(LAGS[3], inner_swap)
            at(LAGS[4], inner_total)
        at(LAGS[5], stage_last)

    def over_rows(body):
        body(slice(None), 0)

    def add_row(r, value, k):
        small_s[0, pl.ds(r, 1), 0 : value.shape[1]] = value

    def column_sums(value):
        return jnp.sum(value.astype(wide), axis=0, keepdims=True)

    def put(t, start, value):
        width = value.shape[1]
        gbuf[t % 3, :, :, :, start : start + width] = value.reshape(4, 2, tile // 8, width)

    def slot_free(t):
        @pl.when(t >= 3)
        def _():
            core_copy(t - 3).wait_send()

    def flat(value):
        return value.reshape(tile, value.shape[-1])

    def settle(q, r):
        load_sl(q).wait()

        def body(rows, k):
            low_dz = (da[rows, :] * sl[q % 3, rows, :].astype(wide)).astype(low)
            dz[rows, :] = low_dz
            add_row(r, column_sums(low_dz), k)
        over_rows(body)

        @pl.when(q + 3 < 12)
        def _():
            load_sl(q + 3).start()

    def fore_two_a(t):
        load_g().wait()
        load_a4(2).wait()
        put(t, 0, mul(a4[0], g[:, 0:tile], TN))
        r = bias_rows[2, "fore"][0]
        small_s[0, r : r + 1, :] = column_sums(g[:, 0:tile])

    def fore_two_b(t):
        width = wf2.shape[2]
        put(t, 0, mul(a4[0], g[:, tile:width], TN))
        load_a4(0).start()
        load_a4(1).wait()
        put(t, width - tile, mul(a4[1], g[:, 896:1024], TN))
        done = width - tile + 128
        gbuf[t % 3, :, :, :, done:] = jnp.zeros((4, 2, tile // 8, tile - done), wide)
        emit(t)
        r = bias_rows[2, "fore"][0]
        small_s[0, r + 1 : r + 2, 0 : width - tile] = column_sums(g[:, tile:width])
        load_wf2().wait()

        def body(rows, k):
            da[rows, :] = mul(g[rows, 0:width], flat(wf2[...]), NT)
        over_rows(body)
        settle(jnp.int32(0), bias_rows[2, 2][0])

    def hidden(t, i):
        load_ah(i).wait()
        slot_free(t)
        wait_wh(i)
        q = i + 1 + i // 3
        load_sl(q).wait()
        r = 4 * (2 - i // 3) + 2 - i % 3
        put(t, 0, mul(ah[i % 3], dz[...], TN))

        def body(rows, k):
            d = mul(dz[rows, :], flat(wh[i]), NT)
            low_dz = (d * sl[q % 3, rows, :].astype(wide)).astype(low)
            dz[rows, :] = low_dz
            add_row(r, column_sums(low_dz), k)
        over_rows(body)
        emit(t)

        @pl.when(i + 3 < 9)
        def _():
            load_ah(i + 3).start()

        @pl.when(q + 3 < 12)
        def _():
            load_sl(q + 3).start()

    def first_two(t, k):
        wait_y(k)
        slot_free(t)
        m = 2 * k
        wait_wtile(m)

        @pl.when(k >= 2)
        def _():
            dx_store(k - 2).wait()
        r = bias_rows[1, "back"][0] + k
        put(t, 0, mul(dz[...], ytile[k % 2], TN))

        def body(rows, b):
            dx = mul(dz[rows, :], flat(wtile[m % 3]))
            dxb[k % 2, rows, :] = dx
            low_gb = (-dx).astype(low)
            gb[rows, :] = low_gb
            add_row(r, column_sums(low_gb), b)
        over_rows(body)
        emit(t)
        start_y(k + 2)
        dx_store(k).start()
        start_wtile(m + 3)

    def back_head(m):
        da[...] = da[...] + mul(gb[...], flat(wtile[m % 3]), NT)

    def clear_da(k):
        @pl.when(k == 0)
        def _():
            da[...] = jnp.zeros(da.shape, wide)

    def back_one(t, k):
        clear_da(k)
        slot_free(t)
        m = 2 * k + 1
        wait_wtile(m)
        put(t, 0, mul(a4[1], gb[...], TN))
        back_head(m)
        emit(t)
        start_wtile(m + 3)
        pl.when(k == full - 1)(tail_one)

    def tail_one():
        load_x2tail().wait()
        for k in range(3):
            load_wtail(k).wait()
        load_wf(1).wait()

        def body(rows, k):
            dx = mul(dz[rows, :], flat(wtail[0]))
            dxt[rows, :] = dx
            low_gb = (-dx).astype(low)
            gb[rows, 0:rest] = low_gb
            add_row(bias_rows[1, "back"][0] + full, column_sums(low_gb), k)
            add_row(bias_rows[1, "fore"][0], column_sums(g[rows, 896:1024]), k)
            da[rows, :] = (
                da[rows, :] + mul(low_gb, flat(wtail[1]), NT) + mul(g[rows, 896:1024], flat(wf[1]), NT)
            )
        over_rows(body)
        hold[:, 0:rest] = mul(dz[...], x2tail[...], TN)
        hold[:, rest : 2 * rest] = mul(a4[1], gb[:, 0:rest], TN)
        for k in (full - 2, full - 1):
            dx_store(jnp.int32(k)).wait()
        for k in range(2):
            dx_load(jnp.int32(k)).start()
        settle(jnp.int32(4), bias_rows[1, 2][0])

    def first_one(t, k):
        wait_y(k)
        slot_free(t)
        put(t, 0, mul(dz[...], ytile[k % 2], TN))
        emit(t)
        start_y(k + 2)

    def pooled_back(rows, cols, width):
        high, tail = parts_low(mul(dz[rows, :], flat(w1[:, :, cols])))
        return mul(high, spread[:, 0:width]) + mul(tail, spread[:, 0:width])

    def back_zero(t, k):
        @pl.when(k == 0)
        def _():
            load_w1().wait()
            load_a4(0).wait()
        dx_load(k).wait()
        clear_da(k)
        slot_free(t)
        m = 2 * full + k
        wait_wtile(m)
        r = bias_rows[0, "back"][0] + k

        def body(rows, b):
            cols = pl.ds(pl.multiple_of(k * 128, 128), 128)
            low_gb = (-(dxb[k % 2, rows, :] + pooled_back(rows, cols, tile))).astype(low)
            gb[rows, :] = low_gb
            add_row(r, column_sums(low_gb), b)
        over_rows(body)
        put(t, 0, mul(a4[0], gb[...], TN))
        back_head(m)
        emit(t)
        start_wtile(m + 3)

        @pl.when(k + 2 < full)
        def _():
            dx_load(k + 2).start()

    def tail_zero(t):
        load_wf(0).wait()

        def body(rows, k):
            low_gb = (-(dxt[rows, :] + pooled_back(rows, slice(full * 128, full * 128 + 128), rest))).astype(low)
            gb[rows, 0:rest] = low_gb
            gb[rows, rest : rest + 128] = g[rows, 768:896]
            add_row(bias_rows[0, "back"][0] + full, column_sums(low_gb), k)
            add_row(bias_rows[0, "fore"][0], column_sums(g[rows, 768:896]), k)
            da[rows, :] = (
                da[rows, :] + mul(low_gb, flat(wtail[2]), NT) + mul(g[rows, 768:896], flat(wf[0]), NT)
            )
        over_rows(body)
        slot_free(t)
        put(t, 0, hold[...])
        put(t, 2 * rest, mul(a4[0], gb[:, 0 : rest + 128], TN))
        emit(t)
        settle(jnp.int32(8), bias_rows[0, 2][0])

    row_pair = row + 1 - 2 * (row % 2)
    row_far = row + 2 - 4 * (row // 2)
    hops = ((row, other), (row, over_x), (row, over_y), (row_pair, me), (row_far, me))

    def small_step(k):
        return remote(small_s.at[k], small_r.at[k], small_ss.at[k], small_rs.at[k], hops[k])

    def small_stage(k):
        if k > 0:
            small_step(k - 1).wait_recv()
            total = small_s[k - 1] + small_r[k - 1]
            if k < len(hops):
                small_s[k] = total
            else:
                small_sum[...] = total
        if k < len(hops):
            small_step(k).start()

    square_s[...] = jnp.zeros_like(square_s)
    small_s[0] = jnp.zeros(small_s.shape[1:], wide)
    extra = small_s.shape[1] - 8
    small_s[0, extra:, :] = forward_small_ref[...]
    ids = lax.broadcasted_iota(jnp.int32, spread.shape, 0) * KERNELS[1]
    col = lax.broadcasted_iota(jnp.int32, spread.shape, 1)
    spread[...] = jnp.where((col >= ids) & (col < ids + KERNELS[1]), 1.0 / KERNELS[1], 0.0).astype(low)

    fore_two_a(0)
    pl.semaphore_wait(barrier, 10)

    def compute(t):
        @pl.when(t < 2)
        def _():
            pl.when(t == 0)(lambda: emit(t))
            pl.when(t == 1)(lambda: fore_two_b(t))

        in_pair = (t >= 5) & (t < t_hidden1)
        in_back = (t >= t_back0) & (t < t_tail0)

        @pl.when(in_pair)
        def _():
            pl.when(t % 2 == 1)(lambda: first_two(t, (t - 5) // 2))
            pl.when(t % 2 == 0)(lambda: back_one(t, (t - 6) // 2))

        pl.when(in_back)(lambda: back_zero(t, t - t_back0))

        @pl.when((t >= 2) & jnp.logical_not(in_pair) & jnp.logical_not(in_back))
        def _():
            @pl.when((t < 5) | ((t >= t_hidden1) & (t < t_first1)) | ((t > t_tail0) & (t < t_tail0 + 4)))
            def _():
                past_one = (t + count - t_hidden1) // count
                past_zero = (t + count - t_tail0) // count
                hidden(t, t - 2 - past_one * (t_hidden1 - 5) - past_zero * (t_tail0 - t_hidden1 - 2))

            pl.when((t >= t_first1) & (t < t_back0))(lambda: first_one(t, t - t_first1 + full))
            pl.when(t == t_tail0)(lambda: tail_zero(t))
            pl.when(t == t_tail0 + 4)(lambda: first_one(t, t - t_tail0 - 4 + full + 2))

    def turn(t, carry):
        pl.when(t < count)(lambda: compute(t))

        @pl.when(t >= count)
        def _():
            for k in range(len(hops) + 1):
                pl.when(t == count + 2 * k)(functools.partial(small_stage, k))
        steady = (t >= LAGS[-1]) & (t < count - 3)
        pl.when(steady)(lambda: reduce_turn(t, True))
        pl.when(jnp.logical_not(steady))(lambda: reduce_turn(t, False))
        return carry

    lax.fori_loop(0, count + LAGS[-1], turn, 0)

    def square_copy(peer):
        return remote(square_s, square_r.at[me], sq_ss.at[peer], sq_rs.at[peer], (row, (me + peer) % 8))

    def square_wait(peer):
        return remote(square_s, square_r.at[(me - peer + 8) % 8], sq_ss.at[peer], sq_rs.at[peer], (row, (me + peer) % 8))

    for peer in range(1, 8):
        square_copy(peer).start()
    square_r[me] = square_s[...]
    for peer in range(1, 8):
        square_wait(peer).wait_recv()
    acc = square_r[0]
    for k in range(1, 8):
        acc = acc + square_r[k]
    tile_rows = small_s.shape[1] - 8
    biases = small_sum[0:tile_rows, :]
    total = jnp.sum(acc, keepdims=True) + jnp.sum(biases * biases, keepdims=True)
    tally = small_sum[tile_rows + 2 : tile_rows + 3, 0:1]
    factor = (1.0 / scale) / tally
    norm = jnp.sqrt(total) * factor
    result_ref[0:1, :] = jnp.broadcast_to(norm, (1, 128))
    loss = jnp.sum(small_sum[tile_rows : tile_rows + 2, :], keepdims=True) / tally
    result_ref[1:2, :] = jnp.broadcast_to(loss, (1, 128))
    result_ref[2:3, :] = jnp.broadcast_to(jnp.minimum(1.0, CLIP_MAX / norm) * factor, (1, 128))
    flat_ref[...] = jnp.zeros_like(flat_ref)
    for key, (at, width) in bias_rows.items():
        for k in range(0, width, tile):
            begin = spans[key] + k
            todo = min(tile, width - k)
            r, o = begin // tile, begin % tile
            here = min(todo, tile - o)
            line = slice(at + k // tile, at + k // tile + 1)
            flat_ref[r : r + 1, o : o + here] = small_sum[line, 0:here]
            if here < todo:
                flat_ref[r + 1 : r + 2, 0 : todo - here] = small_sum[line, here:todo]

    def finish(t, carry):
        @pl.when(t >= count - 3)
        def _():
            core_copy(t).wait_send()

        @pl.when(t >= count - 4)
        def _():
            first_to(t).wait_send()
            second_to(t).wait_send()

            @pl.when(is_edge)
            def _():
                z_all(t).wait_send()

            @pl.when(jnp.logical_not(is_edge))
            def _():
                z_swap(t).wait_send()

        @pl.when(jnp.logical_not(is_edge))
        def _():
            z_final(t).wait_send()
            pl.when(precise(t))(lambda: z_low(t).wait_send())
        local(final.at[t], out_ref.at[t], out_sem.at[t]).wait()
        return carry

    lax.fori_loop(0, count, finish, 0)
    for k in range(len(hops)):
        small_step(k).wait_send()
    for peer in range(1, 8):
        square_copy(peer).wait_send()


def backward(w, a, slope, p0, p1, x2, g, small, pieces, bias_rows, spans, scale, row_count, flat_rows, count):
    low, wide = jnp.bfloat16, jnp.float32
    rows, tile = a.shape[2], a.shape[3]
    part = tile // 8
    full, rest = x2.shape[1] // tile, x2.shape[1] % tile
    wide_steps = g.shape[1] - 256
    small_rows = row_count + 8
    hbm = pl.BlockSpec(memory_space=pltpu.HBM)
    vmem = pl.BlockSpec(memory_space=pltpu.VMEM)
    dma = pltpu.SemaphoreType.DMA
    shape = jax.ShapeDtypeStruct
    return pl.pallas_call(
        functools.partial(backward_kernel, (pieces, bias_rows, spans, scale, count, full)),
        out_shape=(
            shape((count, part, tile), low),
            shape((rows, full * tile), wide),
            shape((flat_rows, tile), wide),
            shape((8, 128), wide),
        ),
        in_specs=[hbm] * 7 + [vmem],
        out_specs=(hbm, hbm, vmem, vmem),
        scratch_shapes=[
            pltpu.VMEM((9, 8, part, tile), low),
            pltpu.VMEM((8, part, wide_steps), low),
            pltpu.VMEM((2, 8, part, 128), low),
            pltpu.VMEM((8, part, p1.shape[1]), low),
            pltpu.VMEM((3, 8, part, tile), low),
            pltpu.VMEM((3, 8, part, rest), low),
            pltpu.VMEM((2, rows, tile), low),
            pltpu.VMEM((3, rows, tile), low),
            pltpu.VMEM((3, rows, tile), low),
            pltpu.VMEM((2, rows, tile), low),
            pltpu.VMEM((rows, rest), low),
            pltpu.VMEM(g.shape, low),
            pltpu.VMEM((rows, tile), low),
            pltpu.VMEM((rows, tile), low),
            pltpu.VMEM((2, rows, tile), wide),
            pltpu.VMEM((rows, rest), wide),
            pltpu.VMEM((rows, tile), wide),
            pltpu.VMEM((128, tile), low),
            pltpu.VMEM((tile, 2 * rest), wide),
            pltpu.VMEM((3, 4, 2, part, tile), wide),
            pltpu.VMEM((4, 4, part, tile), wide),
            pltpu.VMEM((4, 2, part, tile), low),
            pltpu.VMEM((count, 2, part, tile), low),
            pltpu.VMEM((8, 2, part, tile), wide),
            pltpu.VMEM((4, part, tile), low),
            pltpu.VMEM((count, part, tile), low),
            pltpu.VMEM((8, part, tile), wide),
            pltpu.VMEM((4, part, tile), low),
            pltpu.VMEM((count, part, tile), low),
            pltpu.VMEM((4, part, tile), low),
            pltpu.VMEM((count, part, tile), low),
            pltpu.VMEM((2, part, tile), low),
            pltpu.VMEM((2, part, tile), low),
            pltpu.VMEM((count, part, tile), low),
            pltpu.VMEM((5, small_rows, tile), wide),
            pltpu.VMEM((5, small_rows, tile), wide),
            pltpu.VMEM((small_rows, tile), wide),
            pltpu.VMEM((8, 128), wide),
            pltpu.VMEM((8, 8, 128), wide),
            dma((9,)),
            dma((2,)),
            dma((3,)),
            dma((3,)),
            dma((3,)),
            dma((3,)),
            dma((3,)),
            dma((2,)),
            dma((4,)),
            dma((2,)),
            dma((3,)),
            dma((4,)),
            pltpu.SemaphoreType.REGULAR,
            dma((4,)),
            dma((count,)),
            dma((4,)),
            dma((count,)),
            dma((4,)),
            dma((count,)),
            dma((4,)),
            dma((count,)),
            dma((2,)),
            dma((2,)),
            dma((count,)),
            dma((count,)),
            dma((5,)),
            dma((5,)),
            dma((8,)),
            dma((8,)),
            dma((count,)),
        ],
        compiler_params=pltpu.CompilerParams(
            collective_id=1, has_side_effects=True, vmem_limit_bytes=63 * 1024 * 1024
        ),
        name="backward",
    )(w, a, slope, p0, p1, x2, g, small)


def adamw_kernel(
    plan, step_ref, result_ref, grad_ref, *refs,
):
    where, pieces, count = plan
    groups = [refs[3 * k : 3 * k + 3] for k in range(4)]
    outs = [refs[12 + 4 * k : 16 + 4 * k] for k in range(4)]
    held = [refs[28 + 3 * k : 31 + 3 * k] for k in range(4)]
    copies = refs[40:44]
    grads, first_g, fore_g, grad_sem, in_sem, out_sem = refs[44:]
    wide, low = jnp.float32, jnp.bfloat16
    clip = result_ref[2:3, 0:1]
    steps = jnp.full((1, 1), 1.0, wide) * step_ref[0].astype(wide)
    mean_fix = 1.0 / (1.0 - jnp.exp(steps * float(np.log(BETA_ONE))))
    square_fix = 1.0 / (1.0 - jnp.exp(steps * float(np.log(BETA_TWO))))
    tile = grads.shape[2]

    units = [(1, k) for k in range(0, 9, 3)] + [(2, 0), (2, 1), (3, None), (0, None)]

    def view(ref, group, lead):
        if lead is None:
            return ref
        return ref.at[lead : lead + 3] if group == 1 else ref.at[lead]

    loads = []
    for n, (group, lead) in enumerate(units):
        loads.append(
            [
                pltpu.make_async_copy(view(groups[group][k], group, lead), view(held[group][k], group, lead), in_sem.at[n, k])
                for k in range(3)
            ]
        )
    whole = pltpu.make_async_copy(grad_ref, grads, grad_sem)
    whole.start()
    for unit in loads:
        for copy in unit:
            copy.start()
    whole.wait()

    for key_group, target in (("first", first_g), ("fore", fore_g)):
        begin = 0
        for stack_id in range(3):
            done = 0
            width = pieces[stack_id, key_group][1]
            for t, start, size in where[stack_id, key_group]:
                size = min(size, width - done)
                if size > 0:
                    target[:, begin + done : begin + done + size] = grads[t, :, start : start + size].astype(wide)
                done += size
            begin += width

    def update(group, index, grad):
        weight, avg, square = (held[group][k][index] for k in range(3))
        grad = grad * clip
        new_avg = BETA_ONE * avg + (1.0 - BETA_ONE) * grad
        new_sq = BETA_TWO * square + (1.0 - BETA_TWO) * grad * grad
        step = (new_avg * mean_fix) / (jnp.sqrt(new_sq * square_fix) + EPSILON) + DECAY * weight
        new_weight = weight - RATE * step
        held[group][0][index] = new_weight
        held[group][1][index] = new_avg
        held[group][2][index] = new_sq
        copies[group][index] = new_weight.astype(low)

    def rows_of(body, rows=64, step=16):
        def go(k, carry):
            body(pl.ds(pl.multiple_of(k * step, step), step))
            return carry
        lax.fori_loop(0, rows // step, go, 0)

    part = grads.shape[1]
    stores = []
    for n, (group, lead) in enumerate(units):
        for copy in loads[n]:
            copy.wait()
        if group == 1:
            for k in range(lead, lead + 3):
                t = where[k // 3, k % 3][0][0]
                rows_of(lambda rows: update(1, (k, rows), grads[t, rows, :].astype(wide)), part)
        elif group == 2:
            spots = where[lead, "back"]
            length = held[2][0].shape[2]

            def tiles(rows):
                done = 0
                for t, start, size in spots:
                    size = min(size, length - done)
                    update(2, (lead, rows, slice(done, done + size)), grads[t, rows, start : start + size].astype(wide))
                    done += size
            rows_of(tiles, part)
        else:
            target = first_g if group == 0 else fore_g
            rows_of(lambda rows: update(group, (rows,), target[rows, :]), part)
        for k in range(3):
            stores.append(
                pltpu.make_async_copy(view(held[group][k], group, lead), view(outs[group][k], group, lead), out_sem.at[n, k])
            )
        stores.append(
            pltpu.make_async_copy(view(copies[group], group, lead), view(outs[group][3], group, lead), out_sem.at[n, 3])
        )
        for copy in stores[-4:]:
            copy.start()
    for copy in stores:
        copy.wait()


def adamw_all(step_count, result, grads, states, where, pieces):
    low, wide = jnp.bfloat16, jnp.float32
    hbm = pl.BlockSpec(memory_space=pltpu.HBM)
    shape = jax.ShapeDtypeStruct
    shapes = [state[0].shape for state in states]
    dma = pltpu.SemaphoreType.DMA
    return pl.pallas_call(
        functools.partial(adamw_kernel, (where, pieces, grads.shape[0])),
        out_shape=tuple(shape(s, kind) for s in shapes for kind in (wide, wide, wide, low)),
        in_specs=[pl.BlockSpec(memory_space=pltpu.SMEM), pl.BlockSpec(memory_space=pltpu.VMEM)] + [hbm] * 13,
        out_specs=(hbm,) * 16,
        scratch_shapes=[pltpu.VMEM(s, wide) for s in shapes for _ in range(3)]
        + [pltpu.VMEM(s, low) for s in shapes]
        + [
            pltpu.VMEM(grads.shape, low),
            pltpu.VMEM(shapes[0], wide),
            pltpu.VMEM(shapes[3], wide),
            dma,
            dma((7, 3)),
            dma((7, 4)),
        ],
        compiler_params=pltpu.CompilerParams(vmem_limit_bytes=60 * 1024 * 1024),
        name="adamw",
    )(step_count, result, grads, *[array for state in states for array in state])


def fast_body(
    devices,
    windows,
    targets,
    horizon,
    step_count,
    first_w,
    first_w_avg,
    first_w_sq,
    hidden_w,
    hidden_w_avg,
    hidden_w_sq,
    back_w,
    back_w_avg,
    back_w_sq,
    fore_w,
    fore_w_avg,
    fore_w_sq,
    bias_vec,
    bias_avg,
    bias_sq,
):
    length, steps_ahead_total, hidden_size = windows.shape[1], targets.shape[1], hidden_w.shape[-1]
    part = hidden_w.shape[2]
    pieces, total = packing(length, steps_ahead_total, hidden_size)
    rows, row_count = row_plan(length, steps_ahead_total, hidden_size)
    row_count = -(-row_count // 8) * 8
    where, count = chunk_plan(length, steps_ahead_total, hidden_size)
    spans = {}
    cursor = 0
    for key in bias_order(length, steps_ahead_total, hidden_size):
        spans[key] = cursor
        cursor += rows[key][1]
    bias_count = bias_vec.shape[0]
    flat_rows = -(-bias_count // (8 * hidden_size)) * 8
    flat = jnp.pad(bias_vec, (0, flat_rows * hidden_size - bias_count)).reshape(flat_rows, hidden_size)
    ups = np.zeros((256, tiled(steps_ahead_total)), np.float32)
    for stack_id in range(2):
        knots = steps_ahead_total // RATIOS[stack_id]
        ups[128 * stack_id : 128 * stack_id + knots, :steps_ahead_total] = blend_coefficients(steps_ahead_total, knots)
    up_high = ups.astype(jnp.bfloat16)
    up_low = (ups - up_high.astype(np.float32)).astype(jnp.bfloat16)
    scale = 2.0 ** -int(np.ceil(np.log2(devices * windows.shape[0] * steps_ahead_total)))

    def lead(array):
        return array.reshape((-1,) + array.shape[2:]) if array.ndim == 4 else array

    states = (
        (first_w.T, first_w_avg.T, first_w_sq.T),
        (lead(hidden_w), lead(hidden_w_avg), lead(hidden_w_sq)),
        (back_w, back_w_avg, back_w_sq),
        (fore_w, fore_w_avg, fore_w_sq),
    )
    w, a, slope, p0, p1, x2, g, small = forward(
        states[0][0], states[1][0], back_w, fore_w, windows, targets, horizon, flat,
        jnp.asarray(up_high), jnp.asarray(up_low), pieces, rows, spans, scale, total,
    )
    owned, _, flat_grad, result = backward(
        w, a, slope, p0, p1, x2, g, small, pieces, rows, spans, scale, row_count, flat_rows, count
    )
    new = adamw_all(step_count, result, owned, states, where, pieces)
    first_new, hidden_new, back_new, fore_new = (new[4 * k : 4 * k + 4] for k in range(4))
    grad_bias = flat_grad.reshape(-1)[:bias_count] * result[2, 0]
    bias_new = adamw(bias_vec, bias_avg, bias_sq, grad_bias, step_count[0].astype(jnp.float32))
    shape = hidden_w.shape
    first_new = [array.T for array in first_new]
    hidden_new = [array.reshape(shape) for array in hidden_new]
    flat_out = [result[1, 0], result[0, 0]]
    for weight, avg, square, _ in (first_new, hidden_new, back_new, fore_new):
        flat_out += [avg, square, weight]
    flat_out += list(bias_new)
    flat_out += [group[3] for group in (first_new, hidden_new, back_new, fore_new)]
    return tuple(flat_out)


def solution(mesh):
    fast = mesh.shape["fsdp"] == 8 and mesh.shape["dp"] == 4
    step = functools.partial(fast_body, mesh.shape["dp"] * mesh.shape["fsdp"]) if fast else body
    placed = (
        P(("dp", "fsdp"), None),
        P(("dp", "fsdp"), None),
        P(("dp", "fsdp")),
        P(),
        P(None, "fsdp"),
        P(None, "fsdp"),
        P(None, "fsdp"),
        P(None, None, "fsdp", None),
        P(None, None, "fsdp", None),
        P(None, None, "fsdp", None),
        P(None, "fsdp", None),
        P(None, "fsdp", None),
        P(None, "fsdp", None),
        P("fsdp", None),
        P("fsdp", None),
        P("fsdp", None),
        P(),
        P(),
        P(),
    )
    return jax.shard_map(
        step,
        mesh=mesh,
        in_specs=placed,
        out_specs=(
            P(),
            P(),
            P(None, "fsdp"),
            P(None, "fsdp"),
            P(None, "fsdp"),
            P(None, None, "fsdp", None),
            P(None, None, "fsdp", None),
            P(None, None, "fsdp", None),
            P(None, "fsdp", None),
            P(None, "fsdp", None),
            P(None, "fsdp", None),
            P("fsdp", None),
            P("fsdp", None),
            P("fsdp", None),
            P(),
            P(),
            P(),
            P(None, "fsdp"),
            P(None, None, "fsdp", None),
            P(None, "fsdp", None),
            P("fsdp", None),
        ),
        check_vma=False,
    )
```
